32 devices in a mesh: grp: 1, dap: 32 (over z, y, x, core), ch: 1.
Axes of the slice: x: 2, y: 2, z: 4, core: 2. Of those that a mesh axis runs over, the one named last changes fastest.
Arguments:
- pair_act: bfloat16 [128, 128, 128], P(('grp', 'dap')), may hold values from -24 to 24
- out_grad: bfloat16 [128, 128, 128], P(('grp', 'dap'), 'ch'), may hold values from -6 to 6
- residue_mask: int32 [128], P('grp'), may hold values 0 or 1
- ln_in_gain: float32 [128], replicated, may hold values from 0.1 to 1.9
- ln_in_bias: float32 [128], replicated, may hold values from -3 to 3
- w_a_proj: bfloat16 [128, 128], P(None, 'ch'), may hold values from -4 to 4
- w_a_gate: bfloat16 [128, 128], P(None, 'ch'), may hold values from -0.5 to 0.5
- w_b_proj: bfloat16 [128, 128], P(None, 'ch'), may hold values from -0.5 to 0.5
- w_b_gate: bfloat16 [128, 128], P(None, 'ch'), may hold values from -0.5 to 0.5
- w_gate: bfloat16 [128, 128], replicated, may hold values from -0.5 to 0.5
- ln_out_gain: float32 [128], replicated, may hold values from 0.1 to 1.9
- ln_out_bias: float32 [128], replicated, may hold values from -4 to 4
- w_out: bfloat16 [128, 128], replicated, may hold values from -0.5 to 0.5
Outputs:
- pair_grad: bfloat16 [128, 128, 128], P(('grp', 'dap'), 'ch')
The draws below stay inside these ranges and needn't reach their ends.
All inputs are finite; a program needn't handle non-finite values.
Results may differ from the reference program's by a relative error of at most 0.009.
Values may be sent and summed in bfloat16 or wider, within the bound.
No kernel may reach another device: no remote copies, remote signals or barrier semaphores. Data moves between devices by JAX's collectives and lax.ppermute only.
A program may use at most 128 MiB of HBM per device.

```python
import math
import jax
import jax.numpy as jnp
from jax import lax

C = 128
HID = 128
RES = 128


def draw_pair_act(key, part):
    key = jax.random.fold_in(key, 11)
    key_base, key_chan, key_place = jax.random.split(key, 3)
    chan_scale = jnp.exp(jax.random.uniform(key_chan, (C,), jnp.float32, math.log(0.3), math.log(3.0)))
    place_scale = jnp.exp(jax.random.uniform(key_place, (RES, RES, 1), jnp.float32, math.log(0.5), math.log(2.0)))
    base = jnp.clip(jax.random.normal(key_base, (RES, RES, C), jnp.float32), -4.0, 4.0)
    return (base * chan_scale * place_scale).astype(jnp.bfloat16)


def draw_w_a_proj(key, part):
    key = jax.random.fold_in(key, 23)
    key_base, key_cols = jax.random.split(key, 2)
    col_scale = jnp.exp(jax.random.uniform(key_cols, (HID,), jnp.float32, math.log(0.5), math.log(5.0)))
    base = jnp.clip(jax.random.normal(key_base, (C, HID), jnp.float32), -3.0, 3.0)
    return (base * col_scale / math.sqrt(C)).astype(jnp.bfloat16)


def set_ends(entries, key, low, high):
    dims = entries.shape
    index_at = [jax.random.randint(jax.random.fold_in(key, axis), (), 0, dims[axis]) for axis in range(len(dims))]
    entries = entries.at[tuple(index_at)].set(low)
    longest = dims.index(max(dims))
    index_at[longest] = (index_at[longest] + 1) % dims[longest]
    return entries.at[tuple(index_at)].set(high)


def level_of(stream_key, shape, pieces, smallest, largest):
    def one(position, shards_of):
        steps = jax.random.uniform(jax.random.fold_in(jax.random.fold_in(stream_key, 6), position), (shards_of,), jnp.float32, smallest / len(pieces), largest / len(pieces))
        return jnp.repeat(jnp.exp(steps), shape[position] // shards_of).reshape((-1,) + (1,) * (len(shape) - position - 1))

    loudness = one(*pieces[0])
    for cut in pieces[1:]:
        loudness = loudness * one(*cut)
    return loudness


def bell_draw(rng, extent, width, reach, cuts=(), kind=jnp.bfloat16):
    level = level_of(rng, extent, cuts, -0.22, 0.18) if cuts else 1.0
    result = jax.random.normal(rng, extent, jnp.float32) * width * level
    return jnp.minimum(jnp.maximum(result, -reach), reach).astype(kind)


def setup_inputs(seed: int = 0, part: int = 0) -> dict:
    splits = jax.random.split(jax.random.key(seed), 14)
    part_splits = jax.random.split(jax.random.fold_in(splits[13], part), 14)
    pair_act = draw_pair_act(jax.random.fold_in(jax.random.fold_in(splits[13], part), 71), part)
    out_grad = bell_draw(part_splits[1], (RES, RES, C), 1.0, 6.0, ((0, 32),))
    residue_mask = set_ends((jax.random.randint(part_splits[2], (RES,), 0, 8) < 7).astype(jnp.int32), jax.random.fold_in(part_splits[2], 1), 0, 1)
    ln_in_gain = jnp.clip(1.0 + 0.18 * jax.random.normal(splits[3], (C,), jnp.float32), 0.1, 1.9)
    ln_in_bias = bell_draw(splits[4], (C,), 0.5, 3.0, (), jnp.float32)
    w_a_proj = draw_w_a_proj(jax.random.fold_in(splits[13], 71), part)
    w_a_gate = bell_draw(splits[6], (C, HID), C ** -0.5, 0.5)
    w_b_proj = bell_draw(splits[7], (C, HID), C ** -0.5, 0.5)
    w_b_gate = bell_draw(splits[8], (C, HID), C ** -0.5, 0.5)
    w_gate = bell_draw(splits[9], (C, C), C ** -0.5, 0.5)
    ln_out_gain = jnp.clip(1.0 + 0.18 * jax.random.normal(splits[10], (HID,), jnp.float32), 0.1, 1.9)
    ln_out_bias = bell_draw(splits[11], (HID,), 1.0, 4.0, (), jnp.float32)
    w_out = bell_draw(splits[12], (HID, C), HID ** -0.5, 0.5)
    return {"pair_act": pair_act, "out_grad": out_grad, "residue_mask": residue_mask, "ln_in_gain": ln_in_gain, "ln_in_bias": ln_in_bias, "w_a_proj": w_a_proj, "w_a_gate": w_a_gate, "w_b_proj": w_b_proj, "w_b_gate": w_b_gate, "w_gate": w_gate, "ln_out_gain": ln_out_gain, "ln_out_bias": ln_out_bias, "w_out": w_out}


EPSILON = 1e-05

def normalise(values, reduce_dim):
    centre = values - lax.optimization_barrier(jnp.mean(values, axis=reduce_dim, keepdims=True))
    inverse = lax.rsqrt(lax.optimization_barrier(jnp.mean(centre * centre, axis=reduce_dim, keepdims=True)) + EPSILON)
    return (centre * inverse, inverse)

def norm_backward(grad_hat, normed, inverse, reduce_dim):
    mean_grad = lax.optimization_barrier(jnp.mean(grad_hat, axis=reduce_dim, keepdims=True))
    mean_proj = lax.optimization_barrier(jnp.mean(grad_hat * normed, axis=reduce_dim, keepdims=True))
    return inverse * (grad_hat - mean_grad - normed * mean_proj)

def reference(pair_act, out_grad, residue_mask, ln_in_gain, ln_in_bias, w_a_proj, w_a_gate, w_b_proj, w_b_gate, w_gate, ln_out_gain, ln_out_bias, w_out):
    normed_in, rstd_in = normalise(pair_act.astype(jnp.float32), 2)
    pair_norm = (normed_in * ln_in_gain.astype(jnp.float32) + ln_in_bias.astype(jnp.float32)).astype(jnp.bfloat16)
    norm_wide = pair_norm.astype(jnp.float32)
    valid_all = residue_mask.astype(jnp.float32)
    pair_mask = (valid_all[:, None] * valid_all[None, :])[:, :, None]

    def project(weight):
        return jnp.einsum('ikc,ch->ikh', norm_wide, weight.astype(jnp.float32))
    a_proj = project(w_a_proj)
    a_sig = jax.nn.sigmoid(project(w_a_gate))
    b_proj = project(w_b_proj)
    b_sig = jax.nn.sigmoid(project(w_b_gate))
    edge_a = (pair_mask * a_sig * a_proj).astype(jnp.bfloat16)
    edge_b = (pair_mask * b_sig * b_proj).astype(jnp.bfloat16)
    edge_a_wide = edge_a.astype(jnp.float32)
    edge_b_wide = edge_b.astype(jnp.float32)
    tri_sum = jnp.einsum('ikh,jkh->ijh', edge_a_wide, edge_b_wide).astype(jnp.bfloat16)
    normed_out, rstd_out = normalise(tri_sum.astype(jnp.float32), 2)
    gain_out = ln_out_gain.astype(jnp.float32)
    tri_norm = (normed_out * gain_out + ln_out_bias.astype(jnp.float32)).astype(jnp.bfloat16)
    out_wide = w_out.astype(jnp.float32)
    gate_wide = w_gate.astype(jnp.float32)
    proj_out = jnp.einsum('ijh,hc->ijc', tri_norm.astype(jnp.float32), out_wide)
    gate_act = jax.nn.sigmoid(jnp.einsum('ijc,cd->ijd', norm_wide, gate_wide))
    upstream = out_grad.astype(jnp.float32)
    d_proj = (upstream * gate_act).astype(jnp.bfloat16)
    d_gate = (upstream * proj_out * gate_act * (1.0 - gate_act)).astype(jnp.bfloat16)
    d_normed = jnp.einsum('ijc,hc->ijh', d_proj.astype(jnp.float32), out_wide) * gain_out
    d_tri = norm_backward(d_normed, normed_out, rstd_out, 2).astype(jnp.bfloat16)
    d_tri_wide = d_tri.astype(jnp.float32)
    d_edge_a = jnp.einsum('ijh,jkh->ikh', d_tri_wide, edge_b_wide)
    d_edge_b = jnp.einsum('ijh,ikh->jkh', d_tri_wide, edge_a_wide)

    def split_grad(d_edge, sig_val, proj_val):
        masked = d_edge * pair_mask
        return ((masked * sig_val).astype(jnp.bfloat16), (masked * proj_val * sig_val * (1.0 - sig_val)).astype(jnp.bfloat16))
    d_a_proj, d_a_gate = split_grad(d_edge_a, a_sig, a_proj)
    d_b_proj, d_b_gate = split_grad(d_edge_b, b_sig, b_proj)

    def back_project(grad_piece, weight):
        return jnp.einsum('ikh,ch->ikc', grad_piece.astype(jnp.float32), weight.astype(jnp.float32))
    d_pair_norm = back_project(d_a_proj, w_a_proj) + back_project(d_a_gate, w_a_gate)
    d_pair_norm = d_pair_norm + back_project(d_b_proj, w_b_proj) + back_project(d_b_gate, w_b_gate)
    d_pair_norm = d_pair_norm + jnp.einsum('ijd,cd->ijc', d_gate.astype(jnp.float32), gate_wide)
    grad_hat = d_pair_norm * ln_in_gain.astype(jnp.float32)
    return norm_backward(grad_hat, normed_in, rstd_in, 2).astype(jnp.bfloat16)
```

```python
import jax
import jax.numpy as jnp
from jax import lax
from jax.sharding import PartitionSpec as P

EPSILON = 1e-05


def normalise(values, reduce_dim):
    centre = values - jnp.mean(values, axis=reduce_dim, keepdims=True)
    inverse = lax.rsqrt(jnp.mean(centre * centre, axis=reduce_dim, keepdims=True) + EPSILON)
    return (centre * inverse, inverse)


def norm_backward(grad_hat, normed, inverse, reduce_dim):
    mean_grad = jnp.mean(grad_hat, axis=reduce_dim, keepdims=True)
    mean_proj = jnp.mean(grad_hat * normed, axis=reduce_dim, keepdims=True)
    return inverse * (grad_hat - mean_grad - normed * mean_proj)


def on_device(
    dap,
    ch,
    pair_act,
    out_grad,
    residue_mask,
    ln_in_gain,
    ln_in_bias,
    w_a_proj,
    w_a_gate,
    w_b_proj,
    w_b_gate,
    w_gate,
    ln_out_gain,
    ln_out_bias,
    w_out,
):
    own_rows, all_cols = pair_act.shape[:2]
    col_span = out_grad.shape[1]
    hidden_local = w_a_proj.shape[1]
    slice_h = hidden_local // dap
    row_first = lax.axis_index("dap") * own_rows
    col_first = lax.axis_index("ch") * col_span
    normed_in, rstd_in = normalise(pair_act.astype(jnp.float32), 2)
    pair_norm = (normed_in * ln_in_gain + ln_in_bias).astype(jnp.bfloat16)
    valid_all = residue_mask.astype(jnp.float32)
    valid_rows = lax.dynamic_slice_in_dim(valid_all, row_first, own_rows)
    row_mask = (valid_rows[:, None] * valid_all[None, :])[None]
    w_four = jnp.concatenate((w_a_proj, w_a_gate, w_b_proj, w_b_gate), axis=1)
    projected = jnp.einsum("ikc,cg->gik", pair_norm, w_four, preferred_element_type=jnp.float32)
    a_proj = projected[:hidden_local]
    a_sig = jax.nn.sigmoid(projected[hidden_local : 2 * hidden_local])
    b_proj = projected[2 * hidden_local : 3 * hidden_local]
    b_sig = jax.nn.sigmoid(projected[3 * hidden_local :])
    edge_a = (row_mask * a_sig * a_proj).astype(jnp.bfloat16)
    edge_b = (row_mask * b_sig * b_proj).astype(jnp.bfloat16)

    split = (dap, slice_h, own_rows, all_cols)
    edges = jnp.stack((edge_a.reshape(split), edge_b.reshape(split)), axis=1)
    edges = lax.all_to_all(edges, "dap", split_axis=0, concat_axis=0, tiled=True)
    edges = jnp.transpose(edges, (1, 2, 0, 3, 4)).reshape(2, slice_h, dap * own_rows, all_cols)
    a_all, b_all = edges[0], edges[1]
    tri = jnp.einsum("hik,hjk->hij", a_all, b_all, preferred_element_type=jnp.float32).astype(
        jnp.bfloat16
    )
    tri = tri.reshape(slice_h, dap, own_rows, ch, col_span)
    tri = jnp.transpose(tri, (1, 3, 0, 2, 4)).reshape(dap * ch, slice_h, own_rows, col_span)
    tri = lax.all_to_all(tri, ("dap", "ch"), split_axis=0, concat_axis=0, tiled=True)
    tri = tri.reshape(dap, ch, slice_h, own_rows, col_span)
    tri_full = jnp.transpose(tri, (1, 0, 2, 3, 4)).reshape(-1, own_rows, col_span)

    normed_out, rstd_out = normalise(tri_full.astype(jnp.float32), 0)
    gain_out = ln_out_gain.reshape(-1, 1, 1)
    bias_out = ln_out_bias.reshape(-1, 1, 1)
    tri_norm = (normed_out * gain_out + bias_out).astype(jnp.bfloat16)
    proj_out = jnp.einsum("hij,hc->ijc", tri_norm, w_out, preferred_element_type=jnp.float32)
    norm_cols = lax.dynamic_slice_in_dim(pair_norm, col_first, col_span, 1)
    gate_act = jax.nn.sigmoid(
        jnp.einsum("ijc,cd->ijd", norm_cols, w_gate, preferred_element_type=jnp.float32)
    )
    upstream = out_grad.astype(jnp.float32)
    d_proj = (upstream * gate_act).astype(jnp.bfloat16)
    d_gate = (upstream * proj_out * gate_act * (1.0 - gate_act)).astype(jnp.bfloat16)
    d_normed = (
        jnp.einsum("ijc,hc->hij", d_proj, w_out, preferred_element_type=jnp.float32) * gain_out
    )
    d_tri = norm_backward(d_normed, normed_out, rstd_out, 0).astype(jnp.bfloat16)

    d_tri = d_tri.reshape(ch, dap, slice_h, own_rows, col_span)
    d_tri = jnp.transpose(d_tri, (1, 0, 2, 3, 4)).reshape(dap * ch, slice_h, own_rows, col_span)
    d_tri = lax.all_to_all(d_tri, ("dap", "ch"), split_axis=0, concat_axis=0, tiled=True)
    d_tri = d_tri.reshape(dap, ch, slice_h, own_rows, col_span)
    d_tri = jnp.transpose(d_tri, (2, 0, 3, 1, 4)).reshape(slice_h, dap * own_rows, all_cols)
    d_edge_a = jnp.einsum("hij,hjk->hik", d_tri, b_all, preferred_element_type=jnp.float32)
    d_edge_b = jnp.einsum("hij,hik->hjk", d_tri, a_all, preferred_element_type=jnp.float32)
    d_edges = jnp.stack((d_edge_a, d_edge_b)).astype(jnp.bfloat16)
    d_edges = d_edges.reshape(2, slice_h, dap, own_rows, all_cols)
    d_edges = jnp.transpose(d_edges, (2, 0, 1, 3, 4))
    d_edges = lax.all_to_all(d_edges, "dap", split_axis=0, concat_axis=0, tiled=True)
    d_edges = jnp.transpose(d_edges, (1, 0, 2, 3, 4)).reshape(2, hidden_local, own_rows, all_cols)

    def split_grad(d_edge, sig_val, proj_val):
        masked = d_edge * row_mask
        return (
            (masked * sig_val).astype(jnp.bfloat16),
            (masked * proj_val * sig_val * (1.0 - sig_val)).astype(jnp.bfloat16),
        )

    d_four = jnp.concatenate(
        split_grad(d_edges[0].astype(jnp.float32), a_sig, a_proj)
        + split_grad(d_edges[1].astype(jnp.float32), b_sig, b_proj),
        axis=0,
    )
    d_hidden = jnp.einsum("gik,cg->ikc", d_four, w_four, preferred_element_type=jnp.float32)
    if ch > 1:
        d_hidden = lax.psum_scatter(
            d_hidden.astype(jnp.bfloat16), "ch", scatter_dimension=1, tiled=True
        ).astype(jnp.float32)
    d_pair_norm = d_hidden + jnp.einsum(
        "ijd,cd->ijc", d_gate, w_gate, preferred_element_type=jnp.float32
    )
    normed_cols = lax.dynamic_slice_in_dim(normed_in, col_first, col_span, 1)
    rstd_cols = lax.dynamic_slice_in_dim(rstd_in, col_first, col_span, 1)
    grad_hat = d_pair_norm * ln_in_gain
    return norm_backward(grad_hat, normed_cols, rstd_cols, 2).astype(jnp.bfloat16)


def solution(mesh):
    sizes = dict(mesh.shape)

    def program(*args):
        return on_device(sizes["dap"], sizes["ch"], *args)

    in_specs = (
        P(("grp", "dap"), None, None),
        P(("grp", "dap"), "ch", None),
        P("grp"),
        P(),
        P(),
        P(None, "ch"),
        P(None, "ch"),
        P(None, "ch"),
        P(None, "ch"),
        P(),
        P(),
        P(),
        P(),
    )
    out_specs = P(("grp", "dap"), "ch", None)
    return jax.shard_map(
        program, mesh=mesh, in_specs=in_specs, out_specs=out_specs, check_vma=False
    )
```

```python
import jax
import jax.numpy as jnp
from jax import lax
from jax.sharding import PartitionSpec as P

EPSILON = 1e-05


def normalise(values, reduce_dim):
    centre = values - jnp.mean(values, axis=reduce_dim, keepdims=True)
    inverse = lax.rsqrt(jnp.mean(centre * centre, axis=reduce_dim, keepdims=True) + EPSILON)
    return (centre * inverse, inverse)


def norm_backward(grad_hat, normed, inverse, reduce_dim):
    mean_grad = jnp.mean(grad_hat, axis=reduce_dim, keepdims=True)
    mean_proj = jnp.mean(grad_hat * normed, axis=reduce_dim, keepdims=True)
    return inverse * (grad_hat - mean_grad - normed * mean_proj)


def channel_shards(
    dap,
    ch,
    pair_act,
    out_grad,
    residue_mask,
    ln_in_gain,
    ln_in_bias,
    w_a_proj,
    w_a_gate,
    w_b_proj,
    w_b_gate,
    w_gate,
    ln_out_gain,
    ln_out_bias,
    w_out,
):
    own_rows, all_cols = pair_act.shape[:2]
    col_span = out_grad.shape[1]
    hidden_local = w_a_proj.shape[1]
    slice_h = hidden_local // dap
    row_first = lax.axis_index("dap") * own_rows
    col_first = lax.axis_index("ch") * col_span
    normed_in, rstd_in = normalise(pair_act.astype(jnp.float32), 2)
    pair_norm = (normed_in * ln_in_gain + ln_in_bias).astype(jnp.bfloat16)
    valid_all = residue_mask.astype(jnp.float32)
    valid_rows = lax.dynamic_slice_in_dim(valid_all, row_first, own_rows)
    row_mask = (valid_rows[:, None] * valid_all[None, :])[None]
    w_four = jnp.concatenate((w_a_proj, w_a_gate, w_b_proj, w_b_gate), axis=1)
    projected = jnp.einsum("ikc,cg->gik", pair_norm, w_four, preferred_element_type=jnp.float32)
    a_proj = projected[:hidden_local]
    a_sig = jax.nn.sigmoid(projected[hidden_local : 2 * hidden_local])
    b_proj = projected[2 * hidden_local : 3 * hidden_local]
    b_sig = jax.nn.sigmoid(projected[3 * hidden_local :])
    edge_a = (row_mask * a_sig * a_proj).astype(jnp.bfloat16)
    edge_b = (row_mask * b_sig * b_proj).astype(jnp.bfloat16)

    split = (dap, slice_h, own_rows, all_cols)
    edges = jnp.stack((edge_a.reshape(split), edge_b.reshape(split)), axis=1)
    edges = lax.all_to_all(edges, "dap", split_axis=0, concat_axis=0, tiled=True)
    edges = jnp.transpose(edges, (1, 2, 0, 3, 4)).reshape(2, slice_h, dap * own_rows, all_cols)
    a_all, b_all = edges[0], edges[1]
    tri = jnp.einsum("hik,hjk->hij", a_all, b_all, preferred_element_type=jnp.float32).astype(
        jnp.bfloat16
    )
    tri = tri.reshape(slice_h, dap, own_rows, ch, col_span)
    tri = jnp.transpose(tri, (1, 3, 0, 2, 4)).reshape(dap * ch, slice_h, own_rows, col_span)
    tri = lax.all_to_all(tri, ("dap", "ch"), split_axis=0, concat_axis=0, tiled=True)
    tri = tri.reshape(dap, ch, slice_h, own_rows, col_span)
    tri_full = jnp.transpose(tri, (1, 0, 2, 3, 4)).reshape(-1, own_rows, col_span)

    normed_out, rstd_out = normalise(tri_full.astype(jnp.float32), 0)
    gain_out = ln_out_gain.reshape(-1, 1, 1)
    bias_out = ln_out_bias.reshape(-1, 1, 1)
    tri_norm = (normed_out * gain_out + bias_out).astype(jnp.bfloat16)
    proj_out = jnp.einsum("hij,hc->ijc", tri_norm, w_out, preferred_element_type=jnp.float32)
    norm_cols = lax.dynamic_slice_in_dim(pair_norm, col_first, col_span, 1)
    gate_act = jax.nn.sigmoid(
        jnp.einsum("ijc,cd->ijd", norm_cols, w_gate, preferred_element_type=jnp.float32)
    )
    upstream = out_grad.astype(jnp.float32)
    d_proj = (upstream * gate_act).astype(jnp.bfloat16)
    d_gate = (upstream * proj_out * gate_act * (1.0 - gate_act)).astype(jnp.bfloat16)
    d_normed = (
        jnp.einsum("ijc,hc->hij", d_proj, w_out, preferred_element_type=jnp.float32) * gain_out
    )
    d_tri = norm_backward(d_normed, normed_out, rstd_out, 0).astype(jnp.bfloat16)

    d_tri = d_tri.reshape(ch, dap, slice_h, own_rows, col_span)
    d_tri = jnp.transpose(d_tri, (1, 0, 2, 3, 4)).reshape(dap * ch, slice_h, own_rows, col_span)
    d_tri = lax.all_to_all(d_tri, ("dap", "ch"), split_axis=0, concat_axis=0, tiled=True)
    d_tri = d_tri.reshape(dap, ch, slice_h, own_rows, col_span)
    d_tri = jnp.transpose(d_tri, (2, 0, 3, 1, 4)).reshape(slice_h, dap * own_rows, all_cols)
    d_edge_a = jnp.einsum("hij,hjk->hik", d_tri, b_all, preferred_element_type=jnp.float32)
    d_edge_b = jnp.einsum("hij,hik->hjk", d_tri, a_all, preferred_element_type=jnp.float32)
    d_edges = jnp.stack((d_edge_a, d_edge_b)).astype(jnp.bfloat16)
    d_edges = d_edges.reshape(2, slice_h, dap, own_rows, all_cols)
    d_edges = jnp.transpose(d_edges, (2, 0, 1, 3, 4))
    d_edges = lax.all_to_all(d_edges, "dap", split_axis=0, concat_axis=0, tiled=True)
    d_edges = jnp.transpose(d_edges, (1, 0, 2, 3, 4)).reshape(2, hidden_local, own_rows, all_cols)

    def split_grad(d_edge, sig_val, proj_val):
        masked = d_edge * row_mask
        return (
            (masked * sig_val).astype(jnp.bfloat16),
            (masked * proj_val * sig_val * (1.0 - sig_val)).astype(jnp.bfloat16),
        )

    d_four = jnp.concatenate(
        split_grad(d_edges[0].astype(jnp.float32), a_sig, a_proj)
        + split_grad(d_edges[1].astype(jnp.float32), b_sig, b_proj),
        axis=0,
    )
    d_hidden = jnp.einsum("gik,cg->ikc", d_four, w_four, preferred_element_type=jnp.float32)
    if ch > 1:
        d_hidden = lax.psum_scatter(
            d_hidden.astype(jnp.bfloat16), "ch", scatter_dimension=1, tiled=True
        ).astype(jnp.float32)
    d_pair_norm = d_hidden + jnp.einsum(
        "ijd,cd->ijc", d_gate, w_gate, preferred_element_type=jnp.float32
    )
    normed_cols = lax.dynamic_slice_in_dim(normed_in, col_first, col_span, 1)
    rstd_cols = lax.dynamic_slice_in_dim(rstd_in, col_first, col_span, 1)
    grad_hat = d_pair_norm * ln_in_gain
    return norm_backward(grad_hat, normed_cols, rstd_cols, 2).astype(jnp.bfloat16)


def gather_tiles(
    dap,
    pair_act,
    out_grad,
    residue_mask,
    ln_in_gain,
    ln_in_bias,
    w_a_proj,
    w_a_gate,
    w_b_proj,
    w_b_gate,
    w_gate,
    ln_out_gain,
    ln_out_bias,
    w_out,
):
    own, cols, chan = pair_act.shape
    plane = 1 << ((dap.bit_length()) // 2)
    column = dap // plane
    me = lax.axis_index("dap")
    place, level = me % plane, me // plane
    span = plane * own

    def send(value, mask):
        return lax.ppermute(value, "dap", [(i, i ^ mask) for i in range(dap)])

    row_acts = [pair_act] + [send(pair_act, t * plane) for t in range(1, column)]
    col_acts = [pair_act] + [send(pair_act, s) for s in range(1, plane)]
    grads = []
    for t in range(column):
        part = lax.dynamic_slice_in_dim(out_grad, (level ^ t) * span, span, 1)
        grads.append(send(part, t * plane) if t else part)
    upstream = jnp.concatenate(grads, axis=0).astype(jnp.float32)
    row_act = jnp.concatenate(row_acts, axis=0)
    col_act = jnp.concatenate(col_acts, axis=0)
    valid = residue_mask.astype(jnp.float32)
    ids_row = jnp.concatenate([(me ^ (t * plane)) * own + jnp.arange(own) for t in range(column)])
    ids_col = jnp.concatenate([(me ^ s) * own + jnp.arange(own) for s in range(plane)])

    def edges(act, ids, w_proj, w_sig):
        normed, _ = normalise(act.astype(jnp.float32), 2)
        pair_norm = (normed * ln_in_gain + ln_in_bias).astype(jnp.bfloat16)
        proj = jnp.einsum("ikc,ch->hik", pair_norm, w_proj, preferred_element_type=jnp.float32)
        sig = jax.nn.sigmoid(
            jnp.einsum("ikc,ch->hik", pair_norm, w_sig, preferred_element_type=jnp.float32)
        )
        mask = valid[ids][:, None] * valid[None, :]
        return pair_norm, proj, sig, mask, (mask * sig * proj).astype(jnp.bfloat16)

    norm_a, a_proj, a_sig, mask_a, edge_a = edges(row_act, ids_row, w_a_proj, w_a_gate)
    _, b_proj, b_sig, mask_b, edge_b = edges(col_act, ids_col, w_b_proj, w_b_gate)
    order = jnp.bitwise_xor(place, jnp.arange(plane))

    def to_slots(value):
        value = value.reshape(value.shape[0], plane, own, chan)
        return jnp.take(value, order, axis=1).reshape(-1, span, chan)

    tri = jnp.einsum("hik,hjk->hij", edge_a, edge_b, preferred_element_type=jnp.float32)
    normed_out, rstd_out = normalise(tri.astype(jnp.bfloat16).astype(jnp.float32), 0)
    gain_out = ln_out_gain.reshape(-1, 1, 1)
    tri_norm = (normed_out * gain_out + ln_out_bias.reshape(-1, 1, 1)).astype(jnp.bfloat16)
    proj_out = jnp.einsum("hij,hc->ijc", tri_norm, w_out, preferred_element_type=jnp.float32)
    norm_tile = to_slots(lax.dynamic_slice_in_dim(norm_a, level * span, span, 1))
    upstream = to_slots(upstream)
    gate_act = jax.nn.sigmoid(
        jnp.einsum("ijc,cd->ijd", norm_tile, w_gate, preferred_element_type=jnp.float32)
    )
    d_proj = (upstream * gate_act).astype(jnp.bfloat16)
    d_gate = (upstream * proj_out * gate_act * (1.0 - gate_act)).astype(jnp.bfloat16)
    d_normed = (
        jnp.einsum("ijc,hc->hij", d_proj, w_out, preferred_element_type=jnp.float32) * gain_out
    )
    d_tri = norm_backward(d_normed, normed_out, rstd_out, 0).astype(jnp.bfloat16)
    d_edge_a = jnp.einsum("hij,hjk->hik", d_tri, edge_b, preferred_element_type=jnp.float32)
    d_edge_b = jnp.einsum("hij,hik->hjk", d_tri, edge_a, preferred_element_type=jnp.float32)

    def back(d_edge, mask, sig, proj, w_proj, w_sig):
        masked = d_edge * mask * sig
        d_proj_in = masked.astype(jnp.bfloat16)
        d_sig_in = (masked * proj * (1.0 - sig)).astype(jnp.bfloat16)
        both = jnp.concatenate((d_proj_in, d_sig_in), axis=0)
        weights = jnp.concatenate((w_proj, w_sig), axis=1)
        return jnp.einsum("gik,cg->ikc", both, weights, preferred_element_type=jnp.float32)

    share_b = back(d_edge_b, mask_b, b_sig, b_proj, w_b_proj, w_b_gate).astype(jnp.bfloat16)
    share_a = back(d_edge_a, mask_a, a_sig, a_proj, w_a_proj, w_a_gate)
    gate_part = jnp.einsum("ijd,cd->ijc", d_gate, w_gate, preferred_element_type=jnp.float32)
    gate_part = to_slots(gate_part)
    old = lax.dynamic_slice_in_dim(share_a, level * span, span, 1)
    share_a = lax.dynamic_update_slice_in_dim(share_a, old + gate_part, level * span, 1)
    share_a = share_a.astype(jnp.bfloat16)
    total = jnp.zeros(pair_act.shape, jnp.float32)
    for t in range(column):
        part = share_a[t * own : (t + 1) * own]
        total = total + (send(part, t * plane) if t else part).astype(jnp.float32)
    for s in range(plane):
        part = share_b[s * own : (s + 1) * own]
        total = total + (send(part, s) if s else part).astype(jnp.float32)
    normed_in, rstd_in = normalise(pair_act.astype(jnp.float32), 2)
    return norm_backward(total * ln_in_gain, normed_in, rstd_in, 2).astype(jnp.bfloat16)


def solution(mesh):
    sizes = dict(mesh.shape)

    def program(*args):
        if sizes["ch"] == 1 and sizes["dap"] & (sizes["dap"] - 1) == 0:
            return gather_tiles(sizes["dap"], *args)
        return channel_shards(sizes["dap"], sizes["ch"], *args)

    in_specs = (
        P(("grp", "dap"), None, None),
        P(("grp", "dap"), "ch", None),
        P("grp"),
        P(),
        P(),
        P(None, "ch"),
        P(None, "ch"),
        P(None, "ch"),
        P(None, "ch"),
        P(),
        P(),
        P(),
        P(),
    )
    out_specs = P(("grp", "dap"), "ch", None)
    return jax.shard_map(
        program, mesh=mesh, in_specs=in_specs, out_specs=out_specs, check_vma=False
    )
```

```python
import jax
import jax.numpy as jnp
from jax import lax
from jax.sharding import PartitionSpec as P

EPSILON = 1e-05


def normalise(values, reduce_dim):
    centre = values - jnp.mean(values, axis=reduce_dim, keepdims=True)
    inverse = lax.rsqrt(jnp.mean(centre * centre, axis=reduce_dim, keepdims=True) + EPSILON)
    return (centre * inverse, inverse)


def norm_backward(grad_hat, normed, inverse, reduce_dim):
    mean_grad = jnp.mean(grad_hat, axis=reduce_dim, keepdims=True)
    mean_proj = jnp.mean(grad_hat * normed, axis=reduce_dim, keepdims=True)
    return inverse * (grad_hat - mean_grad - normed * mean_proj)


def channel_shards(
    dap,
    ch,
    pair_act,
    out_grad,
    residue_mask,
    ln_in_gain,
    ln_in_bias,
    w_a_proj,
    w_a_gate,
    w_b_proj,
    w_b_gate,
    w_gate,
    ln_out_gain,
    ln_out_bias,
    w_out,
):
    own_rows, all_cols = pair_act.shape[:2]
    col_span = out_grad.shape[1]
    hidden_local = w_a_proj.shape[1]
    slice_h = hidden_local // dap
    row_first = lax.axis_index("dap") * own_rows
    col_first = lax.axis_index("ch") * col_span
    normed_in, rstd_in = normalise(pair_act.astype(jnp.float32), 2)
    pair_norm = (normed_in * ln_in_gain + ln_in_bias).astype(jnp.bfloat16)
    valid_all = residue_mask.astype(jnp.float32)
    valid_rows = lax.dynamic_slice_in_dim(valid_all, row_first, own_rows)
    row_mask = (valid_rows[:, None] * valid_all[None, :])[None]
    w_four = jnp.concatenate((w_a_proj, w_a_gate, w_b_proj, w_b_gate), axis=1)
    projected = jnp.einsum("ikc,cg->gik", pair_norm, w_four, preferred_element_type=jnp.float32)
    a_proj = projected[:hidden_local]
    a_sig = jax.nn.sigmoid(projected[hidden_local : 2 * hidden_local])
    b_proj = projected[2 * hidden_local : 3 * hidden_local]
    b_sig = jax.nn.sigmoid(projected[3 * hidden_local :])
    edge_a = (row_mask * a_sig * a_proj).astype(jnp.bfloat16)
    edge_b = (row_mask * b_sig * b_proj).astype(jnp.bfloat16)

    split = (dap, slice_h, own_rows, all_cols)
    edges = jnp.stack((edge_a.reshape(split), edge_b.reshape(split)), axis=1)
    edges = lax.all_to_all(edges, "dap", split_axis=0, concat_axis=0, tiled=True)
    edges = jnp.transpose(edges, (1, 2, 0, 3, 4)).reshape(2, slice_h, dap * own_rows, all_cols)
    a_all, b_all = edges[0], edges[1]
    tri = jnp.einsum("hik,hjk->hij", a_all, b_all, preferred_element_type=jnp.float32).astype(
        jnp.bfloat16
    )
    tri = tri.reshape(slice_h, dap, own_rows, ch, col_span)
    tri = jnp.transpose(tri, (1, 3, 0, 2, 4)).reshape(dap * ch, slice_h, own_rows, col_span)
    tri = lax.all_to_all(tri, ("dap", "ch"), split_axis=0, concat_axis=0, tiled=True)
    tri = tri.reshape(dap, ch, slice_h, own_rows, col_span)
    tri_full = jnp.transpose(tri, (1, 0, 2, 3, 4)).reshape(-1, own_rows, col_span)

    normed_out, rstd_out = normalise(tri_full.astype(jnp.float32), 0)
    gain_out = ln_out_gain.reshape(-1, 1, 1)
    bias_out = ln_out_bias.reshape(-1, 1, 1)
    tri_norm = (normed_out * gain_out + bias_out).astype(jnp.bfloat16)
    proj_out = jnp.einsum("hij,hc->ijc", tri_norm, w_out, preferred_element_type=jnp.float32)
    norm_cols = lax.dynamic_slice_in_dim(pair_norm, col_first, col_span, 1)
    gate_act = jax.nn.sigmoid(
        jnp.einsum("ijc,cd->ijd", norm_cols, w_gate, preferred_element_type=jnp.float32)
    )
    upstream = out_grad.astype(jnp.float32)
    d_proj = (upstream * gate_act).astype(jnp.bfloat16)
    d_gate = (upstream * proj_out * gate_act * (1.0 - gate_act)).astype(jnp.bfloat16)
    d_normed = (
        jnp.einsum("ijc,hc->hij", d_proj, w_out, preferred_element_type=jnp.float32) * gain_out
    )
    d_tri = norm_backward(d_normed, normed_out, rstd_out, 0).astype(jnp.bfloat16)

    d_tri = d_tri.reshape(ch, dap, slice_h, own_rows, col_span)
    d_tri = jnp.transpose(d_tri, (1, 0, 2, 3, 4)).reshape(dap * ch, slice_h, own_rows, col_span)
    d_tri = lax.all_to_all(d_tri, ("dap", "ch"), split_axis=0, concat_axis=0, tiled=True)
    d_tri = d_tri.reshape(dap, ch, slice_h, own_rows, col_span)
    d_tri = jnp.transpose(d_tri, (2, 0, 3, 1, 4)).reshape(slice_h, dap * own_rows, all_cols)
    d_edge_a = jnp.einsum("hij,hjk->hik", d_tri, b_all, preferred_element_type=jnp.float32)
    d_edge_b = jnp.einsum("hij,hik->hjk", d_tri, a_all, preferred_element_type=jnp.float32)
    d_edges = jnp.stack((d_edge_a, d_edge_b)).astype(jnp.bfloat16)
    d_edges = d_edges.reshape(2, slice_h, dap, own_rows, all_cols)
    d_edges = jnp.transpose(d_edges, (2, 0, 1, 3, 4))
    d_edges = lax.all_to_all(d_edges, "dap", split_axis=0, concat_axis=0, tiled=True)
    d_edges = jnp.transpose(d_edges, (1, 0, 2, 3, 4)).reshape(2, hidden_local, own_rows, all_cols)

    def split_grad(d_edge, sig_val, proj_val):
        masked = d_edge * row_mask
        return (
            (masked * sig_val).astype(jnp.bfloat16),
            (masked * proj_val * sig_val * (1.0 - sig_val)).astype(jnp.bfloat16),
        )

    d_four = jnp.concatenate(
        split_grad(d_edges[0].astype(jnp.float32), a_sig, a_proj)
        + split_grad(d_edges[1].astype(jnp.float32), b_sig, b_proj),
        axis=0,
    )
    d_hidden = jnp.einsum("gik,cg->ikc", d_four, w_four, preferred_element_type=jnp.float32)
    if ch > 1:
        d_hidden = lax.psum_scatter(
            d_hidden.astype(jnp.bfloat16), "ch", scatter_dimension=1, tiled=True
        ).astype(jnp.float32)
    d_pair_norm = d_hidden + jnp.einsum(
        "ijd,cd->ijc", d_gate, w_gate, preferred_element_type=jnp.float32
    )
    normed_cols = lax.dynamic_slice_in_dim(normed_in, col_first, col_span, 1)
    rstd_cols = lax.dynamic_slice_in_dim(rstd_in, col_first, col_span, 1)
    grad_hat = d_pair_norm * ln_in_gain
    return norm_backward(grad_hat, normed_cols, rstd_cols, 2).astype(jnp.bfloat16)


def gather_tiles(
    dap,
    pair_act,
    out_grad,
    residue_mask,
    ln_in_gain,
    ln_in_bias,
    w_a_proj,
    w_a_gate,
    w_b_proj,
    w_b_gate,
    w_gate,
    ln_out_gain,
    ln_out_bias,
    w_out,
):
    own, cols, chan = pair_act.shape
    plane = 1 << ((dap.bit_length()) // 2)
    column = dap // plane
    me = lax.axis_index("dap")
    place, level = me % plane, me // plane
    span = plane * own
    planes = [[p * plane + q for q in range(plane)] for p in range(column)]
    columns = [[p * plane + q for p in range(column)] for q in range(plane)]
    col_act = lax.all_gather(pair_act, "dap", axis_index_groups=planes, tiled=True)
    row_act = lax.all_gather(pair_act, "dap", axis_index_groups=columns, tiled=True)
    upstream = jnp.swapaxes(out_grad.reshape(own, column, span, chan), 0, 1)
    upstream = lax.all_to_all(
        upstream, "dap", split_axis=0, concat_axis=0, axis_index_groups=columns, tiled=True
    )
    upstream = upstream.reshape(column * own, span, chan).astype(jnp.float32)
    valid = residue_mask.astype(jnp.float32)
    ids_row = jnp.concatenate([(p * plane + place) * own + jnp.arange(own) for p in range(column)])
    ids_col = level * span + jnp.arange(span)

    def edges(act, ids, w_proj, w_sig):
        normed, _ = normalise(act.astype(jnp.float32), 2)
        pair_norm = (normed * ln_in_gain + ln_in_bias).astype(jnp.bfloat16)
        proj = jnp.einsum("ikc,ch->hik", pair_norm, w_proj, preferred_element_type=jnp.float32)
        sig = jax.nn.sigmoid(
            jnp.einsum("ikc,ch->hik", pair_norm, w_sig, preferred_element_type=jnp.float32)
        )
        mask = valid[ids][:, None] * valid[None, :]
        return pair_norm, proj, sig, mask, (mask * sig * proj).astype(jnp.bfloat16)

    norm_a, a_proj, a_sig, mask_a, edge_a = edges(row_act, ids_row, w_a_proj, w_a_gate)
    _, b_proj, b_sig, mask_b, edge_b = edges(col_act, ids_col, w_b_proj, w_b_gate)
    tri = jnp.einsum("hik,hjk->hij", edge_a, edge_b, preferred_element_type=jnp.float32)
    normed_out, rstd_out = normalise(tri.astype(jnp.bfloat16).astype(jnp.float32), 0)
    gain_out = ln_out_gain.reshape(-1, 1, 1)
    tri_norm = (normed_out * gain_out + ln_out_bias.reshape(-1, 1, 1)).astype(jnp.bfloat16)
    proj_out = jnp.einsum("hij,hc->ijc", tri_norm, w_out, preferred_element_type=jnp.float32)
    norm_tile = lax.dynamic_slice_in_dim(norm_a, level * span, span, 1)
    gate_act = jax.nn.sigmoid(
        jnp.einsum("ijc,cd->ijd", norm_tile, w_gate, preferred_element_type=jnp.float32)
    )
    d_proj = (upstream * gate_act).astype(jnp.bfloat16)
    d_gate = (upstream * proj_out * gate_act * (1.0 - gate_act)).astype(jnp.bfloat16)
    d_normed = (
        jnp.einsum("ijc,hc->hij", d_proj, w_out, preferred_element_type=jnp.float32) * gain_out
    )
    d_tri = norm_backward(d_normed, normed_out, rstd_out, 0).astype(jnp.bfloat16)
    d_edge_a = jnp.einsum("hij,hjk->hik", d_tri, edge_b, preferred_element_type=jnp.float32)
    d_edge_b = jnp.einsum("hij,hik->hjk", d_tri, edge_a, preferred_element_type=jnp.float32)

    def back(d_edge, mask, sig, proj, w_proj, w_sig):
        masked = d_edge * mask * sig
        d_proj_in = masked.astype(jnp.bfloat16)
        d_sig_in = (masked * proj * (1.0 - sig)).astype(jnp.bfloat16)
        both = jnp.concatenate((d_proj_in, d_sig_in), axis=0)
        weights = jnp.concatenate((w_proj, w_sig), axis=1)
        return jnp.einsum("gik,cg->ikc", both, weights, preferred_element_type=jnp.float32)

    share_b = back(d_edge_b, mask_b, b_sig, b_proj, w_b_proj, w_b_gate).astype(jnp.bfloat16)
    share_a = back(d_edge_a, mask_a, a_sig, a_proj, w_a_proj, w_a_gate)
    gate_part = jnp.einsum("ijd,cd->ijc", d_gate, w_gate, preferred_element_type=jnp.float32)
    old = lax.dynamic_slice_in_dim(share_a, level * span, span, 1)
    share_a = lax.dynamic_update_slice_in_dim(share_a, old + gate_part, level * span, 1)
    share_a = share_a.astype(jnp.bfloat16)
    share_a = lax.all_to_all(
        share_a, "dap", split_axis=0, concat_axis=0, axis_index_groups=columns, tiled=True
    ).reshape(column, *pair_act.shape)
    share_b = lax.all_to_all(
        share_b, "dap", split_axis=0, concat_axis=0, axis_index_groups=planes, tiled=True
    ).reshape(plane, *pair_act.shape)
    total = jnp.sum(share_a.astype(jnp.float32), axis=0)
    total = total + jnp.sum(share_b.astype(jnp.float32), axis=0)
    normed_in, rstd_in = normalise(pair_act.astype(jnp.float32), 2)
    return norm_backward(total * ln_in_gain, normed_in, rstd_in, 2).astype(jnp.bfloat16)


def solution(mesh):
    sizes = dict(mesh.shape)

    def program(*args):
        if sizes["ch"] == 1 and sizes["dap"] & (sizes["dap"] - 1) == 0:
            return gather_tiles(sizes["dap"], *args)
        return channel_shards(sizes["dap"], sizes["ch"], *args)

    in_specs = (
        P(("grp", "dap"), None, None),
        P(("grp", "dap"), "ch", None),
        P("grp"),
        P(),
        P(),
        P(None, "ch"),
        P(None, "ch"),
        P(None, "ch"),
        P(None, "ch"),
        P(),
        P(),
        P(),
        P(),
    )
    out_specs = P(("grp", "dap"), "ch", None)
    return jax.shard_map(
        program, mesh=mesh, in_specs=in_specs, out_specs=out_specs, check_vma=False
    )
```

```python
import functools

import jax
import jax.numpy as jnp
from jax import lax
from jax.experimental import pallas as pl
from jax.experimental.pallas import tpu as pltpu
from jax.sharding import PartitionSpec as P

EPSILON = 1e-05


def normalise(values, reduce_dim):
    centre = values - jnp.mean(values, axis=reduce_dim, keepdims=True)
    inverse = lax.rsqrt(jnp.mean(centre * centre, axis=reduce_dim, keepdims=True) + EPSILON)
    return (centre * inverse, inverse)


def norm_backward(grad_hat, normed, inverse, reduce_dim):
    mean_grad = jnp.mean(grad_hat, axis=reduce_dim, keepdims=True)
    mean_proj = jnp.mean(grad_hat * normed, axis=reduce_dim, keepdims=True)
    return inverse * (grad_hat - mean_grad - normed * mean_proj)


def channel_shards(
    dap,
    ch,
    pair_act,
    out_grad,
    residue_mask,
    ln_in_gain,
    ln_in_bias,
    w_a_proj,
    w_a_gate,
    w_b_proj,
    w_b_gate,
    w_gate,
    ln_out_gain,
    ln_out_bias,
    w_out,
):
    own_rows, all_cols = pair_act.shape[:2]
    col_span = out_grad.shape[1]
    hidden_local = w_a_proj.shape[1]
    slice_h = hidden_local // dap
    row_first = lax.axis_index("dap") * own_rows
    col_first = lax.axis_index("ch") * col_span
    normed_in, rstd_in = normalise(pair_act.astype(jnp.float32), 2)
    pair_norm = (normed_in * ln_in_gain + ln_in_bias).astype(jnp.bfloat16)
    valid_all = residue_mask.astype(jnp.float32)
    valid_rows = lax.dynamic_slice_in_dim(valid_all, row_first, own_rows)
    row_mask = (valid_rows[:, None] * valid_all[None, :])[None]
    w_four = jnp.concatenate((w_a_proj, w_a_gate, w_b_proj, w_b_gate), axis=1)
    projected = jnp.einsum("ikc,cg->gik", pair_norm, w_four, preferred_element_type=jnp.float32)
    a_proj = projected[:hidden_local]
    a_sig = jax.nn.sigmoid(projected[hidden_local : 2 * hidden_local])
    b_proj = projected[2 * hidden_local : 3 * hidden_local]
    b_sig = jax.nn.sigmoid(projected[3 * hidden_local :])
    edge_a = (row_mask * a_sig * a_proj).astype(jnp.bfloat16)
    edge_b = (row_mask * b_sig * b_proj).astype(jnp.bfloat16)

    split = (dap, slice_h, own_rows, all_cols)
    edges = jnp.stack((edge_a.reshape(split), edge_b.reshape(split)), axis=1)
    edges = lax.all_to_all(edges, "dap", split_axis=0, concat_axis=0, tiled=True)
    edges = jnp.transpose(edges, (1, 2, 0, 3, 4)).reshape(2, slice_h, dap * own_rows, all_cols)
    a_all, b_all = edges[0], edges[1]
    tri = jnp.einsum("hik,hjk->hij", a_all, b_all, preferred_element_type=jnp.float32).astype(
        jnp.bfloat16
    )
    tri = tri.reshape(slice_h, dap, own_rows, ch, col_span)
    tri = jnp.transpose(tri, (1, 3, 0, 2, 4)).reshape(dap * ch, slice_h, own_rows, col_span)
    tri = lax.all_to_all(tri, ("dap", "ch"), split_axis=0, concat_axis=0, tiled=True)
    tri = tri.reshape(dap, ch, slice_h, own_rows, col_span)
    tri_full = jnp.transpose(tri, (1, 0, 2, 3, 4)).reshape(-1, own_rows, col_span)

    normed_out, rstd_out = normalise(tri_full.astype(jnp.float32), 0)
    gain_out = ln_out_gain.reshape(-1, 1, 1)
    bias_out = ln_out_bias.reshape(-1, 1, 1)
    tri_norm = (normed_out * gain_out + bias_out).astype(jnp.bfloat16)
    proj_out = jnp.einsum("hij,hc->ijc", tri_norm, w_out, preferred_element_type=jnp.float32)
    norm_cols = lax.dynamic_slice_in_dim(pair_norm, col_first, col_span, 1)
    gate_act = jax.nn.sigmoid(
        jnp.einsum("ijc,cd->ijd", norm_cols, w_gate, preferred_element_type=jnp.float32)
    )
    upstream = out_grad.astype(jnp.float32)
    d_proj = (upstream * gate_act).astype(jnp.bfloat16)
    d_gate = (upstream * proj_out * gate_act * (1.0 - gate_act)).astype(jnp.bfloat16)
    d_normed = (
        jnp.einsum("ijc,hc->hij", d_proj, w_out, preferred_element_type=jnp.float32) * gain_out
    )
    d_tri = norm_backward(d_normed, normed_out, rstd_out, 0).astype(jnp.bfloat16)

    d_tri = d_tri.reshape(ch, dap, slice_h, own_rows, col_span)
    d_tri = jnp.transpose(d_tri, (1, 0, 2, 3, 4)).reshape(dap * ch, slice_h, own_rows, col_span)
    d_tri = lax.all_to_all(d_tri, ("dap", "ch"), split_axis=0, concat_axis=0, tiled=True)
    d_tri = d_tri.reshape(dap, ch, slice_h, own_rows, col_span)
    d_tri = jnp.transpose(d_tri, (2, 0, 3, 1, 4)).reshape(slice_h, dap * own_rows, all_cols)
    d_edge_a = jnp.einsum("hij,hjk->hik", d_tri, b_all, preferred_element_type=jnp.float32)
    d_edge_b = jnp.einsum("hij,hik->hjk", d_tri, a_all, preferred_element_type=jnp.float32)
    d_edges = jnp.stack((d_edge_a, d_edge_b)).astype(jnp.bfloat16)
    d_edges = d_edges.reshape(2, slice_h, dap, own_rows, all_cols)
    d_edges = jnp.transpose(d_edges, (2, 0, 1, 3, 4))
    d_edges = lax.all_to_all(d_edges, "dap", split_axis=0, concat_axis=0, tiled=True)
    d_edges = jnp.transpose(d_edges, (1, 0, 2, 3, 4)).reshape(2, hidden_local, own_rows, all_cols)

    def split_grad(d_edge, sig_val, proj_val):
        masked = d_edge * row_mask
        return (
            (masked * sig_val).astype(jnp.bfloat16),
            (masked * proj_val * sig_val * (1.0 - sig_val)).astype(jnp.bfloat16),
        )

    d_four = jnp.concatenate(
        split_grad(d_edges[0].astype(jnp.float32), a_sig, a_proj)
        + split_grad(d_edges[1].astype(jnp.float32), b_sig, b_proj),
        axis=0,
    )
    d_hidden = jnp.einsum("gik,cg->ikc", d_four, w_four, preferred_element_type=jnp.float32)
    if ch > 1:
        d_hidden = lax.psum_scatter(
            d_hidden.astype(jnp.bfloat16), "ch", scatter_dimension=1, tiled=True
        ).astype(jnp.float32)
    d_pair_norm = d_hidden + jnp.einsum(
        "ijd,cd->ijc", d_gate, w_gate, preferred_element_type=jnp.float32
    )
    normed_cols = lax.dynamic_slice_in_dim(normed_in, col_first, col_span, 1)
    rstd_cols = lax.dynamic_slice_in_dim(rstd_in, col_first, col_span, 1)
    grad_hat = d_pair_norm * ln_in_gain
    return norm_backward(grad_hat, normed_cols, rstd_cols, 2).astype(jnp.bfloat16)


F32 = jnp.float32
BF16 = jnp.bfloat16
SUBLANES = 8


def dot(lhs, rhs, lhs_dim, rhs_dim):
    return lax.dot_general(
        lhs, rhs, (((lhs_dim,), (rhs_dim,)), ((), ())), preferred_element_type=F32
    )


def across(row, count):
    return jnp.transpose(jnp.broadcast_to(row, (count, row.shape[1])))


def normed_rows(act):
    centre = act - jnp.mean(act, axis=1, keepdims=True)
    return centre * lax.rsqrt(jnp.mean(centre * centre, axis=1, keepdims=True) + EPSILON)


def edges_kernel(me_ref, rows_ref, valid_ref, act_ref, gain_ref, bias_ref, wap, wag, wbp, wbg, out_ref, wide):
    own, cols, _ = act_ref.shape
    devices, block, _ = out_ref.shape
    hidden = wap.shape[1]
    half = block // 2
    valid = valid_ref[...].astype(F32)
    for r in range(own):
        normed = normed_rows(act_ref[r].astype(F32))
        pair_norm = (normed * gain_ref[...] + bias_ref[...]).astype(BF16)
        mask = valid * rows_ref[me_ref[0] * own + r].astype(F32)
        for side, (w_proj, w_sig) in enumerate(((wap, wag), (wbp, wbg))):
            proj = dot(w_proj[...], pair_norm, 0, 1)
            sig = jax.nn.sigmoid(dot(w_sig[...], pair_norm, 0, 1))
            wide[side, pl.ds(r, hidden, stride=own), :] = mask * sig * proj
    for side in range(2):
        out_ref[:, side * half : (side + 1) * half, :] = (
            wide[side].reshape(devices, half, cols).astype(BF16)
        )


def gates_kernel(
    me_ref, rows_ref, valid_ref, act_ref, grad_ref, gain_ref, bias_ref, gain_out_ref,
    wap, wag, wbp, wbg, w_gate, w_out, factors, normed_t, rstd_t, gain_t, d_normed, slope,
):
    own, cols, _ = act_ref.shape
    hidden = wap.shape[1]
    valid = valid_ref[...].astype(F32)
    gain = across(gain_ref[...], cols)
    bias = across(bias_ref[...], cols)
    gain_out = across(gain_out_ref[...], cols)
    gain_t[...] = gain
    for r in range(own):
        act = jnp.transpose(act_ref[r].astype(F32))
        centre = act - jnp.mean(act, axis=0, keepdims=True)
        inverse = lax.rsqrt(jnp.mean(centre * centre, axis=0, keepdims=True) + EPSILON)
        normed = centre * inverse
        normed_t[r] = normed
        rstd_t[r] = inverse
        pair_norm = (normed * gain + bias).astype(BF16)
        mask = valid * rows_ref[me_ref[0] * own + r].astype(F32)
        for side, (w_proj, w_sig) in enumerate(((wap, wag), (wbp, wbg))):
            proj = dot(w_proj[...], pair_norm, 0, 0)
            sig = jax.nn.sigmoid(dot(w_sig[...], pair_norm, 0, 0))
            kept = mask * sig
            factors[2 * side, r] = kept
            factors[2 * side + 1, r] = kept * proj * (1.0 - sig)
        gate_act = jax.nn.sigmoid(dot(pair_norm, w_gate[...], 0, 0))
        d_proj = grad_ref[r].astype(F32) * gate_act
        slope[r] = d_proj * (1.0 - gate_act)
        d_normed[pl.ds(r, hidden, stride=own), :] = (
            dot(w_out[...], d_proj.astype(BF16), 1, 1) * gain_out
        )


def triangle_kernel(in_ref, out_ref, a_ref, b_ref, wide, back):
    devices, block, cols = in_ref.shape
    slice_h, rows, _ = a_ref.shape
    half = block // 2
    own = half // slice_h
    for side in range(2):
        wide[side] = (
            in_ref[:, side * half : (side + 1) * half, :].astype(F32).reshape(devices * half, cols)
        )
    for c in range(slice_h):
        for r in range(own):
            at = pl.ds(c * own + r, devices, stride=half)
            a_ref[c, r * devices : (r + 1) * devices, :] = wide[0, at, :].astype(BF16)
            back[pl.ds(r, devices, stride=own), :] = wide[1, at, :]
        b_ref[c] = back[...].astype(BF16)
        tri = dot(a_ref[c], b_ref[c], 1, 1)
        for r in range(own):
            wide[0, pl.ds(c * own + r, devices, stride=half), :] = tri[
                r * devices : (r + 1) * devices
            ]
    out_ref[...] = wide[0].reshape(devices, half, cols).astype(BF16)


def fold(values, own):
    total = jnp.sum(values, axis=0)
    rows = total
    for shift in range(own, SUBLANES, own):
        rows = rows + pltpu.roll(total, shift, 0)
    return rows[None]


def tri_normed(tri_ref, hidden, own):
    cols = tri_ref.shape[-1]
    tri = tri_ref[...].astype(F32).reshape(hidden * own // SUBLANES, SUBLANES, cols)
    centre = tri - fold(tri, own) / hidden
    inverse = lax.rsqrt(fold(centre * centre, own) / hidden + EPSILON)
    return centre * inverse, inverse


def norm_kernel(hidden, tri_ref, grad_ref, out_ref):
    devices, block, cols = tri_ref.shape
    own = devices * block // hidden
    normed, inverse = tri_normed(tri_ref, hidden, own)
    grad = grad_ref[...].reshape(normed.shape)
    mean_grad = fold(grad, own) / hidden
    mean_proj = fold(grad * normed, own) / hidden
    d_tri = inverse * (grad - mean_grad - normed * mean_proj)
    out_ref[...] = d_tri.reshape(devices, block, cols).astype(BF16)


def gate_grad_kernel(tri_ref, slope, gain_ref, bias_ref, w_out, w_gate, out_ref, wide):
    own, cols, _ = slope.shape
    hidden = w_out.shape[0]
    normed, _ = tri_normed(tri_ref, hidden, own)
    wide[...] = normed.reshape(hidden * own, cols)
    gain = across(gain_ref[...], cols)
    bias = across(bias_ref[...], cols)
    for r in range(own):
        tri_norm = (wide[pl.ds(r, hidden, stride=own), :] * gain + bias).astype(BF16)
        proj_out = dot(tri_norm, w_out[...], 0, 0)
        d_gate = (slope[r] * proj_out).astype(BF16)
        out_ref[r] = dot(w_gate[...], d_gate, 1, 1)


def edge_grad_kernel(in_ref, a_ref, b_ref, out_ref, wide, whole):
    devices, block, cols = in_ref.shape
    slice_h, rows, _ = a_ref.shape
    own = block // slice_h
    wide[0] = in_ref[...].astype(F32).reshape(devices * block, cols)
    for c in range(slice_h):
        at = [pl.ds(c * own + r, devices, stride=block) for r in range(own)]
        d_tri = jnp.concatenate([wide[0, at[r], :] for r in range(own)], axis=0).astype(BF16)
        d_a = dot(d_tri, b_ref[c], 1, 0)
        whole[...] = dot(d_tri, a_ref[c], 0, 0)
        for r in range(own):
            wide[1, at[r], :] = d_a[r * devices : (r + 1) * devices]
            wide[2, at[r], :] = whole[pl.ds(r, devices, stride=own), :]
    for side in range(2):
        out_ref[:, side * block : (side + 1) * block, :] = (
            wide[1 + side].reshape(devices, block, cols).astype(BF16)
        )


def input_grad_kernel(in_ref, factors, normed_t, rstd_t, gain_t, gate_part, wap, wag, wbp, wbg, out_ref, wide):
    own, cols, _ = out_ref.shape
    devices, block, _ = in_ref.shape
    hidden = wap.shape[1]
    half = block // 2
    for side in range(2):
        wide[side] = (
            in_ref[:, side * half : (side + 1) * half, :].astype(F32).reshape(devices * half, cols)
        )
    for r in range(own):
        total = gate_part[r]
        for side, (w_proj, w_sig) in enumerate(((wap, wag), (wbp, wbg))):
            d_edge = wide[side, pl.ds(r, hidden, stride=own), :]
            total = total + dot(w_proj[...], (d_edge * factors[2 * side, r]).astype(BF16), 1, 0)
            total = total + dot(w_sig[...], (d_edge * factors[2 * side + 1, r]).astype(BF16), 1, 0)
        grad_hat = total * gain_t[...]
        normed = normed_t[r]
        mean_grad = jnp.mean(grad_hat, axis=0, keepdims=True)
        mean_proj = jnp.mean(grad_hat * normed, axis=0, keepdims=True)
        grad = rstd_t[r] * (grad_hat - mean_grad - normed * mean_proj)
        out_ref[r] = jnp.transpose(grad).astype(BF16)


VMEM = pl.BlockSpec(memory_space=pltpu.VMEM)
SMEM = pl.BlockSpec(memory_space=pltpu.SMEM)


def call(kernel, name, outs, args, scratch=(), scalars=0, flops=0):
    shapes = [jax.ShapeDtypeStruct(shape, dtype) for shape, dtype in outs]
    moved = sum(value.size * value.dtype.itemsize for value in list(args) + shapes)
    result = pl.pallas_call(
        kernel,
        name=name,
        out_shape=shapes,
        in_specs=[SMEM] * scalars + [VMEM] * (len(args) - scalars),
        out_specs=[VMEM] * len(outs),
        scratch_shapes=[pltpu.VMEM(shape, F32) for shape in scratch],
        cost_estimate=pl.CostEstimate(flops=flops, bytes_accessed=moved, transcendentals=0),
        compiler_params=pltpu.CompilerParams(vmem_limit_bytes=32 * 2**20),
    )(*args)
    return result[0] if len(outs) == 1 else result


def kernel_shards(
    dap,
    pair_act,
    out_grad,
    residue_mask,
    ln_in_gain,
    ln_in_bias,
    w_a_proj,
    w_a_gate,
    w_b_proj,
    w_b_gate,
    w_gate,
    ln_out_gain,
    ln_out_bias,
    w_out,
):
    own, cols, chan = pair_act.shape
    hidden = w_a_proj.shape[1]
    slice_h = hidden // dap
    rows = dap * own
    block = slice_h * own
    me = lax.axis_index("dap").reshape(1)
    valid = residue_mask.reshape(1, -1)
    gain_in, bias_in, gain_out, bias_out = (
        value.reshape(1, -1) for value in (ln_in_gain, ln_in_bias, ln_out_gain, ln_out_bias)
    )
    w_edges = (w_a_proj, w_a_gate, w_b_proj, w_b_gate)
    product = 2 * own * cols * chan * hidden

    def exchange(value):
        return lax.all_to_all(value, "dap", split_axis=0, concat_axis=0, tiled=True)

    edges = call(
        edges_kernel,
        "edges",
        [((dap, 2 * block, cols), BF16)],
        (me, residue_mask, valid, pair_act, gain_in, bias_in, *w_edges),
        scratch=[(2, hidden * own, cols)],
        scalars=2,
        flops=4 * product,
    )
    edges = exchange(edges)
    factors, normed_t, rstd_t, gain_t, d_normed, slope = call(
        gates_kernel,
        "gates",
        [
            ((4, own, hidden, cols), F32),
            ((own, chan, cols), F32),
            ((own, 1, cols), F32),
            ((chan, cols), F32),
            ((hidden * own, cols), F32),
            ((own, cols, chan), F32),
        ],
        (me, residue_mask, valid, pair_act, out_grad, gain_in, bias_in, gain_out)
        + (*w_edges, w_gate, w_out),
        scalars=2,
        flops=6 * product,
    )
    tri, edge_a, edge_b = call(
        triangle_kernel,
        "triangle",
        [
            ((dap, block, cols), BF16),
            ((slice_h, rows, cols), BF16),
            ((slice_h, rows, cols), BF16),
        ],
        (edges,),
        scratch=[(2, dap * block, cols), (rows, cols)],
        flops=product,
    )
    tri = exchange(tri)
    d_tri = call(
        functools.partial(norm_kernel, hidden),
        "norm",
        [((dap, block, cols), BF16)],
        (tri, d_normed),
    )
    d_tri = exchange(d_tri)
    gate_part = call(
        gate_grad_kernel,
        "gate_grad",
        [((own, chan, cols), F32)],
        (tri, slope, gain_out, bias_out, w_out, w_gate),
        scratch=[(hidden * own, cols)],
        flops=2 * product,
    )
    d_edges = call(
        edge_grad_kernel,
        "edge_grad",
        [((dap, 2 * block, cols), BF16)],
        (d_tri, edge_a, edge_b),
        scratch=[(3, dap * block, cols), (rows, cols)],
        flops=2 * product,
    )
    d_edges = exchange(d_edges)
    return call(
        input_grad_kernel,
        "input_grad",
        [((own, cols, chan), BF16)],
        (d_edges, factors, normed_t, rstd_t, gain_t, gate_part, *w_edges),
        scratch=[(2, hidden * own, cols)],
        flops=4 * product,
    )


def fits_kernels(dap, ch, pair_act, w_proj):
    own, cols, chan = pair_act.shape
    hidden = w_proj.shape[1]
    block = hidden // dap * own
    return (
        ch == 1
        and hidden % dap == 0
        and own in (1, 2, 4, 8)
        and block % 16 == 0
        and dap % SUBLANES == 0
        and cols == dap * own
        and cols % 128 == chan % 128 == hidden % 128 == 0
    )


def solution(mesh):
    sizes = dict(mesh.shape)

    def program(*args):
        dap, ch = sizes["dap"], sizes["ch"]
        if fits_kernels(dap, ch, args[0], args[5]):
            return kernel_shards(dap, *args)
        return channel_shards(dap, ch, *args)

    in_specs = (
        P(("grp", "dap"), None, None),
        P(("grp", "dap"), "ch", None),
        P("grp"),
        P(),
        P(),
        P(None, "ch"),
        P(None, "ch"),
        P(None, "ch"),
        P(None, "ch"),
        P(),
        P(),
        P(),
        P(),
    )
    out_specs = P(("grp", "dap"), "ch", None)
    return jax.shard_map(
        program, mesh=mesh, in_specs=in_specs, out_specs=out_specs, check_vma=False
    )
```

```python
import functools

import jax
import jax.numpy as jnp
from jax import lax
from jax.experimental import pallas as pl
from jax.experimental.pallas import tpu as pltpu
from jax.sharding import PartitionSpec as P

EPSILON = 1e-05


def normalise(values, reduce_dim):
    centre = values - jnp.mean(values, axis=reduce_dim, keepdims=True)
    inverse = lax.rsqrt(jnp.mean(centre * centre, axis=reduce_dim, keepdims=True) + EPSILON)
    return (centre * inverse, inverse)


def norm_backward(grad_hat, normed, inverse, reduce_dim):
    mean_grad = jnp.mean(grad_hat, axis=reduce_dim, keepdims=True)
    mean_proj = jnp.mean(grad_hat * normed, axis=reduce_dim, keepdims=True)
    return inverse * (grad_hat - mean_grad - normed * mean_proj)


def channel_shards(
    dap,
    ch,
    pair_act,
    out_grad,
    residue_mask,
    ln_in_gain,
    ln_in_bias,
    w_a_proj,
    w_a_gate,
    w_b_proj,
    w_b_gate,
    w_gate,
    ln_out_gain,
    ln_out_bias,
    w_out,
):
    own_rows, all_cols = pair_act.shape[:2]
    col_span = out_grad.shape[1]
    hidden_local = w_a_proj.shape[1]
    slice_h = hidden_local // dap
    row_first = lax.axis_index("dap") * own_rows
    col_first = lax.axis_index("ch") * col_span
    normed_in, rstd_in = normalise(pair_act.astype(jnp.float32), 2)
    pair_norm = (normed_in * ln_in_gain + ln_in_bias).astype(jnp.bfloat16)
    valid_all = residue_mask.astype(jnp.float32)
    valid_rows = lax.dynamic_slice_in_dim(valid_all, row_first, own_rows)
    row_mask = (valid_rows[:, None] * valid_all[None, :])[None]
    w_four = jnp.concatenate((w_a_proj, w_a_gate, w_b_proj, w_b_gate), axis=1)
    projected = jnp.einsum("ikc,cg->gik", pair_norm, w_four, preferred_element_type=jnp.float32)
    a_proj = projected[:hidden_local]
    a_sig = jax.nn.sigmoid(projected[hidden_local : 2 * hidden_local])
    b_proj = projected[2 * hidden_local : 3 * hidden_local]
    b_sig = jax.nn.sigmoid(projected[3 * hidden_local :])
    edge_a = (row_mask * a_sig * a_proj).astype(jnp.bfloat16)
    edge_b = (row_mask * b_sig * b_proj).astype(jnp.bfloat16)

    split = (dap, slice_h, own_rows, all_cols)
    edges = jnp.stack((edge_a.reshape(split), edge_b.reshape(split)), axis=1)
    edges = lax.all_to_all(edges, "dap", split_axis=0, concat_axis=0, tiled=True)
    edges = jnp.transpose(edges, (1, 2, 0, 3, 4)).reshape(2, slice_h, dap * own_rows, all_cols)
    a_all, b_all = edges[0], edges[1]
    tri = jnp.einsum("hik,hjk->hij", a_all, b_all, preferred_element_type=jnp.float32).astype(
        jnp.bfloat16
    )
    tri = tri.reshape(slice_h, dap, own_rows, ch, col_span)
    tri = jnp.transpose(tri, (1, 3, 0, 2, 4)).reshape(dap * ch, slice_h, own_rows, col_span)
    tri = lax.all_to_all(tri, ("dap", "ch"), split_axis=0, concat_axis=0, tiled=True)
    tri = tri.reshape(dap, ch, slice_h, own_rows, col_span)
    tri_full = jnp.transpose(tri, (1, 0, 2, 3, 4)).reshape(-1, own_rows, col_span)

    normed_out, rstd_out = normalise(tri_full.astype(jnp.float32), 0)
    gain_out = ln_out_gain.reshape(-1, 1, 1)
    bias_out = ln_out_bias.reshape(-1, 1, 1)
    tri_norm = (normed_out * gain_out + bias_out).astype(jnp.bfloat16)
    proj_out = jnp.einsum("hij,hc->ijc", tri_norm, w_out, preferred_element_type=jnp.float32)
    norm_cols = lax.dynamic_slice_in_dim(pair_norm, col_first, col_span, 1)
    gate_act = jax.nn.sigmoid(
        jnp.einsum("ijc,cd->ijd", norm_cols, w_gate, preferred_element_type=jnp.float32)
    )
    upstream = out_grad.astype(jnp.float32)
    d_proj = (upstream * gate_act).astype(jnp.bfloat16)
    d_gate = (upstream * proj_out * gate_act * (1.0 - gate_act)).astype(jnp.bfloat16)
    d_normed = (
        jnp.einsum("ijc,hc->hij", d_proj, w_out, preferred_element_type=jnp.float32) * gain_out
    )
    d_tri = norm_backward(d_normed, normed_out, rstd_out, 0).astype(jnp.bfloat16)

    d_tri = d_tri.reshape(ch, dap, slice_h, own_rows, col_span)
    d_tri = jnp.transpose(d_tri, (1, 0, 2, 3, 4)).reshape(dap * ch, slice_h, own_rows, col_span)
    d_tri = lax.all_to_all(d_tri, ("dap", "ch"), split_axis=0, concat_axis=0, tiled=True)
    d_tri = d_tri.reshape(dap, ch, slice_h, own_rows, col_span)
    d_tri = jnp.transpose(d_tri, (2, 0, 3, 1, 4)).reshape(slice_h, dap * own_rows, all_cols)
    d_edge_a = jnp.einsum("hij,hjk->hik", d_tri, b_all, preferred_element_type=jnp.float32)
    d_edge_b = jnp.einsum("hij,hik->hjk", d_tri, a_all, preferred_element_type=jnp.float32)
    d_edges = jnp.stack((d_edge_a, d_edge_b)).astype(jnp.bfloat16)
    d_edges = d_edges.reshape(2, slice_h, dap, own_rows, all_cols)
    d_edges = jnp.transpose(d_edges, (2, 0, 1, 3, 4))
    d_edges = lax.all_to_all(d_edges, "dap", split_axis=0, concat_axis=0, tiled=True)
    d_edges = jnp.transpose(d_edges, (1, 0, 2, 3, 4)).reshape(2, hidden_local, own_rows, all_cols)

    def split_grad(d_edge, sig_val, proj_val):
        masked = d_edge * row_mask
        return (
            (masked * sig_val).astype(jnp.bfloat16),
            (masked * proj_val * sig_val * (1.0 - sig_val)).astype(jnp.bfloat16),
        )

    d_four = jnp.concatenate(
        split_grad(d_edges[0].astype(jnp.float32), a_sig, a_proj)
        + split_grad(d_edges[1].astype(jnp.float32), b_sig, b_proj),
        axis=0,
    )
    d_hidden = jnp.einsum("gik,cg->ikc", d_four, w_four, preferred_element_type=jnp.float32)
    if ch > 1:
        d_hidden = lax.psum_scatter(
            d_hidden.astype(jnp.bfloat16), "ch", scatter_dimension=1, tiled=True
        ).astype(jnp.float32)
    d_pair_norm = d_hidden + jnp.einsum(
        "ijd,cd->ijc", d_gate, w_gate, preferred_element_type=jnp.float32
    )
    normed_cols = lax.dynamic_slice_in_dim(normed_in, col_first, col_span, 1)
    rstd_cols = lax.dynamic_slice_in_dim(rstd_in, col_first, col_span, 1)
    grad_hat = d_pair_norm * ln_in_gain
    return norm_backward(grad_hat, normed_cols, rstd_cols, 2).astype(jnp.bfloat16)


F32 = jnp.float32
BF16 = jnp.bfloat16
SUBLANES = 8


def dot(lhs, rhs, lhs_dim, rhs_dim):
    return lax.dot_general(
        lhs, rhs, (((lhs_dim,), (rhs_dim,)), ((), ())), preferred_element_type=F32
    )


def across(row, count):
    return jnp.transpose(jnp.broadcast_to(row, (count, row.shape[1])))


def normed_rows(act):
    centre = act - jnp.mean(act, axis=1, keepdims=True)
    return centre * lax.rsqrt(jnp.mean(centre * centre, axis=1, keepdims=True) + EPSILON)


def edges_kernel(me_ref, *refs):
    sources, (out_ref, *local), (wide, arrived) = refs[:9], refs[9:19], refs[19:]
    copies = [
        pltpu.make_async_copy(source, target, arrived.at[index])
        for index, (source, target) in enumerate(zip(sources, local))
    ]
    for copy in copies:
        copy.start()
    rows_ref, valid_ref, act_ref, gain_ref, bias_ref, *weights = local
    own, cols, _ = act_ref.shape
    devices, block, _ = out_ref.shape
    hidden = weights[0].shape[1]
    half = block // 2
    for copy in copies:
        copy.wait()
    valid = valid_ref[...].astype(F32)
    for r in range(own):
        normed = normed_rows(act_ref[r].astype(F32))
        pair_norm = (normed * gain_ref[...] + bias_ref[...]).astype(BF16)
        mask = valid * rows_ref[me_ref[0] * own + r].astype(F32)
        for side in range(2):
            proj = dot(weights[2 * side][...], pair_norm, 0, 1)
            sig = jax.nn.sigmoid(dot(weights[2 * side + 1][...], pair_norm, 0, 1))
            wide[side, pl.ds(r, hidden, stride=own), :] = mask * sig * proj
    for side in range(2):
        out_ref[:, side * half : (side + 1) * half, :] = (
            wide[side].reshape(devices, half, cols).astype(BF16)
        )


def gates_kernel(
    me_ref, rows_ref, valid_ref, act_ref, grad_ref, gain_ref, bias_ref, gain_out_ref,
    wap, wag, wbp, wbg, w_gate, w_out, factors, normed_t, rstd_t, gain_t, d_normed, slope,
):
    own, cols, _ = act_ref.shape
    hidden = wap.shape[1]
    valid = valid_ref[...].astype(F32)
    gain = across(gain_ref[...], cols)
    bias = across(bias_ref[...], cols)
    gain_out = across(gain_out_ref[...], cols)
    gain_t[...] = gain
    for r in range(own):
        act = jnp.transpose(act_ref[r].astype(F32))
        centre = act - jnp.mean(act, axis=0, keepdims=True)
        inverse = lax.rsqrt(jnp.mean(centre * centre, axis=0, keepdims=True) + EPSILON)
        normed = centre * inverse
        normed_t[r] = normed
        rstd_t[r] = inverse
        pair_norm = (normed * gain + bias).astype(BF16)
        mask = valid * rows_ref[me_ref[0] * own + r].astype(F32)
        for side, (w_proj, w_sig) in enumerate(((wap, wag), (wbp, wbg))):
            proj = dot(w_proj[...], pair_norm, 0, 0)
            sig = jax.nn.sigmoid(dot(w_sig[...], pair_norm, 0, 0))
            kept = mask * sig
            factors[2 * side, r] = kept
            factors[2 * side + 1, r] = kept * proj * (1.0 - sig)
        gate_act = jax.nn.sigmoid(dot(pair_norm, w_gate[...], 0, 0))
        d_proj = grad_ref[r].astype(F32) * gate_act
        slope[r] = d_proj * (1.0 - gate_act)
        d_normed[pl.ds(r, hidden, stride=own), :] = (
            dot(w_out[...], d_proj.astype(BF16), 1, 1) * gain_out
        )


def same_channel(values, own, block):
    rows, lanes = values.shape
    shape = (1, block, lanes)
    row = lax.broadcasted_iota(jnp.int32, shape, 1) % block // own
    lane = lax.broadcasted_iota(jnp.int32, shape, 2) % block // own
    kept = jnp.where(row == lane, values.reshape(rows // block, block, lanes), 0.0)
    return kept.reshape(rows, lanes).astype(BF16)


def spread(devices, own, block):
    shape = (devices * block, devices * own)
    row = lax.broadcasted_iota(jnp.int32, shape, 0)
    lane = lax.broadcasted_iota(jnp.int32, shape, 1)
    return jnp.where(row // block * own + row % own == lane, 1.0, 0.0).astype(BF16)


def side_of(edges_ref, side):
    devices, block, cols = edges_ref.shape
    half = block // 2
    return edges_ref[:, side * half : (side + 1) * half, :].reshape(devices * half, cols)


def triangle_kernel(own, edges_ref, out_ref):
    devices, block, cols = out_ref.shape
    pairs = same_channel(dot(side_of(edges_ref, 0), side_of(edges_ref, 1), 1, 1), own, block)
    tri = dot(pairs, spread(devices, own, block), 1, 0)
    out_ref[...] = tri.reshape(devices, block, cols).astype(BF16)


def fold(values, own):
    total = jnp.sum(values, axis=0)
    rows = total
    for shift in range(own, SUBLANES, own):
        rows = rows + pltpu.roll(total, shift, 0)
    return rows[None]


def tri_normed(tri_ref, hidden, own):
    cols = tri_ref.shape[-1]
    tri = tri_ref[...].astype(F32).reshape(hidden * own // SUBLANES, SUBLANES, cols)
    centre = tri - fold(tri, own) / hidden
    inverse = lax.rsqrt(fold(centre * centre, own) / hidden + EPSILON)
    return centre * inverse, inverse


def norm_kernel(hidden, tri_ref, grad_ref, out_ref):
    devices, block, cols = tri_ref.shape
    own = devices * block // hidden
    normed, inverse = tri_normed(tri_ref, hidden, own)
    grad = grad_ref[...].reshape(normed.shape)
    mean_grad = fold(grad, own) / hidden
    mean_proj = fold(grad * normed, own) / hidden
    d_tri = inverse * (grad - mean_grad - normed * mean_proj)
    out_ref[...] = d_tri.reshape(devices, block, cols).astype(BF16)


def gate_grad_kernel(tri_ref, slope, gain_ref, bias_ref, w_out, w_gate, out_ref, wide):
    own, cols, _ = slope.shape
    hidden = w_out.shape[0]
    normed, _ = tri_normed(tri_ref, hidden, own)
    wide[...] = normed.reshape(hidden * own, cols)
    gain = across(gain_ref[...], cols)
    bias = across(bias_ref[...], cols)
    for r in range(own):
        tri_norm = (wide[pl.ds(r, hidden, stride=own), :] * gain + bias).astype(BF16)
        proj_out = dot(tri_norm, w_out[...], 0, 0)
        d_gate = (slope[r] * proj_out).astype(BF16)
        out_ref[r] = dot(w_gate[...], d_gate, 1, 1)


def edge_grad_kernel(own, tri_ref, edges_ref, out_ref):
    devices, block, cols = tri_ref.shape
    d_tri = tri_ref[...].reshape(devices * block, cols)
    columns = spread(devices, own, block)
    d_a = dot(same_channel(dot(d_tri, columns, 1, 1), own, block), side_of(edges_ref, 1), 1, 0)
    d_b = dot(same_channel(dot(columns, d_tri, 1, 1), own, block), side_of(edges_ref, 0), 1, 0)
    for side, grad in enumerate((d_a, d_b)):
        out_ref[:, side * block : (side + 1) * block, :] = (
            grad.reshape(devices, block, cols).astype(BF16)
        )


def input_grad_kernel(in_ref, factors, normed_t, rstd_t, gain_t, gate_part, wap, wag, wbp, wbg, out_ref, wide):
    own, cols, _ = out_ref.shape
    devices, block, _ = in_ref.shape
    hidden = wap.shape[1]
    half = block // 2
    for side in range(2):
        wide[side] = (
            in_ref[:, side * half : (side + 1) * half, :].astype(F32).reshape(devices * half, cols)
        )
    for r in range(own):
        total = gate_part[r]
        for side, (w_proj, w_sig) in enumerate(((wap, wag), (wbp, wbg))):
            d_edge = wide[side, pl.ds(r, hidden, stride=own), :]
            total = total + dot(w_proj[...], (d_edge * factors[2 * side, r]).astype(BF16), 1, 0)
            total = total + dot(w_sig[...], (d_edge * factors[2 * side + 1, r]).astype(BF16), 1, 0)
        grad_hat = total * gain_t[...]
        normed = normed_t[r]
        mean_grad = jnp.mean(grad_hat, axis=0, keepdims=True)
        mean_proj = jnp.mean(grad_hat * normed, axis=0, keepdims=True)
        grad = rstd_t[r] * (grad_hat - mean_grad - normed * mean_proj)
        out_ref[r] = jnp.transpose(grad).astype(BF16)


VMEM = pl.BlockSpec(memory_space=pltpu.VMEM)
SMEM = pl.BlockSpec(memory_space=pltpu.SMEM)
HBM = pl.BlockSpec(memory_space=pltpu.HBM)


def call(kernel, name, outs, args, scratch=(), scalars=0, flops=0, space=VMEM):
    shapes = [jax.ShapeDtypeStruct(shape, dtype) for shape, dtype in outs]
    moved = sum(value.size * value.dtype.itemsize for value in list(args) + shapes)
    result = pl.pallas_call(
        kernel,
        name=name,
        out_shape=shapes,
        in_specs=[SMEM] * scalars + [space] * (len(args) - scalars),
        out_specs=[VMEM] * len(outs),
        scratch_shapes=scratch,
        cost_estimate=pl.CostEstimate(flops=flops, bytes_accessed=moved, transcendentals=0),
        compiler_params=pltpu.CompilerParams(vmem_limit_bytes=32 * 2**20),
    )(*args)
    return result[0] if len(outs) == 1 else result


def kernel_shards(
    dap,
    pair_act,
    out_grad,
    residue_mask,
    ln_in_gain,
    ln_in_bias,
    w_a_proj,
    w_a_gate,
    w_b_proj,
    w_b_gate,
    w_gate,
    ln_out_gain,
    ln_out_bias,
    w_out,
):
    own, cols, chan = pair_act.shape
    hidden = w_a_proj.shape[1]
    slice_h = hidden // dap
    block = slice_h * own
    me = lax.axis_index("dap").reshape(1)
    valid = residue_mask.reshape(1, -1)
    gain_in, bias_in, gain_out, bias_out = (
        value.reshape(1, -1) for value in (ln_in_gain, ln_in_bias, ln_out_gain, ln_out_bias)
    )
    w_edges = (w_a_proj, w_a_gate, w_b_proj, w_b_gate)
    product = 2 * own * cols * chan * hidden

    def exchange(value):
        return lax.all_to_all(value, "dap", split_axis=0, concat_axis=0, tiled=True)

    first = (residue_mask, valid, pair_act, gain_in, bias_in, *w_edges)
    edges = call(
        edges_kernel,
        "edges",
        [((dap, 2 * block, cols), BF16)],
        (me, *first),
        scratch=[
            (pltpu.VMEM if index else pltpu.SMEM)(value.shape, value.dtype)
            for index, value in enumerate(first)
        ]
        + [pltpu.VMEM((2, hidden * own, cols), F32), pltpu.SemaphoreType.DMA((len(first),))],
        scalars=1,
        flops=4 * product,
        space=HBM,
    )
    edges = exchange(edges)
    factors, normed_t, rstd_t, gain_t, d_normed, slope = call(
        gates_kernel,
        "gates",
        [
            ((4, own, hidden, cols), F32),
            ((own, chan, cols), F32),
            ((own, 1, cols), F32),
            ((chan, cols), F32),
            ((hidden * own, cols), F32),
            ((own, cols, chan), F32),
        ],
        (me, residue_mask, valid, pair_act, out_grad, gain_in, bias_in, gain_out)
        + (*w_edges, w_gate, w_out),
        scalars=2,
        flops=6 * product,
    )
    tri = call(
        functools.partial(triangle_kernel, own),
        "triangle",
        [((dap, block, cols), BF16)],
        (edges,),
        flops=8 * product,
    )
    tri = exchange(tri)
    d_tri = call(
        functools.partial(norm_kernel, hidden),
        "norm",
        [((dap, block, cols), BF16)],
        (tri, d_normed),
    )
    d_tri = exchange(d_tri)
    gate_part = call(
        gate_grad_kernel,
        "gate_grad",
        [((own, chan, cols), F32)],
        (tri, slope, gain_out, bias_out, w_out, w_gate),
        scratch=[pltpu.VMEM((hidden * own, cols), F32)],
        flops=2 * product,
    )
    d_edges = call(
        functools.partial(edge_grad_kernel, own),
        "edge_grad",
        [((dap, 2 * block, cols), BF16)],
        (d_tri, edges),
        flops=16 * product,
    )
    d_edges = exchange(d_edges)
    return call(
        input_grad_kernel,
        "input_grad",
        [((own, cols, chan), BF16)],
        (d_edges, factors, normed_t, rstd_t, gain_t, gate_part, *w_edges),
        scratch=[pltpu.VMEM((2, hidden * own, cols), F32)],
        flops=4 * product,
    )


def fits_kernels(dap, ch, pair_act, w_proj):
    own, cols, chan = pair_act.shape
    hidden = w_proj.shape[1]
    block = hidden // dap * own
    return (
        ch == 1
        and hidden % dap == 0
        and own in (1, 2, 4, 8)
        and block % 16 == 0
        and dap % SUBLANES == 0
        and cols == dap * own
        and cols % 128 == chan % 128 == hidden % 128 == 0
    )


def solution(mesh):
    sizes = dict(mesh.shape)

    def program(*args):
        dap, ch = sizes["dap"], sizes["ch"]
        if fits_kernels(dap, ch, args[0], args[5]):
            return kernel_shards(dap, *args)
        return channel_shards(dap, ch, *args)

    in_specs = (
        P(("grp", "dap"), None, None),
        P(("grp", "dap"), "ch", None),
        P("grp"),
        P(),
        P(),
        P(None, "ch"),
        P(None, "ch"),
        P(None, "ch"),
        P(None, "ch"),
        P(),
        P(),
        P(),
        P(),
    )
    out_specs = P(("grp", "dap"), "ch", None)
    return jax.shard_map(
        program, mesh=mesh, in_specs=in_specs, out_specs=out_specs, check_vma=False
    )
```

```python
import functools

import jax
import jax.numpy as jnp
from jax import lax
from jax.experimental import pallas as pl
from jax.experimental.pallas import tpu as pltpu
from jax.sharding import PartitionSpec as P

EPSILON = 1e-05


def normalise(values, reduce_dim):
    centre = values - jnp.mean(values, axis=reduce_dim, keepdims=True)
    inverse = lax.rsqrt(jnp.mean(centre * centre, axis=reduce_dim, keepdims=True) + EPSILON)
    return (centre * inverse, inverse)


def norm_backward(grad_hat, normed, inverse, reduce_dim):
    mean_grad = jnp.mean(grad_hat, axis=reduce_dim, keepdims=True)
    mean_proj = jnp.mean(grad_hat * normed, axis=reduce_dim, keepdims=True)
    return inverse * (grad_hat - mean_grad - normed * mean_proj)


def channel_shards(
    dap,
    ch,
    pair_act,
    out_grad,
    residue_mask,
    ln_in_gain,
    ln_in_bias,
    w_a_proj,
    w_a_gate,
    w_b_proj,
    w_b_gate,
    w_gate,
    ln_out_gain,
    ln_out_bias,
    w_out,
):
    own_rows, all_cols = pair_act.shape[:2]
    col_span = out_grad.shape[1]
    hidden_local = w_a_proj.shape[1]
    slice_h = hidden_local // dap
    row_first = lax.axis_index("dap") * own_rows
    col_first = lax.axis_index("ch") * col_span
    normed_in, rstd_in = normalise(pair_act.astype(jnp.float32), 2)
    pair_norm = (normed_in * ln_in_gain + ln_in_bias).astype(jnp.bfloat16)
    valid_all = residue_mask.astype(jnp.float32)
    valid_rows = lax.dynamic_slice_in_dim(valid_all, row_first, own_rows)
    row_mask = (valid_rows[:, None] * valid_all[None, :])[None]
    w_four = jnp.concatenate((w_a_proj, w_a_gate, w_b_proj, w_b_gate), axis=1)
    projected = jnp.einsum("ikc,cg->gik", pair_norm, w_four, preferred_element_type=jnp.float32)
    a_proj = projected[:hidden_local]
    a_sig = jax.nn.sigmoid(projected[hidden_local : 2 * hidden_local])
    b_proj = projected[2 * hidden_local : 3 * hidden_local]
    b_sig = jax.nn.sigmoid(projected[3 * hidden_local :])
    edge_a = (row_mask * a_sig * a_proj).astype(jnp.bfloat16)
    edge_b = (row_mask * b_sig * b_proj).astype(jnp.bfloat16)

    split = (dap, slice_h, own_rows, all_cols)
    edges = jnp.stack((edge_a.reshape(split), edge_b.reshape(split)), axis=1)
    edges = lax.all_to_all(edges, "dap", split_axis=0, concat_axis=0, tiled=True)
    edges = jnp.transpose(edges, (1, 2, 0, 3, 4)).reshape(2, slice_h, dap * own_rows, all_cols)
    a_all, b_all = edges[0], edges[1]
    tri = jnp.einsum("hik,hjk->hij", a_all, b_all, preferred_element_type=jnp.float32).astype(
        jnp.bfloat16
    )
    tri = tri.reshape(slice_h, dap, own_rows, ch, col_span)
    tri = jnp.transpose(tri, (1, 3, 0, 2, 4)).reshape(dap * ch, slice_h, own_rows, col_span)
    tri = lax.all_to_all(tri, ("dap", "ch"), split_axis=0, concat_axis=0, tiled=True)
    tri = tri.reshape(dap, ch, slice_h, own_rows, col_span)
    tri_full = jnp.transpose(tri, (1, 0, 2, 3, 4)).reshape(-1, own_rows, col_span)

    normed_out, rstd_out = normalise(tri_full.astype(jnp.float32), 0)
    gain_out = ln_out_gain.reshape(-1, 1, 1)
    bias_out = ln_out_bias.reshape(-1, 1, 1)
    tri_norm = (normed_out * gain_out + bias_out).astype(jnp.bfloat16)
    proj_out = jnp.einsum("hij,hc->ijc", tri_norm, w_out, preferred_element_type=jnp.float32)
    norm_cols = lax.dynamic_slice_in_dim(pair_norm, col_first, col_span, 1)
    gate_act = jax.nn.sigmoid(
        jnp.einsum("ijc,cd->ijd", norm_cols, w_gate, preferred_element_type=jnp.float32)
    )
    upstream = out_grad.astype(jnp.float32)
    d_proj = (upstream * gate_act).astype(jnp.bfloat16)
    d_gate = (upstream * proj_out * gate_act * (1.0 - gate_act)).astype(jnp.bfloat16)
    d_normed = (
        jnp.einsum("ijc,hc->hij", d_proj, w_out, preferred_element_type=jnp.float32) * gain_out
    )
    d_tri = norm_backward(d_normed, normed_out, rstd_out, 0).astype(jnp.bfloat16)

    d_tri = d_tri.reshape(ch, dap, slice_h, own_rows, col_span)
    d_tri = jnp.transpose(d_tri, (1, 0, 2, 3, 4)).reshape(dap * ch, slice_h, own_rows, col_span)
    d_tri = lax.all_to_all(d_tri, ("dap", "ch"), split_axis=0, concat_axis=0, tiled=True)
    d_tri = d_tri.reshape(dap, ch, slice_h, own_rows, col_span)
    d_tri = jnp.transpose(d_tri, (2, 0, 3, 1, 4)).reshape(slice_h, dap * own_rows, all_cols)
    d_edge_a = jnp.einsum("hij,hjk->hik", d_tri, b_all, preferred_element_type=jnp.float32)
    d_edge_b = jnp.einsum("hij,hik->hjk", d_tri, a_all, preferred_element_type=jnp.float32)
    d_edges = jnp.stack((d_edge_a, d_edge_b)).astype(jnp.bfloat16)
    d_edges = d_edges.reshape(2, slice_h, dap, own_rows, all_cols)
    d_edges = jnp.transpose(d_edges, (2, 0, 1, 3, 4))
    d_edges = lax.all_to_all(d_edges, "dap", split_axis=0, concat_axis=0, tiled=True)
    d_edges = jnp.transpose(d_edges, (1, 0, 2, 3, 4)).reshape(2, hidden_local, own_rows, all_cols)

    def split_grad(d_edge, sig_val, proj_val):
        masked = d_edge * row_mask
        return (
            (masked * sig_val).astype(jnp.bfloat16),
            (masked * proj_val * sig_val * (1.0 - sig_val)).astype(jnp.bfloat16),
        )

    d_four = jnp.concatenate(
        split_grad(d_edges[0].astype(jnp.float32), a_sig, a_proj)
        + split_grad(d_edges[1].astype(jnp.float32), b_sig, b_proj),
        axis=0,
    )
    d_hidden = jnp.einsum("gik,cg->ikc", d_four, w_four, preferred_element_type=jnp.float32)
    if ch > 1:
        d_hidden = lax.psum_scatter(
            d_hidden.astype(jnp.bfloat16), "ch", scatter_dimension=1, tiled=True
        ).astype(jnp.float32)
    d_pair_norm = d_hidden + jnp.einsum(
        "ijd,cd->ijc", d_gate, w_gate, preferred_element_type=jnp.float32
    )
    normed_cols = lax.dynamic_slice_in_dim(normed_in, col_first, col_span, 1)
    rstd_cols = lax.dynamic_slice_in_dim(rstd_in, col_first, col_span, 1)
    grad_hat = d_pair_norm * ln_in_gain
    return norm_backward(grad_hat, normed_cols, rstd_cols, 2).astype(jnp.bfloat16)


F32 = jnp.float32
BF16 = jnp.bfloat16
SUBLANES = 8


def dot(lhs, rhs, lhs_dim, rhs_dim):
    return lax.dot_general(
        lhs, rhs, (((lhs_dim,), (rhs_dim,)), ((), ())), preferred_element_type=F32
    )


def across(row, count):
    return jnp.transpose(jnp.broadcast_to(row, (count, row.shape[1])))


def normed_rows(act):
    centre = act - jnp.mean(act, axis=1, keepdims=True)
    return centre * lax.rsqrt(jnp.mean(centre * centre, axis=1, keepdims=True) + EPSILON)


def edges_kernel(me_ref, *refs):
    sources, (out_ref, *local), (wide, arrived) = refs[:9], refs[9:19], refs[19:]
    copies = [
        pltpu.make_async_copy(source, target, arrived.at[index])
        for index, (source, target) in enumerate(zip(sources, local))
    ]
    for copy in copies:
        copy.start()
    rows_ref, valid_ref, act_ref, gain_ref, bias_ref, *weights = local
    own, cols, _ = act_ref.shape
    devices, block, _ = out_ref.shape
    hidden = weights[0].shape[1]
    half = block // 2
    for copy in copies:
        copy.wait()
    valid = valid_ref[...].astype(F32)
    for r in range(own):
        normed = normed_rows(act_ref[r].astype(F32))
        pair_norm = (normed * gain_ref[...] + bias_ref[...]).astype(BF16)
        mask = valid * rows_ref[me_ref[0] * own + r].astype(F32)
        for side in range(2):
            proj = dot(weights[2 * side][...], pair_norm, 0, 1)
            sig = jax.nn.sigmoid(dot(weights[2 * side + 1][...], pair_norm, 0, 1))
            wide[side, pl.ds(r, hidden, stride=own), :] = mask * sig * proj
    for side in range(2):
        out_ref[:, side * half : (side + 1) * half, :] = (
            wide[side].reshape(devices, half, cols).astype(BF16)
        )


def gates_kernel(
    me_ref, rows_ref, valid_ref, act_ref, grad_ref, gain_ref, bias_ref, gain_out_ref,
    wap, wag, wbp, wbg, w_gate, w_out, factors, normed_t, rstd_t, gain_t, d_normed, slope,
):
    own, cols, _ = act_ref.shape
    hidden = wap.shape[1]
    valid = valid_ref[...].astype(F32)
    gain = across(gain_ref[...], cols)
    bias = across(bias_ref[...], cols)
    gain_out = across(gain_out_ref[...], cols)
    gain_t[...] = gain
    for r in range(own):
        act = jnp.transpose(act_ref[r].astype(F32))
        centre = act - jnp.mean(act, axis=0, keepdims=True)
        inverse = lax.rsqrt(jnp.mean(centre * centre, axis=0, keepdims=True) + EPSILON)
        normed = centre * inverse
        normed_t[r] = normed
        rstd_t[r] = inverse
        pair_norm = (normed * gain + bias).astype(BF16)
        mask = valid * rows_ref[me_ref[0] * own + r].astype(F32)
        for side, (w_proj, w_sig) in enumerate(((wap, wag), (wbp, wbg))):
            proj = dot(w_proj[...], pair_norm, 0, 0)
            sig = jax.nn.sigmoid(dot(w_sig[...], pair_norm, 0, 0))
            kept = mask * sig
            factors[2 * side, r] = kept
            factors[2 * side + 1, r] = kept * proj * (1.0 - sig)
        gate_act = jax.nn.sigmoid(dot(pair_norm, w_gate[...], 0, 0))
        d_proj = grad_ref[r].astype(F32) * gate_act
        slope[r] = d_proj * (1.0 - gate_act)
        d_normed[pl.ds(r, hidden, stride=own), :] = (
            dot(w_out[...], d_proj.astype(BF16), 1, 1) * gain_out
        )


def triangle_kernel(in_ref, out_ref, a_ref, b_ref, wide, back):
    devices, block, cols = in_ref.shape
    slice_h, rows, _ = a_ref.shape
    half = block // 2
    own = half // slice_h
    for side in range(2):
        wide[side] = (
            in_ref[:, side * half : (side + 1) * half, :].astype(F32).reshape(devices * half, cols)
        )
    for c in range(slice_h):
        for r in range(own):
            at = pl.ds(c * own + r, devices, stride=half)
            a_ref[c, r * devices : (r + 1) * devices, :] = wide[0, at, :].astype(BF16)
            back[pl.ds(r, devices, stride=own), :] = wide[1, at, :]
        b_ref[c] = back[...].astype(BF16)
        tri = dot(a_ref[c], b_ref[c], 1, 1)
        for r in range(own):
            wide[0, pl.ds(c * own + r, devices, stride=half), :] = tri[
                r * devices : (r + 1) * devices
            ]
    out_ref[...] = wide[0].reshape(devices, half, cols).astype(BF16)


def fold(values, own):
    total = jnp.sum(values, axis=0)
    rows = total
    for shift in range(own, SUBLANES, own):
        rows = rows + pltpu.roll(total, shift, 0)
    return rows[None]


def tri_normed(tri_ref, hidden, own):
    cols = tri_ref.shape[-1]
    tri = tri_ref[...].astype(F32).reshape(hidden * own // SUBLANES, SUBLANES, cols)
    centre = tri - fold(tri, own) / hidden
    inverse = lax.rsqrt(fold(centre * centre, own) / hidden + EPSILON)
    return centre * inverse, inverse


def norm_kernel(hidden, tri_ref, grad_ref, out_ref):
    devices, block, cols = tri_ref.shape
    own = devices * block // hidden
    normed, inverse = tri_normed(tri_ref, hidden, own)
    grad = grad_ref[...].reshape(normed.shape)
    mean_grad = fold(grad, own) / hidden
    mean_proj = fold(grad * normed, own) / hidden
    d_tri = inverse * (grad - mean_grad - normed * mean_proj)
    out_ref[...] = d_tri.reshape(devices, block, cols).astype(BF16)


def gate_grad_kernel(tri_ref, slope, gain_ref, bias_ref, w_out, w_gate, out_ref, wide):
    own, cols, _ = slope.shape
    hidden = w_out.shape[0]
    normed, _ = tri_normed(tri_ref, hidden, own)
    wide[...] = normed.reshape(hidden * own, cols)
    gain = across(gain_ref[...], cols)
    bias = across(bias_ref[...], cols)
    for r in range(own):
        tri_norm = (wide[pl.ds(r, hidden, stride=own), :] * gain + bias).astype(BF16)
        proj_out = dot(tri_norm, w_out[...], 0, 0)
        d_gate = (slope[r] * proj_out).astype(BF16)
        out_ref[r] = dot(w_gate[...], d_gate, 1, 1)


def edge_grad_kernel(in_ref, a_ref, b_ref, out_ref, wide, whole):
    devices, block, cols = in_ref.shape
    slice_h, rows, _ = a_ref.shape
    own = block // slice_h
    wide[0] = in_ref[...].astype(F32).reshape(devices * block, cols)
    for c in range(slice_h):
        at = [pl.ds(c * own + r, devices, stride=block) for r in range(own)]
        d_tri = jnp.concatenate([wide[0, at[r], :] for r in range(own)], axis=0).astype(BF16)
        d_a = dot(d_tri, b_ref[c], 1, 0)
        whole[...] = dot(d_tri, a_ref[c], 0, 0)
        for r in range(own):
            wide[1, at[r], :] = d_a[r * devices : (r + 1) * devices]
            wide[2, at[r], :] = whole[pl.ds(r, devices, stride=own), :]
    for side in range(2):
        out_ref[:, side * block : (side + 1) * block, :] = (
            wide[1 + side].reshape(devices, block, cols).astype(BF16)
        )


def input_grad_kernel(in_ref, factors, normed_t, rstd_t, gain_t, gate_part, wap, wag, wbp, wbg, out_ref, wide):
    own, cols, _ = out_ref.shape
    devices, block, _ = in_ref.shape
    hidden = wap.shape[1]
    half = block // 2
    for side in range(2):
        wide[side] = (
            in_ref[:, side * half : (side + 1) * half, :].astype(F32).reshape(devices * half, cols)
        )
    for r in range(own):
        total = gate_part[r]
        for side, (w_proj, w_sig) in enumerate(((wap, wag), (wbp, wbg))):
            d_edge = wide[side, pl.ds(r, hidden, stride=own), :]
            total = total + dot(w_proj[...], (d_edge * factors[2 * side, r]).astype(BF16), 1, 0)
            total = total + dot(w_sig[...], (d_edge * factors[2 * side + 1, r]).astype(BF16), 1, 0)
        grad_hat = total * gain_t[...]
        normed = normed_t[r]
        mean_grad = jnp.mean(grad_hat, axis=0, keepdims=True)
        mean_proj = jnp.mean(grad_hat * normed, axis=0, keepdims=True)
        grad = rstd_t[r] * (grad_hat - mean_grad - normed * mean_proj)
        out_ref[r] = jnp.transpose(grad).astype(BF16)


VMEM = pl.BlockSpec(memory_space=pltpu.VMEM)
SMEM = pl.BlockSpec(memory_space=pltpu.SMEM)
HBM = pl.BlockSpec(memory_space=pltpu.HBM)


def wide(*shape):
    return pltpu.VMEM(shape, F32)


def call(kernel, name, outs, args, scratch=(), scalars=0, flops=0, space=VMEM, limit=32 * 2**20):
    shapes = [jax.ShapeDtypeStruct(shape, dtype) for shape, dtype in outs]
    moved = sum(value.size * value.dtype.itemsize for value in list(args) + shapes)
    result = pl.pallas_call(
        kernel,
        name=name,
        out_shape=shapes,
        in_specs=[SMEM] * scalars + [space] * (len(args) - scalars),
        out_specs=[VMEM] * len(outs),
        scratch_shapes=scratch,
        cost_estimate=pl.CostEstimate(flops=flops, bytes_accessed=moved, transcendentals=0),
        compiler_params=pltpu.CompilerParams(vmem_limit_bytes=limit),
    )(*args)
    return result[0] if len(outs) == 1 else result


def kernel_shards(
    dap,
    pair_act,
    out_grad,
    residue_mask,
    ln_in_gain,
    ln_in_bias,
    w_a_proj,
    w_a_gate,
    w_b_proj,
    w_b_gate,
    w_gate,
    ln_out_gain,
    ln_out_bias,
    w_out,
):
    own, cols, chan = pair_act.shape
    hidden = w_a_proj.shape[1]
    slice_h = hidden // dap
    rows = dap * own
    block = slice_h * own
    me = lax.axis_index("dap").reshape(1)
    valid = residue_mask.reshape(1, -1)
    gain_in, bias_in, gain_out, bias_out = (
        value.reshape(1, -1) for value in (ln_in_gain, ln_in_bias, ln_out_gain, ln_out_bias)
    )
    w_edges = (w_a_proj, w_a_gate, w_b_proj, w_b_gate)
    product = 2 * own * cols * chan * hidden

    def exchange(value):
        return lax.all_to_all(value, "dap", split_axis=0, concat_axis=0, tiled=True)

    first = (residue_mask, valid, pair_act, gain_in, bias_in, *w_edges)
    edges = call(
        edges_kernel,
        "edges",
        [((dap, 2 * block, cols), BF16)],
        (me, *first),
        scratch=[
            (pltpu.VMEM if index else pltpu.SMEM)(value.shape, value.dtype)
            for index, value in enumerate(first)
        ]
        + [wide(2, hidden * own, cols), pltpu.SemaphoreType.DMA((len(first),))],
        scalars=1,
        flops=4 * product,
        space=HBM,
        limit=None,
    )
    edges = exchange(edges)
    factors, normed_t, rstd_t, gain_t, d_normed, slope = call(
        gates_kernel,
        "gates",
        [
            ((4, own, hidden, cols), F32),
            ((own, chan, cols), F32),
            ((own, 1, cols), F32),
            ((chan, cols), F32),
            ((hidden * own, cols), F32),
            ((own, cols, chan), F32),
        ],
        (me, residue_mask, valid, pair_act, out_grad, gain_in, bias_in, gain_out)
        + (*w_edges, w_gate, w_out),
        scalars=2,
        flops=6 * product,
    )
    tri, edge_a, edge_b = call(
        triangle_kernel,
        "triangle",
        [
            ((dap, block, cols), BF16),
            ((slice_h, rows, cols), BF16),
            ((slice_h, rows, cols), BF16),
        ],
        (edges,),
        scratch=[wide(2, dap * block, cols), wide(rows, cols)],
        flops=product,
    )
    tri = exchange(tri)
    d_tri = call(
        functools.partial(norm_kernel, hidden),
        "norm",
        [((dap, block, cols), BF16)],
        (tri, d_normed),
    )
    d_tri = exchange(d_tri)
    gate_part = call(
        gate_grad_kernel,
        "gate_grad",
        [((own, chan, cols), F32)],
        (tri, slope, gain_out, bias_out, w_out, w_gate),
        scratch=[wide(hidden * own, cols)],
        flops=2 * product,
    )
    d_edges = call(
        edge_grad_kernel,
        "edge_grad",
        [((dap, 2 * block, cols), BF16)],
        (d_tri, edge_a, edge_b),
        scratch=[wide(3, dap * block, cols), wide(rows, cols)],
        flops=2 * product,
    )
    d_edges = exchange(d_edges)
    return call(
        input_grad_kernel,
        "input_grad",
        [((own, cols, chan), BF16)],
        (d_edges, factors, normed_t, rstd_t, gain_t, gate_part, *w_edges),
        scratch=[wide(2, hidden * own, cols)],
        flops=4 * product,
    )


def fits_kernels(dap, ch, pair_act, w_proj):
    own, cols, chan = pair_act.shape
    hidden = w_proj.shape[1]
    block = hidden // dap * own
    return (
        ch == 1
        and hidden % dap == 0
        and own in (1, 2, 4, 8)
        and block % 16 == 0
        and dap % SUBLANES == 0
        and cols == dap * own
        and cols % 128 == chan % 128 == hidden % 128 == 0
    )


def solution(mesh):
    sizes = dict(mesh.shape)

    def program(*args):
        dap, ch = sizes["dap"], sizes["ch"]
        if fits_kernels(dap, ch, args[0], args[5]):
            return kernel_shards(dap, *args)
        return channel_shards(dap, ch, *args)

    in_specs = (
        P(("grp", "dap"), None, None),
        P(("grp", "dap"), "ch", None),
        P("grp"),
        P(),
        P(),
        P(None, "ch"),
        P(None, "ch"),
        P(None, "ch"),
        P(None, "ch"),
        P(),
        P(),
        P(),
        P(),
    )
    out_specs = P(("grp", "dap"), "ch", None)
    return jax.shard_map(
        program, mesh=mesh, in_specs=in_specs, out_specs=out_specs, check_vma=False
    )
```

```python
import functools

import jax
import jax.numpy as jnp
from jax import lax
from jax.experimental import pallas as pl
from jax.experimental.pallas import tpu as pltpu
from jax.sharding import PartitionSpec as P

EPSILON = 1e-05


def normalise(values, reduce_dim):
    centre = values - jnp.mean(values, axis=reduce_dim, keepdims=True)
    inverse = lax.rsqrt(jnp.mean(centre * centre, axis=reduce_dim, keepdims=True) + EPSILON)
    return (centre * inverse, inverse)


def norm_backward(grad_hat, normed, inverse, reduce_dim):
    mean_grad = jnp.mean(grad_hat, axis=reduce_dim, keepdims=True)
    mean_proj = jnp.mean(grad_hat * normed, axis=reduce_dim, keepdims=True)
    return inverse * (grad_hat - mean_grad - normed * mean_proj)


def channel_shards(
    dap,
    ch,
    pair_act,
    out_grad,
    residue_mask,
    ln_in_gain,
    ln_in_bias,
    w_a_proj,
    w_a_gate,
    w_b_proj,
    w_b_gate,
    w_gate,
    ln_out_gain,
    ln_out_bias,
    w_out,
):
    own_rows, all_cols = pair_act.shape[:2]
    col_span = out_grad.shape[1]
    hidden_local = w_a_proj.shape[1]
    slice_h = hidden_local // dap
    row_first = lax.axis_index("dap") * own_rows
    col_first = lax.axis_index("ch") * col_span
    normed_in, rstd_in = normalise(pair_act.astype(jnp.float32), 2)
    pair_norm = (normed_in * ln_in_gain + ln_in_bias).astype(jnp.bfloat16)
    valid_all = residue_mask.astype(jnp.float32)
    valid_rows = lax.dynamic_slice_in_dim(valid_all, row_first, own_rows)
    row_mask = (valid_rows[:, None] * valid_all[None, :])[None]
    w_four = jnp.concatenate((w_a_proj, w_a_gate, w_b_proj, w_b_gate), axis=1)
    projected = jnp.einsum("ikc,cg->gik", pair_norm, w_four, preferred_element_type=jnp.float32)
    a_proj = projected[:hidden_local]
    a_sig = jax.nn.sigmoid(projected[hidden_local : 2 * hidden_local])
    b_proj = projected[2 * hidden_local : 3 * hidden_local]
    b_sig = jax.nn.sigmoid(projected[3 * hidden_local :])
    edge_a = (row_mask * a_sig * a_proj).astype(jnp.bfloat16)
    edge_b = (row_mask * b_sig * b_proj).astype(jnp.bfloat16)

    split = (dap, slice_h, own_rows, all_cols)
    edges = jnp.stack((edge_a.reshape(split), edge_b.reshape(split)), axis=1)
    edges = lax.all_to_all(edges, "dap", split_axis=0, concat_axis=0, tiled=True)
    edges = jnp.transpose(edges, (1, 2, 0, 3, 4)).reshape(2, slice_h, dap * own_rows, all_cols)
    a_all, b_all = edges[0], edges[1]
    tri = jnp.einsum("hik,hjk->hij", a_all, b_all, preferred_element_type=jnp.float32).astype(
        jnp.bfloat16
    )
    tri = tri.reshape(slice_h, dap, own_rows, ch, col_span)
    tri = jnp.transpose(tri, (1, 3, 0, 2, 4)).reshape(dap * ch, slice_h, own_rows, col_span)
    tri = lax.all_to_all(tri, ("dap", "ch"), split_axis=0, concat_axis=0, tiled=True)
    tri = tri.reshape(dap, ch, slice_h, own_rows, col_span)
    tri_full = jnp.transpose(tri, (1, 0, 2, 3, 4)).reshape(-1, own_rows, col_span)

    normed_out, rstd_out = normalise(tri_full.astype(jnp.float32), 0)
    gain_out = ln_out_gain.reshape(-1, 1, 1)
    bias_out = ln_out_bias.reshape(-1, 1, 1)
    tri_norm = (normed_out * gain_out + bias_out).astype(jnp.bfloat16)
    proj_out = jnp.einsum("hij,hc->ijc", tri_norm, w_out, preferred_element_type=jnp.float32)
    norm_cols = lax.dynamic_slice_in_dim(pair_norm, col_first, col_span, 1)
    gate_act = jax.nn.sigmoid(
        jnp.einsum("ijc,cd->ijd", norm_cols, w_gate, preferred_element_type=jnp.float32)
    )
    upstream = out_grad.astype(jnp.float32)
    d_proj = (upstream * gate_act).astype(jnp.bfloat16)
    d_gate = (upstream * proj_out * gate_act * (1.0 - gate_act)).astype(jnp.bfloat16)
    d_normed = (
        jnp.einsum("ijc,hc->hij", d_proj, w_out, preferred_element_type=jnp.float32) * gain_out
    )
    d_tri = norm_backward(d_normed, normed_out, rstd_out, 0).astype(jnp.bfloat16)

    d_tri = d_tri.reshape(ch, dap, slice_h, own_rows, col_span)
    d_tri = jnp.transpose(d_tri, (1, 0, 2, 3, 4)).reshape(dap * ch, slice_h, own_rows, col_span)
    d_tri = lax.all_to_all(d_tri, ("dap", "ch"), split_axis=0, concat_axis=0, tiled=True)
    d_tri = d_tri.reshape(dap, ch, slice_h, own_rows, col_span)
    d_tri = jnp.transpose(d_tri, (2, 0, 3, 1, 4)).reshape(slice_h, dap * own_rows, all_cols)
    d_edge_a = jnp.einsum("hij,hjk->hik", d_tri, b_all, preferred_element_type=jnp.float32)
    d_edge_b = jnp.einsum("hij,hik->hjk", d_tri, a_all, preferred_element_type=jnp.float32)
    d_edges = jnp.stack((d_edge_a, d_edge_b)).astype(jnp.bfloat16)
    d_edges = d_edges.reshape(2, slice_h, dap, own_rows, all_cols)
    d_edges = jnp.transpose(d_edges, (2, 0, 1, 3, 4))
    d_edges = lax.all_to_all(d_edges, "dap", split_axis=0, concat_axis=0, tiled=True)
    d_edges = jnp.transpose(d_edges, (1, 0, 2, 3, 4)).reshape(2, hidden_local, own_rows, all_cols)

    def split_grad(d_edge, sig_val, proj_val):
        masked = d_edge * row_mask
        return (
            (masked * sig_val).astype(jnp.bfloat16),
            (masked * proj_val * sig_val * (1.0 - sig_val)).astype(jnp.bfloat16),
        )

    d_four = jnp.concatenate(
        split_grad(d_edges[0].astype(jnp.float32), a_sig, a_proj)
        + split_grad(d_edges[1].astype(jnp.float32), b_sig, b_proj),
        axis=0,
    )
    d_hidden = jnp.einsum("gik,cg->ikc", d_four, w_four, preferred_element_type=jnp.float32)
    if ch > 1:
        d_hidden = lax.psum_scatter(
            d_hidden.astype(jnp.bfloat16), "ch", scatter_dimension=1, tiled=True
        ).astype(jnp.float32)
    d_pair_norm = d_hidden + jnp.einsum(
        "ijd,cd->ijc", d_gate, w_gate, preferred_element_type=jnp.float32
    )
    normed_cols = lax.dynamic_slice_in_dim(normed_in, col_first, col_span, 1)
    rstd_cols = lax.dynamic_slice_in_dim(rstd_in, col_first, col_span, 1)
    grad_hat = d_pair_norm * ln_in_gain
    return norm_backward(grad_hat, normed_cols, rstd_cols, 2).astype(jnp.bfloat16)


F32 = jnp.float32
BF16 = jnp.bfloat16
SUBLANES = 8


def dot(lhs, rhs, lhs_dim, rhs_dim):
    return lax.dot_general(
        lhs, rhs, (((lhs_dim,), (rhs_dim,)), ((), ())), preferred_element_type=F32
    )


def across(row, count):
    return jnp.transpose(jnp.broadcast_to(row, (count, row.shape[1])))


def normed_rows(act):
    centre = act - jnp.mean(act, axis=1, keepdims=True)
    return centre * lax.rsqrt(jnp.mean(centre * centre, axis=1, keepdims=True) + EPSILON)


def edges_kernel(me_ref, *refs):
    sources, (out_ref, *local), (wide, arrived) = refs[:9], refs[9:19], refs[19:]
    copies = [
        pltpu.make_async_copy(source, target, arrived.at[index])
        for index, (source, target) in enumerate(zip(sources, local))
    ]
    for copy in copies:
        copy.start()
    act_ref, gain_ref, bias_ref, rows_ref, valid_ref, *weights = local
    own, cols, chan = act_ref.shape
    devices, block, _ = out_ref.shape
    hidden = weights[0].shape[1]
    half = block // 2
    for copy in copies[:3]:
        copy.wait()
    normed = normed_rows(act_ref[...].reshape(own * cols, chan).astype(F32))
    pair_norm = (normed * gain_ref[...] + bias_ref[...]).astype(BF16)
    for copy in copies[3:]:
        copy.wait()
    valid = valid_ref[...].astype(F32)
    mask = jnp.concatenate(
        [valid * rows_ref[me_ref[0] * own + r].astype(F32) for r in range(own)], axis=1
    )
    for side in range(2):
        proj = dot(weights[2 * side][...], pair_norm, 0, 1)
        edge = mask * jax.nn.sigmoid(dot(weights[2 * side + 1][...], pair_norm, 0, 1)) * proj
        for r in range(own):
            wide[side, pl.ds(r, hidden, stride=own), :] = edge[:, r * cols : (r + 1) * cols]
        out_ref[:, side * half : (side + 1) * half, :] = (
            wide[side].reshape(devices, half, cols).astype(BF16)
        )


def gates_kernel(
    me_ref, rows_ref, valid_ref, act_ref, grad_ref, gain_ref, bias_ref, gain_out_ref,
    wap, wag, wbp, wbg, w_gate, w_out, factors, normed_t, rstd_t, gain_t, d_normed, slope,
):
    own, cols, _ = act_ref.shape
    hidden = wap.shape[1]
    valid = valid_ref[...].astype(F32)
    gain = across(gain_ref[...], cols)
    bias = across(bias_ref[...], cols)
    gain_out = across(gain_out_ref[...], cols)
    gain_t[...] = gain
    for r in range(own):
        act = jnp.transpose(act_ref[r].astype(F32))
        centre = act - jnp.mean(act, axis=0, keepdims=True)
        inverse = lax.rsqrt(jnp.mean(centre * centre, axis=0, keepdims=True) + EPSILON)
        normed = centre * inverse
        lanes = pl.ds(r * cols, cols)
        normed_t[:, lanes] = normed
        rstd_t[:, lanes] = inverse
        pair_norm = (normed * gain + bias).astype(BF16)
        mask = valid * rows_ref[me_ref[0] * own + r].astype(F32)
        for side, (w_proj, w_sig) in enumerate(((wap, wag), (wbp, wbg))):
            proj = dot(w_proj[...], pair_norm, 0, 0)
            sig = jax.nn.sigmoid(dot(w_sig[...], pair_norm, 0, 0))
            kept = mask * sig
            factors[2 * side, :, lanes] = kept
            factors[2 * side + 1, :, lanes] = kept * proj * (1.0 - sig)
        gate_act = jax.nn.sigmoid(dot(pair_norm, w_gate[...], 0, 0))
        d_proj = grad_ref[r].astype(F32) * gate_act
        slope[r] = d_proj * (1.0 - gate_act)
        d_normed[pl.ds(r, hidden, stride=own), :] = (
            dot(w_out[...], d_proj.astype(BF16), 1, 1) * gain_out
        )


def low_rows(shape):
    return lax.broadcasted_iota(jnp.int32, shape, 1) < SUBLANES // 2


def swap(values):
    return pltpu.roll(values, SUBLANES // 2, 1)


def split_channels(blocks, own):
    devices, block, cols = blocks.shape
    tiles = blocks.reshape(devices // 2, 2, block // SUBLANES, SUBLANES, cols)
    parts = []
    for tile in range(block // SUBLANES):
        even, odd = tiles[:, 0, tile], tiles[:, 1, tile]
        low = low_rows(even.shape)
        parts.append(jnp.where(low, even, swap(odd)))
        parts.append(jnp.where(low, swap(even), odd))
    return [part.reshape(devices * own, cols) for part in parts]


def merge_channels(parts, own):
    rows, cols = parts[0].shape
    devices = rows // own
    tiles = [part.reshape(devices // 2, SUBLANES, cols) for part in parts]
    low = low_rows(tiles[0].shape)
    even, odd = [], []
    for first, second in zip(tiles[::2], tiles[1::2]):
        even.append(jnp.where(low, first, swap(second)))
        odd.append(jnp.where(low, swap(first), second))
    both = [jnp.concatenate(side, axis=1) for side in (even, odd)]
    block = len(parts) * own
    return jnp.stack(both, axis=1).reshape(devices, block, cols)


def triangle_kernel(own, in_ref, _, out_ref, a_ref, b_ref):
    half = out_ref.shape[1]
    sides = [
        split_channels(in_ref[:, side * half : (side + 1) * half, :].astype(F32), own)
        for side in range(2)
    ]
    tri = []
    for c, (edge_a, edge_b) in enumerate(zip(*sides)):
        a_ref[c] = edge_a.astype(BF16)
        b_ref[c] = edge_b.astype(BF16)
        tri.append(dot(a_ref[c], b_ref[c], 1, 1))
    out_ref[...] = merge_channels(tri, own).astype(BF16)


def fold(values, own):
    total = jnp.sum(values, axis=0)
    rows = total
    for shift in range(own, SUBLANES, own):
        rows = rows + pltpu.roll(total, shift, 0)
    return rows[None]


def tri_normed(tri_ref, hidden, own):
    cols = tri_ref.shape[-1]
    tri = tri_ref[...].astype(F32).reshape(hidden * own // SUBLANES, SUBLANES, cols)
    centre = tri - fold(tri, own) / hidden
    inverse = lax.rsqrt(fold(centre * centre, own) / hidden + EPSILON)
    return centre * inverse, inverse


def norm_kernel(hidden, tri_ref, grad_ref, out_ref):
    devices, block, cols = tri_ref.shape
    own = devices * block // hidden
    normed, inverse = tri_normed(tri_ref, hidden, own)
    grad = grad_ref[...].reshape(normed.shape)
    mean_grad = fold(grad, own) / hidden
    mean_proj = fold(grad * normed, own) / hidden
    d_tri = inverse * (grad - mean_grad - normed * mean_proj)
    out_ref[...] = d_tri.reshape(devices, block, cols).astype(BF16)


def gate_grad_kernel(tri_ref, slope, gain_ref, bias_ref, w_out, w_gate, out_ref, wide):
    own, cols, _ = slope.shape
    hidden = w_out.shape[0]
    normed, _ = tri_normed(tri_ref, hidden, own)
    wide[...] = normed.reshape(hidden * own, cols)
    gain = across(gain_ref[...], cols)
    bias = across(bias_ref[...], cols)
    for r in range(own):
        tri_norm = (wide[pl.ds(r, hidden, stride=own), :] * gain + bias).astype(BF16)
        proj_out = dot(tri_norm, w_out[...], 0, 0)
        d_gate = (slope[r] * proj_out).astype(BF16)
        out_ref[:, r * cols : (r + 1) * cols] = dot(w_gate[...], d_gate, 1, 1)


def edge_grad_kernel(own, in_ref, a_ref, b_ref, out_ref):
    block = in_ref.shape[1]
    grads = ([], [])
    for c, part in enumerate(split_channels(in_ref[...].astype(F32), own)):
        d_tri = part.astype(BF16)
        grads[0].append(dot(d_tri, b_ref[c], 1, 0))
        grads[1].append(dot(d_tri, a_ref[c], 0, 0))
    for side in range(2):
        out_ref[:, side * block : (side + 1) * block, :] = (
            merge_channels(grads[side], own).astype(BF16)
        )


def input_grad_kernel(in_ref, factors, normed_t, rstd_t, gain_t, gate_part, wap, wag, wbp, wbg, out_ref, wide):
    own, cols, _ = out_ref.shape
    devices, block, _ = in_ref.shape
    hidden = wap.shape[1]
    half = block // 2
    for side in range(2):
        wide[side] = (
            in_ref[:, side * half : (side + 1) * half, :].astype(F32).reshape(devices * half, cols)
        )
    total = gate_part[...]
    for side, weights in enumerate(((wap, wag), (wbp, wbg))):
        d_edge = jnp.concatenate(
            [wide[side, pl.ds(r, hidden, stride=own), :] for r in range(own)], axis=1
        )
        for at, weight in enumerate(weights):
            total = total + dot(weight[...], (d_edge * factors[2 * side + at]).astype(BF16), 1, 0)
    grad_hat = total * jnp.concatenate([gain_t[...]] * own, axis=1)
    normed = normed_t[...]
    mean_grad = jnp.mean(grad_hat, axis=0, keepdims=True)
    mean_proj = jnp.mean(grad_hat * normed, axis=0, keepdims=True)
    grad = rstd_t[...] * (grad_hat - mean_grad - normed * mean_proj)
    for r in range(own):
        out_ref[r] = jnp.transpose(grad[:, r * cols : (r + 1) * cols]).astype(BF16)


VMEM = pl.BlockSpec(memory_space=pltpu.VMEM)
SMEM = pl.BlockSpec(memory_space=pltpu.SMEM)
HBM = pl.BlockSpec(memory_space=pltpu.HBM)


def wide(*shape):
    return pltpu.VMEM(shape, F32)


def call(kernel, name, outs, args, scratch=(), scalars=0, flops=0, spaces=None, limit=32 * 2**20):
    shapes = [jax.ShapeDtypeStruct(shape, dtype) for shape, dtype in outs]
    moved = sum(value.size * value.dtype.itemsize for value in list(args) + shapes)
    result = pl.pallas_call(
        kernel,
        name=name,
        out_shape=shapes,
        in_specs=[SMEM] * scalars + (spaces or [VMEM] * (len(args) - scalars)),
        out_specs=[VMEM] * len(outs),
        scratch_shapes=scratch,
        cost_estimate=pl.CostEstimate(flops=flops, bytes_accessed=moved, transcendentals=0),
        compiler_params=pltpu.CompilerParams(vmem_limit_bytes=limit),
    )(*args)
    return result[0] if len(outs) == 1 else result


def kernel_shards(
    dap,
    pair_act,
    out_grad,
    residue_mask,
    ln_in_gain,
    ln_in_bias,
    w_a_proj,
    w_a_gate,
    w_b_proj,
    w_b_gate,
    w_gate,
    ln_out_gain,
    ln_out_bias,
    w_out,
):
    own, cols, chan = pair_act.shape
    hidden = w_a_proj.shape[1]
    slice_h = hidden // dap
    rows = dap * own
    block = slice_h * own
    me = lax.axis_index("dap").reshape(1)
    valid = residue_mask.reshape(1, -1)
    gain_in, bias_in, gain_out, bias_out = (
        value.reshape(1, -1) for value in (ln_in_gain, ln_in_bias, ln_out_gain, ln_out_bias)
    )
    w_edges = (w_a_proj, w_a_gate, w_b_proj, w_b_gate)
    product = 2 * own * cols * chan * hidden

    def exchange(value):
        return lax.all_to_all(value, "dap", split_axis=0, concat_axis=0, tiled=True)

    first = (pair_act, gain_in, bias_in, residue_mask, valid, *w_edges)
    edges = call(
        edges_kernel,
        "edges",
        [((dap, 2 * block, cols), BF16)],
        (me, *first),
        scratch=[
            (pltpu.SMEM if value is residue_mask else pltpu.VMEM)(value.shape, value.dtype)
            for value in first
        ]
        + [wide(2, hidden * own, cols), pltpu.SemaphoreType.DMA((len(first),))],
        scalars=1,
        flops=4 * product,
        spaces=[HBM] * len(first),
        limit=None,
    )
    edges = exchange(edges)
    factors, normed_t, rstd_t, gain_t, d_normed, slope = call(
        gates_kernel,
        "gates",
        [
            ((4, hidden, own * cols), F32),
            ((chan, own * cols), F32),
            ((1, own * cols), F32),
            ((chan, cols), F32),
            ((hidden * own, cols), F32),
            ((own, cols, chan), F32),
        ],
        (me, residue_mask, valid, pair_act, out_grad, gain_in, bias_in, gain_out)
        + (*w_edges, w_gate, w_out),
        scalars=2,
        flops=6 * product,
    )
    tri, edge_a, edge_b = call(
        functools.partial(triangle_kernel, own),
        "triangle",
        [
            ((dap, block, cols), BF16),
            ((slice_h, rows, cols), BF16),
            ((slice_h, rows, cols), BF16),
        ],
        (edges, d_normed),
        flops=product,
        spaces=[VMEM, pl.BlockSpec(memory_space=pl.ANY)],
    )
    tri = exchange(tri)
    d_tri = call(
        functools.partial(norm_kernel, hidden),
        "norm",
        [((dap, block, cols), BF16)],
        (tri, d_normed),
    )
    d_tri = exchange(d_tri)
    gate_part = call(
        gate_grad_kernel,
        "gate_grad",
        [((chan, own * cols), F32)],
        (tri, slope, gain_out, bias_out, w_out, w_gate),
        scratch=[wide(hidden * own, cols)],
        flops=2 * product,
    )
    d_edges = call(
        functools.partial(edge_grad_kernel, own),
        "edge_grad",
        [((dap, 2 * block, cols), BF16)],
        (d_tri, edge_a, edge_b),
        flops=2 * product,
    )
    d_edges = exchange(d_edges)
    return call(
        input_grad_kernel,
        "input_grad",
        [((own, cols, chan), BF16)],
        (d_edges, factors, normed_t, rstd_t, gain_t, gate_part, *w_edges),
        scratch=[wide(2, hidden * own, cols)],
        flops=4 * product,
    )


def fits_kernels(dap, ch, pair_act, w_proj):
    own, cols, chan = pair_act.shape
    hidden = w_proj.shape[1]
    block = hidden // dap * own
    return (
        ch == 1
        and hidden % dap == 0
        and own == SUBLANES // 2
        and block % 16 == 0
        and dap % SUBLANES == 0
        and cols == dap * own
        and cols % 128 == chan % 128 == hidden % 128 == 0
    )


def solution(mesh):
    sizes = dict(mesh.shape)

    def program(*args):
        dap, ch = sizes["dap"], sizes["ch"]
        if fits_kernels(dap, ch, args[0], args[5]):
            return kernel_shards(dap, *args)
        return channel_shards(dap, ch, *args)

    in_specs = (
        P(("grp", "dap"), None, None),
        P(("grp", "dap"), "ch", None),
        P("grp"),
        P(),
        P(),
        P(None, "ch"),
        P(None, "ch"),
        P(None, "ch"),
        P(None, "ch"),
        P(),
        P(),
        P(),
        P(),
    )
    out_specs = P(("grp", "dap"), "ch", None)
    return jax.shard_map(
        program, mesh=mesh, in_specs=in_specs, out_specs=out_specs, check_vma=False
    )
```

```python
import functools

import jax
import jax.numpy as jnp
from jax import lax
from jax.experimental import pallas as pl
from jax.experimental.pallas import tpu as pltpu
from jax.sharding import PartitionSpec as P

EPSILON = 1e-05


def normalise(values, reduce_dim):
    centre = values - jnp.mean(values, axis=reduce_dim, keepdims=True)
    inverse = lax.rsqrt(jnp.mean(centre * centre, axis=reduce_dim, keepdims=True) + EPSILON)
    return (centre * inverse, inverse)


def norm_backward(grad_hat, normed, inverse, reduce_dim):
    mean_grad = jnp.mean(grad_hat, axis=reduce_dim, keepdims=True)
    mean_proj = jnp.mean(grad_hat * normed, axis=reduce_dim, keepdims=True)
    return inverse * (grad_hat - mean_grad - normed * mean_proj)


def channel_shards(
    dap,
    ch,
    pair_act,
    out_grad,
    residue_mask,
    ln_in_gain,
    ln_in_bias,
    w_a_proj,
    w_a_gate,
    w_b_proj,
    w_b_gate,
    w_gate,
    ln_out_gain,
    ln_out_bias,
    w_out,
):
    own_rows, all_cols = pair_act.shape[:2]
    col_span = out_grad.shape[1]
    hidden_local = w_a_proj.shape[1]
    slice_h = hidden_local // dap
    row_first = lax.axis_index("dap") * own_rows
    col_first = lax.axis_index("ch") * col_span
    normed_in, rstd_in = normalise(pair_act.astype(jnp.float32), 2)
    pair_norm = (normed_in * ln_in_gain + ln_in_bias).astype(jnp.bfloat16)
    valid_all = residue_mask.astype(jnp.float32)
    valid_rows = lax.dynamic_slice_in_dim(valid_all, row_first, own_rows)
    row_mask = (valid_rows[:, None] * valid_all[None, :])[None]
    w_four = jnp.concatenate((w_a_proj, w_a_gate, w_b_proj, w_b_gate), axis=1)
    projected = jnp.einsum("ikc,cg->gik", pair_norm, w_four, preferred_element_type=jnp.float32)
    a_proj = projected[:hidden_local]
    a_sig = jax.nn.sigmoid(projected[hidden_local : 2 * hidden_local])
    b_proj = projected[2 * hidden_local : 3 * hidden_local]
    b_sig = jax.nn.sigmoid(projected[3 * hidden_local :])
    edge_a = (row_mask * a_sig * a_proj).astype(jnp.bfloat16)
    edge_b = (row_mask * b_sig * b_proj).astype(jnp.bfloat16)

    split = (dap, slice_h, own_rows, all_cols)
    edges = jnp.stack((edge_a.reshape(split), edge_b.reshape(split)), axis=1)
    edges = lax.all_to_all(edges, "dap", split_axis=0, concat_axis=0, tiled=True)
    edges = jnp.transpose(edges, (1, 2, 0, 3, 4)).reshape(2, slice_h, dap * own_rows, all_cols)
    a_all, b_all = edges[0], edges[1]
    tri = jnp.einsum("hik,hjk->hij", a_all, b_all, preferred_element_type=jnp.float32).astype(
        jnp.bfloat16
    )
    tri = tri.reshape(slice_h, dap, own_rows, ch, col_span)
    tri = jnp.transpose(tri, (1, 3, 0, 2, 4)).reshape(dap * ch, slice_h, own_rows, col_span)
    tri = lax.all_to_all(tri, ("dap", "ch"), split_axis=0, concat_axis=0, tiled=True)
    tri = tri.reshape(dap, ch, slice_h, own_rows, col_span)
    tri_full = jnp.transpose(tri, (1, 0, 2, 3, 4)).reshape(-1, own_rows, col_span)

    normed_out, rstd_out = normalise(tri_full.astype(jnp.float32), 0)
    gain_out = ln_out_gain.reshape(-1, 1, 1)
    bias_out = ln_out_bias.reshape(-1, 1, 1)
    tri_norm = (normed_out * gain_out + bias_out).astype(jnp.bfloat16)
    proj_out = jnp.einsum("hij,hc->ijc", tri_norm, w_out, preferred_element_type=jnp.float32)
    norm_cols = lax.dynamic_slice_in_dim(pair_norm, col_first, col_span, 1)
    gate_act = jax.nn.sigmoid(
        jnp.einsum("ijc,cd->ijd", norm_cols, w_gate, preferred_element_type=jnp.float32)
    )
    upstream = out_grad.astype(jnp.float32)
    d_proj = (upstream * gate_act).astype(jnp.bfloat16)
    d_gate = (upstream * proj_out * gate_act * (1.0 - gate_act)).astype(jnp.bfloat16)
    d_normed = (
        jnp.einsum("ijc,hc->hij", d_proj, w_out, preferred_element_type=jnp.float32) * gain_out
    )
    d_tri = norm_backward(d_normed, normed_out, rstd_out, 0).astype(jnp.bfloat16)

    d_tri = d_tri.reshape(ch, dap, slice_h, own_rows, col_span)
    d_tri = jnp.transpose(d_tri, (1, 0, 2, 3, 4)).reshape(dap * ch, slice_h, own_rows, col_span)
    d_tri = lax.all_to_all(d_tri, ("dap", "ch"), split_axis=0, concat_axis=0, tiled=True)
    d_tri = d_tri.reshape(dap, ch, slice_h, own_rows, col_span)
    d_tri = jnp.transpose(d_tri, (2, 0, 3, 1, 4)).reshape(slice_h, dap * own_rows, all_cols)
    d_edge_a = jnp.einsum("hij,hjk->hik", d_tri, b_all, preferred_element_type=jnp.float32)
    d_edge_b = jnp.einsum("hij,hik->hjk", d_tri, a_all, preferred_element_type=jnp.float32)
    d_edges = jnp.stack((d_edge_a, d_edge_b)).astype(jnp.bfloat16)
    d_edges = d_edges.reshape(2, slice_h, dap, own_rows, all_cols)
    d_edges = jnp.transpose(d_edges, (2, 0, 1, 3, 4))
    d_edges = lax.all_to_all(d_edges, "dap", split_axis=0, concat_axis=0, tiled=True)
    d_edges = jnp.transpose(d_edges, (1, 0, 2, 3, 4)).reshape(2, hidden_local, own_rows, all_cols)

    def split_grad(d_edge, sig_val, proj_val):
        masked = d_edge * row_mask
        return (
            (masked * sig_val).astype(jnp.bfloat16),
            (masked * proj_val * sig_val * (1.0 - sig_val)).astype(jnp.bfloat16),
        )

    d_four = jnp.concatenate(
        split_grad(d_edges[0].astype(jnp.float32), a_sig, a_proj)
        + split_grad(d_edges[1].astype(jnp.float32), b_sig, b_proj),
        axis=0,
    )
    d_hidden = jnp.einsum("gik,cg->ikc", d_four, w_four, preferred_element_type=jnp.float32)
    if ch > 1:
        d_hidden = lax.psum_scatter(
            d_hidden.astype(jnp.bfloat16), "ch", scatter_dimension=1, tiled=True
        ).astype(jnp.float32)
    d_pair_norm = d_hidden + jnp.einsum(
        "ijd,cd->ijc", d_gate, w_gate, preferred_element_type=jnp.float32
    )
    normed_cols = lax.dynamic_slice_in_dim(normed_in, col_first, col_span, 1)
    rstd_cols = lax.dynamic_slice_in_dim(rstd_in, col_first, col_span, 1)
    grad_hat = d_pair_norm * ln_in_gain
    return norm_backward(grad_hat, normed_cols, rstd_cols, 2).astype(jnp.bfloat16)


F32 = jnp.float32
BF16 = jnp.bfloat16
SUBLANES = 8


def dot(lhs, rhs, lhs_dim, rhs_dim):
    return lax.dot_general(
        lhs, rhs, (((lhs_dim,), (rhs_dim,)), ((), ())), preferred_element_type=F32
    )


def across(row, count):
    return jnp.transpose(jnp.broadcast_to(row, (count, row.shape[1])))


def normed_rows(act):
    centre = act - jnp.mean(act, axis=1, keepdims=True)
    return centre * lax.rsqrt(jnp.mean(centre * centre, axis=1, keepdims=True) + EPSILON)


def exchange_bit(first, second, weight):
    sublane = lax.broadcasted_iota(jnp.int32, first.shape, 1)
    low = sublane & weight == 0
    return (
        jnp.where(low, first, pltpu.roll(second, weight, 1)),
        jnp.where(low, pltpu.roll(first, SUBLANES - weight, 1), second),
    )


def split_channels(blocks, own):
    devices, block, cols = blocks.shape
    tiles = blocks.reshape(devices // 2, 2, block // SUBLANES, SUBLANES, cols)
    parts = []
    for tile in range(block // SUBLANES):
        parts.extend(exchange_bit(tiles[:, 0, tile], tiles[:, 1, tile], own))
    return [part.reshape(devices * own, cols) for part in parts]


def merge_channels(parts, own):
    rows, cols = parts[0].shape
    devices = rows // own
    tiles = [part.reshape(devices // 2, SUBLANES, cols) for part in parts]
    pairs = [exchange_bit(*pair, own) for pair in zip(tiles[::2], tiles[1::2])]
    both = [jnp.concatenate(side, axis=1) for side in zip(*pairs)]
    block = len(parts) * own
    return jnp.stack(both, axis=1).reshape(devices, block, cols)


def trade(parts):
    rows, cols = parts[0].shape
    a, b, c, d = (part.reshape(rows // SUBLANES, SUBLANES, cols) for part in parts)
    (a, b), (c, d) = exchange_bit(a, b, 1), exchange_bit(c, d, 1)
    (a, c), (b, d) = exchange_bit(a, c, 2), exchange_bit(b, d, 2)
    return [part.reshape(rows, cols) for part in (a, b, c, d)]


def edges_kernel(me_ref, *refs):
    sources, (out_ref, *local), arrived = refs[:9], refs[9:19], refs[19]
    copies = [
        pltpu.make_async_copy(source, target, arrived.at[index])
        for index, (source, target) in enumerate(zip(sources, local))
    ]
    for copy in copies:
        copy.start()
    act_ref, gain_ref, bias_ref, rows_ref, valid_ref, *weights = local
    own, cols, chan = act_ref.shape
    half = out_ref.shape[1] // 2
    for copy in copies[:3]:
        copy.wait()
    normed = normed_rows(act_ref[...].reshape(own * cols, chan).astype(F32))
    pair_norm = (normed * gain_ref[...] + bias_ref[...]).astype(BF16)
    for copy in copies[3:]:
        copy.wait()
    valid = valid_ref[...].astype(F32)
    mask = jnp.concatenate(
        [valid * rows_ref[me_ref[0] * own + r].astype(F32) for r in range(own)], axis=1
    )
    for side in range(2):
        proj = dot(weights[2 * side][...], pair_norm, 0, 1)
        edge = mask * jax.nn.sigmoid(dot(weights[2 * side + 1][...], pair_norm, 0, 1)) * proj
        parts = trade([edge[:, r * cols : (r + 1) * cols] for r in range(own)])
        out_ref[:, side * half : (side + 1) * half, :] = merge_channels(parts, own).astype(BF16)


def gates_kernel(
    me_ref, rows_ref, valid_ref, act_ref, grad_ref, gain_ref, bias_ref, gain_out_ref,
    wap, wag, wbp, wbg, w_gate, w_out, factors, normed_t, rstd_t, gain_t, d_normed, slope,
):
    own, cols, _ = act_ref.shape
    hidden = wap.shape[1]
    valid = valid_ref[...].astype(F32)
    gain = across(gain_ref[...], cols)
    bias = across(bias_ref[...], cols)
    gain_out = across(gain_out_ref[...], cols)
    gain_t[...] = gain
    for r in range(own):
        act = jnp.transpose(act_ref[r].astype(F32))
        centre = act - jnp.mean(act, axis=0, keepdims=True)
        inverse = lax.rsqrt(jnp.mean(centre * centre, axis=0, keepdims=True) + EPSILON)
        normed = centre * inverse
        lanes = pl.ds(r * cols, cols)
        normed_t[:, lanes] = normed
        rstd_t[:, lanes] = inverse
        pair_norm = (normed * gain + bias).astype(BF16)
        mask = valid * rows_ref[me_ref[0] * own + r].astype(F32)
        for side, (w_proj, w_sig) in enumerate(((wap, wag), (wbp, wbg))):
            proj = dot(w_proj[...], pair_norm, 0, 0)
            sig = jax.nn.sigmoid(dot(w_sig[...], pair_norm, 0, 0))
            kept = mask * sig
            factors[2 * side, :, lanes] = kept
            factors[2 * side + 1, :, lanes] = kept * proj * (1.0 - sig)
        gate_act = jax.nn.sigmoid(dot(w_gate[...], pair_norm, 0, 0))
        d_proj = jnp.transpose(grad_ref[r].astype(F32)) * gate_act
        slope[:, lanes] = d_proj * (1.0 - gate_act)
        d_normed[pl.ds(r, hidden, stride=own), :] = (
            dot(w_out[...], d_proj.astype(BF16), 1, 0) * gain_out
        )


def triangle_kernel(own, in_ref, _, out_ref, a_ref, b_ref):
    half = out_ref.shape[1]
    sides = [
        split_channels(in_ref[:, side * half : (side + 1) * half, :].astype(F32), own)
        for side in range(2)
    ]
    tri = []
    for c, (edge_a, edge_b) in enumerate(zip(*sides)):
        a_ref[c] = edge_a.astype(BF16)
        b_ref[c] = edge_b.astype(BF16)
        tri.append(dot(a_ref[c], b_ref[c], 1, 1))
    out_ref[...] = merge_channels(tri, own).astype(BF16)


def fold(values, own):
    total = jnp.sum(values, axis=0)
    rows = total
    for shift in range(own, SUBLANES, own):
        rows = rows + pltpu.roll(total, shift, 0)
    return rows[None]


def tri_normed(tri_ref, hidden, own):
    cols = tri_ref.shape[-1]
    tri = tri_ref[...].astype(F32).reshape(hidden * own // SUBLANES, SUBLANES, cols)
    centre = tri - fold(tri, own) / hidden
    inverse = lax.rsqrt(fold(centre * centre, own) / hidden + EPSILON)
    return centre * inverse, inverse


def norm_kernel(own, tri_ref, grad_ref, slope, gain_ref, bias_ref, w_out, w_gate, out_ref, part_ref):
    devices, block, cols = tri_ref.shape
    hidden = w_out.shape[0]
    normed, inverse = tri_normed(tri_ref, hidden, own)
    grad = grad_ref[...].reshape(normed.shape)
    mean_grad = fold(grad, own) / hidden
    mean_proj = fold(grad * normed, own) / hidden
    d_tri = inverse * (grad - mean_grad - normed * mean_proj)
    out_ref[...] = d_tri.reshape(devices, block, cols).astype(BF16)
    gain = across(gain_ref[...], cols)
    bias = across(bias_ref[...], cols)
    parts = trade(split_channels(normed.reshape(devices, block, cols), own))
    tri_norm = jnp.concatenate([(part * gain + bias).astype(BF16) for part in parts], axis=1)
    d_gate = (slope[...] * dot(w_out[...], tri_norm, 0, 0)).astype(BF16)
    part_ref[...] = dot(w_gate[...], d_gate, 1, 0)


def edge_grad_kernel(own, in_ref, a_ref, b_ref, out_ref):
    block = in_ref.shape[1]
    grads = ([], [])
    for c, part in enumerate(split_channels(in_ref[...].astype(F32), own)):
        d_tri = part.astype(BF16)
        grads[0].append(dot(d_tri, b_ref[c], 1, 0))
        grads[1].append(dot(d_tri, a_ref[c], 0, 0))
    for side in range(2):
        out_ref[:, side * block : (side + 1) * block, :] = (
            merge_channels(grads[side], own).astype(BF16)
        )


def input_grad_kernel(in_ref, factors, normed_t, rstd_t, gain_t, gate_part, wap, wag, wbp, wbg, out_ref):
    own, cols, _ = out_ref.shape
    half = in_ref.shape[1] // 2
    total = gate_part[...]
    for side, weights in enumerate(((wap, wag), (wbp, wbg))):
        blocks = in_ref[:, side * half : (side + 1) * half, :].astype(F32)
        d_edge = jnp.concatenate(trade(split_channels(blocks, own)), axis=1)
        for at, weight in enumerate(weights):
            total = total + dot(weight[...], (d_edge * factors[2 * side + at]).astype(BF16), 1, 0)
    grad_hat = total * jnp.concatenate([gain_t[...]] * own, axis=1)
    normed = normed_t[...]
    mean_grad = jnp.mean(grad_hat, axis=0, keepdims=True)
    mean_proj = jnp.mean(grad_hat * normed, axis=0, keepdims=True)
    grad = rstd_t[...] * (grad_hat - mean_grad - normed * mean_proj)
    for r in range(own):
        out_ref[r] = jnp.transpose(grad[:, r * cols : (r + 1) * cols]).astype(BF16)


VMEM = pl.BlockSpec(memory_space=pltpu.VMEM)
SMEM = pl.BlockSpec(memory_space=pltpu.SMEM)
HBM = pl.BlockSpec(memory_space=pltpu.HBM)


def call(kernel, name, outs, args, scratch=(), scalars=0, flops=0, spaces=None, limit=32 * 2**20):
    shapes = [jax.ShapeDtypeStruct(shape, dtype) for shape, dtype in outs]
    moved = sum(value.size * value.dtype.itemsize for value in list(args) + shapes)
    result = pl.pallas_call(
        kernel,
        name=name,
        out_shape=shapes,
        in_specs=[SMEM] * scalars + (spaces or [VMEM] * (len(args) - scalars)),
        out_specs=[VMEM] * len(outs),
        scratch_shapes=scratch,
        cost_estimate=pl.CostEstimate(flops=flops, bytes_accessed=moved, transcendentals=0),
        compiler_params=pltpu.CompilerParams(vmem_limit_bytes=limit),
    )(*args)
    return result[0] if len(outs) == 1 else result


def kernel_shards(
    dap,
    pair_act,
    out_grad,
    residue_mask,
    ln_in_gain,
    ln_in_bias,
    w_a_proj,
    w_a_gate,
    w_b_proj,
    w_b_gate,
    w_gate,
    ln_out_gain,
    ln_out_bias,
    w_out,
):
    own, cols, chan = pair_act.shape
    hidden = w_a_proj.shape[1]
    slice_h = hidden // dap
    rows = dap * own
    block = slice_h * own
    me = lax.axis_index("dap").reshape(1)
    valid = residue_mask.reshape(1, -1)
    gain_in, bias_in, gain_out, bias_out = (
        value.reshape(1, -1) for value in (ln_in_gain, ln_in_bias, ln_out_gain, ln_out_bias)
    )
    w_edges = (w_a_proj, w_a_gate, w_b_proj, w_b_gate)
    product = 2 * own * cols * chan * hidden

    def exchange(value):
        return lax.all_to_all(value, "dap", split_axis=0, concat_axis=0, tiled=True)

    first = (pair_act, gain_in, bias_in, residue_mask, valid, *w_edges)
    edges = call(
        edges_kernel,
        "edges",
        [((dap, 2 * block, cols), BF16)],
        (me, *first),
        scratch=[
            (pltpu.SMEM if value is residue_mask else pltpu.VMEM)(value.shape, value.dtype)
            for value in first
        ]
        + [pltpu.SemaphoreType.DMA((len(first),))],
        scalars=1,
        flops=4 * product,
        spaces=[HBM] * len(first),
        limit=None,
    )
    edges = exchange(edges)
    factors, normed_t, rstd_t, gain_t, d_normed, slope = call(
        gates_kernel,
        "gates",
        [
            ((4, hidden, own * cols), F32),
            ((chan, own * cols), F32),
            ((1, own * cols), F32),
            ((chan, cols), F32),
            ((hidden * own, cols), F32),
            ((chan, own * cols), F32),
        ],
        (me, residue_mask, valid, pair_act, out_grad, gain_in, bias_in, gain_out)
        + (*w_edges, w_gate, w_out),
        scalars=2,
        flops=6 * product,
    )
    tri, edge_a, edge_b = call(
        functools.partial(triangle_kernel, own),
        "triangle",
        [
            ((dap, block, cols), BF16),
            ((slice_h, rows, cols), BF16),
            ((slice_h, rows, cols), BF16),
        ],
        (edges, d_normed),
        flops=product,
        spaces=[VMEM, pl.BlockSpec(memory_space=pl.ANY)],
    )
    tri = exchange(tri)
    d_tri, gate_part = call(
        functools.partial(norm_kernel, own),
        "norm",
        [((dap, block, cols), BF16), ((chan, own * cols), F32)],
        (tri, d_normed, slope, gain_out, bias_out, w_out, w_gate),
        flops=2 * product,
    )
    d_tri = exchange(d_tri)
    d_edges = call(
        functools.partial(edge_grad_kernel, own),
        "edge_grad",
        [((dap, 2 * block, cols), BF16)],
        (d_tri, edge_a, edge_b),
        flops=2 * product,
    )
    d_edges = exchange(d_edges)
    return call(
        input_grad_kernel,
        "input_grad",
        [((own, cols, chan), BF16)],
        (d_edges, factors, normed_t, rstd_t, gain_t, gate_part, *w_edges),
        flops=4 * product,
    )


def fits_kernels(dap, ch, pair_act, w_proj):
    own, cols, chan = pair_act.shape
    hidden = w_proj.shape[1]
    block = hidden // dap * own
    return (
        ch == 1
        and hidden % dap == 0
        and own == SUBLANES // 2
        and block == own * own
        and dap % SUBLANES == 0
        and cols == dap * own
        and cols % 128 == chan % 128 == hidden % 128 == 0
    )


def solution(mesh):
    sizes = dict(mesh.shape)

    def program(*args):
        dap, ch = sizes["dap"], sizes["ch"]
        if fits_kernels(dap, ch, args[0], args[5]):
            return kernel_shards(dap, *args)
        return channel_shards(dap, ch, *args)

    in_specs = (
        P(("grp", "dap"), None, None),
        P(("grp", "dap"), "ch", None),
        P("grp"),
        P(),
        P(),
        P(None, "ch"),
        P(None, "ch"),
        P(None, "ch"),
        P(None, "ch"),
        P(),
        P(),
        P(),
        P(),
    )
    out_specs = P(("grp", "dap"), "ch", None)
    return jax.shard_map(
        program, mesh=mesh, in_specs=in_specs, out_specs=out_specs, check_vma=False
    )
```

```python
import functools

import jax
import jax.numpy as jnp
from jax import lax
from jax.experimental import pallas as pl
from jax.experimental.pallas import tpu as pltpu
from jax.sharding import PartitionSpec as P

EPSILON = 1e-05


def normalise(values, reduce_dim):
    centre = values - jnp.mean(values, axis=reduce_dim, keepdims=True)
    inverse = lax.rsqrt(jnp.mean(centre * centre, axis=reduce_dim, keepdims=True) + EPSILON)
    return (centre * inverse, inverse)


def norm_backward(grad_hat, normed, inverse, reduce_dim):
    mean_grad = jnp.mean(grad_hat, axis=reduce_dim, keepdims=True)
    mean_proj = jnp.mean(grad_hat * normed, axis=reduce_dim, keepdims=True)
    return inverse * (grad_hat - mean_grad - normed * mean_proj)


def channel_shards(
    dap,
    ch,
    pair_act,
    out_grad,
    residue_mask,
    ln_in_gain,
    ln_in_bias,
    w_a_proj,
    w_a_gate,
    w_b_proj,
    w_b_gate,
    w_gate,
    ln_out_gain,
    ln_out_bias,
    w_out,
):
    own_rows, all_cols = pair_act.shape[:2]
    col_span = out_grad.shape[1]
    hidden_local = w_a_proj.shape[1]
    slice_h = hidden_local // dap
    row_first = lax.axis_index("dap") * own_rows
    col_first = lax.axis_index("ch") * col_span
    normed_in, rstd_in = normalise(pair_act.astype(jnp.float32), 2)
    pair_norm = (normed_in * ln_in_gain + ln_in_bias).astype(jnp.bfloat16)
    valid_all = residue_mask.astype(jnp.float32)
    valid_rows = lax.dynamic_slice_in_dim(valid_all, row_first, own_rows)
    row_mask = (valid_rows[:, None] * valid_all[None, :])[None]
    w_four = jnp.concatenate((w_a_proj, w_a_gate, w_b_proj, w_b_gate), axis=1)
    projected = jnp.einsum("ikc,cg->gik", pair_norm, w_four, preferred_element_type=jnp.float32)
    a_proj = projected[:hidden_local]
    a_sig = jax.nn.sigmoid(projected[hidden_local : 2 * hidden_local])
    b_proj = projected[2 * hidden_local : 3 * hidden_local]
    b_sig = jax.nn.sigmoid(projected[3 * hidden_local :])
    edge_a = (row_mask * a_sig * a_proj).astype(jnp.bfloat16)
    edge_b = (row_mask * b_sig * b_proj).astype(jnp.bfloat16)

    split = (dap, slice_h, own_rows, all_cols)
    edges = jnp.stack((edge_a.reshape(split), edge_b.reshape(split)), axis=1)
    edges = lax.all_to_all(edges, "dap", split_axis=0, concat_axis=0, tiled=True)
    edges = jnp.transpose(edges, (1, 2, 0, 3, 4)).reshape(2, slice_h, dap * own_rows, all_cols)
    a_all, b_all = edges[0], edges[1]
    tri = jnp.einsum("hik,hjk->hij", a_all, b_all, preferred_element_type=jnp.float32).astype(
        jnp.bfloat16
    )
    tri = tri.reshape(slice_h, dap, own_rows, ch, col_span)
    tri = jnp.transpose(tri, (1, 3, 0, 2, 4)).reshape(dap * ch, slice_h, own_rows, col_span)
    tri = lax.all_to_all(tri, ("dap", "ch"), split_axis=0, concat_axis=0, tiled=True)
    tri = tri.reshape(dap, ch, slice_h, own_rows, col_span)
    tri_full = jnp.transpose(tri, (1, 0, 2, 3, 4)).reshape(-1, own_rows, col_span)

    normed_out, rstd_out = normalise(tri_full.astype(jnp.float32), 0)
    gain_out = ln_out_gain.reshape(-1, 1, 1)
    bias_out = ln_out_bias.reshape(-1, 1, 1)
    tri_norm = (normed_out * gain_out + bias_out).astype(jnp.bfloat16)
    proj_out = jnp.einsum("hij,hc->ijc", tri_norm, w_out, preferred_element_type=jnp.float32)
    norm_cols = lax.dynamic_slice_in_dim(pair_norm, col_first, col_span, 1)
    gate_act = jax.nn.sigmoid(
        jnp.einsum("ijc,cd->ijd", norm_cols, w_gate, preferred_element_type=jnp.float32)
    )
    upstream = out_grad.astype(jnp.float32)
    d_proj = (upstream * gate_act).astype(jnp.bfloat16)
    d_gate = (upstream * proj_out * gate_act * (1.0 - gate_act)).astype(jnp.bfloat16)
    d_normed = (
        jnp.einsum("ijc,hc->hij", d_proj, w_out, preferred_element_type=jnp.float32) * gain_out
    )
    d_tri = norm_backward(d_normed, normed_out, rstd_out, 0).astype(jnp.bfloat16)

    d_tri = d_tri.reshape(ch, dap, slice_h, own_rows, col_span)
    d_tri = jnp.transpose(d_tri, (1, 0, 2, 3, 4)).reshape(dap * ch, slice_h, own_rows, col_span)
    d_tri = lax.all_to_all(d_tri, ("dap", "ch"), split_axis=0, concat_axis=0, tiled=True)
    d_tri = d_tri.reshape(dap, ch, slice_h, own_rows, col_span)
    d_tri = jnp.transpose(d_tri, (2, 0, 3, 1, 4)).reshape(slice_h, dap * own_rows, all_cols)
    d_edge_a = jnp.einsum("hij,hjk->hik", d_tri, b_all, preferred_element_type=jnp.float32)
    d_edge_b = jnp.einsum("hij,hik->hjk", d_tri, a_all, preferred_element_type=jnp.float32)
    d_edges = jnp.stack((d_edge_a, d_edge_b)).astype(jnp.bfloat16)
    d_edges = d_edges.reshape(2, slice_h, dap, own_rows, all_cols)
    d_edges = jnp.transpose(d_edges, (2, 0, 1, 3, 4))
    d_edges = lax.all_to_all(d_edges, "dap", split_axis=0, concat_axis=0, tiled=True)
    d_edges = jnp.transpose(d_edges, (1, 0, 2, 3, 4)).reshape(2, hidden_local, own_rows, all_cols)

    def split_grad(d_edge, sig_val, proj_val):
        masked = d_edge * row_mask
        return (
            (masked * sig_val).astype(jnp.bfloat16),
            (masked * proj_val * sig_val * (1.0 - sig_val)).astype(jnp.bfloat16),
        )

    d_four = jnp.concatenate(
        split_grad(d_edges[0].astype(jnp.float32), a_sig, a_proj)
        + split_grad(d_edges[1].astype(jnp.float32), b_sig, b_proj),
        axis=0,
    )
    d_hidden = jnp.einsum("gik,cg->ikc", d_four, w_four, preferred_element_type=jnp.float32)
    if ch > 1:
        d_hidden = lax.psum_scatter(
            d_hidden.astype(jnp.bfloat16), "ch", scatter_dimension=1, tiled=True
        ).astype(jnp.float32)
    d_pair_norm = d_hidden + jnp.einsum(
        "ijd,cd->ijc", d_gate, w_gate, preferred_element_type=jnp.float32
    )
    normed_cols = lax.dynamic_slice_in_dim(normed_in, col_first, col_span, 1)
    rstd_cols = lax.dynamic_slice_in_dim(rstd_in, col_first, col_span, 1)
    grad_hat = d_pair_norm * ln_in_gain
    return norm_backward(grad_hat, normed_cols, rstd_cols, 2).astype(jnp.bfloat16)


F32 = jnp.float32
BF16 = jnp.bfloat16
SUBLANES = 8


def dot(lhs, rhs, lhs_dim, rhs_dim):
    return lax.dot_general(
        lhs, rhs, (((lhs_dim,), (rhs_dim,)), ((), ())), preferred_element_type=F32
    )


def across(row, count):
    return jnp.transpose(jnp.broadcast_to(row, (count, row.shape[1])))


def normed_rows(act):
    centre = act - jnp.mean(act, axis=1, keepdims=True)
    return centre * lax.rsqrt(jnp.mean(centre * centre, axis=1, keepdims=True) + EPSILON)


def exchange_bit(first, second, weight):
    sublane = lax.broadcasted_iota(jnp.int32, first.shape, 1)
    low = sublane & weight == 0
    return (
        jnp.where(low, first, pltpu.roll(second, weight, 1)),
        jnp.where(low, pltpu.roll(first, SUBLANES - weight, 1), second),
    )


def split_channels(blocks, own):
    devices, block, cols = blocks.shape
    tiles = blocks.reshape(devices // 2, 2, block // SUBLANES, SUBLANES, cols)
    parts = []
    for tile in range(block // SUBLANES):
        parts.extend(exchange_bit(tiles[:, 0, tile], tiles[:, 1, tile], own))
    return [part.reshape(devices * own, cols) for part in parts]


def merge_channels(parts, own):
    rows, cols = parts[0].shape
    devices = rows // own
    tiles = [part.reshape(devices // 2, SUBLANES, cols) for part in parts]
    pairs = [exchange_bit(*pair, own) for pair in zip(tiles[::2], tiles[1::2])]
    both = [jnp.concatenate(side, axis=1) for side in zip(*pairs)]
    block = len(parts) * own
    return jnp.stack(both, axis=1).reshape(devices, block, cols)


def trade(parts):
    rows, cols = parts[0].shape
    a, b, c, d = (part.reshape(rows // SUBLANES, SUBLANES, cols) for part in parts)
    (a, b), (c, d) = exchange_bit(a, b, 1), exchange_bit(c, d, 1)
    (a, c), (b, d) = exchange_bit(a, c, 2), exchange_bit(b, d, 2)
    return [part.reshape(rows, cols) for part in (a, b, c, d)]


def edges_kernel(me_ref, *refs):
    sources, (out_ref, *local), arrived = refs[:9], refs[9:19], refs[19]
    copies = [
        pltpu.make_async_copy(source, target, arrived.at[index])
        for index, (source, target) in enumerate(zip(sources, local))
    ]
    for copy in copies:
        copy.start()
    act_ref, gain_ref, bias_ref, rows_ref, valid_ref, *weights = local
    own, cols, chan = act_ref.shape
    half = out_ref.shape[1] // 2
    for copy in copies[:3]:
        copy.wait()
    normed = normed_rows(act_ref[...].reshape(own * cols, chan).astype(F32))
    pair_norm = (normed * gain_ref[...] + bias_ref[...]).astype(BF16)
    for copy in copies[3:]:
        copy.wait()
    valid = valid_ref[...].astype(F32)
    mask = jnp.concatenate(
        [valid * rows_ref[me_ref[0] * own + r].astype(F32) for r in range(own)], axis=1
    )
    for side in range(2):
        proj = dot(weights[2 * side][...], pair_norm, 0, 1)
        edge = mask * jax.nn.sigmoid(dot(weights[2 * side + 1][...], pair_norm, 0, 1)) * proj
        parts = trade([edge[:, r * cols : (r + 1) * cols] for r in range(own)])
        out_ref[:, side * half : (side + 1) * half, :] = merge_channels(parts, own).astype(BF16)


def gates_kernel(
    me_ref, rows_ref, valid_ref, act_ref, grad_ref, gain_ref, bias_ref, gain_out_ref, bias_out_ref,
    wap, wag, wbp, wbg, w_gate, w_out,
    factors, normed_t, rstd_t, gain_t, d_normed, slope, gain_out_t, bias_out_t,
):
    own, cols, _ = act_ref.shape
    hidden = wap.shape[1]
    valid = valid_ref[...].astype(F32)
    gain = across(gain_ref[...], cols)
    bias = across(bias_ref[...], cols)
    gain_out = across(gain_out_ref[...], cols)
    gain_t[...] = gain
    gain_out_t[...] = gain_out
    bias_out_t[...] = across(bias_out_ref[...], cols)
    for r in range(own):
        act = jnp.transpose(act_ref[r].astype(F32))
        centre = act - jnp.mean(act, axis=0, keepdims=True)
        inverse = lax.rsqrt(jnp.mean(centre * centre, axis=0, keepdims=True) + EPSILON)
        normed = centre * inverse
        lanes = pl.ds(r * cols, cols)
        normed_t[:, lanes] = normed
        rstd_t[:, lanes] = inverse
        pair_norm = (normed * gain + bias).astype(BF16)
        mask = valid * rows_ref[me_ref[0] * own + r].astype(F32)
        for side, (w_proj, w_sig) in enumerate(((wap, wag), (wbp, wbg))):
            proj = dot(w_proj[...], pair_norm, 0, 0)
            sig = jax.nn.sigmoid(dot(w_sig[...], pair_norm, 0, 0))
            kept = mask * sig
            factors[2 * side, :, lanes] = kept
            factors[2 * side + 1, :, lanes] = kept * proj * (1.0 - sig)
        gate_act = jax.nn.sigmoid(dot(w_gate[...], pair_norm, 0, 0))
        d_proj = jnp.transpose(grad_ref[r].astype(F32)) * gate_act
        slope[:, lanes] = d_proj * (1.0 - gate_act)
        d_normed[pl.ds(r, hidden, stride=own), :] = (
            dot(w_out[...], d_proj.astype(BF16), 1, 0) * gain_out
        )


def triangle_kernel(own, in_ref, _, out_ref, a_ref, b_ref):
    half = out_ref.shape[1]
    sides = [
        split_channels(in_ref[:, side * half : (side + 1) * half, :].astype(F32), own)
        for side in range(2)
    ]
    tri = []
    for c, (edge_a, edge_b) in enumerate(zip(*sides)):
        a_ref[c] = edge_a.astype(BF16)
        b_ref[c] = edge_b.astype(BF16)
        tri.append(dot(a_ref[c], b_ref[c], 1, 1))
    out_ref[...] = merge_channels(tri, own).astype(BF16)


def fold(values, own):
    total = jnp.sum(values, axis=0)
    rows = total
    for shift in range(own, SUBLANES, own):
        rows = rows + pltpu.roll(total, shift, 0)
    return rows[None]


def tri_normed(tri_ref, hidden, own):
    cols = tri_ref.shape[-1]
    tri = tri_ref[...].astype(F32).reshape(hidden * own // SUBLANES, SUBLANES, cols)
    centre = tri - fold(tri, own) / hidden
    inverse = lax.rsqrt(fold(centre * centre, own) / hidden + EPSILON)
    return centre * inverse, inverse


def norm_kernel(own, tri_ref, grad_ref, slope, gain, bias, w_out, w_gate, out_ref, part_ref):
    devices, block, cols = tri_ref.shape
    hidden = w_out.shape[0]
    normed, inverse = tri_normed(tri_ref, hidden, own)
    grad = grad_ref[...].reshape(normed.shape)
    mean_grad = fold(grad, own) / hidden
    mean_proj = fold(grad * normed, own) / hidden
    d_tri = inverse * (grad - mean_grad - normed * mean_proj)
    out_ref[...] = d_tri.reshape(devices, block, cols).astype(BF16)
    parts = trade(split_channels(normed.reshape(devices, block, cols), own))
    tri_norm = jnp.concatenate([(part * gain[...] + bias[...]).astype(BF16) for part in parts], axis=1)
    d_gate = (slope[...] * dot(w_out[...], tri_norm, 0, 0)).astype(BF16)
    part_ref[...] = dot(w_gate[...], d_gate, 1, 0)


def edge_grad_kernel(own, in_ref, a_ref, b_ref, out_ref):
    block = in_ref.shape[1]
    grads = ([], [])
    for c, part in enumerate(split_channels(in_ref[...].astype(F32), own)):
        d_tri = part.astype(BF16)
        grads[0].append(dot(d_tri, b_ref[c], 1, 0))
        grads[1].append(dot(d_tri, a_ref[c], 0, 0))
    for side in range(2):
        out_ref[:, side * block : (side + 1) * block, :] = (
            merge_channels(grads[side], own).astype(BF16)
        )


def input_grad_kernel(in_ref, factors, normed_t, rstd_t, gain_t, gate_part, wap, wag, wbp, wbg, out_ref):
    own, cols, _ = out_ref.shape
    half = in_ref.shape[1] // 2
    total = gate_part[...]
    for side, weights in enumerate(((wap, wag), (wbp, wbg))):
        blocks = in_ref[:, side * half : (side + 1) * half, :].astype(F32)
        d_edge = jnp.concatenate(trade(split_channels(blocks, own)), axis=1)
        for at, weight in enumerate(weights):
            total = total + dot(weight[...], (d_edge * factors[2 * side + at]).astype(BF16), 1, 0)
    grad_hat = total * jnp.concatenate([gain_t[...]] * own, axis=1)
    normed = normed_t[...]
    mean_grad = jnp.mean(grad_hat, axis=0, keepdims=True)
    mean_proj = jnp.mean(grad_hat * normed, axis=0, keepdims=True)
    grad = rstd_t[...] * (grad_hat - mean_grad - normed * mean_proj)
    for r in range(own):
        out_ref[r] = jnp.transpose(grad[:, r * cols : (r + 1) * cols]).astype(BF16)


VMEM = pl.BlockSpec(memory_space=pltpu.VMEM)
SMEM = pl.BlockSpec(memory_space=pltpu.SMEM)
HBM = pl.BlockSpec(memory_space=pltpu.HBM)


def call(kernel, name, outs, args, scratch=(), scalars=0, flops=0, spaces=None, limit=32 * 2**20):
    shapes = [jax.ShapeDtypeStruct(shape, dtype) for shape, dtype in outs]
    moved = sum(value.size * value.dtype.itemsize for value in list(args) + shapes)
    result = pl.pallas_call(
        kernel,
        name=name,
        out_shape=shapes,
        in_specs=[SMEM] * scalars + (spaces or [VMEM] * (len(args) - scalars)),
        out_specs=[VMEM] * len(outs),
        scratch_shapes=scratch,
        cost_estimate=pl.CostEstimate(flops=flops, bytes_accessed=moved, transcendentals=0),
        compiler_params=pltpu.CompilerParams(vmem_limit_bytes=limit),
    )(*args)
    return result[0] if len(outs) == 1 else result


def kernel_shards(
    dap,
    pair_act,
    out_grad,
    residue_mask,
    ln_in_gain,
    ln_in_bias,
    w_a_proj,
    w_a_gate,
    w_b_proj,
    w_b_gate,
    w_gate,
    ln_out_gain,
    ln_out_bias,
    w_out,
):
    own, cols, chan = pair_act.shape
    hidden = w_a_proj.shape[1]
    slice_h = hidden // dap
    rows = dap * own
    block = slice_h * own
    me = lax.axis_index("dap").reshape(1)
    valid = residue_mask.reshape(1, -1)
    gain_in, bias_in, gain_out, bias_out = (
        value.reshape(1, -1) for value in (ln_in_gain, ln_in_bias, ln_out_gain, ln_out_bias)
    )
    w_edges = (w_a_proj, w_a_gate, w_b_proj, w_b_gate)
    product = 2 * own * cols * chan * hidden

    def exchange(value):
        return lax.all_to_all(value, "dap", split_axis=0, concat_axis=0, tiled=True)

    first = (pair_act, gain_in, bias_in, residue_mask, valid, *w_edges)
    edges = call(
        edges_kernel,
        "edges",
        [((dap, 2 * block, cols), BF16)],
        (me, *first),
        scratch=[
            (pltpu.SMEM if value is residue_mask else pltpu.VMEM)(value.shape, value.dtype)
            for value in first
        ]
        + [pltpu.SemaphoreType.DMA((len(first),))],
        scalars=1,
        flops=4 * product,
        spaces=[HBM] * len(first),
        limit=None,
    )
    edges = exchange(edges)
    factors, normed_t, rstd_t, gain_t, d_normed, slope, gain_out_t, bias_out_t = call(
        gates_kernel,
        "gates",
        [
            ((4, hidden, own * cols), F32),
            ((chan, own * cols), F32),
            ((1, own * cols), F32),
            ((chan, cols), F32),
            ((hidden * own, cols), F32),
            ((chan, own * cols), F32),
            ((hidden, cols), F32),
            ((hidden, cols), F32),
        ],
        (me, residue_mask, valid, pair_act, out_grad, gain_in, bias_in, gain_out)
        + (bias_out, *w_edges, w_gate, w_out),
        scalars=2,
        flops=6 * product,
    )
    tri, edge_a, edge_b = call(
        functools.partial(triangle_kernel, own),
        "triangle",
        [
            ((dap, block, cols), BF16),
            ((slice_h, rows, cols), BF16),
            ((slice_h, rows, cols), BF16),
        ],
        (edges, d_normed),
        flops=product,
        spaces=[VMEM, pl.BlockSpec(memory_space=pl.ANY)],
    )
    tri = exchange(tri)
    d_tri, gate_part = call(
        functools.partial(norm_kernel, own),
        "norm",
        [((dap, block, cols), BF16), ((chan, own * cols), F32)],
        (tri, d_normed, slope, gain_out_t, bias_out_t, w_out, w_gate),
        flops=2 * product,
    )
    d_tri = exchange(d_tri)
    d_edges = call(
        functools.partial(edge_grad_kernel, own),
        "edge_grad",
        [((dap, 2 * block, cols), BF16)],
        (d_tri, edge_a, edge_b),
        flops=2 * product,
    )
    d_edges = exchange(d_edges)
    return call(
        input_grad_kernel,
        "input_grad",
        [((own, cols, chan), BF16)],
        (d_edges, factors, normed_t, rstd_t, gain_t, gate_part, *w_edges),
        flops=4 * product,
    )


def fits_kernels(dap, ch, pair_act, w_proj):
    own, cols, chan = pair_act.shape
    hidden = w_proj.shape[1]
    block = hidden // dap * own
    return (
        ch == 1
        and hidden % dap == 0
        and own == SUBLANES // 2
        and block == own * own
        and dap % SUBLANES == 0
        and cols == dap * own
        and cols % 128 == chan % 128 == hidden % 128 == 0
    )


def solution(mesh):
    sizes = dict(mesh.shape)

    def program(*args):
        dap, ch = sizes["dap"], sizes["ch"]
        if fits_kernels(dap, ch, args[0], args[5]):
            return kernel_shards(dap, *args)
        return channel_shards(dap, ch, *args)

    in_specs = (
        P(("grp", "dap"), None, None),
        P(("grp", "dap"), "ch", None),
        P("grp"),
        P(),
        P(),
        P(None, "ch"),
        P(None, "ch"),
        P(None, "ch"),
        P(None, "ch"),
        P(),
        P(),
        P(),
        P(),
    )
    out_specs = P(("grp", "dap"), "ch", None)
    return jax.shard_map(
        program, mesh=mesh, in_specs=in_specs, out_specs=out_specs, check_vma=False
    )
```

```python
import functools

import jax
import jax.numpy as jnp
from jax import lax
from jax.experimental import pallas as pl
from jax.experimental.pallas import tpu as pltpu
from jax.sharding import PartitionSpec as P

EPSILON = 1e-05


def normalise(values, reduce_dim):
    centre = values - jnp.mean(values, axis=reduce_dim, keepdims=True)
    inverse = lax.rsqrt(jnp.mean(centre * centre, axis=reduce_dim, keepdims=True) + EPSILON)
    return (centre * inverse, inverse)


def norm_backward(grad_hat, normed, inverse, reduce_dim):
    mean_grad = jnp.mean(grad_hat, axis=reduce_dim, keepdims=True)
    mean_proj = jnp.mean(grad_hat * normed, axis=reduce_dim, keepdims=True)
    return inverse * (grad_hat - mean_grad - normed * mean_proj)


def channel_shards(
    dap,
    ch,
    pair_act,
    out_grad,
    residue_mask,
    ln_in_gain,
    ln_in_bias,
    w_a_proj,
    w_a_gate,
    w_b_proj,
    w_b_gate,
    w_gate,
    ln_out_gain,
    ln_out_bias,
    w_out,
):
    own_rows, all_cols = pair_act.shape[:2]
    col_span = out_grad.shape[1]
    hidden_local = w_a_proj.shape[1]
    slice_h = hidden_local // dap
    row_first = lax.axis_index("dap") * own_rows
    col_first = lax.axis_index("ch") * col_span
    normed_in, rstd_in = normalise(pair_act.astype(jnp.float32), 2)
    pair_norm = (normed_in * ln_in_gain + ln_in_bias).astype(jnp.bfloat16)
    valid_all = residue_mask.astype(jnp.float32)
    valid_rows = lax.dynamic_slice_in_dim(valid_all, row_first, own_rows)
    row_mask = (valid_rows[:, None] * valid_all[None, :])[None]
    w_four = jnp.concatenate((w_a_proj, w_a_gate, w_b_proj, w_b_gate), axis=1)
    projected = jnp.einsum("ikc,cg->gik", pair_norm, w_four, preferred_element_type=jnp.float32)
    a_proj = projected[:hidden_local]
    a_sig = jax.nn.sigmoid(projected[hidden_local : 2 * hidden_local])
    b_proj = projected[2 * hidden_local : 3 * hidden_local]
    b_sig = jax.nn.sigmoid(projected[3 * hidden_local :])
    edge_a = (row_mask * a_sig * a_proj).astype(jnp.bfloat16)
    edge_b = (row_mask * b_sig * b_proj).astype(jnp.bfloat16)

    split = (dap, slice_h, own_rows, all_cols)
    edges = jnp.stack((edge_a.reshape(split), edge_b.reshape(split)), axis=1)
    edges = lax.all_to_all(edges, "dap", split_axis=0, concat_axis=0, tiled=True)
    edges = jnp.transpose(edges, (1, 2, 0, 3, 4)).reshape(2, slice_h, dap * own_rows, all_cols)
    a_all, b_all = edges[0], edges[1]
    tri = jnp.einsum("hik,hjk->hij", a_all, b_all, preferred_element_type=jnp.float32).astype(
        jnp.bfloat16
    )
    tri = tri.reshape(slice_h, dap, own_rows, ch, col_span)
    tri = jnp.transpose(tri, (1, 3, 0, 2, 4)).reshape(dap * ch, slice_h, own_rows, col_span)
    tri = lax.all_to_all(tri, ("dap", "ch"), split_axis=0, concat_axis=0, tiled=True)
    tri = tri.reshape(dap, ch, slice_h, own_rows, col_span)
    tri_full = jnp.transpose(tri, (1, 0, 2, 3, 4)).reshape(-1, own_rows, col_span)

    normed_out, rstd_out = normalise(tri_full.astype(jnp.float32), 0)
    gain_out = ln_out_gain.reshape(-1, 1, 1)
    bias_out = ln_out_bias.reshape(-1, 1, 1)
    tri_norm = (normed_out * gain_out + bias_out).astype(jnp.bfloat16)
    proj_out = jnp.einsum("hij,hc->ijc", tri_norm, w_out, preferred_element_type=jnp.float32)
    norm_cols = lax.dynamic_slice_in_dim(pair_norm, col_first, col_span, 1)
    gate_act = jax.nn.sigmoid(
        jnp.einsum("ijc,cd->ijd", norm_cols, w_gate, preferred_element_type=jnp.float32)
    )
    upstream = out_grad.astype(jnp.float32)
    d_proj = (upstream * gate_act).astype(jnp.bfloat16)
    d_gate = (upstream * proj_out * gate_act * (1.0 - gate_act)).astype(jnp.bfloat16)
    d_normed = (
        jnp.einsum("ijc,hc->hij", d_proj, w_out, preferred_element_type=jnp.float32) * gain_out
    )
    d_tri = norm_backward(d_normed, normed_out, rstd_out, 0).astype(jnp.bfloat16)

    d_tri = d_tri.reshape(ch, dap, slice_h, own_rows, col_span)
    d_tri = jnp.transpose(d_tri, (1, 0, 2, 3, 4)).reshape(dap * ch, slice_h, own_rows, col_span)
    d_tri = lax.all_to_all(d_tri, ("dap", "ch"), split_axis=0, concat_axis=0, tiled=True)
    d_tri = d_tri.reshape(dap, ch, slice_h, own_rows, col_span)
    d_tri = jnp.transpose(d_tri, (2, 0, 3, 1, 4)).reshape(slice_h, dap * own_rows, all_cols)
    d_edge_a = jnp.einsum("hij,hjk->hik", d_tri, b_all, preferred_element_type=jnp.float32)
    d_edge_b = jnp.einsum("hij,hik->hjk", d_tri, a_all, preferred_element_type=jnp.float32)
    d_edges = jnp.stack((d_edge_a, d_edge_b)).astype(jnp.bfloat16)
    d_edges = d_edges.reshape(2, slice_h, dap, own_rows, all_cols)
    d_edges = jnp.transpose(d_edges, (2, 0, 1, 3, 4))
    d_edges = lax.all_to_all(d_edges, "dap", split_axis=0, concat_axis=0, tiled=True)
    d_edges = jnp.transpose(d_edges, (1, 0, 2, 3, 4)).reshape(2, hidden_local, own_rows, all_cols)

    def split_grad(d_edge, sig_val, proj_val):
        masked = d_edge * row_mask
        return (
            (masked * sig_val).astype(jnp.bfloat16),
            (masked * proj_val * sig_val * (1.0 - sig_val)).astype(jnp.bfloat16),
        )

    d_four = jnp.concatenate(
        split_grad(d_edges[0].astype(jnp.float32), a_sig, a_proj)
        + split_grad(d_edges[1].astype(jnp.float32), b_sig, b_proj),
        axis=0,
    )
    d_hidden = jnp.einsum("gik,cg->ikc", d_four, w_four, preferred_element_type=jnp.float32)
    if ch > 1:
        d_hidden = lax.psum_scatter(
            d_hidden.astype(jnp.bfloat16), "ch", scatter_dimension=1, tiled=True
        ).astype(jnp.float32)
    d_pair_norm = d_hidden + jnp.einsum(
        "ijd,cd->ijc", d_gate, w_gate, preferred_element_type=jnp.float32
    )
    normed_cols = lax.dynamic_slice_in_dim(normed_in, col_first, col_span, 1)
    rstd_cols = lax.dynamic_slice_in_dim(rstd_in, col_first, col_span, 1)
    grad_hat = d_pair_norm * ln_in_gain
    return norm_backward(grad_hat, normed_cols, rstd_cols, 2).astype(jnp.bfloat16)


F32 = jnp.float32
BF16 = jnp.bfloat16
SUBLANES = 8
LEVELS = 4


def dot(lhs, rhs, lhs_dim, rhs_dim):
    return lax.dot_general(
        lhs, rhs, (((lhs_dim,), (rhs_dim,)), ((), ())), preferred_element_type=F32
    )


def across(row, count):
    return jnp.transpose(jnp.broadcast_to(row, (count, row.shape[1])))


def normed_rows(act):
    centre = act - jnp.mean(act, axis=1, keepdims=True)
    return centre * lax.rsqrt(jnp.mean(centre * centre, axis=1, keepdims=True) + EPSILON)


def exchange_bit(first, second, weight):
    sublane = lax.broadcasted_iota(jnp.int32, first.shape, 1)
    low = sublane & weight == 0
    return (
        jnp.where(low, first, pltpu.roll(second, weight, 1)),
        jnp.where(low, pltpu.roll(first, SUBLANES - weight, 1), second),
    )


def mesh_order(blocks):
    count, *rest = blocks.shape
    return jnp.swapaxes(blocks.reshape(count // LEVELS, LEVELS, *rest), 0, 1).reshape(blocks.shape)


def list_order(blocks):
    count, *rest = blocks.shape
    return jnp.swapaxes(blocks.reshape(LEVELS, count // LEVELS, *rest), 0, 1).reshape(blocks.shape)


def split_channels(blocks, own):
    devices, block, cols = blocks.shape
    tiles = blocks.reshape(devices // 2, 2, block // SUBLANES, SUBLANES, cols)
    parts = []
    for tile in range(block // SUBLANES):
        parts.extend(exchange_bit(tiles[:, 0, tile], tiles[:, 1, tile], own))
    return [part.reshape(devices * own, cols) for part in parts]


def merge_channels(parts, own):
    rows, cols = parts[0].shape
    devices = rows // own
    tiles = [part.reshape(devices // 2, SUBLANES, cols) for part in parts]
    pairs = [exchange_bit(*pair, own) for pair in zip(tiles[::2], tiles[1::2])]
    both = [jnp.concatenate(side, axis=1) for side in zip(*pairs)]
    block = len(parts) * own
    return jnp.stack(both, axis=1).reshape(devices, block, cols)


def trade(parts):
    rows, cols = parts[0].shape
    a, b, c, d = (part.reshape(rows // SUBLANES, SUBLANES, cols) for part in parts)
    (a, b), (c, d) = exchange_bit(a, b, 1), exchange_bit(c, d, 1)
    (a, c), (b, d) = exchange_bit(a, c, 2), exchange_bit(b, d, 2)
    return [part.reshape(rows, cols) for part in (a, b, c, d)]


def edges_kernel(me_ref, *refs):
    sources, (out_ref, *local), arrived = refs[:9], refs[9:19], refs[19]
    copies = [
        pltpu.make_async_copy(source, target, arrived.at[index])
        for index, (source, target) in enumerate(zip(sources, local))
    ]
    for copy in copies:
        copy.start()
    act_ref, gain_ref, bias_ref, rows_ref, valid_ref, *weights = local
    own, cols, chan = act_ref.shape
    half = out_ref.shape[1] // 2
    for copy in copies[:3]:
        copy.wait()
    normed = normed_rows(act_ref[...].reshape(own * cols, chan).astype(F32))
    pair_norm = (normed * gain_ref[...] + bias_ref[...]).astype(BF16)
    for copy in copies[3:]:
        copy.wait()
    valid = valid_ref[...].astype(F32)
    mask = jnp.concatenate(
        [valid * rows_ref[me_ref[0] * own + r].astype(F32) for r in range(own)], axis=1
    )
    for side in range(2):
        proj = dot(weights[2 * side][...], pair_norm, 0, 1)
        edge = mask * jax.nn.sigmoid(dot(weights[2 * side + 1][...], pair_norm, 0, 1)) * proj
        parts = trade([edge[:, r * cols : (r + 1) * cols] for r in range(own)])
        out_ref[:, side * half : (side + 1) * half, :] = merge_channels(parts, own).astype(BF16)


def gates_kernel(
    me_ref, rows_ref, valid_ref, act_ref, grad_ref, gain_ref, bias_ref, gain_out_ref, bias_out_ref,
    wap, wag, wbp, wbg, w_gate, w_out,
    factors, normed_t, rstd_t, gain_t, d_normed, slope, gain_out_t, bias_out_t,
):
    own, cols, _ = act_ref.shape
    hidden = wap.shape[1]
    valid = valid_ref[...].astype(F32)
    gain = across(gain_ref[...], cols)
    bias = across(bias_ref[...], cols)
    gain_out = across(gain_out_ref[...], cols)
    gain_t[...] = gain
    gain_out_t[...] = gain_out
    bias_out_t[...] = across(bias_out_ref[...], cols)
    for r in range(own):
        act = jnp.transpose(act_ref[r].astype(F32))
        centre = act - jnp.mean(act, axis=0, keepdims=True)
        inverse = lax.rsqrt(jnp.mean(centre * centre, axis=0, keepdims=True) + EPSILON)
        normed = centre * inverse
        lanes = pl.ds(r * cols, cols)
        normed_t[:, lanes] = normed
        rstd_t[:, lanes] = inverse
        pair_norm = (normed * gain + bias).astype(BF16)
        mask = valid * rows_ref[me_ref[0] * own + r].astype(F32)
        for side, (w_proj, w_sig) in enumerate(((wap, wag), (wbp, wbg))):
            proj = dot(w_proj[...], pair_norm, 0, 0)
            sig = jax.nn.sigmoid(dot(w_sig[...], pair_norm, 0, 0))
            kept = mask * sig
            factors[2 * side, :, lanes] = kept
            factors[2 * side + 1, :, lanes] = kept * proj * (1.0 - sig)
        gate_act = jax.nn.sigmoid(dot(w_gate[...], pair_norm, 0, 0))
        d_proj = jnp.transpose(grad_ref[r].astype(F32)) * gate_act
        slope[:, lanes] = d_proj * (1.0 - gate_act)
        d_normed[pl.ds(r, hidden, stride=own), :] = (
            dot(w_out[...], d_proj.astype(BF16), 1, 0) * gain_out
        )


def triangle_kernel(own, in_ref, _, out_ref, a_ref, b_ref):
    half = out_ref.shape[1]
    sides = [
        split_channels(
            mesh_order(in_ref[:, side * half : (side + 1) * half, :].astype(F32)), own
        )
        for side in range(2)
    ]
    tri = []
    for c, (edge_a, edge_b) in enumerate(zip(*sides)):
        a_ref[c] = edge_a.astype(BF16)
        b_ref[c] = edge_b.astype(BF16)
        tri.append(dot(a_ref[c], b_ref[c], 1, 1))
    out_ref[...] = list_order(merge_channels(tri, own)).astype(BF16)


def fold(values, own):
    total = jnp.sum(values, axis=0)
    rows = total
    for shift in range(own, SUBLANES, own):
        rows = rows + pltpu.roll(total, shift, 0)
    return rows[None]


def tri_normed(tri_ref, hidden, own):
    cols = tri_ref.shape[-1]
    tri = tri_ref[...].astype(F32).reshape(hidden * own // SUBLANES, SUBLANES, cols)
    centre = tri - fold(tri, own) / hidden
    inverse = lax.rsqrt(fold(centre * centre, own) / hidden + EPSILON)
    return centre * inverse, inverse


def norm_kernel(own, tri_ref, grad_ref, slope, gain, bias, w_out, w_gate, out_ref, part_ref):
    devices, block, cols = tri_ref.shape
    hidden = w_out.shape[0]
    normed, inverse = tri_normed(tri_ref, hidden, own)
    grad = grad_ref[...].reshape(normed.shape)
    mean_grad = fold(grad, own) / hidden
    mean_proj = fold(grad * normed, own) / hidden
    d_tri = inverse * (grad - mean_grad - normed * mean_proj)
    out_ref[...] = d_tri.reshape(devices, block, cols).astype(BF16)
    parts = trade(split_channels(normed.reshape(devices, block, cols), own))
    tri_norm = jnp.concatenate([(part * gain[...] + bias[...]).astype(BF16) for part in parts], axis=1)
    d_gate = (slope[...] * dot(w_out[...], tri_norm, 0, 0)).astype(BF16)
    part_ref[...] = dot(w_gate[...], d_gate, 1, 0)


def edge_grad_kernel(own, in_ref, a_ref, b_ref, out_ref):
    block = in_ref.shape[1]
    grads = ([], [])
    for c, part in enumerate(split_channels(mesh_order(in_ref[...].astype(F32)), own)):
        d_tri = part.astype(BF16)
        grads[0].append(dot(d_tri, b_ref[c], 1, 0))
        grads[1].append(dot(d_tri, a_ref[c], 0, 0))
    for side in range(2):
        out_ref[:, side * block : (side + 1) * block, :] = (
            list_order(merge_channels(grads[side], own)).astype(BF16)
        )


def input_grad_kernel(in_ref, factors, normed_t, rstd_t, gain_t, gate_part, wap, wag, wbp, wbg, out_ref):
    own, cols, _ = out_ref.shape
    half = in_ref.shape[1] // 2
    total = gate_part[...]
    for side, weights in enumerate(((wap, wag), (wbp, wbg))):
        blocks = in_ref[:, side * half : (side + 1) * half, :].astype(F32)
        d_edge = jnp.concatenate(trade(split_channels(blocks, own)), axis=1)
        for at, weight in enumerate(weights):
            total = total + dot(weight[...], (d_edge * factors[2 * side + at]).astype(BF16), 1, 0)
    grad_hat = total * jnp.concatenate([gain_t[...]] * own, axis=1)
    normed = normed_t[...]
    mean_grad = jnp.mean(grad_hat, axis=0, keepdims=True)
    mean_proj = jnp.mean(grad_hat * normed, axis=0, keepdims=True)
    grad = rstd_t[...] * (grad_hat - mean_grad - normed * mean_proj)
    for r in range(own):
        out_ref[r] = jnp.transpose(grad[:, r * cols : (r + 1) * cols]).astype(BF16)


VMEM = pl.BlockSpec(memory_space=pltpu.VMEM)
SMEM = pl.BlockSpec(memory_space=pltpu.SMEM)
HBM = pl.BlockSpec(memory_space=pltpu.HBM)


def call(kernel, name, outs, args, scratch=(), scalars=0, flops=0, spaces=None, limit=32 * 2**20):
    shapes = [jax.ShapeDtypeStruct(shape, dtype) for shape, dtype in outs]
    moved = sum(value.size * value.dtype.itemsize for value in list(args) + shapes)
    result = pl.pallas_call(
        kernel,
        name=name,
        out_shape=shapes,
        in_specs=[SMEM] * scalars + (spaces or [VMEM] * (len(args) - scalars)),
        out_specs=[VMEM] * len(outs),
        scratch_shapes=scratch,
        cost_estimate=pl.CostEstimate(flops=flops, bytes_accessed=moved, transcendentals=0),
        compiler_params=pltpu.CompilerParams(vmem_limit_bytes=limit),
    )(*args)
    return result[0] if len(outs) == 1 else result


def kernel_shards(
    dap,
    pair_act,
    out_grad,
    residue_mask,
    ln_in_gain,
    ln_in_bias,
    w_a_proj,
    w_a_gate,
    w_b_proj,
    w_b_gate,
    w_gate,
    ln_out_gain,
    ln_out_bias,
    w_out,
):
    own, cols, chan = pair_act.shape
    hidden = w_a_proj.shape[1]
    slice_h = hidden // dap
    rows = dap * own
    block = slice_h * own
    me = lax.axis_index("dap").reshape(1)
    valid = residue_mask.reshape(1, -1)
    gain_in, bias_in, gain_out, bias_out = (
        value.reshape(1, -1) for value in (ln_in_gain, ln_in_bias, ln_out_gain, ln_out_bias)
    )
    w_edges = (w_a_proj, w_a_gate, w_b_proj, w_b_gate)
    product = 2 * own * cols * chan * hidden

    listed = [quarter * (dap // LEVELS) + at for at in range(dap // LEVELS) for quarter in range(LEVELS)]

    def exchange(value):
        return lax.all_to_all(
            value, "dap", split_axis=0, concat_axis=0, axis_index_groups=[listed], tiled=True
        )

    first = (pair_act, gain_in, bias_in, residue_mask, valid, *w_edges)
    edges = call(
        edges_kernel,
        "edges",
        [((dap, 2 * block, cols), BF16)],
        (me, *first),
        scratch=[
            (pltpu.SMEM if value is residue_mask else pltpu.VMEM)(value.shape, value.dtype)
            for value in first
        ]
        + [pltpu.SemaphoreType.DMA((len(first),))],
        scalars=1,
        flops=4 * product,
        spaces=[HBM] * len(first),
        limit=None,
    )
    edges = exchange(edges)
    factors, normed_t, rstd_t, gain_t, d_normed, slope, gain_out_t, bias_out_t = call(
        gates_kernel,
        "gates",
        [
            ((4, hidden, own * cols), F32),
            ((chan, own * cols), F32),
            ((1, own * cols), F32),
            ((chan, cols), F32),
            ((hidden * own, cols), F32),
            ((chan, own * cols), F32),
            ((hidden, cols), F32),
            ((hidden, cols), F32),
        ],
        (me, residue_mask, valid, pair_act, out_grad, gain_in, bias_in, gain_out)
        + (bias_out, *w_edges, w_gate, w_out),
        scalars=2,
        flops=6 * product,
    )
    tri, edge_a, edge_b = call(
        functools.partial(triangle_kernel, own),
        "triangle",
        [
            ((dap, block, cols), BF16),
            ((slice_h, rows, cols), BF16),
            ((slice_h, rows, cols), BF16),
        ],
        (edges, d_normed),
        flops=product,
        spaces=[VMEM, pl.BlockSpec(memory_space=pl.ANY)],
    )
    tri = exchange(tri)
    d_tri, gate_part = call(
        functools.partial(norm_kernel, own),
        "norm",
        [((dap, block, cols), BF16), ((chan, own * cols), F32)],
        (tri, d_normed, slope, gain_out_t, bias_out_t, w_out, w_gate),
        flops=2 * product,
    )
    d_tri = exchange(d_tri)
    d_edges = call(
        functools.partial(edge_grad_kernel, own),
        "edge_grad",
        [((dap, 2 * block, cols), BF16)],
        (d_tri, edge_a, edge_b),
        flops=2 * product,
    )
    d_edges = exchange(d_edges)
    return call(
        input_grad_kernel,
        "input_grad",
        [((own, cols, chan), BF16)],
        (d_edges, factors, normed_t, rstd_t, gain_t, gate_part, *w_edges),
        flops=4 * product,
    )


def fits_kernels(dap, ch, pair_act, w_proj):
    own, cols, chan = pair_act.shape
    hidden = w_proj.shape[1]
    block = hidden // dap * own
    return (
        ch == 1
        and hidden % dap == 0
        and own == SUBLANES // 2
        and block == own * own
        and dap % SUBLANES == 0
        and cols == dap * own
        and cols % 128 == chan % 128 == hidden % 128 == 0
    )


def solution(mesh):
    sizes = dict(mesh.shape)

    def program(*args):
        dap, ch = sizes["dap"], sizes["ch"]
        if fits_kernels(dap, ch, args[0], args[5]):
            return kernel_shards(dap, *args)
        return channel_shards(dap, ch, *args)

    in_specs = (
        P(("grp", "dap"), None, None),
        P(("grp", "dap"), "ch", None),
        P("grp"),
        P(),
        P(),
        P(None, "ch"),
        P(None, "ch"),
        P(None, "ch"),
        P(None, "ch"),
        P(),
        P(),
        P(),
        P(),
    )
    out_specs = P(("grp", "dap"), "ch", None)
    return jax.shard_map(
        program, mesh=mesh, in_specs=in_specs, out_specs=out_specs, check_vma=False
    )
```

```python
import functools

import jax
import jax.numpy as jnp
from jax import lax
from jax.experimental import pallas as pl
from jax.experimental.pallas import tpu as pltpu
from jax.sharding import PartitionSpec as P

EPSILON = 1e-05


def normalise(values, reduce_dim):
    centre = values - jnp.mean(values, axis=reduce_dim, keepdims=True)
    inverse = lax.rsqrt(jnp.mean(centre * centre, axis=reduce_dim, keepdims=True) + EPSILON)
    return (centre * inverse, inverse)


def norm_backward(grad_hat, normed, inverse, reduce_dim):
    mean_grad = jnp.mean(grad_hat, axis=reduce_dim, keepdims=True)
    mean_proj = jnp.mean(grad_hat * normed, axis=reduce_dim, keepdims=True)
    return inverse * (grad_hat - mean_grad - normed * mean_proj)


def channel_shards(
    dap,
    ch,
    pair_act,
    out_grad,
    residue_mask,
    ln_in_gain,
    ln_in_bias,
    w_a_proj,
    w_a_gate,
    w_b_proj,
    w_b_gate,
    w_gate,
    ln_out_gain,
    ln_out_bias,
    w_out,
):
    own_rows, all_cols = pair_act.shape[:2]
    col_span = out_grad.shape[1]
    hidden_local = w_a_proj.shape[1]
    slice_h = hidden_local // dap
    row_first = lax.axis_index("dap") * own_rows
    col_first = lax.axis_index("ch") * col_span
    normed_in, rstd_in = normalise(pair_act.astype(jnp.float32), 2)
    pair_norm = (normed_in * ln_in_gain + ln_in_bias).astype(jnp.bfloat16)
    valid_all = residue_mask.astype(jnp.float32)
    valid_rows = lax.dynamic_slice_in_dim(valid_all, row_first, own_rows)
    row_mask = (valid_rows[:, None] * valid_all[None, :])[None]
    w_four = jnp.concatenate((w_a_proj, w_a_gate, w_b_proj, w_b_gate), axis=1)
    projected = jnp.einsum("ikc,cg->gik", pair_norm, w_four, preferred_element_type=jnp.float32)
    a_proj = projected[:hidden_local]
    a_sig = jax.nn.sigmoid(projected[hidden_local : 2 * hidden_local])
    b_proj = projected[2 * hidden_local : 3 * hidden_local]
    b_sig = jax.nn.sigmoid(projected[3 * hidden_local :])
    edge_a = (row_mask * a_sig * a_proj).astype(jnp.bfloat16)
    edge_b = (row_mask * b_sig * b_proj).astype(jnp.bfloat16)

    split = (dap, slice_h, own_rows, all_cols)
    edges = jnp.stack((edge_a.reshape(split), edge_b.reshape(split)), axis=1)
    edges = lax.all_to_all(edges, "dap", split_axis=0, concat_axis=0, tiled=True)
    edges = jnp.transpose(edges, (1, 2, 0, 3, 4)).reshape(2, slice_h, dap * own_rows, all_cols)
    a_all, b_all = edges[0], edges[1]
    tri = jnp.einsum("hik,hjk->hij", a_all, b_all, preferred_element_type=jnp.float32).astype(
        jnp.bfloat16
    )
    tri = tri.reshape(slice_h, dap, own_rows, ch, col_span)
    tri = jnp.transpose(tri, (1, 3, 0, 2, 4)).reshape(dap * ch, slice_h, own_rows, col_span)
    tri = lax.all_to_all(tri, ("dap", "ch"), split_axis=0, concat_axis=0, tiled=True)
    tri = tri.reshape(dap, ch, slice_h, own_rows, col_span)
    tri_full = jnp.transpose(tri, (1, 0, 2, 3, 4)).reshape(-1, own_rows, col_span)

    normed_out, rstd_out = normalise(tri_full.astype(jnp.float32), 0)
    gain_out = ln_out_gain.reshape(-1, 1, 1)
    bias_out = ln_out_bias.reshape(-1, 1, 1)
    tri_norm = (normed_out * gain_out + bias_out).astype(jnp.bfloat16)
    proj_out = jnp.einsum("hij,hc->ijc", tri_norm, w_out, preferred_element_type=jnp.float32)
    norm_cols = lax.dynamic_slice_in_dim(pair_norm, col_first, col_span, 1)
    gate_act = jax.nn.sigmoid(
        jnp.einsum("ijc,cd->ijd", norm_cols, w_gate, preferred_element_type=jnp.float32)
    )
    upstream = out_grad.astype(jnp.float32)
    d_proj = (upstream * gate_act).astype(jnp.bfloat16)
    d_gate = (upstream * proj_out * gate_act * (1.0 - gate_act)).astype(jnp.bfloat16)
    d_normed = (
        jnp.einsum("ijc,hc->hij", d_proj, w_out, preferred_element_type=jnp.float32) * gain_out
    )
    d_tri = norm_backward(d_normed, normed_out, rstd_out, 0).astype(jnp.bfloat16)

    d_tri = d_tri.reshape(ch, dap, slice_h, own_rows, col_span)
    d_tri = jnp.transpose(d_tri, (1, 0, 2, 3, 4)).reshape(dap * ch, slice_h, own_rows, col_span)
    d_tri = lax.all_to_all(d_tri, ("dap", "ch"), split_axis=0, concat_axis=0, tiled=True)
    d_tri = d_tri.reshape(dap, ch, slice_h, own_rows, col_span)
    d_tri = jnp.transpose(d_tri, (2, 0, 3, 1, 4)).reshape(slice_h, dap * own_rows, all_cols)
    d_edge_a = jnp.einsum("hij,hjk->hik", d_tri, b_all, preferred_element_type=jnp.float32)
    d_edge_b = jnp.einsum("hij,hik->hjk", d_tri, a_all, preferred_element_type=jnp.float32)
    d_edges = jnp.stack((d_edge_a, d_edge_b)).astype(jnp.bfloat16)
    d_edges = d_edges.reshape(2, slice_h, dap, own_rows, all_cols)
    d_edges = jnp.transpose(d_edges, (2, 0, 1, 3, 4))
    d_edges = lax.all_to_all(d_edges, "dap", split_axis=0, concat_axis=0, tiled=True)
    d_edges = jnp.transpose(d_edges, (1, 0, 2, 3, 4)).reshape(2, hidden_local, own_rows, all_cols)

    def split_grad(d_edge, sig_val, proj_val):
        masked = d_edge * row_mask
        return (
            (masked * sig_val).astype(jnp.bfloat16),
            (masked * proj_val * sig_val * (1.0 - sig_val)).astype(jnp.bfloat16),
        )

    d_four = jnp.concatenate(
        split_grad(d_edges[0].astype(jnp.float32), a_sig, a_proj)
        + split_grad(d_edges[1].astype(jnp.float32), b_sig, b_proj),
        axis=0,
    )
    d_hidden = jnp.einsum("gik,cg->ikc", d_four, w_four, preferred_element_type=jnp.float32)
    if ch > 1:
        d_hidden = lax.psum_scatter(
            d_hidden.astype(jnp.bfloat16), "ch", scatter_dimension=1, tiled=True
        ).astype(jnp.float32)
    d_pair_norm = d_hidden + jnp.einsum(
        "ijd,cd->ijc", d_gate, w_gate, preferred_element_type=jnp.float32
    )
    normed_cols = lax.dynamic_slice_in_dim(normed_in, col_first, col_span, 1)
    rstd_cols = lax.dynamic_slice_in_dim(rstd_in, col_first, col_span, 1)
    grad_hat = d_pair_norm * ln_in_gain
    return norm_backward(grad_hat, normed_cols, rstd_cols, 2).astype(jnp.bfloat16)


F32 = jnp.float32
BF16 = jnp.bfloat16
SUBLANES = 8
LEVELS = 4


def dot(lhs, rhs, lhs_dim, rhs_dim):
    return lax.dot_general(
        lhs, rhs, (((lhs_dim,), (rhs_dim,)), ((), ())), preferred_element_type=F32
    )


def across(row, count):
    return jnp.transpose(jnp.broadcast_to(row, (count, row.shape[1])))


def exchange_bit(first, second, weight):
    sublane = lax.broadcasted_iota(jnp.int32, first.shape, 1)
    low = sublane & weight == 0
    return (
        jnp.where(low, first, pltpu.roll(second, weight, 1)),
        jnp.where(low, pltpu.roll(first, SUBLANES - weight, 1), second),
    )


def mesh_order(blocks):
    count, *rest = blocks.shape
    return jnp.swapaxes(blocks.reshape(count // LEVELS, LEVELS, *rest), 0, 1).reshape(blocks.shape)


def list_order(blocks):
    count, *rest = blocks.shape
    return jnp.swapaxes(blocks.reshape(LEVELS, count // LEVELS, *rest), 0, 1).reshape(blocks.shape)


def split_channels(blocks, own):
    devices, block, cols = blocks.shape
    tiles = blocks.reshape(devices // 2, 2, block // SUBLANES, SUBLANES, cols)
    parts = []
    for tile in range(block // SUBLANES):
        parts.extend(exchange_bit(tiles[:, 0, tile], tiles[:, 1, tile], own))
    return [part.reshape(devices * own, cols) for part in parts]


def merge_channels(parts, own):
    rows, cols = parts[0].shape
    devices = rows // own
    tiles = [part.reshape(devices // 2, SUBLANES, cols) for part in parts]
    pairs = [exchange_bit(*pair, own) for pair in zip(tiles[::2], tiles[1::2])]
    both = [jnp.concatenate(side, axis=1) for side in zip(*pairs)]
    block = len(parts) * own
    return jnp.stack(both, axis=1).reshape(devices, block, cols)


def trade(parts):
    rows, cols = parts[0].shape
    a, b, c, d = (part.reshape(rows // SUBLANES, SUBLANES, cols) for part in parts)
    (a, b), (c, d) = exchange_bit(a, b, 1), exchange_bit(c, d, 1)
    (a, c), (b, d) = exchange_bit(a, c, 2), exchange_bit(b, d, 2)
    return [part.reshape(rows, cols) for part in (a, b, c, d)]


def edges_kernel(me_ref, *refs):
    sources, (out_ref, *local), (blocks, arrived, left) = refs[:9], refs[9:19], refs[19:]
    copies = [
        pltpu.make_async_copy(source, target, arrived.at[index])
        for index, (source, target) in enumerate(zip(sources, local))
    ]
    for copy in copies:
        copy.start()
    act_ref, gain_ref, bias_ref, rows_ref, valid_ref, *weights = local
    own, cols, chan = act_ref.shape
    half = out_ref.shape[1] // 2
    for copy in copies[:3]:
        copy.wait()
    act = jnp.concatenate([jnp.transpose(act_ref[r].astype(F32)) for r in range(own)], axis=1)
    gain = across(gain_ref[...], cols)
    bias = across(bias_ref[...], cols)
    centre = act - jnp.mean(act, axis=0, keepdims=True)
    inverse = lax.rsqrt(jnp.mean(centre * centre, axis=0, keepdims=True) + EPSILON)
    wide_gain, wide_bias = (jnp.concatenate([value] * own, axis=1) for value in (gain, bias))
    pair_norm = (centre * inverse * wide_gain + wide_bias).astype(BF16)
    for copy in copies[3:]:
        copy.wait()
    valid = valid_ref[...].astype(F32)
    mask = jnp.concatenate(
        [valid * rows_ref[me_ref[0] * own + r].astype(F32) for r in range(own)], axis=1
    )
    sent = []
    for side in range(2):
        proj = dot(weights[2 * side][...], pair_norm, 0, 0)
        edge = mask * jax.nn.sigmoid(dot(weights[2 * side + 1][...], pair_norm, 0, 0)) * proj
        parts = trade([edge[:, r * cols : (r + 1) * cols] for r in range(own)])
        blocks[side] = merge_channels(parts, own).astype(BF16)
        copy = pltpu.make_async_copy(
            blocks.at[side], out_ref.at[:, side * half : (side + 1) * half, :], left.at[side]
        )
        copy.start()
        sent.append(copy)
    for copy in sent:
        copy.wait()


def gates_kernel(
    me_ref, rows_ref, valid_ref, act_ref, grad_ref, gain_ref, bias_ref, gain_out_ref, bias_out_ref,
    wap, wag, wbp, wbg, w_gate, w_out,
    factors, normed_t, rstd_t, gain_t, d_normed, slope, gain_out_t, bias_out_t,
):
    own, cols, _ = act_ref.shape
    hidden = wap.shape[1]
    valid = valid_ref[...].astype(F32)
    gain = across(gain_ref[...], cols)
    bias = across(bias_ref[...], cols)
    gain_out = across(gain_out_ref[...], cols)
    gain_t[...] = gain
    gain_out_t[...] = gain_out
    bias_out_t[...] = across(bias_out_ref[...], cols)
    for r in range(own):
        act = jnp.transpose(act_ref[r].astype(F32))
        centre = act - jnp.mean(act, axis=0, keepdims=True)
        inverse = lax.rsqrt(jnp.mean(centre * centre, axis=0, keepdims=True) + EPSILON)
        normed = centre * inverse
        lanes = pl.ds(r * cols, cols)
        normed_t[:, lanes] = normed
        rstd_t[:, lanes] = inverse
        pair_norm = (normed * gain + bias).astype(BF16)
        mask = valid * rows_ref[me_ref[0] * own + r].astype(F32)
        for side, (w_proj, w_sig) in enumerate(((wap, wag), (wbp, wbg))):
            proj = dot(w_proj[...], pair_norm, 0, 0)
            sig = jax.nn.sigmoid(dot(w_sig[...], pair_norm, 0, 0))
            kept = mask * sig
            factors[2 * side, :, lanes] = kept
            factors[2 * side + 1, :, lanes] = kept * proj * (1.0 - sig)
        gate_act = jax.nn.sigmoid(dot(w_gate[...], pair_norm, 0, 0))
        d_proj = jnp.transpose(grad_ref[r].astype(F32)) * gate_act
        slope[:, lanes] = d_proj * (1.0 - gate_act)
        d_normed[pl.ds(r, hidden, stride=own), :] = (
            dot(w_out[...], d_proj.astype(BF16), 1, 0) * gain_out
        )


def triangle_kernel(own, in_ref, _, out_ref, a_ref, b_ref):
    half = out_ref.shape[1]
    sides = [
        split_channels(
            mesh_order(in_ref[:, side * half : (side + 1) * half, :].astype(F32)), own
        )
        for side in range(2)
    ]
    tri = []
    for c, (edge_a, edge_b) in enumerate(zip(*sides)):
        a_ref[c] = edge_a.astype(BF16)
        b_ref[c] = edge_b.astype(BF16)
        tri.append(dot(a_ref[c], b_ref[c], 1, 1))
    out_ref[...] = list_order(merge_channels(tri, own)).astype(BF16)


def fold(values, own):
    total = jnp.sum(values, axis=0)
    rows = total
    for shift in range(own, SUBLANES, own):
        rows = rows + pltpu.roll(total, shift, 0)
    return rows[None]


def tri_normed(tri_ref, hidden, own):
    cols = tri_ref.shape[-1]
    tri = tri_ref[...].astype(F32).reshape(hidden * own // SUBLANES, SUBLANES, cols)
    centre = tri - fold(tri, own) / hidden
    inverse = lax.rsqrt(fold(centre * centre, own) / hidden + EPSILON)
    return centre * inverse, inverse


def norm_kernel(own, tri_ref, grad_ref, slope, gain, bias, w_out, w_gate, out_ref, part_ref):
    devices, block, cols = tri_ref.shape
    hidden = w_out.shape[0]
    normed, inverse = tri_normed(tri_ref, hidden, own)
    grad = grad_ref[...].reshape(normed.shape)
    mean_grad = fold(grad, own) / hidden
    mean_proj = fold(grad * normed, own) / hidden
    d_tri = inverse * (grad - mean_grad - normed * mean_proj)
    out_ref[...] = d_tri.reshape(devices, block, cols).astype(BF16)
    parts = trade(split_channels(normed.reshape(devices, block, cols), own))
    tri_norm = jnp.concatenate([(part * gain[...] + bias[...]).astype(BF16) for part in parts], axis=1)
    d_gate = (slope[...] * dot(w_out[...], tri_norm, 0, 0)).astype(BF16)
    part_ref[...] = dot(w_gate[...], d_gate, 1, 0)


def edge_grad_kernel(own, in_ref, a_ref, b_ref, out_ref):
    block = in_ref.shape[1]
    grads = ([], [])
    for c, part in enumerate(split_channels(mesh_order(in_ref[...].astype(F32)), own)):
        d_tri = part.astype(BF16)
        grads[0].append(dot(d_tri, b_ref[c], 1, 0))
        grads[1].append(dot(d_tri, a_ref[c], 0, 0))
    for side in range(2):
        out_ref[:, side * block : (side + 1) * block, :] = (
            list_order(merge_channels(grads[side], own)).astype(BF16)
        )


def input_grad_kernel(in_ref, factors, normed_t, rstd_t, gain_t, gate_part, wap, wag, wbp, wbg, out_ref):
    own, cols, _ = out_ref.shape
    half = in_ref.shape[1] // 2
    total = gate_part[...]
    for side, weights in enumerate(((wap, wag), (wbp, wbg))):
        blocks = in_ref[:, side * half : (side + 1) * half, :].astype(F32)
        d_edge = jnp.concatenate(trade(split_channels(blocks, own)), axis=1)
        for at, weight in enumerate(weights):
            total = total + dot(weight[...], (d_edge * factors[2 * side + at]).astype(BF16), 1, 0)
    grad_hat = total * jnp.concatenate([gain_t[...]] * own, axis=1)
    normed = normed_t[...]
    mean_grad = jnp.mean(grad_hat, axis=0, keepdims=True)
    mean_proj = jnp.mean(grad_hat * normed, axis=0, keepdims=True)
    grad = rstd_t[...] * (grad_hat - mean_grad - normed * mean_proj)
    for r in range(own):
        out_ref[r] = jnp.transpose(grad[:, r * cols : (r + 1) * cols]).astype(BF16)


VMEM = pl.BlockSpec(memory_space=pltpu.VMEM)
SMEM = pl.BlockSpec(memory_space=pltpu.SMEM)
HBM = pl.BlockSpec(memory_space=pltpu.HBM)


def call(kernel, name, outs, args, scratch=(), scalars=0, flops=0, spaces=None, to=VMEM, limit=32 * 2**20):
    shapes = [jax.ShapeDtypeStruct(shape, dtype) for shape, dtype in outs]
    moved = sum(value.size * value.dtype.itemsize for value in list(args) + shapes)
    result = pl.pallas_call(
        kernel,
        name=name,
        out_shape=shapes,
        in_specs=[SMEM] * scalars + (spaces or [VMEM] * (len(args) - scalars)),
        out_specs=[to] * len(outs),
        scratch_shapes=scratch,
        cost_estimate=pl.CostEstimate(flops=flops, bytes_accessed=moved, transcendentals=0),
        compiler_params=pltpu.CompilerParams(vmem_limit_bytes=limit),
    )(*args)
    return result[0] if len(outs) == 1 else result


def kernel_shards(
    dap,
    pair_act,
    out_grad,
    residue_mask,
    ln_in_gain,
    ln_in_bias,
    w_a_proj,
    w_a_gate,
    w_b_proj,
    w_b_gate,
    w_gate,
    ln_out_gain,
    ln_out_bias,
    w_out,
):
    own, cols, chan = pair_act.shape
    hidden = w_a_proj.shape[1]
    slice_h = hidden // dap
    rows = dap * own
    block = slice_h * own
    me = lax.axis_index("dap").reshape(1)
    valid = residue_mask.reshape(1, -1)
    gain_in, bias_in, gain_out, bias_out = (
        value.reshape(1, -1) for value in (ln_in_gain, ln_in_bias, ln_out_gain, ln_out_bias)
    )
    w_edges = (w_a_proj, w_a_gate, w_b_proj, w_b_gate)
    product = 2 * own * cols * chan * hidden

    listed = [quarter * (dap // LEVELS) + at for at in range(dap // LEVELS) for quarter in range(LEVELS)]

    def exchange(value):
        return lax.all_to_all(
            value, "dap", split_axis=0, concat_axis=0, axis_index_groups=[listed], tiled=True
        )

    first = (pair_act, gain_in, bias_in, residue_mask, valid, *w_edges)
    edges = call(
        edges_kernel,
        "edges",
        [((dap, 2 * block, cols), BF16)],
        (me, *first),
        scratch=[
            (pltpu.SMEM if value is residue_mask else pltpu.VMEM)(value.shape, value.dtype)
            for value in first
        ]
        + [pltpu.VMEM((2, dap, block, cols), BF16)]
        + [pltpu.SemaphoreType.DMA((len(first),)), pltpu.SemaphoreType.DMA((2,))],
        scalars=1,
        flops=4 * product,
        to=HBM,
        spaces=[HBM] * len(first),
        limit=None,
    )
    edges = exchange(edges)
    factors, normed_t, rstd_t, gain_t, d_normed, slope, gain_out_t, bias_out_t = call(
        gates_kernel,
        "gates",
        [
            ((4, hidden, own * cols), F32),
            ((chan, own * cols), F32),
            ((1, own * cols), F32),
            ((chan, cols), F32),
            ((hidden * own, cols), F32),
            ((chan, own * cols), F32),
            ((hidden, cols), F32),
            ((hidden, cols), F32),
        ],
        (me, residue_mask, valid, pair_act, out_grad, gain_in, bias_in, gain_out)
        + (bias_out, *w_edges, w_gate, w_out),
        scalars=2,
        flops=6 * product,
    )
    tri, edge_a, edge_b = call(
        functools.partial(triangle_kernel, own),
        "triangle",
        [
            ((dap, block, cols), BF16),
            ((slice_h, rows, cols), BF16),
            ((slice_h, rows, cols), BF16),
        ],
        (edges, d_normed),
        flops=product,
        spaces=[VMEM, pl.BlockSpec(memory_space=pl.ANY)],
    )
    tri = exchange(tri)
    d_tri, gate_part = call(
        functools.partial(norm_kernel, own),
        "norm",
        [((dap, block, cols), BF16), ((chan, own * cols), F32)],
        (tri, d_normed, slope, gain_out_t, bias_out_t, w_out, w_gate),
        flops=2 * product,
    )
    d_tri = exchange(d_tri)
    d_edges = call(
        functools.partial(edge_grad_kernel, own),
        "edge_grad",
        [((dap, 2 * block, cols), BF16)],
        (d_tri, edge_a, edge_b),
        flops=2 * product,
    )
    d_edges = exchange(d_edges)
    return call(
        input_grad_kernel,
        "input_grad",
        [((own, cols, chan), BF16)],
        (d_edges, factors, normed_t, rstd_t, gain_t, gate_part, *w_edges),
        flops=4 * product,
    )


def fits_kernels(dap, ch, pair_act, w_proj):
    own, cols, chan = pair_act.shape
    hidden = w_proj.shape[1]
    block = hidden // dap * own
    return (
        ch == 1
        and hidden % dap == 0
        and own == SUBLANES // 2
        and block == own * own
        and dap % SUBLANES == 0
        and cols == dap * own
        and cols % 128 == chan % 128 == hidden % 128 == 0
    )


def solution(mesh):
    sizes = dict(mesh.shape)

    def program(*args):
        dap, ch = sizes["dap"], sizes["ch"]
        if fits_kernels(dap, ch, args[0], args[5]):
            return kernel_shards(dap, *args)
        return channel_shards(dap, ch, *args)

    in_specs = (
        P(("grp", "dap"), None, None),
        P(("grp", "dap"), "ch", None),
        P("grp"),
        P(),
        P(),
        P(None, "ch"),
        P(None, "ch"),
        P(None, "ch"),
        P(None, "ch"),
        P(),
        P(),
        P(),
        P(),
    )
    out_specs = P(("grp", "dap"), "ch", None)
    return jax.shard_map(
        program, mesh=mesh, in_specs=in_specs, out_specs=out_specs, check_vma=False
    )
```

```python
import functools

import jax
import jax.numpy as jnp
from jax import lax
from jax.experimental import pallas as pl
from jax.experimental.pallas import tpu as pltpu
from jax.sharding import PartitionSpec as P

EPSILON = 1e-05


def normalise(values, reduce_dim):
    centre = values - jnp.mean(values, axis=reduce_dim, keepdims=True)
    inverse = lax.rsqrt(jnp.mean(centre * centre, axis=reduce_dim, keepdims=True) + EPSILON)
    return (centre * inverse, inverse)


def norm_backward(grad_hat, normed, inverse, reduce_dim):
    mean_grad = jnp.mean(grad_hat, axis=reduce_dim, keepdims=True)
    mean_proj = jnp.mean(grad_hat * normed, axis=reduce_dim, keepdims=True)
    return inverse * (grad_hat - mean_grad - normed * mean_proj)


def channel_shards(
    dap,
    ch,
    pair_act,
    out_grad,
    residue_mask,
    ln_in_gain,
    ln_in_bias,
    w_a_proj,
    w_a_gate,
    w_b_proj,
    w_b_gate,
    w_gate,
    ln_out_gain,
    ln_out_bias,
    w_out,
):
    own_rows, all_cols = pair_act.shape[:2]
    col_span = out_grad.shape[1]
    hidden_local = w_a_proj.shape[1]
    slice_h = hidden_local // dap
    row_first = lax.axis_index("dap") * own_rows
    col_first = lax.axis_index("ch") * col_span
    normed_in, rstd_in = normalise(pair_act.astype(jnp.float32), 2)
    pair_norm = (normed_in * ln_in_gain + ln_in_bias).astype(jnp.bfloat16)
    valid_all = residue_mask.astype(jnp.float32)
    valid_rows = lax.dynamic_slice_in_dim(valid_all, row_first, own_rows)
    row_mask = (valid_rows[:, None] * valid_all[None, :])[None]
    w_four = jnp.concatenate((w_a_proj, w_a_gate, w_b_proj, w_b_gate), axis=1)
    projected = jnp.einsum("ikc,cg->gik", pair_norm, w_four, preferred_element_type=jnp.float32)
    a_proj = projected[:hidden_local]
    a_sig = jax.nn.sigmoid(projected[hidden_local : 2 * hidden_local])
    b_proj = projected[2 * hidden_local : 3 * hidden_local]
    b_sig = jax.nn.sigmoid(projected[3 * hidden_local :])
    edge_a = (row_mask * a_sig * a_proj).astype(jnp.bfloat16)
    edge_b = (row_mask * b_sig * b_proj).astype(jnp.bfloat16)

    split = (dap, slice_h, own_rows, all_cols)
    edges = jnp.stack((edge_a.reshape(split), edge_b.reshape(split)), axis=1)
    edges = lax.all_to_all(edges, "dap", split_axis=0, concat_axis=0, tiled=True)
    edges = jnp.transpose(edges, (1, 2, 0, 3, 4)).reshape(2, slice_h, dap * own_rows, all_cols)
    a_all, b_all = edges[0], edges[1]
    tri = jnp.einsum("hik,hjk->hij", a_all, b_all, preferred_element_type=jnp.float32).astype(
        jnp.bfloat16
    )
    tri = tri.reshape(slice_h, dap, own_rows, ch, col_span)
    tri = jnp.transpose(tri, (1, 3, 0, 2, 4)).reshape(dap * ch, slice_h, own_rows, col_span)
    tri = lax.all_to_all(tri, ("dap", "ch"), split_axis=0, concat_axis=0, tiled=True)
    tri = tri.reshape(dap, ch, slice_h, own_rows, col_span)
    tri_full = jnp.transpose(tri, (1, 0, 2, 3, 4)).reshape(-1, own_rows, col_span)

    normed_out, rstd_out = normalise(tri_full.astype(jnp.float32), 0)
    gain_out = ln_out_gain.reshape(-1, 1, 1)
    bias_out = ln_out_bias.reshape(-1, 1, 1)
    tri_norm = (normed_out * gain_out + bias_out).astype(jnp.bfloat16)
    proj_out = jnp.einsum("hij,hc->ijc", tri_norm, w_out, preferred_element_type=jnp.float32)
    norm_cols = lax.dynamic_slice_in_dim(pair_norm, col_first, col_span, 1)
    gate_act = jax.nn.sigmoid(
        jnp.einsum("ijc,cd->ijd", norm_cols, w_gate, preferred_element_type=jnp.float32)
    )
    upstream = out_grad.astype(jnp.float32)
    d_proj = (upstream * gate_act).astype(jnp.bfloat16)
    d_gate = (upstream * proj_out * gate_act * (1.0 - gate_act)).astype(jnp.bfloat16)
    d_normed = (
        jnp.einsum("ijc,hc->hij", d_proj, w_out, preferred_element_type=jnp.float32) * gain_out
    )
    d_tri = norm_backward(d_normed, normed_out, rstd_out, 0).astype(jnp.bfloat16)

    d_tri = d_tri.reshape(ch, dap, slice_h, own_rows, col_span)
    d_tri = jnp.transpose(d_tri, (1, 0, 2, 3, 4)).reshape(dap * ch, slice_h, own_rows, col_span)
    d_tri = lax.all_to_all(d_tri, ("dap", "ch"), split_axis=0, concat_axis=0, tiled=True)
    d_tri = d_tri.reshape(dap, ch, slice_h, own_rows, col_span)
    d_tri = jnp.transpose(d_tri, (2, 0, 3, 1, 4)).reshape(slice_h, dap * own_rows, all_cols)
    d_edge_a = jnp.einsum("hij,hjk->hik", d_tri, b_all, preferred_element_type=jnp.float32)
    d_edge_b = jnp.einsum("hij,hik->hjk", d_tri, a_all, preferred_element_type=jnp.float32)
    d_edges = jnp.stack((d_edge_a, d_edge_b)).astype(jnp.bfloat16)
    d_edges = d_edges.reshape(2, slice_h, dap, own_rows, all_cols)
    d_edges = jnp.transpose(d_edges, (2, 0, 1, 3, 4))
    d_edges = lax.all_to_all(d_edges, "dap", split_axis=0, concat_axis=0, tiled=True)
    d_edges = jnp.transpose(d_edges, (1, 0, 2, 3, 4)).reshape(2, hidden_local, own_rows, all_cols)

    def split_grad(d_edge, sig_val, proj_val):
        masked = d_edge * row_mask
        return (
            (masked * sig_val).astype(jnp.bfloat16),
            (masked * proj_val * sig_val * (1.0 - sig_val)).astype(jnp.bfloat16),
        )

    d_four = jnp.concatenate(
        split_grad(d_edges[0].astype(jnp.float32), a_sig, a_proj)
        + split_grad(d_edges[1].astype(jnp.float32), b_sig, b_proj),
        axis=0,
    )
    d_hidden = jnp.einsum("gik,cg->ikc", d_four, w_four, preferred_element_type=jnp.float32)
    if ch > 1:
        d_hidden = lax.psum_scatter(
            d_hidden.astype(jnp.bfloat16), "ch", scatter_dimension=1, tiled=True
        ).astype(jnp.float32)
    d_pair_norm = d_hidden + jnp.einsum(
        "ijd,cd->ijc", d_gate, w_gate, preferred_element_type=jnp.float32
    )
    normed_cols = lax.dynamic_slice_in_dim(normed_in, col_first, col_span, 1)
    rstd_cols = lax.dynamic_slice_in_dim(rstd_in, col_first, col_span, 1)
    grad_hat = d_pair_norm * ln_in_gain
    return norm_backward(grad_hat, normed_cols, rstd_cols, 2).astype(jnp.bfloat16)


F32 = jnp.float32
BF16 = jnp.bfloat16
SUBLANES = 8
LEVELS = 4


def dot(lhs, rhs, lhs_dim, rhs_dim):
    return lax.dot_general(
        lhs, rhs, (((lhs_dim,), (rhs_dim,)), ((), ())), preferred_element_type=F32
    )


def across(row, count):
    return jnp.transpose(jnp.broadcast_to(row, (count, row.shape[1])))


def exchange_bit(first, second, weight):
    sublane = lax.broadcasted_iota(jnp.int32, first.shape, 1)
    low = sublane & weight == 0
    return (
        jnp.where(low, first, pltpu.roll(second, weight, 1)),
        jnp.where(low, pltpu.roll(first, SUBLANES - weight, 1), second),
    )


def mesh_order(blocks):
    count, *rest = blocks.shape
    return jnp.swapaxes(blocks.reshape(count // LEVELS, LEVELS, *rest), 0, 1).reshape(blocks.shape)


def list_order(blocks):
    count, *rest = blocks.shape
    return jnp.swapaxes(blocks.reshape(LEVELS, count // LEVELS, *rest), 0, 1).reshape(blocks.shape)


def split_channels(blocks, own):
    devices, block, cols = blocks.shape
    tiles = blocks.reshape(devices // 2, 2, block // SUBLANES, SUBLANES, cols)
    parts = []
    for tile in range(block // SUBLANES):
        parts.extend(exchange_bit(tiles[:, 0, tile], tiles[:, 1, tile], own))
    return [part.reshape(devices * own, cols) for part in parts]


def merge_channels(parts, own):
    rows, cols = parts[0].shape
    devices = rows // own
    tiles = [part.reshape(devices // 2, SUBLANES, cols) for part in parts]
    pairs = [exchange_bit(*pair, own) for pair in zip(tiles[::2], tiles[1::2])]
    both = [jnp.concatenate(side, axis=1) for side in zip(*pairs)]
    block = len(parts) * own
    return jnp.stack(both, axis=1).reshape(devices, block, cols)


def trade(parts):
    rows, cols = parts[0].shape
    a, b, c, d = (part.reshape(rows // SUBLANES, SUBLANES, cols) for part in parts)
    (a, b), (c, d) = exchange_bit(a, b, 1), exchange_bit(c, d, 1)
    (a, c), (b, d) = exchange_bit(a, c, 2), exchange_bit(b, d, 2)
    return [part.reshape(rows, cols) for part in (a, b, c, d)]


def edges_kernel(me_ref, *refs):
    sources, (out_ref, *local), (blocks, arrived, left) = refs[:9], refs[9:19], refs[19:]
    copies = [
        pltpu.make_async_copy(source, target, arrived.at[index])
        for index, (source, target) in enumerate(zip(sources, local))
    ]
    for copy in copies:
        copy.start()
    act_ref, gain_ref, bias_ref, rows_ref, valid_ref, *weights = local
    own, cols, chan = act_ref.shape
    half = out_ref.shape[1] // 2
    for copy in copies[:3]:
        copy.wait()
    act = jnp.concatenate([jnp.transpose(act_ref[r].astype(F32)) for r in range(own)], axis=1)
    gain = across(gain_ref[...], cols)
    bias = across(bias_ref[...], cols)
    centre = act - jnp.mean(act, axis=0, keepdims=True)
    inverse = lax.rsqrt(jnp.mean(centre * centre, axis=0, keepdims=True) + EPSILON)
    wide_gain, wide_bias = (jnp.concatenate([value] * own, axis=1) for value in (gain, bias))
    pair_norm = (centre * inverse * wide_gain + wide_bias).astype(BF16)
    for copy in copies[3:]:
        copy.wait()
    valid = valid_ref[...].astype(F32)
    mask = jnp.concatenate(
        [valid * rows_ref[me_ref[0] * own + r].astype(F32) for r in range(own)], axis=1
    )
    sent = []
    for side in range(2):
        proj = dot(weights[2 * side][...], pair_norm, 0, 0)
        edge = mask * jax.nn.sigmoid(dot(weights[2 * side + 1][...], pair_norm, 0, 0)) * proj
        parts = trade([edge[:, r * cols : (r + 1) * cols] for r in range(own)])
        blocks[side] = merge_channels(parts, own).astype(BF16)
        copy = pltpu.make_async_copy(
            blocks.at[side], out_ref.at[:, side * half : (side + 1) * half, :], left.at[side]
        )
        copy.start()
        sent.append(copy)
    for copy in sent:
        copy.wait()


def gates_kernel(
    me_ref, rows_ref, valid_ref, act_ref, grad_ref, gain_ref, bias_ref, gain_out_ref, bias_out_ref,
    wap, wag, wbp, wbg, w_gate, w_out,
    factors, normed_t, rstd_t, gain_t, d_normed, slope, gain_out_t, bias_out_t, w_out_t,
):
    own, cols, _ = act_ref.shape
    hidden = wap.shape[1]
    valid = valid_ref[...].astype(F32)
    gain = across(gain_ref[...], cols)
    bias = across(bias_ref[...], cols)
    gain_out = across(gain_out_ref[...], cols)
    gain_t[...] = gain
    gain_out_t[...] = gain_out
    w_out_t[...] = jnp.transpose(w_out[...].astype(F32)).astype(BF16)
    bias_out_t[...] = across(bias_out_ref[...], cols)
    for r in range(own):
        act = jnp.transpose(act_ref[r].astype(F32))
        centre = act - jnp.mean(act, axis=0, keepdims=True)
        inverse = lax.rsqrt(jnp.mean(centre * centre, axis=0, keepdims=True) + EPSILON)
        normed = centre * inverse
        lanes = pl.ds(r * cols, cols)
        normed_t[:, lanes] = normed
        rstd_t[:, lanes] = inverse
        pair_norm = (normed * gain + bias).astype(BF16)
        mask = valid * rows_ref[me_ref[0] * own + r].astype(F32)
        for side, (w_proj, w_sig) in enumerate(((wap, wag), (wbp, wbg))):
            proj = dot(w_proj[...], pair_norm, 0, 0)
            sig = jax.nn.sigmoid(dot(w_sig[...], pair_norm, 0, 0))
            kept = mask * sig
            factors[2 * side, :, lanes] = kept
            factors[2 * side + 1, :, lanes] = kept * proj * (1.0 - sig)
        gate_act = jax.nn.sigmoid(dot(w_gate[...], pair_norm, 0, 0))
        d_proj = jnp.transpose(grad_ref[r].astype(F32)) * gate_act
        slope[:, lanes] = d_proj * (1.0 - gate_act)
        d_normed[pl.ds(r, hidden, stride=own), :] = (
            dot(w_out[...], d_proj.astype(BF16), 1, 0) * gain_out
        )


def triangle_kernel(own, in_ref, _, out_ref, a_ref, b_ref):
    half = out_ref.shape[1]
    sides = [
        split_channels(
            mesh_order(in_ref[:, side * half : (side + 1) * half, :].astype(F32)), own
        )
        for side in range(2)
    ]
    tri = []
    for c, (edge_a, edge_b) in enumerate(zip(*sides)):
        a_ref[c] = edge_a.astype(BF16)
        b_ref[c] = edge_b.astype(BF16)
        tri.append(dot(a_ref[c], b_ref[c], 1, 1))
    out_ref[...] = list_order(merge_channels(tri, own)).astype(BF16)


def fold(values, own):
    total = jnp.sum(values, axis=0)
    rows = total
    for shift in range(own, SUBLANES, own):
        rows = rows + pltpu.roll(total, shift, 0)
    return rows[None]


def tri_normed(tri_ref, hidden, own):
    cols = tri_ref.shape[-1]
    tri = tri_ref[...].astype(F32).reshape(hidden * own // SUBLANES, SUBLANES, cols)
    centre = tri - fold(tri, own) / hidden
    inverse = lax.rsqrt(fold(centre * centre, own) / hidden + EPSILON)
    return centre * inverse, inverse


def norm_kernel(own, tri_ref, grad_ref, slope, gain, bias, w_out_t, w_gate, out_ref, part_ref):
    devices, block, cols = tri_ref.shape
    hidden = w_out_t.shape[1]
    normed, inverse = tri_normed(tri_ref, hidden, own)
    grad = grad_ref[...].reshape(normed.shape)
    mean_grad = fold(grad, own) / hidden
    mean_proj = fold(grad * normed, own) / hidden
    d_tri = inverse * (grad - mean_grad - normed * mean_proj)
    out_ref[...] = d_tri.reshape(devices, block, cols).astype(BF16)
    parts = trade(split_channels(normed.reshape(devices, block, cols), own))
    tri_norm = jnp.concatenate([(part * gain[...] + bias[...]).astype(BF16) for part in parts], axis=1)
    d_gate = (slope[...] * dot(w_out_t[...], tri_norm, 1, 0)).astype(BF16)
    part_ref[...] = dot(w_gate[...], d_gate, 1, 0)


def edge_grad_kernel(own, in_ref, a_ref, b_ref, out_ref):
    block = in_ref.shape[1]
    grads = ([], [])
    for c, part in enumerate(split_channels(mesh_order(in_ref[...].astype(F32)), own)):
        d_tri = part.astype(BF16)
        grads[0].append(dot(d_tri, b_ref[c], 1, 0))
        grads[1].append(dot(d_tri, a_ref[c], 0, 0))
    for side in range(2):
        out_ref[:, side * block : (side + 1) * block, :] = (
            list_order(merge_channels(grads[side], own)).astype(BF16)
        )


def input_grad_kernel(
    in_ref, factors, normed_t, rstd_t, gain_t, gate_part, wap, wag, wbp, wbg, out_ref, done, left
):
    own, cols, _ = out_ref.shape
    half = in_ref.shape[1] // 2
    sides = [
        trade(split_channels(in_ref[:, side * half : (side + 1) * half, :].astype(F32), own))
        for side in range(2)
    ]
    copies = []
    for r in range(own):
        lanes = pl.ds(r * cols, cols)
        total = gate_part[:, lanes]
        for index, weight in enumerate((wap, wag, wbp, wbg)):
            d_in = (sides[index // 2][r] * factors[index, :, lanes]).astype(BF16)
            total = total + dot(weight[...], d_in, 1, 0)
        grad_hat = total * gain_t[...]
        normed = normed_t[:, lanes]
        mean_grad = jnp.mean(grad_hat, axis=0, keepdims=True)
        mean_proj = jnp.mean(grad_hat * normed, axis=0, keepdims=True)
        grad = rstd_t[:, lanes] * (grad_hat - mean_grad - normed * mean_proj)
        done[r] = jnp.transpose(grad).astype(BF16)
        copy = pltpu.make_async_copy(done.at[r], out_ref.at[r], left.at[r])
        copy.start()
        copies.append(copy)
    for copy in copies:
        copy.wait()


VMEM = pl.BlockSpec(memory_space=pltpu.VMEM)
SMEM = pl.BlockSpec(memory_space=pltpu.SMEM)
HBM = pl.BlockSpec(memory_space=pltpu.HBM)


def call(kernel, name, outs, args, scratch=(), scalars=0, flops=0, spaces=None, to=VMEM, limit=32 * 2**20):
    shapes = [jax.ShapeDtypeStruct(shape, dtype) for shape, dtype in outs]
    moved = sum(value.size * value.dtype.itemsize for value in list(args) + shapes)
    result = pl.pallas_call(
        kernel,
        name=name,
        out_shape=shapes,
        in_specs=[SMEM] * scalars + (spaces or [VMEM] * (len(args) - scalars)),
        out_specs=[to] * len(outs),
        scratch_shapes=scratch,
        cost_estimate=pl.CostEstimate(flops=flops, bytes_accessed=moved, transcendentals=0),
        compiler_params=pltpu.CompilerParams(vmem_limit_bytes=limit),
    )(*args)
    return result[0] if len(outs) == 1 else result


def kernel_shards(
    dap,
    pair_act,
    out_grad,
    residue_mask,
    ln_in_gain,
    ln_in_bias,
    w_a_proj,
    w_a_gate,
    w_b_proj,
    w_b_gate,
    w_gate,
    ln_out_gain,
    ln_out_bias,
    w_out,
):
    own, cols, chan = pair_act.shape
    hidden = w_a_proj.shape[1]
    slice_h = hidden // dap
    rows = dap * own
    block = slice_h * own
    me = lax.axis_index("dap").reshape(1)
    valid = residue_mask.reshape(1, -1)
    gain_in, bias_in, gain_out, bias_out = (
        value.reshape(1, -1) for value in (ln_in_gain, ln_in_bias, ln_out_gain, ln_out_bias)
    )
    w_edges = (w_a_proj, w_a_gate, w_b_proj, w_b_gate)
    product = 2 * own * cols * chan * hidden

    listed = [quarter * (dap // LEVELS) + at for at in range(dap // LEVELS) for quarter in range(LEVELS)]

    def exchange(value):
        return lax.all_to_all(
            value, "dap", split_axis=0, concat_axis=0, axis_index_groups=[listed], tiled=True
        )

    first = (pair_act, gain_in, bias_in, residue_mask, valid, *w_edges)
    edges = call(
        edges_kernel,
        "edges",
        [((dap, 2 * block, cols), BF16)],
        (me, *first),
        scratch=[
            (pltpu.SMEM if value is residue_mask else pltpu.VMEM)(value.shape, value.dtype)
            for value in first
        ]
        + [pltpu.VMEM((2, dap, block, cols), BF16)]
        + [pltpu.SemaphoreType.DMA((len(first),)), pltpu.SemaphoreType.DMA((2,))],
        scalars=1,
        flops=4 * product,
        to=HBM,
        spaces=[HBM] * len(first),
        limit=None,
    )
    edges = exchange(edges)
    factors, normed_t, rstd_t, gain_t, d_normed, slope, gain_out_t, bias_out_t, w_out_t = call(
        gates_kernel,
        "gates",
        [
            ((4, hidden, own * cols), F32),
            ((chan, own * cols), F32),
            ((1, own * cols), F32),
            ((chan, cols), F32),
            ((hidden * own, cols), F32),
            ((chan, own * cols), F32),
            ((hidden, cols), F32),
            ((hidden, cols), F32),
            ((chan, hidden), BF16),
        ],
        (me, residue_mask, valid, pair_act, out_grad, gain_in, bias_in, gain_out)
        + (bias_out, *w_edges, w_gate, w_out),
        scalars=2,
        flops=6 * product,
    )
    tri, edge_a, edge_b = call(
        functools.partial(triangle_kernel, own),
        "triangle",
        [
            ((dap, block, cols), BF16),
            ((slice_h, rows, cols), BF16),
            ((slice_h, rows, cols), BF16),
        ],
        (edges, d_normed),
        flops=product,
        spaces=[VMEM, pl.BlockSpec(memory_space=pl.ANY)],
    )
    tri = exchange(tri)
    d_tri, gate_part = call(
        functools.partial(norm_kernel, own),
        "norm",
        [((dap, block, cols), BF16), ((chan, own * cols), F32)],
        (tri, d_normed, slope, gain_out_t, bias_out_t, w_out_t, w_gate),
        flops=2 * product,
    )
    d_tri = exchange(d_tri)
    d_edges = call(
        functools.partial(edge_grad_kernel, own),
        "edge_grad",
        [((dap, 2 * block, cols), BF16)],
        (d_tri, edge_a, edge_b),
        flops=2 * product,
    )
    d_edges = exchange(d_edges)
    return call(
        input_grad_kernel,
        "input_grad",
        [((own, cols, chan), BF16)],
        (d_edges, factors, normed_t, rstd_t, gain_t, gate_part, *w_edges),
        scratch=[pltpu.VMEM((own, cols, chan), BF16), pltpu.SemaphoreType.DMA((own,))],
        flops=4 * product,
        to=HBM,
    )


def fits_kernels(dap, ch, pair_act, w_proj):
    own, cols, chan = pair_act.shape
    hidden = w_proj.shape[1]
    block = hidden // dap * own
    return (
        ch == 1
        and hidden % dap == 0
        and own == SUBLANES // 2
        and block == own * own
        and dap % SUBLANES == 0
        and cols == dap * own
        and cols % 128 == chan % 128 == hidden % 128 == 0
    )


def solution(mesh):
    sizes = dict(mesh.shape)

    def program(*args):
        dap, ch = sizes["dap"], sizes["ch"]
        if fits_kernels(dap, ch, args[0], args[5]):
            return kernel_shards(dap, *args)
        return channel_shards(dap, ch, *args)

    in_specs = (
        P(("grp", "dap"), None, None),
        P(("grp", "dap"), "ch", None),
        P("grp"),
        P(),
        P(),
        P(None, "ch"),
        P(None, "ch"),
        P(None, "ch"),
        P(None, "ch"),
        P(),
        P(),
        P(),
        P(),
    )
    out_specs = P(("grp", "dap"), "ch", None)
    return jax.shard_map(
        program, mesh=mesh, in_specs=in_specs, out_specs=out_specs, check_vma=False
    )
```

```python
import functools

import jax
import jax.numpy as jnp
from jax import lax
from jax.experimental import pallas as pl
from jax.experimental.pallas import tpu as pltpu
from jax.sharding import PartitionSpec as P

EPSILON = 1e-05


def normalise(values, reduce_dim):
    centre = values - jnp.mean(values, axis=reduce_dim, keepdims=True)
    inverse = lax.rsqrt(jnp.mean(centre * centre, axis=reduce_dim, keepdims=True) + EPSILON)
    return (centre * inverse, inverse)


def norm_backward(grad_hat, normed, inverse, reduce_dim):
    mean_grad = jnp.mean(grad_hat, axis=reduce_dim, keepdims=True)
    mean_proj = jnp.mean(grad_hat * normed, axis=reduce_dim, keepdims=True)
    return inverse * (grad_hat - mean_grad - normed * mean_proj)


def channel_shards(
    dap,
    ch,
    pair_act,
    out_grad,
    residue_mask,
    ln_in_gain,
    ln_in_bias,
    w_a_proj,
    w_a_gate,
    w_b_proj,
    w_b_gate,
    w_gate,
    ln_out_gain,
    ln_out_bias,
    w_out,
):
    own_rows, all_cols = pair_act.shape[:2]
    col_span = out_grad.shape[1]
    hidden_local = w_a_proj.shape[1]
    slice_h = hidden_local // dap
    row_first = lax.axis_index("dap") * own_rows
    col_first = lax.axis_index("ch") * col_span
    normed_in, rstd_in = normalise(pair_act.astype(jnp.float32), 2)
    pair_norm = (normed_in * ln_in_gain + ln_in_bias).astype(jnp.bfloat16)
    valid_all = residue_mask.astype(jnp.float32)
    valid_rows = lax.dynamic_slice_in_dim(valid_all, row_first, own_rows)
    row_mask = (valid_rows[:, None] * valid_all[None, :])[None]
    w_four = jnp.concatenate((w_a_proj, w_a_gate, w_b_proj, w_b_gate), axis=1)
    projected = jnp.einsum("ikc,cg->gik", pair_norm, w_four, preferred_element_type=jnp.float32)
    a_proj = projected[:hidden_local]
    a_sig = jax.nn.sigmoid(projected[hidden_local : 2 * hidden_local])
    b_proj = projected[2 * hidden_local : 3 * hidden_local]
    b_sig = jax.nn.sigmoid(projected[3 * hidden_local :])
    edge_a = (row_mask * a_sig * a_proj).astype(jnp.bfloat16)
    edge_b = (row_mask * b_sig * b_proj).astype(jnp.bfloat16)

    split = (dap, slice_h, own_rows, all_cols)
    edges = jnp.stack((edge_a.reshape(split), edge_b.reshape(split)), axis=1)
    edges = lax.all_to_all(edges, "dap", split_axis=0, concat_axis=0, tiled=True)
    edges = jnp.transpose(edges, (1, 2, 0, 3, 4)).reshape(2, slice_h, dap * own_rows, all_cols)
    a_all, b_all = edges[0], edges[1]
    tri = jnp.einsum("hik,hjk->hij", a_all, b_all, preferred_element_type=jnp.float32).astype(
        jnp.bfloat16
    )
    tri = tri.reshape(slice_h, dap, own_rows, ch, col_span)
    tri = jnp.transpose(tri, (1, 3, 0, 2, 4)).reshape(dap * ch, slice_h, own_rows, col_span)
    tri = lax.all_to_all(tri, ("dap", "ch"), split_axis=0, concat_axis=0, tiled=True)
    tri = tri.reshape(dap, ch, slice_h, own_rows, col_span)
    tri_full = jnp.transpose(tri, (1, 0, 2, 3, 4)).reshape(-1, own_rows, col_span)

    normed_out, rstd_out = normalise(tri_full.astype(jnp.float32), 0)
    gain_out = ln_out_gain.reshape(-1, 1, 1)
    bias_out = ln_out_bias.reshape(-1, 1, 1)
    tri_norm = (normed_out * gain_out + bias_out).astype(jnp.bfloat16)
    proj_out = jnp.einsum("hij,hc->ijc", tri_norm, w_out, preferred_element_type=jnp.float32)
    norm_cols = lax.dynamic_slice_in_dim(pair_norm, col_first, col_span, 1)
    gate_act = jax.nn.sigmoid(
        jnp.einsum("ijc,cd->ijd", norm_cols, w_gate, preferred_element_type=jnp.float32)
    )
    upstream = out_grad.astype(jnp.float32)
    d_proj = (upstream * gate_act).astype(jnp.bfloat16)
    d_gate = (upstream * proj_out * gate_act * (1.0 - gate_act)).astype(jnp.bfloat16)
    d_normed = (
        jnp.einsum("ijc,hc->hij", d_proj, w_out, preferred_element_type=jnp.float32) * gain_out
    )
    d_tri = norm_backward(d_normed, normed_out, rstd_out, 0).astype(jnp.bfloat16)

    d_tri = d_tri.reshape(ch, dap, slice_h, own_rows, col_span)
    d_tri = jnp.transpose(d_tri, (1, 0, 2, 3, 4)).reshape(dap * ch, slice_h, own_rows, col_span)
    d_tri = lax.all_to_all(d_tri, ("dap", "ch"), split_axis=0, concat_axis=0, tiled=True)
    d_tri = d_tri.reshape(dap, ch, slice_h, own_rows, col_span)
    d_tri = jnp.transpose(d_tri, (2, 0, 3, 1, 4)).reshape(slice_h, dap * own_rows, all_cols)
    d_edge_a = jnp.einsum("hij,hjk->hik", d_tri, b_all, preferred_element_type=jnp.float32)
    d_edge_b = jnp.einsum("hij,hik->hjk", d_tri, a_all, preferred_element_type=jnp.float32)
    d_edges = jnp.stack((d_edge_a, d_edge_b)).astype(jnp.bfloat16)
    d_edges = d_edges.reshape(2, slice_h, dap, own_rows, all_cols)
    d_edges = jnp.transpose(d_edges, (2, 0, 1, 3, 4))
    d_edges = lax.all_to_all(d_edges, "dap", split_axis=0, concat_axis=0, tiled=True)
    d_edges = jnp.transpose(d_edges, (1, 0, 2, 3, 4)).reshape(2, hidden_local, own_rows, all_cols)

    def split_grad(d_edge, sig_val, proj_val):
        masked = d_edge * row_mask
        return (
            (masked * sig_val).astype(jnp.bfloat16),
            (masked * proj_val * sig_val * (1.0 - sig_val)).astype(jnp.bfloat16),
        )

    d_four = jnp.concatenate(
        split_grad(d_edges[0].astype(jnp.float32), a_sig, a_proj)
        + split_grad(d_edges[1].astype(jnp.float32), b_sig, b_proj),
        axis=0,
    )
    d_hidden = jnp.einsum("gik,cg->ikc", d_four, w_four, preferred_element_type=jnp.float32)
    if ch > 1:
        d_hidden = lax.psum_scatter(
            d_hidden.astype(jnp.bfloat16), "ch", scatter_dimension=1, tiled=True
        ).astype(jnp.float32)
    d_pair_norm = d_hidden + jnp.einsum(
        "ijd,cd->ijc", d_gate, w_gate, preferred_element_type=jnp.float32
    )
    normed_cols = lax.dynamic_slice_in_dim(normed_in, col_first, col_span, 1)
    rstd_cols = lax.dynamic_slice_in_dim(rstd_in, col_first, col_span, 1)
    grad_hat = d_pair_norm * ln_in_gain
    return norm_backward(grad_hat, normed_cols, rstd_cols, 2).astype(jnp.bfloat16)


F32 = jnp.float32
BF16 = jnp.bfloat16
SUBLANES = 8
LEVELS = 4


def dot(lhs, rhs, lhs_dim, rhs_dim):
    return lax.dot_general(
        lhs, rhs, (((lhs_dim,), (rhs_dim,)), ((), ())), preferred_element_type=F32
    )


def across(row, count):
    return jnp.transpose(jnp.broadcast_to(row, (count, row.shape[1])))


def exchange_bit(first, second, weight):
    sublane = lax.broadcasted_iota(jnp.int32, first.shape, 1)
    low = sublane & weight == 0
    return (
        jnp.where(low, first, pltpu.roll(second, weight, 1)),
        jnp.where(low, pltpu.roll(first, SUBLANES - weight, 1), second),
    )


def mesh_order(blocks):
    count, *rest = blocks.shape
    return jnp.swapaxes(blocks.reshape(count // LEVELS, LEVELS, *rest), 0, 1).reshape(blocks.shape)


def list_order(blocks):
    count, *rest = blocks.shape
    return jnp.swapaxes(blocks.reshape(LEVELS, count // LEVELS, *rest), 0, 1).reshape(blocks.shape)


def split_channels(blocks, own):
    devices, block, cols = blocks.shape
    tiles = blocks.reshape(devices // 2, 2, block // SUBLANES, SUBLANES, cols)
    parts = []
    for tile in range(block // SUBLANES):
        parts.extend(exchange_bit(tiles[:, 0, tile], tiles[:, 1, tile], own))
    return [part.reshape(devices * own, cols) for part in parts]


def merge_channels(parts, own):
    rows, cols = parts[0].shape
    devices = rows // own
    tiles = [part.reshape(devices // 2, SUBLANES, cols) for part in parts]
    pairs = [exchange_bit(*pair, own) for pair in zip(tiles[::2], tiles[1::2])]
    both = [jnp.concatenate(side, axis=1) for side in zip(*pairs)]
    block = len(parts) * own
    return jnp.stack(both, axis=1).reshape(devices, block, cols)


def trade(parts):
    rows, cols = parts[0].shape
    a, b, c, d = (part.reshape(rows // SUBLANES, SUBLANES, cols) for part in parts)
    (a, b), (c, d) = exchange_bit(a, b, 1), exchange_bit(c, d, 1)
    (a, c), (b, d) = exchange_bit(a, c, 2), exchange_bit(b, d, 2)
    return [part.reshape(rows, cols) for part in (a, b, c, d)]


def edges_kernel(me_ref, *refs):
    sources, (out_ref, *local), (blocks, arrived, left) = refs[:9], refs[9:19], refs[19:]
    copies = [
        pltpu.make_async_copy(source, target, arrived.at[index])
        for index, (source, target) in enumerate(zip(sources, local))
    ]
    for copy in copies:
        copy.start()
    act_ref, gain_ref, bias_ref, rows_ref, valid_ref, *weights = local
    own, cols, chan = act_ref.shape
    half = out_ref.shape[1] // 2
    for copy in copies[:3]:
        copy.wait()
    act = jnp.concatenate([jnp.transpose(act_ref[r].astype(F32)) for r in range(own)], axis=1)
    gain = across(gain_ref[...], cols)
    bias = across(bias_ref[...], cols)
    centre = act - jnp.mean(act, axis=0, keepdims=True)
    inverse = lax.rsqrt(jnp.mean(centre * centre, axis=0, keepdims=True) + EPSILON)
    wide_gain, wide_bias = (jnp.concatenate([value] * own, axis=1) for value in (gain, bias))
    pair_norm = (centre * inverse * wide_gain + wide_bias).astype(BF16)
    for copy in copies[3:]:
        copy.wait()
    valid = valid_ref[...].astype(F32)
    mask = jnp.concatenate(
        [valid * rows_ref[me_ref[0] * own + r].astype(F32) for r in range(own)], axis=1
    )
    sent = []
    for side in range(2):
        proj = dot(weights[2 * side][...], pair_norm, 0, 0)
        edge = mask * jax.nn.sigmoid(dot(weights[2 * side + 1][...], pair_norm, 0, 0)) * proj
        parts = trade([edge[:, r * cols : (r + 1) * cols] for r in range(own)])
        blocks[side] = merge_channels(parts, own).astype(BF16)
        copy = pltpu.make_async_copy(
            blocks.at[side], out_ref.at[:, side * half : (side + 1) * half, :], left.at[side]
        )
        copy.start()
        sent.append(copy)
    for copy in sent:
        copy.wait()


def gates_kernel(
    me_ref, rows_ref, valid_ref, act_ref, grad_ref, gain_ref, bias_ref, gain_out_ref, bias_out_ref,
    wap, wag, wbp, wbg, w_gate, w_out,
    factors, normed_t, rstd_t, gain_t, d_normed, slope, gain_out_t, bias_out_t,
):
    own, cols, _ = act_ref.shape
    hidden = wap.shape[1]
    valid = valid_ref[...].astype(F32)
    gain = across(gain_ref[...], cols)
    bias = across(bias_ref[...], cols)
    gain_out = across(gain_out_ref[...], cols)
    gain_t[...] = gain
    gain_out_t[...] = gain_out
    bias_out_t[...] = across(bias_out_ref[...], cols)
    for r in range(own):
        act = jnp.transpose(act_ref[r].astype(F32))
        centre = act - jnp.mean(act, axis=0, keepdims=True)
        inverse = lax.rsqrt(jnp.mean(centre * centre, axis=0, keepdims=True) + EPSILON)
        normed = centre * inverse
        lanes = pl.ds(r * cols, cols)
        normed_t[:, lanes] = normed
        rstd_t[:, lanes] = inverse
        pair_norm = (normed * gain + bias).astype(BF16)
        mask = valid * rows_ref[me_ref[0] * own + r].astype(F32)
        for side, (w_proj, w_sig) in enumerate(((wap, wag), (wbp, wbg))):
            proj = dot(w_proj[...], pair_norm, 0, 0)
            sig = jax.nn.sigmoid(dot(w_sig[...], pair_norm, 0, 0))
            kept = mask * sig
            factors[2 * side, :, lanes] = kept
            factors[2 * side + 1, :, lanes] = kept * proj * (1.0 - sig)
        gate_act = jax.nn.sigmoid(dot(w_gate[...], pair_norm, 0, 0))
        d_proj = jnp.transpose(grad_ref[r].astype(F32)) * gate_act
        slope[:, lanes] = d_proj * (1.0 - gate_act)
        d_normed[pl.ds(r, hidden, stride=own), :] = (
            dot(w_out[...], d_proj.astype(BF16), 1, 0) * gain_out
        )


def triangle_kernel(own, in_ref, _, out_ref, a_ref, b_ref):
    half = out_ref.shape[1]
    sides = [
        split_channels(
            mesh_order(in_ref[:, side * half : (side + 1) * half, :].astype(F32)), own
        )
        for side in range(2)
    ]
    tri = []
    for c, (edge_a, edge_b) in enumerate(zip(*sides)):
        a_ref[c] = edge_a.astype(BF16)
        b_ref[c] = edge_b.astype(BF16)
        tri.append(dot(a_ref[c], b_ref[c], 1, 1))
    out_ref[...] = list_order(merge_channels(tri, own)).astype(BF16)


def fold(values, own):
    total = jnp.sum(values, axis=0)
    rows = total
    for shift in range(own, SUBLANES, own):
        rows = rows + pltpu.roll(total, shift, 0)
    return rows[None]


def tri_normed(tri_ref, hidden, own):
    cols = tri_ref.shape[-1]
    tri = tri_ref[...].astype(F32).reshape(hidden * own // SUBLANES, SUBLANES, cols)
    centre = tri - fold(tri, own) / hidden
    inverse = lax.rsqrt(fold(centre * centre, own) / hidden + EPSILON)
    return centre * inverse, inverse


def norm_kernel(own, tri_ref, grad_ref, slope, gain, bias, w_out, out_ref, gate_ref):
    devices, block, cols = tri_ref.shape
    hidden = w_out.shape[0]
    normed, inverse = tri_normed(tri_ref, hidden, own)
    grad = grad_ref[...].reshape(normed.shape)
    mean_grad = fold(grad, own) / hidden
    mean_proj = fold(grad * normed, own) / hidden
    d_tri = inverse * (grad - mean_grad - normed * mean_proj)
    out_ref[...] = d_tri.reshape(devices, block, cols).astype(BF16)
    parts = trade(split_channels(normed.reshape(devices, block, cols), own))
    tri_norm = jnp.concatenate([(part * gain[...] + bias[...]).astype(BF16) for part in parts], axis=1)
    gate_ref[...] = (slope[...] * dot(w_out[...], tri_norm, 0, 0)).astype(BF16)


def edge_grad_kernel(own, in_ref, a_ref, b_ref, out_ref):
    block = in_ref.shape[1]
    grads = ([], [])
    for c, part in enumerate(split_channels(mesh_order(in_ref[...].astype(F32)), own)):
        d_tri = part.astype(BF16)
        grads[0].append(dot(d_tri, b_ref[c], 1, 0))
        grads[1].append(dot(d_tri, a_ref[c], 0, 0))
    for side in range(2):
        out_ref[:, side * block : (side + 1) * block, :] = (
            list_order(merge_channels(grads[side], own)).astype(BF16)
        )


def input_grad_kernel(
    in_ref, factors, normed_t, rstd_t, gain_t, d_gate, wap, wag, wbp, wbg, w_gate, out_ref
):
    own, cols, _ = out_ref.shape
    half = in_ref.shape[1] // 2
    grads = []
    for side in range(2):
        blocks = in_ref[:, side * half : (side + 1) * half, :].astype(F32)
        d_edge = jnp.concatenate(trade(split_channels(blocks, own)), axis=1)
        for at in range(2):
            grads.append((d_edge * factors[2 * side + at]).astype(BF16))
    weights = [weight[...] for weight in (wap, wag, wbp, wbg, w_gate)]
    grads.append(d_gate[...])
    total = dot(jnp.concatenate(weights, axis=1), jnp.concatenate(grads, axis=0), 1, 0)
    grad_hat = total * jnp.concatenate([gain_t[...]] * own, axis=1)
    normed = normed_t[...]
    mean_grad = jnp.mean(grad_hat, axis=0, keepdims=True)
    mean_proj = jnp.mean(grad_hat * normed, axis=0, keepdims=True)
    grad = rstd_t[...] * (grad_hat - mean_grad - normed * mean_proj)
    for r in range(own):
        out_ref[r] = jnp.transpose(grad[:, r * cols : (r + 1) * cols]).astype(BF16)


VMEM = pl.BlockSpec(memory_space=pltpu.VMEM)
SMEM = pl.BlockSpec(memory_space=pltpu.SMEM)
HBM = pl.BlockSpec(memory_space=pltpu.HBM)


def call(kernel, name, outs, args, scratch=(), scalars=0, flops=0, spaces=None, to=VMEM, limit=32 * 2**20):
    shapes = [jax.ShapeDtypeStruct(shape, dtype) for shape, dtype in outs]
    moved = sum(value.size * value.dtype.itemsize for value in list(args) + shapes)
    result = pl.pallas_call(
        kernel,
        name=name,
        out_shape=shapes,
        in_specs=[SMEM] * scalars + (spaces or [VMEM] * (len(args) - scalars)),
        out_specs=[to] * len(outs),
        scratch_shapes=scratch,
        cost_estimate=pl.CostEstimate(flops=flops, bytes_accessed=moved, transcendentals=0),
        compiler_params=pltpu.CompilerParams(vmem_limit_bytes=limit),
    )(*args)
    return result[0] if len(outs) == 1 else result


def kernel_shards(
    dap,
    pair_act,
    out_grad,
    residue_mask,
    ln_in_gain,
    ln_in_bias,
    w_a_proj,
    w_a_gate,
    w_b_proj,
    w_b_gate,
    w_gate,
    ln_out_gain,
    ln_out_bias,
    w_out,
):
    own, cols, chan = pair_act.shape
    hidden = w_a_proj.shape[1]
    slice_h = hidden // dap
    rows = dap * own
    block = slice_h * own
    me = lax.axis_index("dap").reshape(1)
    valid = residue_mask.reshape(1, -1)
    gain_in, bias_in, gain_out, bias_out = (
        value.reshape(1, -1) for value in (ln_in_gain, ln_in_bias, ln_out_gain, ln_out_bias)
    )
    w_edges = (w_a_proj, w_a_gate, w_b_proj, w_b_gate)
    product = 2 * own * cols * chan * hidden

    listed = [quarter * (dap // LEVELS) + at for at in range(dap // LEVELS) for quarter in range(LEVELS)]

    def exchange(value):
        return lax.all_to_all(
            value, "dap", split_axis=0, concat_axis=0, axis_index_groups=[listed], tiled=True
        )

    first = (pair_act, gain_in, bias_in, residue_mask, valid, *w_edges)
    edges = call(
        edges_kernel,
        "edges",
        [((dap, 2 * block, cols), BF16)],
        (me, *first),
        scratch=[
            (pltpu.SMEM if value is residue_mask else pltpu.VMEM)(value.shape, value.dtype)
            for value in first
        ]
        + [pltpu.VMEM((2, dap, block, cols), BF16)]
        + [pltpu.SemaphoreType.DMA((len(first),)), pltpu.SemaphoreType.DMA((2,))],
        scalars=1,
        flops=4 * product,
        to=HBM,
        spaces=[HBM] * len(first),
        limit=None,
    )
    edges = exchange(edges)
    factors, normed_t, rstd_t, gain_t, d_normed, slope, gain_out_t, bias_out_t = call(
        gates_kernel,
        "gates",
        [
            ((4, hidden, own * cols), F32),
            ((chan, own * cols), F32),
            ((1, own * cols), F32),
            ((chan, cols), F32),
            ((hidden * own, cols), F32),
            ((chan, own * cols), F32),
            ((hidden, cols), F32),
            ((hidden, cols), F32),
        ],
        (me, residue_mask, valid, pair_act, out_grad, gain_in, bias_in, gain_out)
        + (bias_out, *w_edges, w_gate, w_out),
        scalars=2,
        flops=6 * product,
    )
    tri, edge_a, edge_b = call(
        functools.partial(triangle_kernel, own),
        "triangle",
        [
            ((dap, block, cols), BF16),
            ((slice_h, rows, cols), BF16),
            ((slice_h, rows, cols), BF16),
        ],
        (edges, d_normed),
        flops=product,
        spaces=[VMEM, pl.BlockSpec(memory_space=pl.ANY)],
    )
    tri = exchange(tri)
    d_tri, d_gate = call(
        functools.partial(norm_kernel, own),
        "norm",
        [((dap, block, cols), BF16), ((chan, own * cols), BF16)],
        (tri, d_normed, slope, gain_out_t, bias_out_t, w_out),
        flops=2 * product,
    )
    d_tri = exchange(d_tri)
    d_edges = call(
        functools.partial(edge_grad_kernel, own),
        "edge_grad",
        [((dap, 2 * block, cols), BF16)],
        (d_tri, edge_a, edge_b),
        flops=2 * product,
    )
    d_edges = exchange(d_edges)
    return call(
        input_grad_kernel,
        "input_grad",
        [((own, cols, chan), BF16)],
        (d_edges, factors, normed_t, rstd_t, gain_t, d_gate, *w_edges, w_gate),
        flops=4 * product,
    )


def fits_kernels(dap, ch, pair_act, w_proj):
    own, cols, chan = pair_act.shape
    hidden = w_proj.shape[1]
    block = hidden // dap * own
    return (
        ch == 1
        and hidden % dap == 0
        and own == SUBLANES // 2
        and block == own * own
        and dap % SUBLANES == 0
        and cols == dap * own
        and cols % 128 == chan % 128 == hidden % 128 == 0
    )


def solution(mesh):
    sizes = dict(mesh.shape)

    def program(*args):
        dap, ch = sizes["dap"], sizes["ch"]
        if fits_kernels(dap, ch, args[0], args[5]):
            return kernel_shards(dap, *args)
        return channel_shards(dap, ch, *args)

    in_specs = (
        P(("grp", "dap"), None, None),
        P(("grp", "dap"), "ch", None),
        P("grp"),
        P(),
        P(),
        P(None, "ch"),
        P(None, "ch"),
        P(None, "ch"),
        P(None, "ch"),
        P(),
        P(),
        P(),
        P(),
    )
    out_specs = P(("grp", "dap"), "ch", None)
    return jax.shard_map(
        program, mesh=mesh, in_specs=in_specs, out_specs=out_specs, check_vma=False
    )
```

```python
import functools

import jax
import jax.numpy as jnp
from jax import lax
from jax.experimental import pallas as pl
from jax.experimental.pallas import tpu as pltpu
from jax.sharding import PartitionSpec as P

EPSILON = 1e-05


def normalise(values, reduce_dim):
    centre = values - jnp.mean(values, axis=reduce_dim, keepdims=True)
    inverse = lax.rsqrt(jnp.mean(centre * centre, axis=reduce_dim, keepdims=True) + EPSILON)
    return (centre * inverse, inverse)


def norm_backward(grad_hat, normed, inverse, reduce_dim):
    mean_grad = jnp.mean(grad_hat, axis=reduce_dim, keepdims=True)
    mean_proj = jnp.mean(grad_hat * normed, axis=reduce_dim, keepdims=True)
    return inverse * (grad_hat - mean_grad - normed * mean_proj)


def channel_shards(
    dap,
    ch,
    pair_act,
    out_grad,
    residue_mask,
    ln_in_gain,
    ln_in_bias,
    w_a_proj,
    w_a_gate,
    w_b_proj,
    w_b_gate,
    w_gate,
    ln_out_gain,
    ln_out_bias,
    w_out,
):
    own_rows, all_cols = pair_act.shape[:2]
    col_span = out_grad.shape[1]
    hidden_local = w_a_proj.shape[1]
    slice_h = hidden_local // dap
    row_first = lax.axis_index("dap") * own_rows
    col_first = lax.axis_index("ch") * col_span
    normed_in, rstd_in = normalise(pair_act.astype(jnp.float32), 2)
    pair_norm = (normed_in * ln_in_gain + ln_in_bias).astype(jnp.bfloat16)
    valid_all = residue_mask.astype(jnp.float32)
    valid_rows = lax.dynamic_slice_in_dim(valid_all, row_first, own_rows)
    row_mask = (valid_rows[:, None] * valid_all[None, :])[None]
    w_four = jnp.concatenate((w_a_proj, w_a_gate, w_b_proj, w_b_gate), axis=1)
    projected = jnp.einsum("ikc,cg->gik", pair_norm, w_four, preferred_element_type=jnp.float32)
    a_proj = projected[:hidden_local]
    a_sig = jax.nn.sigmoid(projected[hidden_local : 2 * hidden_local])
    b_proj = projected[2 * hidden_local : 3 * hidden_local]
    b_sig = jax.nn.sigmoid(projected[3 * hidden_local :])
    edge_a = (row_mask * a_sig * a_proj).astype(jnp.bfloat16)
    edge_b = (row_mask * b_sig * b_proj).astype(jnp.bfloat16)

    split = (dap, slice_h, own_rows, all_cols)
    edges = jnp.stack((edge_a.reshape(split), edge_b.reshape(split)), axis=1)
    edges = lax.all_to_all(edges, "dap", split_axis=0, concat_axis=0, tiled=True)
    edges = jnp.transpose(edges, (1, 2, 0, 3, 4)).reshape(2, slice_h, dap * own_rows, all_cols)
    a_all, b_all = edges[0], edges[1]
    tri = jnp.einsum("hik,hjk->hij", a_all, b_all, preferred_element_type=jnp.float32).astype(
        jnp.bfloat16
    )
    tri = tri.reshape(slice_h, dap, own_rows, ch, col_span)
    tri = jnp.transpose(tri, (1, 3, 0, 2, 4)).reshape(dap * ch, slice_h, own_rows, col_span)
    tri = lax.all_to_all(tri, ("dap", "ch"), split_axis=0, concat_axis=0, tiled=True)
    tri = tri.reshape(dap, ch, slice_h, own_rows, col_span)
    tri_full = jnp.transpose(tri, (1, 0, 2, 3, 4)).reshape(-1, own_rows, col_span)

    normed_out, rstd_out = normalise(tri_full.astype(jnp.float32), 0)
    gain_out = ln_out_gain.reshape(-1, 1, 1)
    bias_out = ln_out_bias.reshape(-1, 1, 1)
    tri_norm = (normed_out * gain_out + bias_out).astype(jnp.bfloat16)
    proj_out = jnp.einsum("hij,hc->ijc", tri_norm, w_out, preferred_element_type=jnp.float32)
    norm_cols = lax.dynamic_slice_in_dim(pair_norm, col_first, col_span, 1)
    gate_act = jax.nn.sigmoid(
        jnp.einsum("ijc,cd->ijd", norm_cols, w_gate, preferred_element_type=jnp.float32)
    )
    upstream = out_grad.astype(jnp.float32)
    d_proj = (upstream * gate_act).astype(jnp.bfloat16)
    d_gate = (upstream * proj_out * gate_act * (1.0 - gate_act)).astype(jnp.bfloat16)
    d_normed = (
        jnp.einsum("ijc,hc->hij", d_proj, w_out, preferred_element_type=jnp.float32) * gain_out
    )
    d_tri = norm_backward(d_normed, normed_out, rstd_out, 0).astype(jnp.bfloat16)

    d_tri = d_tri.reshape(ch, dap, slice_h, own_rows, col_span)
    d_tri = jnp.transpose(d_tri, (1, 0, 2, 3, 4)).reshape(dap * ch, slice_h, own_rows, col_span)
    d_tri = lax.all_to_all(d_tri, ("dap", "ch"), split_axis=0, concat_axis=0, tiled=True)
    d_tri = d_tri.reshape(dap, ch, slice_h, own_rows, col_span)
    d_tri = jnp.transpose(d_tri, (2, 0, 3, 1, 4)).reshape(slice_h, dap * own_rows, all_cols)
    d_edge_a = jnp.einsum("hij,hjk->hik", d_tri, b_all, preferred_element_type=jnp.float32)
    d_edge_b = jnp.einsum("hij,hik->hjk", d_tri, a_all, preferred_element_type=jnp.float32)
    d_edges = jnp.stack((d_edge_a, d_edge_b)).astype(jnp.bfloat16)
    d_edges = d_edges.reshape(2, slice_h, dap, own_rows, all_cols)
    d_edges = jnp.transpose(d_edges, (2, 0, 1, 3, 4))
    d_edges = lax.all_to_all(d_edges, "dap", split_axis=0, concat_axis=0, tiled=True)
    d_edges = jnp.transpose(d_edges, (1, 0, 2, 3, 4)).reshape(2, hidden_local, own_rows, all_cols)

    def split_grad(d_edge, sig_val, proj_val):
        masked = d_edge * row_mask
        return (
            (masked * sig_val).astype(jnp.bfloat16),
            (masked * proj_val * sig_val * (1.0 - sig_val)).astype(jnp.bfloat16),
        )

    d_four = jnp.concatenate(
        split_grad(d_edges[0].astype(jnp.float32), a_sig, a_proj)
        + split_grad(d_edges[1].astype(jnp.float32), b_sig, b_proj),
        axis=0,
    )
    d_hidden = jnp.einsum("gik,cg->ikc", d_four, w_four, preferred_element_type=jnp.float32)
    if ch > 1:
        d_hidden = lax.psum_scatter(
            d_hidden.astype(jnp.bfloat16), "ch", scatter_dimension=1, tiled=True
        ).astype(jnp.float32)
    d_pair_norm = d_hidden + jnp.einsum(
        "ijd,cd->ijc", d_gate, w_gate, preferred_element_type=jnp.float32
    )
    normed_cols = lax.dynamic_slice_in_dim(normed_in, col_first, col_span, 1)
    rstd_cols = lax.dynamic_slice_in_dim(rstd_in, col_first, col_span, 1)
    grad_hat = d_pair_norm * ln_in_gain
    return norm_backward(grad_hat, normed_cols, rstd_cols, 2).astype(jnp.bfloat16)


F32 = jnp.float32
BF16 = jnp.bfloat16
SUBLANES = 8
LEVELS = 4


def dot(lhs, rhs, lhs_dim, rhs_dim):
    return lax.dot_general(
        lhs, rhs, (((lhs_dim,), (rhs_dim,)), ((), ())), preferred_element_type=F32
    )


def turn(values):
    shape = (values.shape[1], values.shape[1])
    row, lane = (lax.broadcasted_iota(jnp.int32, shape, dim) for dim in range(2))
    return dot(jnp.where(row == lane, 1.0, 0.0).astype(BF16), values, 1, 1)


def across(row, count):
    return jnp.transpose(jnp.broadcast_to(row, (count, row.shape[1])))


def exchange_bit(first, second, weight):
    sublane = lax.broadcasted_iota(jnp.int32, first.shape, 1)
    low = sublane & weight == 0
    return (
        jnp.where(low, first, pltpu.roll(second, weight, 1)),
        jnp.where(low, pltpu.roll(first, SUBLANES - weight, 1), second),
    )


def mesh_order(blocks):
    count, *rest = blocks.shape
    return jnp.swapaxes(blocks.reshape(count // LEVELS, LEVELS, *rest), 0, 1).reshape(blocks.shape)


def list_order(blocks):
    count, *rest = blocks.shape
    return jnp.swapaxes(blocks.reshape(LEVELS, count // LEVELS, *rest), 0, 1).reshape(blocks.shape)


def split_channels(blocks, own):
    devices, block, cols = blocks.shape
    tiles = blocks.reshape(devices // 2, 2, block // SUBLANES, SUBLANES, cols)
    parts = []
    for tile in range(block // SUBLANES):
        parts.extend(exchange_bit(tiles[:, 0, tile], tiles[:, 1, tile], own))
    return [part.reshape(devices * own, cols) for part in parts]


def merge_channels(parts, own):
    rows, cols = parts[0].shape
    devices = rows // own
    tiles = [part.reshape(devices // 2, SUBLANES, cols) for part in parts]
    pairs = [exchange_bit(*pair, own) for pair in zip(tiles[::2], tiles[1::2])]
    both = [jnp.concatenate(side, axis=1) for side in zip(*pairs)]
    block = len(parts) * own
    return jnp.stack(both, axis=1).reshape(devices, block, cols)


def trade(parts):
    rows, cols = parts[0].shape
    a, b, c, d = (part.reshape(rows // SUBLANES, SUBLANES, cols) for part in parts)
    (a, b), (c, d) = exchange_bit(a, b, 1), exchange_bit(c, d, 1)
    (a, c), (b, d) = exchange_bit(a, c, 2), exchange_bit(b, d, 2)
    return [part.reshape(rows, cols) for part in (a, b, c, d)]


def edges_kernel(me_ref, *refs):
    sources, (out_ref, *local), (blocks, arrived, left) = refs[:9], refs[9:19], refs[19:]
    copies = [
        pltpu.make_async_copy(source, target, arrived.at[index])
        for index, (source, target) in enumerate(zip(sources, local))
    ]
    for copy in copies:
        copy.start()
    act_ref, gain_ref, bias_ref, rows_ref, valid_ref, *weights = local
    own, cols, chan = act_ref.shape
    half = out_ref.shape[1] // 2
    for copy in copies[:3]:
        copy.wait()
    act = turn(act_ref[...].reshape(own * cols, chan))
    gain = across(gain_ref[...], cols)
    bias = across(bias_ref[...], cols)
    centre = act - jnp.mean(act, axis=0, keepdims=True)
    inverse = lax.rsqrt(jnp.mean(centre * centre, axis=0, keepdims=True) + EPSILON)
    wide_gain, wide_bias = (jnp.concatenate([value] * own, axis=1) for value in (gain, bias))
    pair_norm = (centre * inverse * wide_gain + wide_bias).astype(BF16)
    for copy in copies[3:]:
        copy.wait()
    valid = valid_ref[...].astype(F32)
    mask = jnp.concatenate(
        [valid * rows_ref[me_ref[0] * own + r].astype(F32) for r in range(own)], axis=1
    )
    sent = []
    for side in range(2):
        proj = dot(weights[2 * side][...], pair_norm, 0, 0)
        edge = mask * jax.nn.sigmoid(dot(weights[2 * side + 1][...], pair_norm, 0, 0)) * proj
        parts = trade([edge[:, r * cols : (r + 1) * cols] for r in range(own)])
        blocks[side] = merge_channels(parts, own).astype(BF16)
        copy = pltpu.make_async_copy(
            blocks.at[side], out_ref.at[:, side * half : (side + 1) * half, :], left.at[side]
        )
        copy.start()
        sent.append(copy)
    for copy in sent:
        copy.wait()


def gates_kernel(
    me_ref, rows_ref, valid_ref, act_ref, grad_ref, gain_ref, bias_ref, gain_out_ref, bias_out_ref,
    wap, wag, wbp, wbg, w_gate, w_out,
    factors, normed_t, rstd_t, gain_t, d_normed, slope, gain_out_t, bias_out_t,
):
    own, cols, _ = act_ref.shape
    hidden = wap.shape[1]
    valid = valid_ref[...].astype(F32)
    gain = across(gain_ref[...], cols)
    bias = across(bias_ref[...], cols)
    gain_out = across(gain_out_ref[...], cols)
    gain_t[...] = gain
    gain_out_t[...] = gain_out
    bias_out_t[...] = across(bias_out_ref[...], cols)
    for r in range(own):
        act = jnp.transpose(act_ref[r].astype(F32))
        centre = act - jnp.mean(act, axis=0, keepdims=True)
        inverse = lax.rsqrt(jnp.mean(centre * centre, axis=0, keepdims=True) + EPSILON)
        normed = centre * inverse
        lanes = pl.ds(r * cols, cols)
        normed_t[:, lanes] = normed
        rstd_t[:, lanes] = inverse
        pair_norm = (normed * gain + bias).astype(BF16)
        mask = valid * rows_ref[me_ref[0] * own + r].astype(F32)
        for side, (w_proj, w_sig) in enumerate(((wap, wag), (wbp, wbg))):
            proj = dot(w_proj[...], pair_norm, 0, 0)
            sig = jax.nn.sigmoid(dot(w_sig[...], pair_norm, 0, 0))
            kept = mask * sig
            factors[2 * side, :, lanes] = kept
            factors[2 * side + 1, :, lanes] = kept * proj * (1.0 - sig)
        gate_act = jax.nn.sigmoid(dot(w_gate[...], pair_norm, 0, 0))
        d_proj = jnp.transpose(grad_ref[r].astype(F32)) * gate_act
        slope[:, lanes] = d_proj * (1.0 - gate_act)
        d_normed[pl.ds(r, hidden, stride=own), :] = (
            dot(w_out[...], d_proj.astype(BF16), 1, 0) * gain_out
        )


def triangle_kernel(own, in_ref, _, out_ref, a_ref, b_ref):
    half = out_ref.shape[1]
    sides = [
        split_channels(
            mesh_order(in_ref[:, side * half : (side + 1) * half, :].astype(F32)), own
        )
        for side in range(2)
    ]
    tri = []
    for c, (edge_a, edge_b) in enumerate(zip(*sides)):
        a_ref[c] = edge_a.astype(BF16)
        b_ref[c] = edge_b.astype(BF16)
        tri.append(dot(a_ref[c], b_ref[c], 1, 1))
    out_ref[...] = list_order(merge_channels(tri, own)).astype(BF16)


def fold(values, own):
    total = jnp.sum(values, axis=0)
    rows = total
    for shift in range(own, SUBLANES, own):
        rows = rows + pltpu.roll(total, shift, 0)
    return rows[None]


def tri_normed(tri_ref, hidden, own):
    cols = tri_ref.shape[-1]
    tri = tri_ref[...].astype(F32).reshape(hidden * own // SUBLANES, SUBLANES, cols)
    centre = tri - fold(tri, own) / hidden
    inverse = lax.rsqrt(fold(centre * centre, own) / hidden + EPSILON)
    return centre * inverse, inverse


def norm_kernel(own, tri_ref, grad_ref, slope, gain, bias, w_out, out_ref, gate_ref):
    devices, block, cols = tri_ref.shape
    hidden = w_out.shape[0]
    normed, inverse = tri_normed(tri_ref, hidden, own)
    grad = grad_ref[...].reshape(normed.shape)
    mean_grad = fold(grad, own) / hidden
    mean_proj = fold(grad * normed, own) / hidden
    d_tri = inverse * (grad - mean_grad - normed * mean_proj)
    out_ref[...] = d_tri.reshape(devices, block, cols).astype(BF16)
    parts = trade(split_channels(normed.reshape(devices, block, cols), own))
    tri_norm = jnp.concatenate([(part * gain[...] + bias[...]).astype(BF16) for part in parts], axis=1)
    gate_ref[...] = (slope[...] * dot(w_out[...], tri_norm, 0, 0)).astype(BF16)


def edge_grad_kernel(own, in_ref, a_ref, b_ref, out_ref):
    block = in_ref.shape[1]
    grads = ([], [])
    for c, part in enumerate(split_channels(mesh_order(in_ref[...].astype(F32)), own)):
        d_tri = part.astype(BF16)
        grads[0].append(dot(d_tri, b_ref[c], 1, 0))
        grads[1].append(dot(d_tri, a_ref[c], 0, 0))
    for side in range(2):
        out_ref[:, side * block : (side + 1) * block, :] = (
            list_order(merge_channels(grads[side], own)).astype(BF16)
        )


def input_grad_kernel(
    in_ref, factors, normed_t, rstd_t, gain_t, d_gate, wap, wag, wbp, wbg, w_gate, out_ref
):
    own, cols, _ = out_ref.shape
    half = in_ref.shape[1] // 2
    grads = []
    for side in range(2):
        blocks = in_ref[:, side * half : (side + 1) * half, :].astype(F32)
        d_edge = jnp.concatenate(trade(split_channels(blocks, own)), axis=1)
        for at in range(2):
            grads.append((d_edge * factors[2 * side + at]).astype(BF16))
    weights = [weight[...] for weight in (wap, wag, wbp, wbg, w_gate)]
    grads.append(d_gate[...])
    total = dot(jnp.concatenate(weights, axis=1), jnp.concatenate(grads, axis=0), 1, 0)
    grad_hat = total * jnp.concatenate([gain_t[...]] * own, axis=1)
    normed = normed_t[...]
    mean_grad = jnp.mean(grad_hat, axis=0, keepdims=True)
    mean_proj = jnp.mean(grad_hat * normed, axis=0, keepdims=True)
    grad = rstd_t[...] * (grad_hat - mean_grad - normed * mean_proj)
    for r in range(own):
        out_ref[r] = turn(grad[:, r * cols : (r + 1) * cols].astype(BF16)).astype(BF16)


VMEM = pl.BlockSpec(memory_space=pltpu.VMEM)
SMEM = pl.BlockSpec(memory_space=pltpu.SMEM)
HBM = pl.BlockSpec(memory_space=pltpu.HBM)


def call(kernel, name, outs, args, scratch=(), scalars=0, flops=0, spaces=None, to=VMEM, limit=32 * 2**20):
    shapes = [jax.ShapeDtypeStruct(shape, dtype) for shape, dtype in outs]
    moved = sum(value.size * value.dtype.itemsize for value in list(args) + shapes)
    result = pl.pallas_call(
        kernel,
        name=name,
        out_shape=shapes,
        in_specs=[SMEM] * scalars + (spaces or [VMEM] * (len(args) - scalars)),
        out_specs=[to] * len(outs),
        scratch_shapes=scratch,
        cost_estimate=pl.CostEstimate(flops=flops, bytes_accessed=moved, transcendentals=0),
        compiler_params=pltpu.CompilerParams(vmem_limit_bytes=limit),
    )(*args)
    return result[0] if len(outs) == 1 else result


def kernel_shards(
    dap,
    pair_act,
    out_grad,
    residue_mask,
    ln_in_gain,
    ln_in_bias,
    w_a_proj,
    w_a_gate,
    w_b_proj,
    w_b_gate,
    w_gate,
    ln_out_gain,
    ln_out_bias,
    w_out,
):
    own, cols, chan = pair_act.shape
    hidden = w_a_proj.shape[1]
    slice_h = hidden // dap
    rows = dap * own
    block = slice_h * own
    me = lax.axis_index("dap").reshape(1)
    valid = residue_mask.reshape(1, -1)
    gain_in, bias_in, gain_out, bias_out = (
        value.reshape(1, -1) for value in (ln_in_gain, ln_in_bias, ln_out_gain, ln_out_bias)
    )
    w_edges = (w_a_proj, w_a_gate, w_b_proj, w_b_gate)
    product = 2 * own * cols * chan * hidden

    listed = [quarter * (dap // LEVELS) + at for at in range(dap // LEVELS) for quarter in range(LEVELS)]

    def exchange(value):
        return lax.all_to_all(
            value, "dap", split_axis=0, concat_axis=0, axis_index_groups=[listed], tiled=True
        )

    first = (pair_act, gain_in, bias_in, residue_mask, valid, *w_edges)
    edges = call(
        edges_kernel,
        "edges",
        [((dap, 2 * block, cols), BF16)],
        (me, *first),
        scratch=[
            (pltpu.SMEM if value is residue_mask else pltpu.VMEM)(value.shape, value.dtype)
            for value in first
        ]
        + [pltpu.VMEM((2, dap, block, cols), BF16)]
        + [pltpu.SemaphoreType.DMA((len(first),)), pltpu.SemaphoreType.DMA((2,))],
        scalars=1,
        flops=4 * product,
        to=HBM,
        spaces=[HBM] * len(first),
        limit=None,
    )
    edges = exchange(edges)
    factors, normed_t, rstd_t, gain_t, d_normed, slope, gain_out_t, bias_out_t = call(
        gates_kernel,
        "gates",
        [
            ((4, hidden, own * cols), F32),
            ((chan, own * cols), F32),
            ((1, own * cols), F32),
            ((chan, cols), F32),
            ((hidden * own, cols), F32),
            ((chan, own * cols), F32),
            ((hidden, cols), F32),
            ((hidden, cols), F32),
        ],
        (me, residue_mask, valid, pair_act, out_grad, gain_in, bias_in, gain_out)
        + (bias_out, *w_edges, w_gate, w_out),
        scalars=2,
        flops=6 * product,
    )
    tri, edge_a, edge_b = call(
        functools.partial(triangle_kernel, own),
        "triangle",
        [
            ((dap, block, cols), BF16),
            ((slice_h, rows, cols), BF16),
            ((slice_h, rows, cols), BF16),
        ],
        (edges, d_normed),
        flops=product,
        spaces=[VMEM, pl.BlockSpec(memory_space=pl.ANY)],
    )
    tri = exchange(tri)
    d_tri, d_gate = call(
        functools.partial(norm_kernel, own),
        "norm",
        [((dap, block, cols), BF16), ((chan, own * cols), BF16)],
        (tri, d_normed, slope, gain_out_t, bias_out_t, w_out),
        flops=2 * product,
    )
    d_tri = exchange(d_tri)
    d_edges = call(
        functools.partial(edge_grad_kernel, own),
        "edge_grad",
        [((dap, 2 * block, cols), BF16)],
        (d_tri, edge_a, edge_b),
        flops=2 * product,
    )
    d_edges = exchange(d_edges)
    return call(
        input_grad_kernel,
        "input_grad",
        [((own, cols, chan), BF16)],
        (d_edges, factors, normed_t, rstd_t, gain_t, d_gate, *w_edges, w_gate),
        flops=4 * product,
    )


def fits_kernels(dap, ch, pair_act, w_proj):
    own, cols, chan = pair_act.shape
    hidden = w_proj.shape[1]
    block = hidden // dap * own
    return (
        ch == 1
        and hidden % dap == 0
        and own == SUBLANES // 2
        and block == own * own
        and dap % SUBLANES == 0
        and cols == dap * own
        and cols % 128 == chan % 128 == hidden % 128 == 0
    )


def solution(mesh):
    sizes = dict(mesh.shape)

    def program(*args):
        dap, ch = sizes["dap"], sizes["ch"]
        if fits_kernels(dap, ch, args[0], args[5]):
            return kernel_shards(dap, *args)
        return channel_shards(dap, ch, *args)

    in_specs = (
        P(("grp", "dap"), None, None),
        P(("grp", "dap"), "ch", None),
        P("grp"),
        P(),
        P(),
        P(None, "ch"),
        P(None, "ch"),
        P(None, "ch"),
        P(None, "ch"),
        P(),
        P(),
        P(),
        P(),
    )
    out_specs = P(("grp", "dap"), "ch", None)
    return jax.shard_map(
        program, mesh=mesh, in_specs=in_specs, out_specs=out_specs, check_vma=False
    )
```

```python
import functools

import jax
import jax.numpy as jnp
from jax import lax
from jax.experimental import pallas as pl
from jax.experimental.pallas import tpu as pltpu
from jax.sharding import PartitionSpec as P

EPSILON = 1e-05


def normalise(values, reduce_dim):
    centre = values - jnp.mean(values, axis=reduce_dim, keepdims=True)
    inverse = lax.rsqrt(jnp.mean(centre * centre, axis=reduce_dim, keepdims=True) + EPSILON)
    return (centre * inverse, inverse)


def norm_backward(grad_hat, normed, inverse, reduce_dim):
    mean_grad = jnp.mean(grad_hat, axis=reduce_dim, keepdims=True)
    mean_proj = jnp.mean(grad_hat * normed, axis=reduce_dim, keepdims=True)
    return inverse * (grad_hat - mean_grad - normed * mean_proj)


def channel_shards(
    dap,
    ch,
    pair_act,
    out_grad,
    residue_mask,
    ln_in_gain,
    ln_in_bias,
    w_a_proj,
    w_a_gate,
    w_b_proj,
    w_b_gate,
    w_gate,
    ln_out_gain,
    ln_out_bias,
    w_out,
):
    own_rows, all_cols = pair_act.shape[:2]
    col_span = out_grad.shape[1]
    hidden_local = w_a_proj.shape[1]
    slice_h = hidden_local // dap
    row_first = lax.axis_index("dap") * own_rows
    col_first = lax.axis_index("ch") * col_span
    normed_in, rstd_in = normalise(pair_act.astype(jnp.float32), 2)
    pair_norm = (normed_in * ln_in_gain + ln_in_bias).astype(jnp.bfloat16)
    valid_all = residue_mask.astype(jnp.float32)
    valid_rows = lax.dynamic_slice_in_dim(valid_all, row_first, own_rows)
    row_mask = (valid_rows[:, None] * valid_all[None, :])[None]
    w_four = jnp.concatenate((w_a_proj, w_a_gate, w_b_proj, w_b_gate), axis=1)
    projected = jnp.einsum("ikc,cg->gik", pair_norm, w_four, preferred_element_type=jnp.float32)
    a_proj = projected[:hidden_local]
    a_sig = jax.nn.sigmoid(projected[hidden_local : 2 * hidden_local])
    b_proj = projected[2 * hidden_local : 3 * hidden_local]
    b_sig = jax.nn.sigmoid(projected[3 * hidden_local :])
    edge_a = (row_mask * a_sig * a_proj).astype(jnp.bfloat16)
    edge_b = (row_mask * b_sig * b_proj).astype(jnp.bfloat16)

    split = (dap, slice_h, own_rows, all_cols)
    edges = jnp.stack((edge_a.reshape(split), edge_b.reshape(split)), axis=1)
    edges = lax.all_to_all(edges, "dap", split_axis=0, concat_axis=0, tiled=True)
    edges = jnp.transpose(edges, (1, 2, 0, 3, 4)).reshape(2, slice_h, dap * own_rows, all_cols)
    a_all, b_all = edges[0], edges[1]
    tri = jnp.einsum("hik,hjk->hij", a_all, b_all, preferred_element_type=jnp.float32).astype(
        jnp.bfloat16
    )
    tri = tri.reshape(slice_h, dap, own_rows, ch, col_span)
    tri = jnp.transpose(tri, (1, 3, 0, 2, 4)).reshape(dap * ch, slice_h, own_rows, col_span)
    tri = lax.all_to_all(tri, ("dap", "ch"), split_axis=0, concat_axis=0, tiled=True)
    tri = tri.reshape(dap, ch, slice_h, own_rows, col_span)
    tri_full = jnp.transpose(tri, (1, 0, 2, 3, 4)).reshape(-1, own_rows, col_span)

    normed_out, rstd_out = normalise(tri_full.astype(jnp.float32), 0)
    gain_out = ln_out_gain.reshape(-1, 1, 1)
    bias_out = ln_out_bias.reshape(-1, 1, 1)
    tri_norm = (normed_out * gain_out + bias_out).astype(jnp.bfloat16)
    proj_out = jnp.einsum("hij,hc->ijc", tri_norm, w_out, preferred_element_type=jnp.float32)
    norm_cols = lax.dynamic_slice_in_dim(pair_norm, col_first, col_span, 1)
    gate_act = jax.nn.sigmoid(
        jnp.einsum("ijc,cd->ijd", norm_cols, w_gate, preferred_element_type=jnp.float32)
    )
    upstream = out_grad.astype(jnp.float32)
    d_proj = (upstream * gate_act).astype(jnp.bfloat16)
    d_gate = (upstream * proj_out * gate_act * (1.0 - gate_act)).astype(jnp.bfloat16)
    d_normed = (
        jnp.einsum("ijc,hc->hij", d_proj, w_out, preferred_element_type=jnp.float32) * gain_out
    )
    d_tri = norm_backward(d_normed, normed_out, rstd_out, 0).astype(jnp.bfloat16)

    d_tri = d_tri.reshape(ch, dap, slice_h, own_rows, col_span)
    d_tri = jnp.transpose(d_tri, (1, 0, 2, 3, 4)).reshape(dap * ch, slice_h, own_rows, col_span)
    d_tri = lax.all_to_all(d_tri, ("dap", "ch"), split_axis=0, concat_axis=0, tiled=True)
    d_tri = d_tri.reshape(dap, ch, slice_h, own_rows, col_span)
    d_tri = jnp.transpose(d_tri, (2, 0, 3, 1, 4)).reshape(slice_h, dap * own_rows, all_cols)
    d_edge_a = jnp.einsum("hij,hjk->hik", d_tri, b_all, preferred_element_type=jnp.float32)
    d_edge_b = jnp.einsum("hij,hik->hjk", d_tri, a_all, preferred_element_type=jnp.float32)
    d_edges = jnp.stack((d_edge_a, d_edge_b)).astype(jnp.bfloat16)
    d_edges = d_edges.reshape(2, slice_h, dap, own_rows, all_cols)
    d_edges = jnp.transpose(d_edges, (2, 0, 1, 3, 4))
    d_edges = lax.all_to_all(d_edges, "dap", split_axis=0, concat_axis=0, tiled=True)
    d_edges = jnp.transpose(d_edges, (1, 0, 2, 3, 4)).reshape(2, hidden_local, own_rows, all_cols)

    def split_grad(d_edge, sig_val, proj_val):
        masked = d_edge * row_mask
        return (
            (masked * sig_val).astype(jnp.bfloat16),
            (masked * proj_val * sig_val * (1.0 - sig_val)).astype(jnp.bfloat16),
        )

    d_four = jnp.concatenate(
        split_grad(d_edges[0].astype(jnp.float32), a_sig, a_proj)
        + split_grad(d_edges[1].astype(jnp.float32), b_sig, b_proj),
        axis=0,
    )
    d_hidden = jnp.einsum("gik,cg->ikc", d_four, w_four, preferred_element_type=jnp.float32)
    if ch > 1:
        d_hidden = lax.psum_scatter(
            d_hidden.astype(jnp.bfloat16), "ch", scatter_dimension=1, tiled=True
        ).astype(jnp.float32)
    d_pair_norm = d_hidden + jnp.einsum(
        "ijd,cd->ijc", d_gate, w_gate, preferred_element_type=jnp.float32
    )
    normed_cols = lax.dynamic_slice_in_dim(normed_in, col_first, col_span, 1)
    rstd_cols = lax.dynamic_slice_in_dim(rstd_in, col_first, col_span, 1)
    grad_hat = d_pair_norm * ln_in_gain
    return norm_backward(grad_hat, normed_cols, rstd_cols, 2).astype(jnp.bfloat16)


F32 = jnp.float32
BF16 = jnp.bfloat16
SUBLANES = 8


def dot(lhs, rhs, lhs_dim, rhs_dim):
    return lax.dot_general(
        lhs, rhs, (((lhs_dim,), (rhs_dim,)), ((), ())), preferred_element_type=F32
    )


def across(row, count):
    return jnp.transpose(jnp.broadcast_to(row, (count, row.shape[1])))


def exchange_bit(first, second, weight):
    sublane = lax.broadcasted_iota(jnp.int32, first.shape, 1)
    low = sublane & weight == 0
    return (
        jnp.where(low, first, pltpu.roll(second, weight, 1)),
        jnp.where(low, pltpu.roll(first, SUBLANES - weight, 1), second),
    )


def split_channels(blocks, own):
    devices, block, cols = blocks.shape
    tiles = blocks.reshape(devices // 2, 2, block // SUBLANES, SUBLANES, cols)
    parts = []
    for tile in range(block // SUBLANES):
        parts.extend(exchange_bit(tiles[:, 0, tile], tiles[:, 1, tile], own))
    return [part.reshape(devices * own, cols) for part in parts]


def merge_channels(parts, own):
    rows, cols = parts[0].shape
    devices = rows // own
    tiles = [part.reshape(devices // 2, SUBLANES, cols) for part in parts]
    pairs = [exchange_bit(*pair, own) for pair in zip(tiles[::2], tiles[1::2])]
    both = [jnp.concatenate(side, axis=1) for side in zip(*pairs)]
    block = len(parts) * own
    return jnp.stack(both, axis=1).reshape(devices, block, cols)


def trade(parts):
    rows, cols = parts[0].shape
    a, b, c, d = (part.reshape(rows // SUBLANES, SUBLANES, cols) for part in parts)
    (a, b), (c, d) = exchange_bit(a, b, 1), exchange_bit(c, d, 1)
    (a, c), (b, d) = exchange_bit(a, c, 2), exchange_bit(b, d, 2)
    return [part.reshape(rows, cols) for part in (a, b, c, d)]


def edges_kernel(me_ref, *refs):
    sources, (out_ref, *local), (blocks, arrived, left) = refs[:9], refs[9:19], refs[19:]
    copies = [
        pltpu.make_async_copy(source, target, arrived.at[index])
        for index, (source, target) in enumerate(zip(sources, local))
    ]
    for copy in copies:
        copy.start()
    act_ref, gain_ref, bias_ref, rows_ref, valid_ref, *weights = local
    own, cols, chan = act_ref.shape
    half = out_ref.shape[1] // 2
    for copy in copies[:3]:
        copy.wait()
    act = jnp.concatenate([jnp.transpose(act_ref[r].astype(F32)) for r in range(own)], axis=1)
    gain = across(gain_ref[...], cols)
    bias = across(bias_ref[...], cols)
    centre = act - jnp.mean(act, axis=0, keepdims=True)
    inverse = lax.rsqrt(jnp.mean(centre * centre, axis=0, keepdims=True) + EPSILON)
    wide_gain, wide_bias = (jnp.concatenate([value] * own, axis=1) for value in (gain, bias))
    pair_norm = (centre * inverse * wide_gain + wide_bias).astype(BF16)
    for copy in copies[3:]:
        copy.wait()
    valid = valid_ref[...].astype(F32)
    mask = jnp.concatenate(
        [valid * rows_ref[me_ref[0] * own + r].astype(F32) for r in range(own)], axis=1
    )
    sent = []
    for side in range(2):
        proj = dot(weights[2 * side][...], pair_norm, 0, 0)
        edge = mask * jax.nn.sigmoid(dot(weights[2 * side + 1][...], pair_norm, 0, 0)) * proj
        parts = trade([edge[:, r * cols : (r + 1) * cols] for r in range(own)])
        blocks[side] = merge_channels(parts, own).astype(BF16)
        copy = pltpu.make_async_copy(
            blocks.at[side], out_ref.at[:, side * half : (side + 1) * half, :], left.at[side]
        )
        copy.start()
        sent.append(copy)
    for copy in sent:
        copy.wait()


def gates_kernel(
    me_ref, rows_ref, valid_ref, act_ref, grad_ref, gain_ref, bias_ref, gain_out_ref, bias_out_ref,
    wap, wag, wbp, wbg, w_gate, w_out,
    factors, normed_t, rstd_t, gain_t, d_normed, slope, gain_out_t, bias_out_t,
):
    own, cols, _ = act_ref.shape
    hidden = wap.shape[1]
    valid = valid_ref[...].astype(F32)
    gain = across(gain_ref[...], cols)
    bias = across(bias_ref[...], cols)
    gain_out = across(gain_out_ref[...], cols)
    gain_t[...] = gain
    gain_out_t[...] = gain_out
    bias_out_t[...] = across(bias_out_ref[...], cols)
    for r in range(own):
        act = jnp.transpose(act_ref[r].astype(F32))
        centre = act - jnp.mean(act, axis=0, keepdims=True)
        inverse = lax.rsqrt(jnp.mean(centre * centre, axis=0, keepdims=True) + EPSILON)
        normed = centre * inverse
        lanes = pl.ds(r * cols, cols)
        normed_t[:, lanes] = normed
        rstd_t[:, lanes] = inverse
        pair_norm = (normed * gain + bias).astype(BF16)
        mask = valid * rows_ref[me_ref[0] * own + r].astype(F32)
        for side, (w_proj, w_sig) in enumerate(((wap, wag), (wbp, wbg))):
            proj = dot(w_proj[...], pair_norm, 0, 0)
            sig = jax.nn.sigmoid(dot(w_sig[...], pair_norm, 0, 0))
            kept = mask * sig
            factors[2 * side, :, lanes] = kept
            factors[2 * side + 1, :, lanes] = kept * proj * (1.0 - sig)
        gate_act = jax.nn.sigmoid(dot(w_gate[...], pair_norm, 0, 0))
        d_proj = jnp.transpose(grad_ref[r].astype(F32)) * gate_act
        slope[:, lanes] = d_proj * (1.0 - gate_act)
        d_normed[pl.ds(r, hidden, stride=own), :] = (
            dot(w_out[...], d_proj.astype(BF16), 1, 0) * gain_out
        )


def triangle_kernel(own, in_ref, _, out_ref, a_ref, b_ref):
    half = out_ref.shape[1]
    sides = [
        split_channels(in_ref[:, side * half : (side + 1) * half, :].astype(F32), own)
        for side in range(2)
    ]
    tri = []
    for c, (edge_a, edge_b) in enumerate(zip(*sides)):
        a_ref[c] = edge_a.astype(BF16)
        b_ref[c] = edge_b.astype(BF16)
        tri.append(dot(a_ref[c], b_ref[c], 1, 1))
    out_ref[...] = merge_channels(tri, own).astype(BF16)


def fold(values, own):
    total = jnp.sum(values, axis=0)
    rows = total
    for shift in range(own, SUBLANES, own):
        rows = rows + pltpu.roll(total, shift, 0)
    return rows[None]


def tri_normed(tri_ref, hidden, own):
    cols = tri_ref.shape[-1]
    tri = tri_ref[...].astype(F32).reshape(hidden * own // SUBLANES, SUBLANES, cols)
    centre = tri - fold(tri, own) / hidden
    inverse = lax.rsqrt(fold(centre * centre, own) / hidden + EPSILON)
    return centre * inverse, inverse


def norm_kernel(own, tri_ref, grad_ref, slope, gain, bias, w_out, out_ref, gate_ref):
    devices, block, cols = tri_ref.shape
    hidden = w_out.shape[0]
    normed, inverse = tri_normed(tri_ref, hidden, own)
    grad = grad_ref[...].reshape(normed.shape)
    mean_grad = fold(grad, own) / hidden
    mean_proj = fold(grad * normed, own) / hidden
    d_tri = inverse * (grad - mean_grad - normed * mean_proj)
    out_ref[...] = d_tri.reshape(devices, block, cols).astype(BF16)
    parts = trade(split_channels(normed.reshape(devices, block, cols), own))
    tri_norm = jnp.concatenate([(part * gain[...] + bias[...]).astype(BF16) for part in parts], axis=1)
    gate_ref[...] = (slope[...] * dot(w_out[...], tri_norm, 0, 0)).astype(BF16)


def edge_grad_kernel(own, in_ref, a_ref, b_ref, out_ref):
    block = in_ref.shape[1]
    grads = ([], [])
    for c, part in enumerate(split_channels(in_ref[...].astype(F32), own)):
        d_tri = part.astype(BF16)
        grads[0].append(dot(d_tri, b_ref[c], 1, 0))
        grads[1].append(dot(d_tri, a_ref[c], 0, 0))
    for side in range(2):
        out_ref[:, side * block : (side + 1) * block, :] = (
            merge_channels(grads[side], own).astype(BF16)
        )


def input_grad_kernel(
    in_ref, factors, normed_t, rstd_t, gain_t, d_gate, wap, wag, wbp, wbg, w_gate, out_ref
):
    own, cols, _ = out_ref.shape
    half = in_ref.shape[1] // 2
    grads = []
    for side in range(2):
        blocks = in_ref[:, side * half : (side + 1) * half, :].astype(F32)
        d_edge = jnp.concatenate(trade(split_channels(blocks, own)), axis=1)
        for at in range(2):
            grads.append((d_edge * factors[2 * side + at]).astype(BF16))
    weights = [weight[...] for weight in (wap, wag, wbp, wbg, w_gate)]
    grads.append(d_gate[...])
    total = dot(jnp.concatenate(weights, axis=1), jnp.concatenate(grads, axis=0), 1, 0)
    grad_hat = total * jnp.concatenate([gain_t[...]] * own, axis=1)
    normed = normed_t[...]
    mean_grad = jnp.mean(grad_hat, axis=0, keepdims=True)
    mean_proj = jnp.mean(grad_hat * normed, axis=0, keepdims=True)
    grad = rstd_t[...] * (grad_hat - mean_grad - normed * mean_proj)
    for r in range(own):
        out_ref[r] = jnp.transpose(grad[:, r * cols : (r + 1) * cols]).astype(BF16)


VMEM = pl.BlockSpec(memory_space=pltpu.VMEM)
SMEM = pl.BlockSpec(memory_space=pltpu.SMEM)
HBM = pl.BlockSpec(memory_space=pltpu.HBM)


def call(kernel, name, outs, args, scratch=(), scalars=0, flops=0, spaces=None, to=VMEM, limit=32 * 2**20):
    shapes = [jax.ShapeDtypeStruct(shape, dtype) for shape, dtype in outs]
    moved = sum(value.size * value.dtype.itemsize for value in list(args) + shapes)
    result = pl.pallas_call(
        kernel,
        name=name,
        out_shape=shapes,
        in_specs=[SMEM] * scalars + (spaces or [VMEM] * (len(args) - scalars)),
        out_specs=[to] * len(outs),
        scratch_shapes=scratch,
        cost_estimate=pl.CostEstimate(flops=flops, bytes_accessed=moved, transcendentals=0),
        compiler_params=pltpu.CompilerParams(vmem_limit_bytes=limit),
    )(*args)
    return result[0] if len(outs) == 1 else result


def kernel_shards(
    dap,
    pair_act,
    out_grad,
    residue_mask,
    ln_in_gain,
    ln_in_bias,
    w_a_proj,
    w_a_gate,
    w_b_proj,
    w_b_gate,
    w_gate,
    ln_out_gain,
    ln_out_bias,
    w_out,
):
    own, cols, chan = pair_act.shape
    hidden = w_a_proj.shape[1]
    slice_h = hidden // dap
    rows = dap * own
    block = slice_h * own
    me = lax.axis_index("dap").reshape(1)
    valid = residue_mask.reshape(1, -1)
    gain_in, bias_in, gain_out, bias_out = (
        value.reshape(1, -1) for value in (ln_in_gain, ln_in_bias, ln_out_gain, ln_out_bias)
    )
    w_edges = (w_a_proj, w_a_gate, w_b_proj, w_b_gate)
    product = 2 * own * cols * chan * hidden

    def exchange(value):
        return lax.all_to_all(value, "dap", split_axis=0, concat_axis=0, tiled=True)

    first = (pair_act, gain_in, bias_in, residue_mask, valid, *w_edges)
    edges = call(
        edges_kernel,
        "edges",
        [((dap, 2 * block, cols), BF16)],
        (me, *first),
        scratch=[
            (pltpu.SMEM if value is residue_mask else pltpu.VMEM)(value.shape, value.dtype)
            for value in first
        ]
        + [pltpu.VMEM((2, dap, block, cols), BF16)]
        + [pltpu.SemaphoreType.DMA((len(first),)), pltpu.SemaphoreType.DMA((2,))],
        scalars=1,
        flops=4 * product,
        to=HBM,
        spaces=[HBM] * len(first),
        limit=None,
    )
    edges = exchange(edges)
    factors, normed_t, rstd_t, gain_t, d_normed, slope, gain_out_t, bias_out_t = call(
        gates_kernel,
        "gates",
        [
            ((4, hidden, own * cols), F32),
            ((chan, own * cols), F32),
            ((1, own * cols), F32),
            ((chan, cols), F32),
            ((hidden * own, cols), F32),
            ((chan, own * cols), F32),
            ((hidden, cols), F32),
            ((hidden, cols), F32),
        ],
        (me, residue_mask, valid, pair_act, out_grad, gain_in, bias_in, gain_out)
        + (bias_out, *w_edges, w_gate, w_out),
        scalars=2,
        flops=6 * product,
    )
    tri, edge_a, edge_b = call(
        functools.partial(triangle_kernel, own),
        "triangle",
        [
            ((dap, block, cols), BF16),
            ((slice_h, rows, cols), BF16),
            ((slice_h, rows, cols), BF16),
        ],
        (edges, d_normed),
        flops=product,
        spaces=[VMEM, pl.BlockSpec(memory_space=pl.ANY)],
    )
    tri = exchange(tri)
    d_tri, d_gate = call(
        functools.partial(norm_kernel, own),
        "norm",
        [((dap, block, cols), BF16), ((chan, own * cols), BF16)],
        (tri, d_normed, slope, gain_out_t, bias_out_t, w_out),
        flops=2 * product,
    )
    d_tri = exchange(d_tri)
    d_edges = call(
        functools.partial(edge_grad_kernel, own),
        "edge_grad",
        [((dap, 2 * block, cols), BF16)],
        (d_tri, edge_a, edge_b),
        flops=2 * product,
    )
    d_edges = exchange(d_edges)
    return call(
        input_grad_kernel,
        "input_grad",
        [((own, cols, chan), BF16)],
        (d_edges, factors, normed_t, rstd_t, gain_t, d_gate, *w_edges, w_gate),
        flops=4 * product,
    )


def fits_kernels(dap, ch, pair_act, w_proj):
    own, cols, chan = pair_act.shape
    hidden = w_proj.shape[1]
    block = hidden // dap * own
    return (
        ch == 1
        and hidden % dap == 0
        and own == SUBLANES // 2
        and block == own * own
        and dap % SUBLANES == 0
        and cols == dap * own
        and cols % 128 == chan % 128 == hidden % 128 == 0
    )


def solution(mesh):
    sizes = dict(mesh.shape)

    def program(*args):
        dap, ch = sizes["dap"], sizes["ch"]
        if fits_kernels(dap, ch, args[0], args[5]):
            return kernel_shards(dap, *args)
        return channel_shards(dap, ch, *args)

    in_specs = (
        P(("grp", "dap"), None, None),
        P(("grp", "dap"), "ch", None),
        P("grp"),
        P(),
        P(),
        P(None, "ch"),
        P(None, "ch"),
        P(None, "ch"),
        P(None, "ch"),
        P(),
        P(),
        P(),
        P(),
    )
    out_specs = P(("grp", "dap"), "ch", None)
    return jax.shard_map(
        program, mesh=mesh, in_specs=in_specs, out_specs=out_specs, check_vma=False
    )
```

```python
import functools

import jax
import jax.numpy as jnp
from jax import lax
from jax.experimental import pallas as pl
from jax.experimental.pallas import tpu as pltpu
from jax.sharding import PartitionSpec as P

EPSILON = 1e-05


def normalise(values, reduce_dim):
    centre = values - jnp.mean(values, axis=reduce_dim, keepdims=True)
    inverse = lax.rsqrt(jnp.mean(centre * centre, axis=reduce_dim, keepdims=True) + EPSILON)
    return (centre * inverse, inverse)


def norm_backward(grad_hat, normed, inverse, reduce_dim):
    mean_grad = jnp.mean(grad_hat, axis=reduce_dim, keepdims=True)
    mean_proj = jnp.mean(grad_hat * normed, axis=reduce_dim, keepdims=True)
    return inverse * (grad_hat - mean_grad - normed * mean_proj)


def channel_shards(
    dap,
    ch,
    pair_act,
    out_grad,
    residue_mask,
    ln_in_gain,
    ln_in_bias,
    w_a_proj,
    w_a_gate,
    w_b_proj,
    w_b_gate,
    w_gate,
    ln_out_gain,
    ln_out_bias,
    w_out,
):
    own_rows, all_cols = pair_act.shape[:2]
    col_span = out_grad.shape[1]
    hidden_local = w_a_proj.shape[1]
    slice_h = hidden_local // dap
    row_first = lax.axis_index("dap") * own_rows
    col_first = lax.axis_index("ch") * col_span
    normed_in, rstd_in = normalise(pair_act.astype(jnp.float32), 2)
    pair_norm = (normed_in * ln_in_gain + ln_in_bias).astype(jnp.bfloat16)
    valid_all = residue_mask.astype(jnp.float32)
    valid_rows = lax.dynamic_slice_in_dim(valid_all, row_first, own_rows)
    row_mask = (valid_rows[:, None] * valid_all[None, :])[None]
    w_four = jnp.concatenate((w_a_proj, w_a_gate, w_b_proj, w_b_gate), axis=1)
    projected = jnp.einsum("ikc,cg->gik", pair_norm, w_four, preferred_element_type=jnp.float32)
    a_proj = projected[:hidden_local]
    a_sig = jax.nn.sigmoid(projected[hidden_local : 2 * hidden_local])
    b_proj = projected[2 * hidden_local : 3 * hidden_local]
    b_sig = jax.nn.sigmoid(projected[3 * hidden_local :])
    edge_a = (row_mask * a_sig * a_proj).astype(jnp.bfloat16)
    edge_b = (row_mask * b_sig * b_proj).astype(jnp.bfloat16)

    split = (dap, slice_h, own_rows, all_cols)
    edges = jnp.stack((edge_a.reshape(split), edge_b.reshape(split)), axis=1)
    edges = lax.all_to_all(edges, "dap", split_axis=0, concat_axis=0, tiled=True)
    edges = jnp.transpose(edges, (1, 2, 0, 3, 4)).reshape(2, slice_h, dap * own_rows, all_cols)
    a_all, b_all = edges[0], edges[1]
    tri = jnp.einsum("hik,hjk->hij", a_all, b_all, preferred_element_type=jnp.float32).astype(
        jnp.bfloat16
    )
    tri = tri.reshape(slice_h, dap, own_rows, ch, col_span)
    tri = jnp.transpose(tri, (1, 3, 0, 2, 4)).reshape(dap * ch, slice_h, own_rows, col_span)
    tri = lax.all_to_all(tri, ("dap", "ch"), split_axis=0, concat_axis=0, tiled=True)
    tri = tri.reshape(dap, ch, slice_h, own_rows, col_span)
    tri_full = jnp.transpose(tri, (1, 0, 2, 3, 4)).reshape(-1, own_rows, col_span)

    normed_out, rstd_out = normalise(tri_full.astype(jnp.float32), 0)
    gain_out = ln_out_gain.reshape(-1, 1, 1)
    bias_out = ln_out_bias.reshape(-1, 1, 1)
    tri_norm = (normed_out * gain_out + bias_out).astype(jnp.bfloat16)
    proj_out = jnp.einsum("hij,hc->ijc", tri_norm, w_out, preferred_element_type=jnp.float32)
    norm_cols = lax.dynamic_slice_in_dim(pair_norm, col_first, col_span, 1)
    gate_act = jax.nn.sigmoid(
        jnp.einsum("ijc,cd->ijd", norm_cols, w_gate, preferred_element_type=jnp.float32)
    )
    upstream = out_grad.astype(jnp.float32)
    d_proj = (upstream * gate_act).astype(jnp.bfloat16)
    d_gate = (upstream * proj_out * gate_act * (1.0 - gate_act)).astype(jnp.bfloat16)
    d_normed = (
        jnp.einsum("ijc,hc->hij", d_proj, w_out, preferred_element_type=jnp.float32) * gain_out
    )
    d_tri = norm_backward(d_normed, normed_out, rstd_out, 0).astype(jnp.bfloat16)

    d_tri = d_tri.reshape(ch, dap, slice_h, own_rows, col_span)
    d_tri = jnp.transpose(d_tri, (1, 0, 2, 3, 4)).reshape(dap * ch, slice_h, own_rows, col_span)
    d_tri = lax.all_to_all(d_tri, ("dap", "ch"), split_axis=0, concat_axis=0, tiled=True)
    d_tri = d_tri.reshape(dap, ch, slice_h, own_rows, col_span)
    d_tri = jnp.transpose(d_tri, (2, 0, 3, 1, 4)).reshape(slice_h, dap * own_rows, all_cols)
    d_edge_a = jnp.einsum("hij,hjk->hik", d_tri, b_all, preferred_element_type=jnp.float32)
    d_edge_b = jnp.einsum("hij,hik->hjk", d_tri, a_all, preferred_element_type=jnp.float32)
    d_edges = jnp.stack((d_edge_a, d_edge_b)).astype(jnp.bfloat16)
    d_edges = d_edges.reshape(2, slice_h, dap, own_rows, all_cols)
    d_edges = jnp.transpose(d_edges, (2, 0, 1, 3, 4))
    d_edges = lax.all_to_all(d_edges, "dap", split_axis=0, concat_axis=0, tiled=True)
    d_edges = jnp.transpose(d_edges, (1, 0, 2, 3, 4)).reshape(2, hidden_local, own_rows, all_cols)

    def split_grad(d_edge, sig_val, proj_val):
        masked = d_edge * row_mask
        return (
            (masked * sig_val).astype(jnp.bfloat16),
            (masked * proj_val * sig_val * (1.0 - sig_val)).astype(jnp.bfloat16),
        )

    d_four = jnp.concatenate(
        split_grad(d_edges[0].astype(jnp.float32), a_sig, a_proj)
        + split_grad(d_edges[1].astype(jnp.float32), b_sig, b_proj),
        axis=0,
    )
    d_hidden = jnp.einsum("gik,cg->ikc", d_four, w_four, preferred_element_type=jnp.float32)
    if ch > 1:
        d_hidden = lax.psum_scatter(
            d_hidden.astype(jnp.bfloat16), "ch", scatter_dimension=1, tiled=True
        ).astype(jnp.float32)
    d_pair_norm = d_hidden + jnp.einsum(
        "ijd,cd->ijc", d_gate, w_gate, preferred_element_type=jnp.float32
    )
    normed_cols = lax.dynamic_slice_in_dim(normed_in, col_first, col_span, 1)
    rstd_cols = lax.dynamic_slice_in_dim(rstd_in, col_first, col_span, 1)
    grad_hat = d_pair_norm * ln_in_gain
    return norm_backward(grad_hat, normed_cols, rstd_cols, 2).astype(jnp.bfloat16)


F32 = jnp.float32
BF16 = jnp.bfloat16
SUBLANES = 8
LEVELS = 4
CORES = 2


def dot(lhs, rhs, lhs_dim, rhs_dim):
    return lax.dot_general(
        lhs, rhs, (((lhs_dim,), (rhs_dim,)), ((), ())), preferred_element_type=F32
    )


def across(row, count):
    return jnp.transpose(jnp.broadcast_to(row, (count, row.shape[1])))


def exchange_bit(first, second, weight):
    sublane = lax.broadcasted_iota(jnp.int32, first.shape, 1)
    low = sublane & weight == 0
    return (
        jnp.where(low, first, pltpu.roll(second, weight, 1)),
        jnp.where(low, pltpu.roll(first, SUBLANES - weight, 1), second),
    )


def mesh_order(blocks):
    count, *rest = blocks.shape
    split = blocks.reshape(count // LEVELS // CORES, LEVELS, CORES, *rest)
    return jnp.swapaxes(split, 0, 1).reshape(blocks.shape)


def list_order(blocks):
    count, *rest = blocks.shape
    split = blocks.reshape(LEVELS, count // LEVELS // CORES, CORES, *rest)
    return jnp.swapaxes(split, 0, 1).reshape(blocks.shape)


def split_channels(blocks, own):
    devices, block, cols = blocks.shape
    tiles = blocks.reshape(devices // 2, 2, block // SUBLANES, SUBLANES, cols)
    parts = []
    for tile in range(block // SUBLANES):
        parts.extend(exchange_bit(tiles[:, 0, tile], tiles[:, 1, tile], own))
    return [part.reshape(devices * own, cols) for part in parts]


def merge_channels(parts, own):
    rows, cols = parts[0].shape
    devices = rows // own
    tiles = [part.reshape(devices // 2, SUBLANES, cols) for part in parts]
    pairs = [exchange_bit(*pair, own) for pair in zip(tiles[::2], tiles[1::2])]
    both = [jnp.concatenate(side, axis=1) for side in zip(*pairs)]
    block = len(parts) * own
    return jnp.stack(both, axis=1).reshape(devices, block, cols)


def trade(parts):
    rows, cols = parts[0].shape
    a, b, c, d = (part.reshape(rows // SUBLANES, SUBLANES, cols) for part in parts)
    (a, b), (c, d) = exchange_bit(a, b, 1), exchange_bit(c, d, 1)
    (a, c), (b, d) = exchange_bit(a, c, 2), exchange_bit(b, d, 2)
    return [part.reshape(rows, cols) for part in (a, b, c, d)]


def edges_kernel(me_ref, *refs):
    sources, (out_ref, *local), (blocks, arrived, left) = refs[:9], refs[9:19], refs[19:]
    copies = [
        pltpu.make_async_copy(source, target, arrived.at[index])
        for index, (source, target) in enumerate(zip(sources, local))
    ]
    for copy in copies:
        copy.start()
    act_ref, gain_ref, bias_ref, rows_ref, valid_ref, *weights = local
    own, cols, chan = act_ref.shape
    half = out_ref.shape[1] // 2
    for copy in copies[:3]:
        copy.wait()
    act = jnp.concatenate([jnp.transpose(act_ref[r].astype(F32)) for r in range(own)], axis=1)
    gain = across(gain_ref[...], cols)
    bias = across(bias_ref[...], cols)
    centre = act - jnp.mean(act, axis=0, keepdims=True)
    inverse = lax.rsqrt(jnp.mean(centre * centre, axis=0, keepdims=True) + EPSILON)
    wide_gain, wide_bias = (jnp.concatenate([value] * own, axis=1) for value in (gain, bias))
    pair_norm = (centre * inverse * wide_gain + wide_bias).astype(BF16)
    for copy in copies[3:]:
        copy.wait()
    valid = valid_ref[...].astype(F32)
    mask = jnp.concatenate(
        [valid * rows_ref[me_ref[0] * own + r].astype(F32) for r in range(own)], axis=1
    )
    sent = []
    for side in range(2):
        proj = dot(weights[2 * side][...], pair_norm, 0, 0)
        edge = mask * jax.nn.sigmoid(dot(weights[2 * side + 1][...], pair_norm, 0, 0)) * proj
        parts = trade([edge[:, r * cols : (r + 1) * cols] for r in range(own)])
        blocks[side] = merge_channels(parts, own).astype(BF16)
        copy = pltpu.make_async_copy(
            blocks.at[side], out_ref.at[:, side * half : (side + 1) * half, :], left.at[side]
        )
        copy.start()
        sent.append(copy)
    for copy in sent:
        copy.wait()


def gates_kernel(
    me_ref, rows_ref, valid_ref, act_ref, grad_ref, gain_ref, bias_ref, gain_out_ref, bias_out_ref,
    wap, wag, wbp, wbg, w_gate, w_out,
    factors, normed_t, rstd_t, gain_t, d_normed, slope, gain_out_t, bias_out_t,
):
    own, cols, _ = act_ref.shape
    hidden = wap.shape[1]
    valid = valid_ref[...].astype(F32)
    gain = across(gain_ref[...], cols)
    bias = across(bias_ref[...], cols)
    gain_out = across(gain_out_ref[...], cols)
    gain_t[...] = gain
    gain_out_t[...] = gain_out
    bias_out_t[...] = across(bias_out_ref[...], cols)
    for r in range(own):
        act = jnp.transpose(act_ref[r].astype(F32))
        centre = act - jnp.mean(act, axis=0, keepdims=True)
        inverse = lax.rsqrt(jnp.mean(centre * centre, axis=0, keepdims=True) + EPSILON)
        normed = centre * inverse
        lanes = pl.ds(r * cols, cols)
        normed_t[:, lanes] = normed
        rstd_t[:, lanes] = inverse
        pair_norm = (normed * gain + bias).astype(BF16)
        mask = valid * rows_ref[me_ref[0] * own + r].astype(F32)
        for side, (w_proj, w_sig) in enumerate(((wap, wag), (wbp, wbg))):
            proj = dot(w_proj[...], pair_norm, 0, 0)
            sig = jax.nn.sigmoid(dot(w_sig[...], pair_norm, 0, 0))
            kept = mask * sig
            factors[2 * side, :, lanes] = kept
            factors[2 * side + 1, :, lanes] = kept * proj * (1.0 - sig)
        gate_act = jax.nn.sigmoid(dot(w_gate[...], pair_norm, 0, 0))
        d_proj = jnp.transpose(grad_ref[r].astype(F32)) * gate_act
        slope[:, lanes] = d_proj * (1.0 - gate_act)
        d_normed[pl.ds(r, hidden, stride=own), :] = (
            dot(w_out[...], d_proj.astype(BF16), 1, 0) * gain_out
        )


def triangle_kernel(own, in_ref, _, out_ref, a_ref, b_ref):
    half = out_ref.shape[1]
    sides = [
        split_channels(
            mesh_order(in_ref[:, side * half : (side + 1) * half, :].astype(F32)), own
        )
        for side in range(2)
    ]
    tri = []
    for c, (edge_a, edge_b) in enumerate(zip(*sides)):
        a_ref[c] = edge_a.astype(BF16)
        b_ref[c] = edge_b.astype(BF16)
        tri.append(dot(a_ref[c], b_ref[c], 1, 1))
    out_ref[...] = list_order(merge_channels(tri, own)).astype(BF16)


def fold(values, own):
    total = jnp.sum(values, axis=0)
    rows = total
    for shift in range(own, SUBLANES, own):
        rows = rows + pltpu.roll(total, shift, 0)
    return rows[None]


def tri_normed(tri_ref, hidden, own):
    cols = tri_ref.shape[-1]
    tri = tri_ref[...].astype(F32).reshape(hidden * own // SUBLANES, SUBLANES, cols)
    centre = tri - fold(tri, own) / hidden
    inverse = lax.rsqrt(fold(centre * centre, own) / hidden + EPSILON)
    return centre * inverse, inverse


def norm_kernel(own, tri_ref, grad_ref, slope, gain, bias, w_out, out_ref, gate_ref):
    devices, block, cols = tri_ref.shape
    hidden = w_out.shape[0]
    normed, inverse = tri_normed(tri_ref, hidden, own)
    grad = grad_ref[...].reshape(normed.shape)
    mean_grad = fold(grad, own) / hidden
    mean_proj = fold(grad * normed, own) / hidden
    d_tri = inverse * (grad - mean_grad - normed * mean_proj)
    out_ref[...] = d_tri.reshape(devices, block, cols).astype(BF16)
    parts = trade(split_channels(normed.reshape(devices, block, cols), own))
    tri_norm = jnp.concatenate([(part * gain[...] + bias[...]).astype(BF16) for part in parts], axis=1)
    gate_ref[...] = (slope[...] * dot(w_out[...], tri_norm, 0, 0)).astype(BF16)


def edge_grad_kernel(own, in_ref, a_ref, b_ref, out_ref):
    block = in_ref.shape[1]
    grads = ([], [])
    for c, part in enumerate(split_channels(mesh_order(in_ref[...].astype(F32)), own)):
        d_tri = part.astype(BF16)
        grads[0].append(dot(d_tri, b_ref[c], 1, 0))
        grads[1].append(dot(d_tri, a_ref[c], 0, 0))
    for side in range(2):
        out_ref[:, side * block : (side + 1) * block, :] = (
            list_order(merge_channels(grads[side], own)).astype(BF16)
        )


def input_grad_kernel(
    in_ref, factors, normed_t, rstd_t, gain_t, d_gate, wap, wag, wbp, wbg, w_gate, out_ref
):
    own, cols, _ = out_ref.shape
    half = in_ref.shape[1] // 2
    grads = []
    for side in range(2):
        blocks = in_ref[:, side * half : (side + 1) * half, :].astype(F32)
        d_edge = jnp.concatenate(trade(split_channels(blocks, own)), axis=1)
        for at in range(2):
            grads.append((d_edge * factors[2 * side + at]).astype(BF16))
    weights = [weight[...] for weight in (wap, wag, wbp, wbg, w_gate)]
    grads.append(d_gate[...])
    total = dot(jnp.concatenate(weights, axis=1), jnp.concatenate(grads, axis=0), 1, 0)
    grad_hat = total * jnp.concatenate([gain_t[...]] * own, axis=1)
    normed = normed_t[...]
    mean_grad = jnp.mean(grad_hat, axis=0, keepdims=True)
    mean_proj = jnp.mean(grad_hat * normed, axis=0, keepdims=True)
    grad = rstd_t[...] * (grad_hat - mean_grad - normed * mean_proj)
    for r in range(own):
        out_ref[r] = jnp.transpose(grad[:, r * cols : (r + 1) * cols]).astype(BF16)


VMEM = pl.BlockSpec(memory_space=pltpu.VMEM)
SMEM = pl.BlockSpec(memory_space=pltpu.SMEM)
HBM = pl.BlockSpec(memory_space=pltpu.HBM)


def call(kernel, name, outs, args, scratch=(), scalars=0, flops=0, spaces=None, to=VMEM, limit=32 * 2**20):
    shapes = [jax.ShapeDtypeStruct(shape, dtype) for shape, dtype in outs]
    moved = sum(value.size * value.dtype.itemsize for value in list(args) + shapes)
    result = pl.pallas_call(
        kernel,
        name=name,
        out_shape=shapes,
        in_specs=[SMEM] * scalars + (spaces or [VMEM] * (len(args) - scalars)),
        out_specs=[to] * len(outs),
        scratch_shapes=scratch,
        cost_estimate=pl.CostEstimate(flops=flops, bytes_accessed=moved, transcendentals=0),
        compiler_params=pltpu.CompilerParams(vmem_limit_bytes=limit),
    )(*args)
    return result[0] if len(outs) == 1 else result


def kernel_shards(
    dap,
    pair_act,
    out_grad,
    residue_mask,
    ln_in_gain,
    ln_in_bias,
    w_a_proj,
    w_a_gate,
    w_b_proj,
    w_b_gate,
    w_gate,
    ln_out_gain,
    ln_out_bias,
    w_out,
):
    own, cols, chan = pair_act.shape
    hidden = w_a_proj.shape[1]
    slice_h = hidden // dap
    rows = dap * own
    block = slice_h * own
    me = lax.axis_index("dap").reshape(1)
    valid = residue_mask.reshape(1, -1)
    gain_in, bias_in, gain_out, bias_out = (
        value.reshape(1, -1) for value in (ln_in_gain, ln_in_bias, ln_out_gain, ln_out_bias)
    )
    w_edges = (w_a_proj, w_a_gate, w_b_proj, w_b_gate)
    product = 2 * own * cols * chan * hidden

    span = dap // LEVELS
    listed = [
        quarter * span + pair * CORES + core
        for pair in range(span // CORES)
        for quarter in range(LEVELS)
        for core in range(CORES)
    ]

    def exchange(value):
        return lax.all_to_all(
            value, "dap", split_axis=0, concat_axis=0, axis_index_groups=[listed], tiled=True
        )

    first = (pair_act, gain_in, bias_in, residue_mask, valid, *w_edges)
    edges = call(
        edges_kernel,
        "edges",
        [((dap, 2 * block, cols), BF16)],
        (me, *first),
        scratch=[
            (pltpu.SMEM if value is residue_mask else pltpu.VMEM)(value.shape, value.dtype)
            for value in first
        ]
        + [pltpu.VMEM((2, dap, block, cols), BF16)]
        + [pltpu.SemaphoreType.DMA((len(first),)), pltpu.SemaphoreType.DMA((2,))],
        scalars=1,
        flops=4 * product,
        to=HBM,
        spaces=[HBM] * len(first),
        limit=None,
    )
    edges = exchange(edges)
    factors, normed_t, rstd_t, gain_t, d_normed, slope, gain_out_t, bias_out_t = call(
        gates_kernel,
        "gates",
        [
            ((4, hidden, own * cols), F32),
            ((chan, own * cols), F32),
            ((1, own * cols), F32),
            ((chan, cols), F32),
            ((hidden * own, cols), F32),
            ((chan, own * cols), F32),
            ((hidden, cols), F32),
            ((hidden, cols), F32),
        ],
        (me, residue_mask, valid, pair_act, out_grad, gain_in, bias_in, gain_out)
        + (bias_out, *w_edges, w_gate, w_out),
        scalars=2,
        flops=6 * product,
    )
    tri, edge_a, edge_b = call(
        functools.partial(triangle_kernel, own),
        "triangle",
        [
            ((dap, block, cols), BF16),
            ((slice_h, rows, cols), BF16),
            ((slice_h, rows, cols), BF16),
        ],
        (edges, d_normed),
        flops=product,
        spaces=[VMEM, pl.BlockSpec(memory_space=pl.ANY)],
    )
    tri = exchange(tri)
    d_tri, d_gate = call(
        functools.partial(norm_kernel, own),
        "norm",
        [((dap, block, cols), BF16), ((chan, own * cols), BF16)],
        (tri, d_normed, slope, gain_out_t, bias_out_t, w_out),
        flops=2 * product,
    )
    d_tri = exchange(d_tri)
    d_edges = call(
        functools.partial(edge_grad_kernel, own),
        "edge_grad",
        [((dap, 2 * block, cols), BF16)],
        (d_tri, edge_a, edge_b),
        flops=2 * product,
    )
    d_edges = exchange(d_edges)
    return call(
        input_grad_kernel,
        "input_grad",
        [((own, cols, chan), BF16)],
        (d_edges, factors, normed_t, rstd_t, gain_t, d_gate, *w_edges, w_gate),
        flops=4 * product,
    )


def fits_kernels(dap, ch, pair_act, w_proj):
    own, cols, chan = pair_act.shape
    hidden = w_proj.shape[1]
    block = hidden // dap * own
    return (
        ch == 1
        and hidden % dap == 0
        and own == SUBLANES // 2
        and block == own * own
        and dap % SUBLANES == 0
        and cols == dap * own
        and cols % 128 == chan % 128 == hidden % 128 == 0
    )


def solution(mesh):
    sizes = dict(mesh.shape)

    def program(*args):
        dap, ch = sizes["dap"], sizes["ch"]
        if fits_kernels(dap, ch, args[0], args[5]):
            return kernel_shards(dap, *args)
        return channel_shards(dap, ch, *args)

    in_specs = (
        P(("grp", "dap"), None, None),
        P(("grp", "dap"), "ch", None),
        P("grp"),
        P(),
        P(),
        P(None, "ch"),
        P(None, "ch"),
        P(None, "ch"),
        P(None, "ch"),
        P(),
        P(),
        P(),
        P(),
    )
    out_specs = P(("grp", "dap"), "ch", None)
    return jax.shard_map(
        program, mesh=mesh, in_specs=in_specs, out_specs=out_specs, check_vma=False
    )
```

```python
import functools

import jax
import jax.numpy as jnp
from jax import lax
from jax.experimental import pallas as pl
from jax.experimental.pallas import tpu as pltpu
from jax.sharding import PartitionSpec as P

EPSILON = 1e-05


def normalise(values, reduce_dim):
    centre = values - jnp.mean(values, axis=reduce_dim, keepdims=True)
    inverse = lax.rsqrt(jnp.mean(centre * centre, axis=reduce_dim, keepdims=True) + EPSILON)
    return (centre * inverse, inverse)


def norm_backward(grad_hat, normed, inverse, reduce_dim):
    mean_grad = jnp.mean(grad_hat, axis=reduce_dim, keepdims=True)
    mean_proj = jnp.mean(grad_hat * normed, axis=reduce_dim, keepdims=True)
    return inverse * (grad_hat - mean_grad - normed * mean_proj)


def channel_shards(
    dap,
    ch,
    pair_act,
    out_grad,
    residue_mask,
    ln_in_gain,
    ln_in_bias,
    w_a_proj,
    w_a_gate,
    w_b_proj,
    w_b_gate,
    w_gate,
    ln_out_gain,
    ln_out_bias,
    w_out,
):
    own_rows, all_cols = pair_act.shape[:2]
    col_span = out_grad.shape[1]
    hidden_local = w_a_proj.shape[1]
    slice_h = hidden_local // dap
    row_first = lax.axis_index("dap") * own_rows
    col_first = lax.axis_index("ch") * col_span
    normed_in, rstd_in = normalise(pair_act.astype(jnp.float32), 2)
    pair_norm = (normed_in * ln_in_gain + ln_in_bias).astype(jnp.bfloat16)
    valid_all = residue_mask.astype(jnp.float32)
    valid_rows = lax.dynamic_slice_in_dim(valid_all, row_first, own_rows)
    row_mask = (valid_rows[:, None] * valid_all[None, :])[None]
    w_four = jnp.concatenate((w_a_proj, w_a_gate, w_b_proj, w_b_gate), axis=1)
    projected = jnp.einsum("ikc,cg->gik", pair_norm, w_four, preferred_element_type=jnp.float32)
    a_proj = projected[:hidden_local]
    a_sig = jax.nn.sigmoid(projected[hidden_local : 2 * hidden_local])
    b_proj = projected[2 * hidden_local : 3 * hidden_local]
    b_sig = jax.nn.sigmoid(projected[3 * hidden_local :])
    edge_a = (row_mask * a_sig * a_proj).astype(jnp.bfloat16)
    edge_b = (row_mask * b_sig * b_proj).astype(jnp.bfloat16)

    split = (dap, slice_h, own_rows, all_cols)
    edges = jnp.stack((edge_a.reshape(split), edge_b.reshape(split)), axis=1)
    edges = lax.all_to_all(edges, "dap", split_axis=0, concat_axis=0, tiled=True)
    edges = jnp.transpose(edges, (1, 2, 0, 3, 4)).reshape(2, slice_h, dap * own_rows, all_cols)
    a_all, b_all = edges[0], edges[1]
    tri = jnp.einsum("hik,hjk->hij", a_all, b_all, preferred_element_type=jnp.float32).astype(
        jnp.bfloat16
    )
    tri = tri.reshape(slice_h, dap, own_rows, ch, col_span)
    tri = jnp.transpose(tri, (1, 3, 0, 2, 4)).reshape(dap * ch, slice_h, own_rows, col_span)
    tri = lax.all_to_all(tri, ("dap", "ch"), split_axis=0, concat_axis=0, tiled=True)
    tri = tri.reshape(dap, ch, slice_h, own_rows, col_span)
    tri_full = jnp.transpose(tri, (1, 0, 2, 3, 4)).reshape(-1, own_rows, col_span)

    normed_out, rstd_out = normalise(tri_full.astype(jnp.float32), 0)
    gain_out = ln_out_gain.reshape(-1, 1, 1)
    bias_out = ln_out_bias.reshape(-1, 1, 1)
    tri_norm = (normed_out * gain_out + bias_out).astype(jnp.bfloat16)
    proj_out = jnp.einsum("hij,hc->ijc", tri_norm, w_out, preferred_element_type=jnp.float32)
    norm_cols = lax.dynamic_slice_in_dim(pair_norm, col_first, col_span, 1)
    gate_act = jax.nn.sigmoid(
        jnp.einsum("ijc,cd->ijd", norm_cols, w_gate, preferred_element_type=jnp.float32)
    )
    upstream = out_grad.astype(jnp.float32)
    d_proj = (upstream * gate_act).astype(jnp.bfloat16)
    d_gate = (upstream * proj_out * gate_act * (1.0 - gate_act)).astype(jnp.bfloat16)
    d_normed = (
        jnp.einsum("ijc,hc->hij", d_proj, w_out, preferred_element_type=jnp.float32) * gain_out
    )
    d_tri = norm_backward(d_normed, normed_out, rstd_out, 0).astype(jnp.bfloat16)

    d_tri = d_tri.reshape(ch, dap, slice_h, own_rows, col_span)
    d_tri = jnp.transpose(d_tri, (1, 0, 2, 3, 4)).reshape(dap * ch, slice_h, own_rows, col_span)
    d_tri = lax.all_to_all(d_tri, ("dap", "ch"), split_axis=0, concat_axis=0, tiled=True)
    d_tri = d_tri.reshape(dap, ch, slice_h, own_rows, col_span)
    d_tri = jnp.transpose(d_tri, (2, 0, 3, 1, 4)).reshape(slice_h, dap * own_rows, all_cols)
    d_edge_a = jnp.einsum("hij,hjk->hik", d_tri, b_all, preferred_element_type=jnp.float32)
    d_edge_b = jnp.einsum("hij,hik->hjk", d_tri, a_all, preferred_element_type=jnp.float32)
    d_edges = jnp.stack((d_edge_a, d_edge_b)).astype(jnp.bfloat16)
    d_edges = d_edges.reshape(2, slice_h, dap, own_rows, all_cols)
    d_edges = jnp.transpose(d_edges, (2, 0, 1, 3, 4))
    d_edges = lax.all_to_all(d_edges, "dap", split_axis=0, concat_axis=0, tiled=True)
    d_edges = jnp.transpose(d_edges, (1, 0, 2, 3, 4)).reshape(2, hidden_local, own_rows, all_cols)

    def split_grad(d_edge, sig_val, proj_val):
        masked = d_edge * row_mask
        return (
            (masked * sig_val).astype(jnp.bfloat16),
            (masked * proj_val * sig_val * (1.0 - sig_val)).astype(jnp.bfloat16),
        )

    d_four = jnp.concatenate(
        split_grad(d_edges[0].astype(jnp.float32), a_sig, a_proj)
        + split_grad(d_edges[1].astype(jnp.float32), b_sig, b_proj),
        axis=0,
    )
    d_hidden = jnp.einsum("gik,cg->ikc", d_four, w_four, preferred_element_type=jnp.float32)
    if ch > 1:
        d_hidden = lax.psum_scatter(
            d_hidden.astype(jnp.bfloat16), "ch", scatter_dimension=1, tiled=True
        ).astype(jnp.float32)
    d_pair_norm = d_hidden + jnp.einsum(
        "ijd,cd->ijc", d_gate, w_gate, preferred_element_type=jnp.float32
    )
    normed_cols = lax.dynamic_slice_in_dim(normed_in, col_first, col_span, 1)
    rstd_cols = lax.dynamic_slice_in_dim(rstd_in, col_first, col_span, 1)
    grad_hat = d_pair_norm * ln_in_gain
    return norm_backward(grad_hat, normed_cols, rstd_cols, 2).astype(jnp.bfloat16)


F32 = jnp.float32
BF16 = jnp.bfloat16
SUBLANES = 8
LEVELS = 4
CORES = 2


def dot(lhs, rhs, lhs_dim, rhs_dim):
    return lax.dot_general(
        lhs, rhs, (((lhs_dim,), (rhs_dim,)), ((), ())), preferred_element_type=F32
    )


def across(row, count):
    return jnp.transpose(jnp.broadcast_to(row, (count, row.shape[1])))


def exchange_bit(first, second, weight):
    sublane = lax.broadcasted_iota(jnp.int32, first.shape, 1)
    low = sublane & weight == 0
    return (
        jnp.where(low, first, pltpu.roll(second, weight, 1)),
        jnp.where(low, pltpu.roll(first, SUBLANES - weight, 1), second),
    )


def falling(blocks):
    return jnp.concatenate([blocks[at : at + 1] for at in reversed(range(LEVELS))], axis=0)


def mesh_order(blocks):
    count, *rest = blocks.shape
    split = blocks.reshape(count // LEVELS // CORES, LEVELS, CORES, *rest)
    return falling(jnp.swapaxes(split, 0, 1)).reshape(blocks.shape)


def list_order(blocks):
    count, *rest = blocks.shape
    split = blocks.reshape(LEVELS, count // LEVELS // CORES, CORES, *rest)
    return jnp.swapaxes(falling(split), 0, 1).reshape(blocks.shape)


def split_channels(blocks, own):
    devices, block, cols = blocks.shape
    tiles = blocks.reshape(devices // 2, 2, block // SUBLANES, SUBLANES, cols)
    parts = []
    for tile in range(block // SUBLANES):
        parts.extend(exchange_bit(tiles[:, 0, tile], tiles[:, 1, tile], own))
    return [part.reshape(devices * own, cols) for part in parts]


def merge_channels(parts, own):
    rows, cols = parts[0].shape
    devices = rows // own
    tiles = [part.reshape(devices // 2, SUBLANES, cols) for part in parts]
    pairs = [exchange_bit(*pair, own) for pair in zip(tiles[::2], tiles[1::2])]
    both = [jnp.concatenate(side, axis=1) for side in zip(*pairs)]
    block = len(parts) * own
    return jnp.stack(both, axis=1).reshape(devices, block, cols)


def trade(parts):
    rows, cols = parts[0].shape
    a, b, c, d = (part.reshape(rows // SUBLANES, SUBLANES, cols) for part in parts)
    (a, b), (c, d) = exchange_bit(a, b, 1), exchange_bit(c, d, 1)
    (a, c), (b, d) = exchange_bit(a, c, 2), exchange_bit(b, d, 2)
    return [part.reshape(rows, cols) for part in (a, b, c, d)]


def edges_kernel(me_ref, *refs):
    sources, (out_ref, *local), (blocks, arrived, left) = refs[:9], refs[9:19], refs[19:]
    copies = [
        pltpu.make_async_copy(source, target, arrived.at[index])
        for index, (source, target) in enumerate(zip(sources, local))
    ]
    for copy in copies:
        copy.start()
    act_ref, gain_ref, bias_ref, rows_ref, valid_ref, *weights = local
    own, cols, chan = act_ref.shape
    half = out_ref.shape[1] // 2
    for copy in copies[:3]:
        copy.wait()
    act = jnp.concatenate([jnp.transpose(act_ref[r].astype(F32)) for r in range(own)], axis=1)
    gain = across(gain_ref[...], cols)
    bias = across(bias_ref[...], cols)
    centre = act - jnp.mean(act, axis=0, keepdims=True)
    inverse = lax.rsqrt(jnp.mean(centre * centre, axis=0, keepdims=True) + EPSILON)
    wide_gain, wide_bias = (jnp.concatenate([value] * own, axis=1) for value in (gain, bias))
    pair_norm = (centre * inverse * wide_gain + wide_bias).astype(BF16)
    for copy in copies[3:]:
        copy.wait()
    valid = valid_ref[...].astype(F32)
    mask = jnp.concatenate(
        [valid * rows_ref[me_ref[0] * own + r].astype(F32) for r in range(own)], axis=1
    )
    sent = []
    for side in range(2):
        proj = dot(weights[2 * side][...], pair_norm, 0, 0)
        edge = mask * jax.nn.sigmoid(dot(weights[2 * side + 1][...], pair_norm, 0, 0)) * proj
        parts = trade([edge[:, r * cols : (r + 1) * cols] for r in range(own)])
        blocks[side] = merge_channels(parts, own).astype(BF16)
        copy = pltpu.make_async_copy(
            blocks.at[side], out_ref.at[:, side * half : (side + 1) * half, :], left.at[side]
        )
        copy.start()
        sent.append(copy)
    for copy in sent:
        copy.wait()


def gates_kernel(
    me_ref, rows_ref, valid_ref, act_ref, grad_ref, gain_ref, bias_ref, gain_out_ref, bias_out_ref,
    wap, wag, wbp, wbg, w_gate, w_out,
    factors, normed_t, rstd_t, gain_t, d_normed, slope, gain_out_t, bias_out_t,
):
    own, cols, _ = act_ref.shape
    hidden = wap.shape[1]
    valid = valid_ref[...].astype(F32)
    gain = across(gain_ref[...], cols)
    bias = across(bias_ref[...], cols)
    gain_out = across(gain_out_ref[...], cols)
    gain_t[...] = gain
    gain_out_t[...] = gain_out
    bias_out_t[...] = across(bias_out_ref[...], cols)
    for r in range(own):
        act = jnp.transpose(act_ref[r].astype(F32))
        centre = act - jnp.mean(act, axis=0, keepdims=True)
        inverse = lax.rsqrt(jnp.mean(centre * centre, axis=0, keepdims=True) + EPSILON)
        normed = centre * inverse
        lanes = pl.ds(r * cols, cols)
        normed_t[:, lanes] = normed
        rstd_t[:, lanes] = inverse
        pair_norm = (normed * gain + bias).astype(BF16)
        mask = valid * rows_ref[me_ref[0] * own + r].astype(F32)
        for side, (w_proj, w_sig) in enumerate(((wap, wag), (wbp, wbg))):
            proj = dot(w_proj[...], pair_norm, 0, 0)
            sig = jax.nn.sigmoid(dot(w_sig[...], pair_norm, 0, 0))
            kept = mask * sig
            factors[2 * side, :, lanes] = kept
            factors[2 * side + 1, :, lanes] = kept * proj * (1.0 - sig)
        gate_act = jax.nn.sigmoid(dot(w_gate[...], pair_norm, 0, 0))
        d_proj = jnp.transpose(grad_ref[r].astype(F32)) * gate_act
        slope[:, lanes] = d_proj * (1.0 - gate_act)
        d_normed[pl.ds(r, hidden, stride=own), :] = (
            dot(w_out[...], d_proj.astype(BF16), 1, 0) * gain_out
        )


def triangle_kernel(own, in_ref, _, out_ref, a_ref, b_ref):
    half = out_ref.shape[1]
    sides = [
        split_channels(
            mesh_order(in_ref[:, side * half : (side + 1) * half, :].astype(F32)), own
        )
        for side in range(2)
    ]
    tri = []
    for c, (edge_a, edge_b) in enumerate(zip(*sides)):
        a_ref[c] = edge_a.astype(BF16)
        b_ref[c] = edge_b.astype(BF16)
        tri.append(dot(a_ref[c], b_ref[c], 1, 1))
    out_ref[...] = list_order(merge_channels(tri, own)).astype(BF16)


def fold(values, own):
    total = jnp.sum(values, axis=0)
    rows = total
    for shift in range(own, SUBLANES, own):
        rows = rows + pltpu.roll(total, shift, 0)
    return rows[None]


def tri_normed(tri_ref, hidden, own):
    cols = tri_ref.shape[-1]
    tri = tri_ref[...].astype(F32).reshape(hidden * own // SUBLANES, SUBLANES, cols)
    centre = tri - fold(tri, own) / hidden
    inverse = lax.rsqrt(fold(centre * centre, own) / hidden + EPSILON)
    return centre * inverse, inverse


def norm_kernel(own, tri_ref, grad_ref, slope, gain, bias, w_out, out_ref, gate_ref):
    devices, block, cols = tri_ref.shape
    hidden = w_out.shape[0]
    normed, inverse = tri_normed(tri_ref, hidden, own)
    grad = grad_ref[...].reshape(normed.shape)
    mean_grad = fold(grad, own) / hidden
    mean_proj = fold(grad * normed, own) / hidden
    d_tri = inverse * (grad - mean_grad - normed * mean_proj)
    out_ref[...] = d_tri.reshape(devices, block, cols).astype(BF16)
    parts = trade(split_channels(normed.reshape(devices, block, cols), own))
    tri_norm = jnp.concatenate([(part * gain[...] + bias[...]).astype(BF16) for part in parts], axis=1)
    gate_ref[...] = (slope[...] * dot(w_out[...], tri_norm, 0, 0)).astype(BF16)


def edge_grad_kernel(own, in_ref, a_ref, b_ref, out_ref):
    block = in_ref.shape[1]
    grads = ([], [])
    for c, part in enumerate(split_channels(mesh_order(in_ref[...].astype(F32)), own)):
        d_tri = part.astype(BF16)
        grads[0].append(dot(d_tri, b_ref[c], 1, 0))
        grads[1].append(dot(d_tri, a_ref[c], 0, 0))
    for side in range(2):
        out_ref[:, side * block : (side + 1) * block, :] = (
            list_order(merge_channels(grads[side], own)).astype(BF16)
        )


def input_grad_kernel(
    in_ref, factors, normed_t, rstd_t, gain_t, d_gate, wap, wag, wbp, wbg, w_gate, out_ref
):
    own, cols, _ = out_ref.shape
    half = in_ref.shape[1] // 2
    grads = []
    for side in range(2):
        blocks = in_ref[:, side * half : (side + 1) * half, :].astype(F32)
        d_edge = jnp.concatenate(trade(split_channels(blocks, own)), axis=1)
        for at in range(2):
            grads.append((d_edge * factors[2 * side + at]).astype(BF16))
    weights = [weight[...] for weight in (wap, wag, wbp, wbg, w_gate)]
    grads.append(d_gate[...])
    total = dot(jnp.concatenate(weights, axis=1), jnp.concatenate(grads, axis=0), 1, 0)
    grad_hat = total * jnp.concatenate([gain_t[...]] * own, axis=1)
    normed = normed_t[...]
    mean_grad = jnp.mean(grad_hat, axis=0, keepdims=True)
    mean_proj = jnp.mean(grad_hat * normed, axis=0, keepdims=True)
    grad = rstd_t[...] * (grad_hat - mean_grad - normed * mean_proj)
    for r in range(own):
        out_ref[r] = jnp.transpose(grad[:, r * cols : (r + 1) * cols]).astype(BF16)


VMEM = pl.BlockSpec(memory_space=pltpu.VMEM)
SMEM = pl.BlockSpec(memory_space=pltpu.SMEM)
HBM = pl.BlockSpec(memory_space=pltpu.HBM)


def call(kernel, name, outs, args, scratch=(), scalars=0, flops=0, spaces=None, to=VMEM, limit=32 * 2**20):
    shapes = [jax.ShapeDtypeStruct(shape, dtype) for shape, dtype in outs]
    moved = sum(value.size * value.dtype.itemsize for value in list(args) + shapes)
    result = pl.pallas_call(
        kernel,
        name=name,
        out_shape=shapes,
        in_specs=[SMEM] * scalars + (spaces or [VMEM] * (len(args) - scalars)),
        out_specs=[to] * len(outs),
        scratch_shapes=scratch,
        cost_estimate=pl.CostEstimate(flops=flops, bytes_accessed=moved, transcendentals=0),
        compiler_params=pltpu.CompilerParams(vmem_limit_bytes=limit),
    )(*args)
    return result[0] if len(outs) == 1 else result


def kernel_shards(
    dap,
    pair_act,
    out_grad,
    residue_mask,
    ln_in_gain,
    ln_in_bias,
    w_a_proj,
    w_a_gate,
    w_b_proj,
    w_b_gate,
    w_gate,
    ln_out_gain,
    ln_out_bias,
    w_out,
):
    own, cols, chan = pair_act.shape
    hidden = w_a_proj.shape[1]
    slice_h = hidden // dap
    rows = dap * own
    block = slice_h * own
    me = lax.axis_index("dap").reshape(1)
    valid = residue_mask.reshape(1, -1)
    gain_in, bias_in, gain_out, bias_out = (
        value.reshape(1, -1) for value in (ln_in_gain, ln_in_bias, ln_out_gain, ln_out_bias)
    )
    w_edges = (w_a_proj, w_a_gate, w_b_proj, w_b_gate)
    product = 2 * own * cols * chan * hidden

    span = dap // LEVELS
    listed = [
        quarter * span + pair * CORES + core
        for pair in range(span // CORES)
        for quarter in reversed(range(LEVELS))
        for core in range(CORES)
    ]

    def exchange(value):
        return lax.all_to_all(
            value, "dap", split_axis=0, concat_axis=0, axis_index_groups=[listed], tiled=True
        )

    first = (pair_act, gain_in, bias_in, residue_mask, valid, *w_edges)
    edges = call(
        edges_kernel,
        "edges",
        [((dap, 2 * block, cols), BF16)],
        (me, *first),
        scratch=[
            (pltpu.SMEM if value is residue_mask else pltpu.VMEM)(value.shape, value.dtype)
            for value in first
        ]
        + [pltpu.VMEM((2, dap, block, cols), BF16)]
        + [pltpu.SemaphoreType.DMA((len(first),)), pltpu.SemaphoreType.DMA((2,))],
        scalars=1,
        flops=4 * product,
        to=HBM,
        spaces=[HBM] * len(first),
        limit=None,
    )
    edges = exchange(edges)
    factors, normed_t, rstd_t, gain_t, d_normed, slope, gain_out_t, bias_out_t = call(
        gates_kernel,
        "gates",
        [
            ((4, hidden, own * cols), F32),
            ((chan, own * cols), F32),
            ((1, own * cols), F32),
            ((chan, cols), F32),
            ((hidden * own, cols), F32),
            ((chan, own * cols), F32),
            ((hidden, cols), F32),
            ((hidden, cols), F32),
        ],
        (me, residue_mask, valid, pair_act, out_grad, gain_in, bias_in, gain_out)
        + (bias_out, *w_edges, w_gate, w_out),
        scalars=2,
        flops=6 * product,
    )
    tri, edge_a, edge_b = call(
        functools.partial(triangle_kernel, own),
        "triangle",
        [
            ((dap, block, cols), BF16),
            ((slice_h, rows, cols), BF16),
            ((slice_h, rows, cols), BF16),
        ],
        (edges, d_normed),
        flops=product,
        spaces=[VMEM, pl.BlockSpec(memory_space=pl.ANY)],
    )
    tri = exchange(tri)
    d_tri, d_gate = call(
        functools.partial(norm_kernel, own),
        "norm",
        [((dap, block, cols), BF16), ((chan, own * cols), BF16)],
        (tri, d_normed, slope, gain_out_t, bias_out_t, w_out),
        flops=2 * product,
    )
    d_tri = exchange(d_tri)
    d_edges = call(
        functools.partial(edge_grad_kernel, own),
        "edge_grad",
        [((dap, 2 * block, cols), BF16)],
        (d_tri, edge_a, edge_b),
        flops=2 * product,
    )
    d_edges = exchange(d_edges)
    return call(
        input_grad_kernel,
        "input_grad",
        [((own, cols, chan), BF16)],
        (d_edges, factors, normed_t, rstd_t, gain_t, d_gate, *w_edges, w_gate),
        flops=4 * product,
    )


def fits_kernels(dap, ch, pair_act, w_proj):
    own, cols, chan = pair_act.shape
    hidden = w_proj.shape[1]
    block = hidden // dap * own
    return (
        ch == 1
        and hidden % dap == 0
        and own == SUBLANES // 2
        and block == own * own
        and dap % SUBLANES == 0
        and cols == dap * own
        and cols % 128 == chan % 128 == hidden % 128 == 0
    )


def solution(mesh):
    sizes = dict(mesh.shape)

    def program(*args):
        dap, ch = sizes["dap"], sizes["ch"]
        if fits_kernels(dap, ch, args[0], args[5]):
            return kernel_shards(dap, *args)
        return channel_shards(dap, ch, *args)

    in_specs = (
        P(("grp", "dap"), None, None),
        P(("grp", "dap"), "ch", None),
        P("grp"),
        P(),
        P(),
        P(None, "ch"),
        P(None, "ch"),
        P(None, "ch"),
        P(None, "ch"),
        P(),
        P(),
        P(),
        P(),
    )
    out_specs = P(("grp", "dap"), "ch", None)
    return jax.shard_map(
        program, mesh=mesh, in_specs=in_specs, out_specs=out_specs, check_vma=False
    )
```

```python
import functools

import jax
import jax.numpy as jnp
from jax import lax
from jax.experimental import pallas as pl
from jax.experimental.pallas import tpu as pltpu
from jax.sharding import PartitionSpec as P

EPSILON = 1e-05


def normalise(values, reduce_dim):
    centre = values - jnp.mean(values, axis=reduce_dim, keepdims=True)
    inverse = lax.rsqrt(jnp.mean(centre * centre, axis=reduce_dim, keepdims=True) + EPSILON)
    return (centre * inverse, inverse)


def norm_backward(grad_hat, normed, inverse, reduce_dim):
    mean_grad = jnp.mean(grad_hat, axis=reduce_dim, keepdims=True)
    mean_proj = jnp.mean(grad_hat * normed, axis=reduce_dim, keepdims=True)
    return inverse * (grad_hat - mean_grad - normed * mean_proj)


def channel_shards(
    dap,
    ch,
    pair_act,
    out_grad,
    residue_mask,
    ln_in_gain,
    ln_in_bias,
    w_a_proj,
    w_a_gate,
    w_b_proj,
    w_b_gate,
    w_gate,
    ln_out_gain,
    ln_out_bias,
    w_out,
):
    own_rows, all_cols = pair_act.shape[:2]
    col_span = out_grad.shape[1]
    hidden_local = w_a_proj.shape[1]
    slice_h = hidden_local // dap
    row_first = lax.axis_index("dap") * own_rows
    col_first = lax.axis_index("ch") * col_span
    normed_in, rstd_in = normalise(pair_act.astype(jnp.float32), 2)
    pair_norm = (normed_in * ln_in_gain + ln_in_bias).astype(jnp.bfloat16)
    valid_all = residue_mask.astype(jnp.float32)
    valid_rows = lax.dynamic_slice_in_dim(valid_all, row_first, own_rows)
    row_mask = (valid_rows[:, None] * valid_all[None, :])[None]
    w_four = jnp.concatenate((w_a_proj, w_a_gate, w_b_proj, w_b_gate), axis=1)
    projected = jnp.einsum("ikc,cg->gik", pair_norm, w_four, preferred_element_type=jnp.float32)
    a_proj = projected[:hidden_local]
    a_sig = jax.nn.sigmoid(projected[hidden_local : 2 * hidden_local])
    b_proj = projected[2 * hidden_local : 3 * hidden_local]
    b_sig = jax.nn.sigmoid(projected[3 * hidden_local :])
    edge_a = (row_mask * a_sig * a_proj).astype(jnp.bfloat16)
    edge_b = (row_mask * b_sig * b_proj).astype(jnp.bfloat16)

    split = (dap, slice_h, own_rows, all_cols)
    edges = jnp.stack((edge_a.reshape(split), edge_b.reshape(split)), axis=1)
    edges = lax.all_to_all(edges, "dap", split_axis=0, concat_axis=0, tiled=True)
    edges = jnp.transpose(edges, (1, 2, 0, 3, 4)).reshape(2, slice_h, dap * own_rows, all_cols)
    a_all, b_all = edges[0], edges[1]
    tri = jnp.einsum("hik,hjk->hij", a_all, b_all, preferred_element_type=jnp.float32).astype(
        jnp.bfloat16
    )
    tri = tri.reshape(slice_h, dap, own_rows, ch, col_span)
    tri = jnp.transpose(tri, (1, 3, 0, 2, 4)).reshape(dap * ch, slice_h, own_rows, col_span)
    tri = lax.all_to_all(tri, ("dap", "ch"), split_axis=0, concat_axis=0, tiled=True)
    tri = tri.reshape(dap, ch, slice_h, own_rows, col_span)
    tri_full = jnp.transpose(tri, (1, 0, 2, 3, 4)).reshape(-1, own_rows, col_span)

    normed_out, rstd_out = normalise(tri_full.astype(jnp.float32), 0)
    gain_out = ln_out_gain.reshape(-1, 1, 1)
    bias_out = ln_out_bias.reshape(-1, 1, 1)
    tri_norm = (normed_out * gain_out + bias_out).astype(jnp.bfloat16)
    proj_out = jnp.einsum("hij,hc->ijc", tri_norm, w_out, preferred_element_type=jnp.float32)
    norm_cols = lax.dynamic_slice_in_dim(pair_norm, col_first, col_span, 1)
    gate_act = jax.nn.sigmoid(
        jnp.einsum("ijc,cd->ijd", norm_cols, w_gate, preferred_element_type=jnp.float32)
    )
    upstream = out_grad.astype(jnp.float32)
    d_proj = (upstream * gate_act).astype(jnp.bfloat16)
    d_gate = (upstream * proj_out * gate_act * (1.0 - gate_act)).astype(jnp.bfloat16)
    d_normed = (
        jnp.einsum("ijc,hc->hij", d_proj, w_out, preferred_element_type=jnp.float32) * gain_out
    )
    d_tri = norm_backward(d_normed, normed_out, rstd_out, 0).astype(jnp.bfloat16)

    d_tri = d_tri.reshape(ch, dap, slice_h, own_rows, col_span)
    d_tri = jnp.transpose(d_tri, (1, 0, 2, 3, 4)).reshape(dap * ch, slice_h, own_rows, col_span)
    d_tri = lax.all_to_all(d_tri, ("dap", "ch"), split_axis=0, concat_axis=0, tiled=True)
    d_tri = d_tri.reshape(dap, ch, slice_h, own_rows, col_span)
    d_tri = jnp.transpose(d_tri, (2, 0, 3, 1, 4)).reshape(slice_h, dap * own_rows, all_cols)
    d_edge_a = jnp.einsum("hij,hjk->hik", d_tri, b_all, preferred_element_type=jnp.float32)
    d_edge_b = jnp.einsum("hij,hik->hjk", d_tri, a_all, preferred_element_type=jnp.float32)
    d_edges = jnp.stack((d_edge_a, d_edge_b)).astype(jnp.bfloat16)
    d_edges = d_edges.reshape(2, slice_h, dap, own_rows, all_cols)
    d_edges = jnp.transpose(d_edges, (2, 0, 1, 3, 4))
    d_edges = lax.all_to_all(d_edges, "dap", split_axis=0, concat_axis=0, tiled=True)
    d_edges = jnp.transpose(d_edges, (1, 0, 2, 3, 4)).reshape(2, hidden_local, own_rows, all_cols)

    def split_grad(d_edge, sig_val, proj_val):
        masked = d_edge * row_mask
        return (
            (masked * sig_val).astype(jnp.bfloat16),
            (masked * proj_val * sig_val * (1.0 - sig_val)).astype(jnp.bfloat16),
        )

    d_four = jnp.concatenate(
        split_grad(d_edges[0].astype(jnp.float32), a_sig, a_proj)
        + split_grad(d_edges[1].astype(jnp.float32), b_sig, b_proj),
        axis=0,
    )
    d_hidden = jnp.einsum("gik,cg->ikc", d_four, w_four, preferred_element_type=jnp.float32)
    if ch > 1:
        d_hidden = lax.psum_scatter(
            d_hidden.astype(jnp.bfloat16), "ch", scatter_dimension=1, tiled=True
        ).astype(jnp.float32)
    d_pair_norm = d_hidden + jnp.einsum(
        "ijd,cd->ijc", d_gate, w_gate, preferred_element_type=jnp.float32
    )
    normed_cols = lax.dynamic_slice_in_dim(normed_in, col_first, col_span, 1)
    rstd_cols = lax.dynamic_slice_in_dim(rstd_in, col_first, col_span, 1)
    grad_hat = d_pair_norm * ln_in_gain
    return norm_backward(grad_hat, normed_cols, rstd_cols, 2).astype(jnp.bfloat16)


F32 = jnp.float32
BF16 = jnp.bfloat16
SUBLANES = 8
LEVELS = 4
CORES = 2


def dot(lhs, rhs, lhs_dim, rhs_dim):
    return lax.dot_general(
        lhs, rhs, (((lhs_dim,), (rhs_dim,)), ((), ())), preferred_element_type=F32
    )


def across(row, count):
    return jnp.transpose(jnp.broadcast_to(row, (count, row.shape[1])))


def exchange_bit(first, second, weight):
    sublane = lax.broadcasted_iota(jnp.int32, first.shape, 1)
    low = sublane & weight == 0
    return (
        jnp.where(low, first, pltpu.roll(second, weight, 1)),
        jnp.where(low, pltpu.roll(first, SUBLANES - weight, 1), second),
    )


def falling(blocks):
    return jnp.concatenate([blocks[at : at + 1] for at in reversed(range(blocks.shape[0]))], axis=0)


def mesh_order(blocks):
    count, *rest = blocks.shape
    split = blocks.reshape(count // LEVELS // CORES, LEVELS, CORES, *rest)
    return falling(jnp.swapaxes(falling(split), 0, 1)).reshape(blocks.shape)


def list_order(blocks):
    count, *rest = blocks.shape
    split = blocks.reshape(LEVELS, count // LEVELS // CORES, CORES, *rest)
    return falling(jnp.swapaxes(falling(split), 0, 1)).reshape(blocks.shape)


def split_channels(blocks, own):
    devices, block, cols = blocks.shape
    tiles = blocks.reshape(devices // 2, 2, block // SUBLANES, SUBLANES, cols)
    parts = []
    for tile in range(block // SUBLANES):
        parts.extend(exchange_bit(tiles[:, 0, tile], tiles[:, 1, tile], own))
    return [part.reshape(devices * own, cols) for part in parts]


def merge_channels(parts, own):
    rows, cols = parts[0].shape
    devices = rows // own
    tiles = [part.reshape(devices // 2, SUBLANES, cols) for part in parts]
    pairs = [exchange_bit(*pair, own) for pair in zip(tiles[::2], tiles[1::2])]
    both = [jnp.concatenate(side, axis=1) for side in zip(*pairs)]
    block = len(parts) * own
    return jnp.stack(both, axis=1).reshape(devices, block, cols)


def trade(parts):
    rows, cols = parts[0].shape
    a, b, c, d = (part.reshape(rows // SUBLANES, SUBLANES, cols) for part in parts)
    (a, b), (c, d) = exchange_bit(a, b, 1), exchange_bit(c, d, 1)
    (a, c), (b, d) = exchange_bit(a, c, 2), exchange_bit(b, d, 2)
    return [part.reshape(rows, cols) for part in (a, b, c, d)]


def edges_kernel(me_ref, *refs):
    sources, (out_ref, *local), (blocks, arrived, left) = refs[:9], refs[9:19], refs[19:]
    copies = [
        pltpu.make_async_copy(source, target, arrived.at[index])
        for index, (source, target) in enumerate(zip(sources, local))
    ]
    for copy in copies:
        copy.start()
    act_ref, gain_ref, bias_ref, rows_ref, valid_ref, *weights = local
    own, cols, chan = act_ref.shape
    half = out_ref.shape[1] // 2
    for copy in copies[:3]:
        copy.wait()
    act = jnp.concatenate([jnp.transpose(act_ref[r].astype(F32)) for r in range(own)], axis=1)
    gain = across(gain_ref[...], cols)
    bias = across(bias_ref[...], cols)
    centre = act - jnp.mean(act, axis=0, keepdims=True)
    inverse = lax.rsqrt(jnp.mean(centre * centre, axis=0, keepdims=True) + EPSILON)
    wide_gain, wide_bias = (jnp.concatenate([value] * own, axis=1) for value in (gain, bias))
    pair_norm = (centre * inverse * wide_gain + wide_bias).astype(BF16)
    for copy in copies[3:]:
        copy.wait()
    valid = valid_ref[...].astype(F32)
    mask = jnp.concatenate(
        [valid * rows_ref[me_ref[0] * own + r].astype(F32) for r in range(own)], axis=1
    )
    sent = []
    for side in range(2):
        proj = dot(weights[2 * side][...], pair_norm, 0, 0)
        edge = mask * jax.nn.sigmoid(dot(weights[2 * side + 1][...], pair_norm, 0, 0)) * proj
        parts = trade([edge[:, r * cols : (r + 1) * cols] for r in range(own)])
        blocks[side] = merge_channels(parts, own).astype(BF16)
        copy = pltpu.make_async_copy(
            blocks.at[side], out_ref.at[:, side * half : (side + 1) * half, :], left.at[side]
        )
        copy.start()
        sent.append(copy)
    for copy in sent:
        copy.wait()


def gates_kernel(
    me_ref, rows_ref, valid_ref, act_ref, grad_ref, gain_ref, bias_ref, gain_out_ref, bias_out_ref,
    wap, wag, wbp, wbg, w_gate, w_out,
    factors, normed_t, rstd_t, gain_t, d_normed, slope, gain_out_t, bias_out_t,
):
    own, cols, _ = act_ref.shape
    hidden = wap.shape[1]
    valid = valid_ref[...].astype(F32)
    gain = across(gain_ref[...], cols)
    bias = across(bias_ref[...], cols)
    gain_out = across(gain_out_ref[...], cols)
    gain_t[...] = gain
    gain_out_t[...] = gain_out
    bias_out_t[...] = across(bias_out_ref[...], cols)
    for r in range(own):
        act = jnp.transpose(act_ref[r].astype(F32))
        centre = act - jnp.mean(act, axis=0, keepdims=True)
        inverse = lax.rsqrt(jnp.mean(centre * centre, axis=0, keepdims=True) + EPSILON)
        normed = centre * inverse
        lanes = pl.ds(r * cols, cols)
        normed_t[:, lanes] = normed
        rstd_t[:, lanes] = inverse
        pair_norm = (normed * gain + bias).astype(BF16)
        mask = valid * rows_ref[me_ref[0] * own + r].astype(F32)
        for side, (w_proj, w_sig) in enumerate(((wap, wag), (wbp, wbg))):
            proj = dot(w_proj[...], pair_norm, 0, 0)
            sig = jax.nn.sigmoid(dot(w_sig[...], pair_norm, 0, 0))
            kept = mask * sig
            factors[2 * side, :, lanes] = kept
            factors[2 * side + 1, :, lanes] = kept * proj * (1.0 - sig)
        gate_act = jax.nn.sigmoid(dot(w_gate[...], pair_norm, 0, 0))
        d_proj = jnp.transpose(grad_ref[r].astype(F32)) * gate_act
        slope[:, lanes] = d_proj * (1.0 - gate_act)
        d_normed[pl.ds(r, hidden, stride=own), :] = (
            dot(w_out[...], d_proj.astype(BF16), 1, 0) * gain_out
        )


def triangle_kernel(own, in_ref, _, out_ref, a_ref, b_ref):
    half = out_ref.shape[1]
    sides = [
        split_channels(
            mesh_order(in_ref[:, side * half : (side + 1) * half, :].astype(F32)), own
        )
        for side in range(2)
    ]
    tri = []
    for c, (edge_a, edge_b) in enumerate(zip(*sides)):
        a_ref[c] = edge_a.astype(BF16)
        b_ref[c] = edge_b.astype(BF16)
        tri.append(dot(a_ref[c], b_ref[c], 1, 1))
    out_ref[...] = list_order(merge_channels(tri, own)).astype(BF16)


def fold(values, own):
    total = jnp.sum(values, axis=0)
    rows = total
    for shift in range(own, SUBLANES, own):
        rows = rows + pltpu.roll(total, shift, 0)
    return rows[None]


def tri_normed(tri_ref, hidden, own):
    cols = tri_ref.shape[-1]
    tri = tri_ref[...].astype(F32).reshape(hidden * own // SUBLANES, SUBLANES, cols)
    centre = tri - fold(tri, own) / hidden
    inverse = lax.rsqrt(fold(centre * centre, own) / hidden + EPSILON)
    return centre * inverse, inverse


def norm_kernel(own, tri_ref, grad_ref, slope, gain, bias, w_out, out_ref, gate_ref):
    devices, block, cols = tri_ref.shape
    hidden = w_out.shape[0]
    normed, inverse = tri_normed(tri_ref, hidden, own)
    grad = grad_ref[...].reshape(normed.shape)
    mean_grad = fold(grad, own) / hidden
    mean_proj = fold(grad * normed, own) / hidden
    d_tri = inverse * (grad - mean_grad - normed * mean_proj)
    out_ref[...] = d_tri.reshape(devices, block, cols).astype(BF16)
    parts = trade(split_channels(normed.reshape(devices, block, cols), own))
    tri_norm = jnp.concatenate([(part * gain[...] + bias[...]).astype(BF16) for part in parts], axis=1)
    gate_ref[...] = (slope[...] * dot(w_out[...], tri_norm, 0, 0)).astype(BF16)


def edge_grad_kernel(own, in_ref, a_ref, b_ref, out_ref):
    block = in_ref.shape[1]
    grads = ([], [])
    for c, part in enumerate(split_channels(mesh_order(in_ref[...].astype(F32)), own)):
        d_tri = part.astype(BF16)
        grads[0].append(dot(d_tri, b_ref[c], 1, 0))
        grads[1].append(dot(d_tri, a_ref[c], 0, 0))
    for side in range(2):
        out_ref[:, side * block : (side + 1) * block, :] = (
            list_order(merge_channels(grads[side], own)).astype(BF16)
        )


def input_grad_kernel(
    in_ref, factors, normed_t, rstd_t, gain_t, d_gate, wap, wag, wbp, wbg, w_gate, out_ref
):
    own, cols, _ = out_ref.shape
    half = in_ref.shape[1] // 2
    grads = []
    for side in range(2):
        blocks = in_ref[:, side * half : (side + 1) * half, :].astype(F32)
        d_edge = jnp.concatenate(trade(split_channels(blocks, own)), axis=1)
        for at in range(2):
            grads.append((d_edge * factors[2 * side + at]).astype(BF16))
    weights = [weight[...] for weight in (wap, wag, wbp, wbg, w_gate)]
    grads.append(d_gate[...])
    total = dot(jnp.concatenate(weights, axis=1), jnp.concatenate(grads, axis=0), 1, 0)
    grad_hat = total * jnp.concatenate([gain_t[...]] * own, axis=1)
    normed = normed_t[...]
    mean_grad = jnp.mean(grad_hat, axis=0, keepdims=True)
    mean_proj = jnp.mean(grad_hat * normed, axis=0, keepdims=True)
    grad = rstd_t[...] * (grad_hat - mean_grad - normed * mean_proj)
    for r in range(own):
        out_ref[r] = jnp.transpose(grad[:, r * cols : (r + 1) * cols]).astype(BF16)


VMEM = pl.BlockSpec(memory_space=pltpu.VMEM)
SMEM = pl.BlockSpec(memory_space=pltpu.SMEM)
HBM = pl.BlockSpec(memory_space=pltpu.HBM)


def call(kernel, name, outs, args, scratch=(), scalars=0, flops=0, spaces=None, to=VMEM, limit=32 * 2**20):
    shapes = [jax.ShapeDtypeStruct(shape, dtype) for shape, dtype in outs]
    moved = sum(value.size * value.dtype.itemsize for value in list(args) + shapes)
    result = pl.pallas_call(
        kernel,
        name=name,
        out_shape=shapes,
        in_specs=[SMEM] * scalars + (spaces or [VMEM] * (len(args) - scalars)),
        out_specs=[to] * len(outs),
        scratch_shapes=scratch,
        cost_estimate=pl.CostEstimate(flops=flops, bytes_accessed=moved, transcendentals=0),
        compiler_params=pltpu.CompilerParams(vmem_limit_bytes=limit),
    )(*args)
    return result[0] if len(outs) == 1 else result


def kernel_shards(
    dap,
    pair_act,
    out_grad,
    residue_mask,
    ln_in_gain,
    ln_in_bias,
    w_a_proj,
    w_a_gate,
    w_b_proj,
    w_b_gate,
    w_gate,
    ln_out_gain,
    ln_out_bias,
    w_out,
):
    own, cols, chan = pair_act.shape
    hidden = w_a_proj.shape[1]
    slice_h = hidden // dap
    rows = dap * own
    block = slice_h * own
    me = lax.axis_index("dap").reshape(1)
    valid = residue_mask.reshape(1, -1)
    gain_in, bias_in, gain_out, bias_out = (
        value.reshape(1, -1) for value in (ln_in_gain, ln_in_bias, ln_out_gain, ln_out_bias)
    )
    w_edges = (w_a_proj, w_a_gate, w_b_proj, w_b_gate)
    product = 2 * own * cols * chan * hidden

    span = dap // LEVELS
    listed = [
        quarter * span + pair * CORES + core
        for pair in reversed(range(span // CORES))
        for quarter in reversed(range(LEVELS))
        for core in range(CORES)
    ]

    def exchange(value):
        return lax.all_to_all(
            value, "dap", split_axis=0, concat_axis=0, axis_index_groups=[listed], tiled=True
        )

    first = (pair_act, gain_in, bias_in, residue_mask, valid, *w_edges)
    edges = call(
        edges_kernel,
        "edges",
        [((dap, 2 * block, cols), BF16)],
        (me, *first),
        scratch=[
            (pltpu.SMEM if value is residue_mask else pltpu.VMEM)(value.shape, value.dtype)
            for value in first
        ]
        + [pltpu.VMEM((2, dap, block, cols), BF16)]
        + [pltpu.SemaphoreType.DMA((len(first),)), pltpu.SemaphoreType.DMA((2,))],
        scalars=1,
        flops=4 * product,
        to=HBM,
        spaces=[HBM] * len(first),
        limit=None,
    )
    edges = exchange(edges)
    factors, normed_t, rstd_t, gain_t, d_normed, slope, gain_out_t, bias_out_t = call(
        gates_kernel,
        "gates",
        [
            ((4, hidden, own * cols), F32),
            ((chan, own * cols), F32),
            ((1, own * cols), F32),
            ((chan, cols), F32),
            ((hidden * own, cols), F32),
            ((chan, own * cols), F32),
            ((hidden, cols), F32),
            ((hidden, cols), F32),
        ],
        (me, residue_mask, valid, pair_act, out_grad, gain_in, bias_in, gain_out)
        + (bias_out, *w_edges, w_gate, w_out),
        scalars=2,
        flops=6 * product,
    )
    tri, edge_a, edge_b = call(
        functools.partial(triangle_kernel, own),
        "triangle",
        [
            ((dap, block, cols), BF16),
            ((slice_h, rows, cols), BF16),
            ((slice_h, rows, cols), BF16),
        ],
        (edges, d_normed),
        flops=product,
        spaces=[VMEM, pl.BlockSpec(memory_space=pl.ANY)],
    )
    tri = exchange(tri)
    d_tri, d_gate = call(
        functools.partial(norm_kernel, own),
        "norm",
        [((dap, block, cols), BF16), ((chan, own * cols), BF16)],
        (tri, d_normed, slope, gain_out_t, bias_out_t, w_out),
        flops=2 * product,
    )
    d_tri = exchange(d_tri)
    d_edges = call(
        functools.partial(edge_grad_kernel, own),
        "edge_grad",
        [((dap, 2 * block, cols), BF16)],
        (d_tri, edge_a, edge_b),
        flops=2 * product,
    )
    d_edges = exchange(d_edges)
    return call(
        input_grad_kernel,
        "input_grad",
        [((own, cols, chan), BF16)],
        (d_edges, factors, normed_t, rstd_t, gain_t, d_gate, *w_edges, w_gate),
        flops=4 * product,
    )


def fits_kernels(dap, ch, pair_act, w_proj):
    own, cols, chan = pair_act.shape
    hidden = w_proj.shape[1]
    block = hidden // dap * own
    return (
        ch == 1
        and hidden % dap == 0
        and own == SUBLANES // 2
        and block == own * own
        and dap % SUBLANES == 0
        and cols == dap * own
        and cols % 128 == chan % 128 == hidden % 128 == 0
    )


def solution(mesh):
    sizes = dict(mesh.shape)

    def program(*args):
        dap, ch = sizes["dap"], sizes["ch"]
        if fits_kernels(dap, ch, args[0], args[5]):
            return kernel_shards(dap, *args)
        return channel_shards(dap, ch, *args)

    in_specs = (
        P(("grp", "dap"), None, None),
        P(("grp", "dap"), "ch", None),
        P("grp"),
        P(),
        P(),
        P(None, "ch"),
        P(None, "ch"),
        P(None, "ch"),
        P(None, "ch"),
        P(),
        P(),
        P(),
        P(),
    )
    out_specs = P(("grp", "dap"), "ch", None)
    return jax.shard_map(
        program, mesh=mesh, in_specs=in_specs, out_specs=out_specs, check_vma=False
    )
```

```python
import functools

import jax
import jax.numpy as jnp
from jax import lax
from jax.experimental import pallas as pl
from jax.experimental.pallas import tpu as pltpu
from jax.sharding import PartitionSpec as P

EPSILON = 1e-05


def normalise(values, reduce_dim):
    centre = values - jnp.mean(values, axis=reduce_dim, keepdims=True)
    inverse = lax.rsqrt(jnp.mean(centre * centre, axis=reduce_dim, keepdims=True) + EPSILON)
    return (centre * inverse, inverse)


def norm_backward(grad_hat, normed, inverse, reduce_dim):
    mean_grad = jnp.mean(grad_hat, axis=reduce_dim, keepdims=True)
    mean_proj = jnp.mean(grad_hat * normed, axis=reduce_dim, keepdims=True)
    return inverse * (grad_hat - mean_grad - normed * mean_proj)


def channel_shards(
    dap,
    ch,
    pair_act,
    out_grad,
    residue_mask,
    ln_in_gain,
    ln_in_bias,
    w_a_proj,
    w_a_gate,
    w_b_proj,
    w_b_gate,
    w_gate,
    ln_out_gain,
    ln_out_bias,
    w_out,
):
    own_rows, all_cols = pair_act.shape[:2]
    col_span = out_grad.shape[1]
    hidden_local = w_a_proj.shape[1]
    slice_h = hidden_local // dap
    row_first = lax.axis_index("dap") * own_rows
    col_first = lax.axis_index("ch") * col_span
    normed_in, rstd_in = normalise(pair_act.astype(jnp.float32), 2)
    pair_norm = (normed_in * ln_in_gain + ln_in_bias).astype(jnp.bfloat16)
    valid_all = residue_mask.astype(jnp.float32)
    valid_rows = lax.dynamic_slice_in_dim(valid_all, row_first, own_rows)
    row_mask = (valid_rows[:, None] * valid_all[None, :])[None]
    w_four = jnp.concatenate((w_a_proj, w_a_gate, w_b_proj, w_b_gate), axis=1)
    projected = jnp.einsum("ikc,cg->gik", pair_norm, w_four, preferred_element_type=jnp.float32)
    a_proj = projected[:hidden_local]
    a_sig = jax.nn.sigmoid(projected[hidden_local : 2 * hidden_local])
    b_proj = projected[2 * hidden_local : 3 * hidden_local]
    b_sig = jax.nn.sigmoid(projected[3 * hidden_local :])
    edge_a = (row_mask * a_sig * a_proj).astype(jnp.bfloat16)
    edge_b = (row_mask * b_sig * b_proj).astype(jnp.bfloat16)

    split = (dap, slice_h, own_rows, all_cols)
    edges = jnp.stack((edge_a.reshape(split), edge_b.reshape(split)), axis=1)
    edges = lax.all_to_all(edges, "dap", split_axis=0, concat_axis=0, tiled=True)
    edges = jnp.transpose(edges, (1, 2, 0, 3, 4)).reshape(2, slice_h, dap * own_rows, all_cols)
    a_all, b_all = edges[0], edges[1]
    tri = jnp.einsum("hik,hjk->hij", a_all, b_all, preferred_element_type=jnp.float32).astype(
        jnp.bfloat16
    )
    tri = tri.reshape(slice_h, dap, own_rows, ch, col_span)
    tri = jnp.transpose(tri, (1, 3, 0, 2, 4)).reshape(dap * ch, slice_h, own_rows, col_span)
    tri = lax.all_to_all(tri, ("dap", "ch"), split_axis=0, concat_axis=0, tiled=True)
    tri = tri.reshape(dap, ch, slice_h, own_rows, col_span)
    tri_full = jnp.transpose(tri, (1, 0, 2, 3, 4)).reshape(-1, own_rows, col_span)

    normed_out, rstd_out = normalise(tri_full.astype(jnp.float32), 0)
    gain_out = ln_out_gain.reshape(-1, 1, 1)
    bias_out = ln_out_bias.reshape(-1, 1, 1)
    tri_norm = (normed_out * gain_out + bias_out).astype(jnp.bfloat16)
    proj_out = jnp.einsum("hij,hc->ijc", tri_norm, w_out, preferred_element_type=jnp.float32)
    norm_cols = lax.dynamic_slice_in_dim(pair_norm, col_first, col_span, 1)
    gate_act = jax.nn.sigmoid(
        jnp.einsum("ijc,cd->ijd", norm_cols, w_gate, preferred_element_type=jnp.float32)
    )
    upstream = out_grad.astype(jnp.float32)
    d_proj = (upstream * gate_act).astype(jnp.bfloat16)
    d_gate = (upstream * proj_out * gate_act * (1.0 - gate_act)).astype(jnp.bfloat16)
    d_normed = (
        jnp.einsum("ijc,hc->hij", d_proj, w_out, preferred_element_type=jnp.float32) * gain_out
    )
    d_tri = norm_backward(d_normed, normed_out, rstd_out, 0).astype(jnp.bfloat16)

    d_tri = d_tri.reshape(ch, dap, slice_h, own_rows, col_span)
    d_tri = jnp.transpose(d_tri, (1, 0, 2, 3, 4)).reshape(dap * ch, slice_h, own_rows, col_span)
    d_tri = lax.all_to_all(d_tri, ("dap", "ch"), split_axis=0, concat_axis=0, tiled=True)
    d_tri = d_tri.reshape(dap, ch, slice_h, own_rows, col_span)
    d_tri = jnp.transpose(d_tri, (2, 0, 3, 1, 4)).reshape(slice_h, dap * own_rows, all_cols)
    d_edge_a = jnp.einsum("hij,hjk->hik", d_tri, b_all, preferred_element_type=jnp.float32)
    d_edge_b = jnp.einsum("hij,hik->hjk", d_tri, a_all, preferred_element_type=jnp.float32)
    d_edges = jnp.stack((d_edge_a, d_edge_b)).astype(jnp.bfloat16)
    d_edges = d_edges.reshape(2, slice_h, dap, own_rows, all_cols)
    d_edges = jnp.transpose(d_edges, (2, 0, 1, 3, 4))
    d_edges = lax.all_to_all(d_edges, "dap", split_axis=0, concat_axis=0, tiled=True)
    d_edges = jnp.transpose(d_edges, (1, 0, 2, 3, 4)).reshape(2, hidden_local, own_rows, all_cols)

    def split_grad(d_edge, sig_val, proj_val):
        masked = d_edge * row_mask
        return (
            (masked * sig_val).astype(jnp.bfloat16),
            (masked * proj_val * sig_val * (1.0 - sig_val)).astype(jnp.bfloat16),
        )

    d_four = jnp.concatenate(
        split_grad(d_edges[0].astype(jnp.float32), a_sig, a_proj)
        + split_grad(d_edges[1].astype(jnp.float32), b_sig, b_proj),
        axis=0,
    )
    d_hidden = jnp.einsum("gik,cg->ikc", d_four, w_four, preferred_element_type=jnp.float32)
    if ch > 1:
        d_hidden = lax.psum_scatter(
            d_hidden.astype(jnp.bfloat16), "ch", scatter_dimension=1, tiled=True
        ).astype(jnp.float32)
    d_pair_norm = d_hidden + jnp.einsum(
        "ijd,cd->ijc", d_gate, w_gate, preferred_element_type=jnp.float32
    )
    normed_cols = lax.dynamic_slice_in_dim(normed_in, col_first, col_span, 1)
    rstd_cols = lax.dynamic_slice_in_dim(rstd_in, col_first, col_span, 1)
    grad_hat = d_pair_norm * ln_in_gain
    return norm_backward(grad_hat, normed_cols, rstd_cols, 2).astype(jnp.bfloat16)


F32 = jnp.float32
BF16 = jnp.bfloat16
SUBLANES = 8
LEVELS = 4
CORES = 2


def dot(lhs, rhs, lhs_dim, rhs_dim):
    return lax.dot_general(
        lhs, rhs, (((lhs_dim,), (rhs_dim,)), ((), ())), preferred_element_type=F32
    )


def across(row, count):
    return jnp.transpose(jnp.broadcast_to(row, (count, row.shape[1])))


def exchange_bit(first, second, weight):
    sublane = lax.broadcasted_iota(jnp.int32, first.shape, 1)
    low = sublane & weight == 0
    return (
        jnp.where(low, first, pltpu.roll(second, weight, 1)),
        jnp.where(low, pltpu.roll(first, SUBLANES - weight, 1), second),
    )


def falling(blocks):
    return jnp.concatenate([blocks[at : at + 1] for at in reversed(range(blocks.shape[0]))], axis=0)


def mesh_order(blocks):
    count, *rest = blocks.shape
    split = falling(blocks).reshape(count // LEVELS // CORES, LEVELS, CORES, *rest)
    return jnp.swapaxes(split, 0, 1).reshape(blocks.shape)


def list_order(blocks):
    count, *rest = blocks.shape
    split = blocks.reshape(LEVELS, count // LEVELS // CORES, CORES, *rest)
    return falling(jnp.swapaxes(split, 0, 1).reshape(blocks.shape))


def split_channels(blocks, own):
    devices, block, cols = blocks.shape
    tiles = blocks.reshape(devices // 2, 2, block // SUBLANES, SUBLANES, cols)
    parts = []
    for tile in range(block // SUBLANES):
        parts.extend(exchange_bit(tiles[:, 0, tile], tiles[:, 1, tile], own))
    return [part.reshape(devices * own, cols) for part in parts]


def merge_channels(parts, own):
    rows, cols = parts[0].shape
    devices = rows // own
    tiles = [part.reshape(devices // 2, SUBLANES, cols) for part in parts]
    pairs = [exchange_bit(*pair, own) for pair in zip(tiles[::2], tiles[1::2])]
    both = [jnp.concatenate(side, axis=1) for side in zip(*pairs)]
    block = len(parts) * own
    return jnp.stack(both, axis=1).reshape(devices, block, cols)


def trade(parts):
    rows, cols = parts[0].shape
    a, b, c, d = (part.reshape(rows // SUBLANES, SUBLANES, cols) for part in parts)
    (a, b), (c, d) = exchange_bit(a, b, 1), exchange_bit(c, d, 1)
    (a, c), (b, d) = exchange_bit(a, c, 2), exchange_bit(b, d, 2)
    return [part.reshape(rows, cols) for part in (a, b, c, d)]


def edges_kernel(me_ref, *refs):
    sources, (out_ref, *local), (blocks, arrived, left) = refs[:9], refs[9:19], refs[19:]
    copies = [
        pltpu.make_async_copy(source, target, arrived.at[index])
        for index, (source, target) in enumerate(zip(sources, local))
    ]
    for copy in copies:
        copy.start()
    act_ref, gain_ref, bias_ref, rows_ref, valid_ref, *weights = local
    own, cols, chan = act_ref.shape
    half = out_ref.shape[1] // 2
    for copy in copies[:3]:
        copy.wait()
    act = jnp.concatenate([jnp.transpose(act_ref[r].astype(F32)) for r in range(own)], axis=1)
    gain = across(gain_ref[...], cols)
    bias = across(bias_ref[...], cols)
    centre = act - jnp.mean(act, axis=0, keepdims=True)
    inverse = lax.rsqrt(jnp.mean(centre * centre, axis=0, keepdims=True) + EPSILON)
    wide_gain, wide_bias = (jnp.concatenate([value] * own, axis=1) for value in (gain, bias))
    pair_norm = (centre * inverse * wide_gain + wide_bias).astype(BF16)
    for copy in copies[3:]:
        copy.wait()
    valid = valid_ref[...].astype(F32)
    mask = jnp.concatenate(
        [valid * rows_ref[me_ref[0] * own + r].astype(F32) for r in range(own)], axis=1
    )
    sent = []
    for side in range(2):
        proj = dot(weights[2 * side][...], pair_norm, 0, 0)
        edge = mask * jax.nn.sigmoid(dot(weights[2 * side + 1][...], pair_norm, 0, 0)) * proj
        parts = trade([edge[:, r * cols : (r + 1) * cols] for r in range(own)])
        blocks[side] = merge_channels(parts, own).astype(BF16)
        copy = pltpu.make_async_copy(
            blocks.at[side], out_ref.at[:, side * half : (side + 1) * half, :], left.at[side]
        )
        copy.start()
        sent.append(copy)
    for copy in sent:
        copy.wait()


def gates_kernel(
    me_ref, rows_ref, valid_ref, act_ref, grad_ref, gain_ref, bias_ref, gain_out_ref, bias_out_ref,
    wap, wag, wbp, wbg, w_gate, w_out,
    factors, normed_t, rstd_t, gain_t, d_normed, slope, gain_out_t, bias_out_t,
):
    own, cols, _ = act_ref.shape
    hidden = wap.shape[1]
    valid = valid_ref[...].astype(F32)
    gain = across(gain_ref[...], cols)
    bias = across(bias_ref[...], cols)
    gain_out = across(gain_out_ref[...], cols)
    gain_t[...] = gain
    gain_out_t[...] = gain_out
    bias_out_t[...] = across(bias_out_ref[...], cols)
    for r in range(own):
        act = jnp.transpose(act_ref[r].astype(F32))
        centre = act - jnp.mean(act, axis=0, keepdims=True)
        inverse = lax.rsqrt(jnp.mean(centre * centre, axis=0, keepdims=True) + EPSILON)
        normed = centre * inverse
        lanes = pl.ds(r * cols, cols)
        normed_t[:, lanes] = normed
        rstd_t[:, lanes] = inverse
        pair_norm = (normed * gain + bias).astype(BF16)
        mask = valid * rows_ref[me_ref[0] * own + r].astype(F32)
        for side, (w_proj, w_sig) in enumerate(((wap, wag), (wbp, wbg))):
            proj = dot(w_proj[...], pair_norm, 0, 0)
            sig = jax.nn.sigmoid(dot(w_sig[...], pair_norm, 0, 0))
            kept = mask * sig
            factors[2 * side, :, lanes] = kept
            factors[2 * side + 1, :, lanes] = kept * proj * (1.0 - sig)
        gate_act = jax.nn.sigmoid(dot(w_gate[...], pair_norm, 0, 0))
        d_proj = jnp.transpose(grad_ref[r].astype(F32)) * gate_act
        slope[:, lanes] = d_proj * (1.0 - gate_act)
        d_normed[pl.ds(r, hidden, stride=own), :] = (
            dot(w_out[...], d_proj.astype(BF16), 1, 0) * gain_out
        )


def triangle_kernel(own, in_ref, _, out_ref, a_ref, b_ref):
    half = out_ref.shape[1]
    sides = [
        split_channels(
            mesh_order(in_ref[:, side * half : (side + 1) * half, :].astype(F32)), own
        )
        for side in range(2)
    ]
    tri = []
    for c, (edge_a, edge_b) in enumerate(zip(*sides)):
        a_ref[c] = edge_a.astype(BF16)
        b_ref[c] = edge_b.astype(BF16)
        tri.append(dot(a_ref[c], b_ref[c], 1, 1))
    out_ref[...] = list_order(merge_channels(tri, own)).astype(BF16)


def fold(values, own):
    total = jnp.sum(values, axis=0)
    rows = total
    for shift in range(own, SUBLANES, own):
        rows = rows + pltpu.roll(total, shift, 0)
    return rows[None]


def tri_normed(tri_ref, hidden, own):
    cols = tri_ref.shape[-1]
    tri = tri_ref[...].astype(F32).reshape(hidden * own // SUBLANES, SUBLANES, cols)
    centre = tri - fold(tri, own) / hidden
    inverse = lax.rsqrt(fold(centre * centre, own) / hidden + EPSILON)
    return centre * inverse, inverse


def norm_kernel(own, tri_ref, grad_ref, slope, gain, bias, w_out, out_ref, gate_ref):
    devices, block, cols = tri_ref.shape
    hidden = w_out.shape[0]
    normed, inverse = tri_normed(tri_ref, hidden, own)
    grad = grad_ref[...].reshape(normed.shape)
    mean_grad = fold(grad, own) / hidden
    mean_proj = fold(grad * normed, own) / hidden
    d_tri = inverse * (grad - mean_grad - normed * mean_proj)
    out_ref[...] = d_tri.reshape(devices, block, cols).astype(BF16)
    parts = trade(split_channels(normed.reshape(devices, block, cols), own))
    tri_norm = jnp.concatenate([(part * gain[...] + bias[...]).astype(BF16) for part in parts], axis=1)
    gate_ref[...] = (slope[...] * dot(w_out[...], tri_norm, 0, 0)).astype(BF16)


def edge_grad_kernel(own, in_ref, a_ref, b_ref, out_ref):
    block = in_ref.shape[1]
    grads = ([], [])
    for c, part in enumerate(split_channels(mesh_order(in_ref[...].astype(F32)), own)):
        d_tri = part.astype(BF16)
        grads[0].append(dot(d_tri, b_ref[c], 1, 0))
        grads[1].append(dot(d_tri, a_ref[c], 0, 0))
    for side in range(2):
        out_ref[:, side * block : (side + 1) * block, :] = (
            list_order(merge_channels(grads[side], own)).astype(BF16)
        )


def input_grad_kernel(
    in_ref, factors, normed_t, rstd_t, gain_t, d_gate, wap, wag, wbp, wbg, w_gate, out_ref
):
    own, cols, _ = out_ref.shape
    half = in_ref.shape[1] // 2
    grads = []
    for side in range(2):
        blocks = in_ref[:, side * half : (side + 1) * half, :].astype(F32)
        d_edge = jnp.concatenate(trade(split_channels(blocks, own)), axis=1)
        for at in range(2):
            grads.append((d_edge * factors[2 * side + at]).astype(BF16))
    weights = [weight[...] for weight in (wap, wag, wbp, wbg, w_gate)]
    grads.append(d_gate[...])
    total = dot(jnp.concatenate(weights, axis=1), jnp.concatenate(grads, axis=0), 1, 0)
    grad_hat = total * jnp.concatenate([gain_t[...]] * own, axis=1)
    normed = normed_t[...]
    mean_grad = jnp.mean(grad_hat, axis=0, keepdims=True)
    mean_proj = jnp.mean(grad_hat * normed, axis=0, keepdims=True)
    grad = rstd_t[...] * (grad_hat - mean_grad - normed * mean_proj)
    for r in range(own):
        out_ref[r] = jnp.transpose(grad[:, r * cols : (r + 1) * cols]).astype(BF16)


VMEM = pl.BlockSpec(memory_space=pltpu.VMEM)
SMEM = pl.BlockSpec(memory_space=pltpu.SMEM)
HBM = pl.BlockSpec(memory_space=pltpu.HBM)


def call(kernel, name, outs, args, scratch=(), scalars=0, flops=0, spaces=None, to=VMEM, limit=32 * 2**20):
    shapes = [jax.ShapeDtypeStruct(shape, dtype) for shape, dtype in outs]
    moved = sum(value.size * value.dtype.itemsize for value in list(args) + shapes)
    result = pl.pallas_call(
        kernel,
        name=name,
        out_shape=shapes,
        in_specs=[SMEM] * scalars + (spaces or [VMEM] * (len(args) - scalars)),
        out_specs=[to] * len(outs),
        scratch_shapes=scratch,
        cost_estimate=pl.CostEstimate(flops=flops, bytes_accessed=moved, transcendentals=0),
        compiler_params=pltpu.CompilerParams(vmem_limit_bytes=limit),
    )(*args)
    return result[0] if len(outs) == 1 else result


def kernel_shards(
    dap,
    pair_act,
    out_grad,
    residue_mask,
    ln_in_gain,
    ln_in_bias,
    w_a_proj,
    w_a_gate,
    w_b_proj,
    w_b_gate,
    w_gate,
    ln_out_gain,
    ln_out_bias,
    w_out,
):
    own, cols, chan = pair_act.shape
    hidden = w_a_proj.shape[1]
    slice_h = hidden // dap
    rows = dap * own
    block = slice_h * own
    me = lax.axis_index("dap").reshape(1)
    valid = residue_mask.reshape(1, -1)
    gain_in, bias_in, gain_out, bias_out = (
        value.reshape(1, -1) for value in (ln_in_gain, ln_in_bias, ln_out_gain, ln_out_bias)
    )
    w_edges = (w_a_proj, w_a_gate, w_b_proj, w_b_gate)
    product = 2 * own * cols * chan * hidden

    span = dap // LEVELS
    listed = [
        quarter * span + pair * CORES + core
        for pair in reversed(range(span // CORES))
        for quarter in reversed(range(LEVELS))
        for core in reversed(range(CORES))
    ]

    def exchange(value):
        return lax.all_to_all(
            value, "dap", split_axis=0, concat_axis=0, axis_index_groups=[listed], tiled=True
        )

    first = (pair_act, gain_in, bias_in, residue_mask, valid, *w_edges)
    edges = call(
        edges_kernel,
        "edges",
        [((dap, 2 * block, cols), BF16)],
        (me, *first),
        scratch=[
            (pltpu.SMEM if value is residue_mask else pltpu.VMEM)(value.shape, value.dtype)
            for value in first
        ]
        + [pltpu.VMEM((2, dap, block, cols), BF16)]
        + [pltpu.SemaphoreType.DMA((len(first),)), pltpu.SemaphoreType.DMA((2,))],
        scalars=1,
        flops=4 * product,
        to=HBM,
        spaces=[HBM] * len(first),
        limit=None,
    )
    edges = exchange(edges)
    factors, normed_t, rstd_t, gain_t, d_normed, slope, gain_out_t, bias_out_t = call(
        gates_kernel,
        "gates",
        [
            ((4, hidden, own * cols), F32),
            ((chan, own * cols), F32),
            ((1, own * cols), F32),
            ((chan, cols), F32),
            ((hidden * own, cols), F32),
            ((chan, own * cols), F32),
            ((hidden, cols), F32),
            ((hidden, cols), F32),
        ],
        (me, residue_mask, valid, pair_act, out_grad, gain_in, bias_in, gain_out)
        + (bias_out, *w_edges, w_gate, w_out),
        scalars=2,
        flops=6 * product,
    )
    tri, edge_a, edge_b = call(
        functools.partial(triangle_kernel, own),
        "triangle",
        [
            ((dap, block, cols), BF16),
            ((slice_h, rows, cols), BF16),
            ((slice_h, rows, cols), BF16),
        ],
        (edges, d_normed),
        flops=product,
        spaces=[VMEM, pl.BlockSpec(memory_space=pl.ANY)],
    )
    tri = exchange(tri)
    d_tri, d_gate = call(
        functools.partial(norm_kernel, own),
        "norm",
        [((dap, block, cols), BF16), ((chan, own * cols), BF16)],
        (tri, d_normed, slope, gain_out_t, bias_out_t, w_out),
        flops=2 * product,
    )
    d_tri = exchange(d_tri)
    d_edges = call(
        functools.partial(edge_grad_kernel, own),
        "edge_grad",
        [((dap, 2 * block, cols), BF16)],
        (d_tri, edge_a, edge_b),
        flops=2 * product,
    )
    d_edges = exchange(d_edges)
    return call(
        input_grad_kernel,
        "input_grad",
        [((own, cols, chan), BF16)],
        (d_edges, factors, normed_t, rstd_t, gain_t, d_gate, *w_edges, w_gate),
        flops=4 * product,
    )


def fits_kernels(dap, ch, pair_act, w_proj):
    own, cols, chan = pair_act.shape
    hidden = w_proj.shape[1]
    block = hidden // dap * own
    return (
        ch == 1
        and hidden % dap == 0
        and own == SUBLANES // 2
        and block == own * own
        and dap % SUBLANES == 0
        and cols == dap * own
        and cols % 128 == chan % 128 == hidden % 128 == 0
    )


def solution(mesh):
    sizes = dict(mesh.shape)

    def program(*args):
        dap, ch = sizes["dap"], sizes["ch"]
        if fits_kernels(dap, ch, args[0], args[5]):
            return kernel_shards(dap, *args)
        return channel_shards(dap, ch, *args)

    in_specs = (
        P(("grp", "dap"), None, None),
        P(("grp", "dap"), "ch", None),
        P("grp"),
        P(),
        P(),
        P(None, "ch"),
        P(None, "ch"),
        P(None, "ch"),
        P(None, "ch"),
        P(),
        P(),
        P(),
        P(),
    )
    out_specs = P(("grp", "dap"), "ch", None)
    return jax.shard_map(
        program, mesh=mesh, in_specs=in_specs, out_specs=out_specs, check_vma=False
    )
```

```python
import functools

import jax
import jax.numpy as jnp
from jax import lax
from jax.experimental import pallas as pl
from jax.experimental.pallas import tpu as pltpu
from jax.sharding import PartitionSpec as P

EPSILON = 1e-05


def normalise(values, reduce_dim):
    centre = values - jnp.mean(values, axis=reduce_dim, keepdims=True)
    inverse = lax.rsqrt(jnp.mean(centre * centre, axis=reduce_dim, keepdims=True) + EPSILON)
    return (centre * inverse, inverse)


def norm_backward(grad_hat, normed, inverse, reduce_dim):
    mean_grad = jnp.mean(grad_hat, axis=reduce_dim, keepdims=True)
    mean_proj = jnp.mean(grad_hat * normed, axis=reduce_dim, keepdims=True)
    return inverse * (grad_hat - mean_grad - normed * mean_proj)


def channel_shards(
    dap,
    ch,
    pair_act,
    out_grad,
    residue_mask,
    ln_in_gain,
    ln_in_bias,
    w_a_proj,
    w_a_gate,
    w_b_proj,
    w_b_gate,
    w_gate,
    ln_out_gain,
    ln_out_bias,
    w_out,
):
    own_rows, all_cols = pair_act.shape[:2]
    col_span = out_grad.shape[1]
    hidden_local = w_a_proj.shape[1]
    slice_h = hidden_local // dap
    row_first = lax.axis_index("dap") * own_rows
    col_first = lax.axis_index("ch") * col_span
    normed_in, rstd_in = normalise(pair_act.astype(jnp.float32), 2)
    pair_norm = (normed_in * ln_in_gain + ln_in_bias).astype(jnp.bfloat16)
    valid_all = residue_mask.astype(jnp.float32)
    valid_rows = lax.dynamic_slice_in_dim(valid_all, row_first, own_rows)
    row_mask = (valid_rows[:, None] * valid_all[None, :])[None]
    w_four = jnp.concatenate((w_a_proj, w_a_gate, w_b_proj, w_b_gate), axis=1)
    projected = jnp.einsum("ikc,cg->gik", pair_norm, w_four, preferred_element_type=jnp.float32)
    a_proj = projected[:hidden_local]
    a_sig = jax.nn.sigmoid(projected[hidden_local : 2 * hidden_local])
    b_proj = projected[2 * hidden_local : 3 * hidden_local]
    b_sig = jax.nn.sigmoid(projected[3 * hidden_local :])
    edge_a = (row_mask * a_sig * a_proj).astype(jnp.bfloat16)
    edge_b = (row_mask * b_sig * b_proj).astype(jnp.bfloat16)

    split = (dap, slice_h, own_rows, all_cols)
    edges = jnp.stack((edge_a.reshape(split), edge_b.reshape(split)), axis=1)
    edges = lax.all_to_all(edges, "dap", split_axis=0, concat_axis=0, tiled=True)
    edges = jnp.transpose(edges, (1, 2, 0, 3, 4)).reshape(2, slice_h, dap * own_rows, all_cols)
    a_all, b_all = edges[0], edges[1]
    tri = jnp.einsum("hik,hjk->hij", a_all, b_all, preferred_element_type=jnp.float32).astype(
        jnp.bfloat16
    )
    tri = tri.reshape(slice_h, dap, own_rows, ch, col_span)
    tri = jnp.transpose(tri, (1, 3, 0, 2, 4)).reshape(dap * ch, slice_h, own_rows, col_span)
    tri = lax.all_to_all(tri, ("dap", "ch"), split_axis=0, concat_axis=0, tiled=True)
    tri = tri.reshape(dap, ch, slice_h, own_rows, col_span)
    tri_full = jnp.transpose(tri, (1, 0, 2, 3, 4)).reshape(-1, own_rows, col_span)

    normed_out, rstd_out = normalise(tri_full.astype(jnp.float32), 0)
    gain_out = ln_out_gain.reshape(-1, 1, 1)
    bias_out = ln_out_bias.reshape(-1, 1, 1)
    tri_norm = (normed_out * gain_out + bias_out).astype(jnp.bfloat16)
    proj_out = jnp.einsum("hij,hc->ijc", tri_norm, w_out, preferred_element_type=jnp.float32)
    norm_cols = lax.dynamic_slice_in_dim(pair_norm, col_first, col_span, 1)
    gate_act = jax.nn.sigmoid(
        jnp.einsum("ijc,cd->ijd", norm_cols, w_gate, preferred_element_type=jnp.float32)
    )
    upstream = out_grad.astype(jnp.float32)
    d_proj = (upstream * gate_act).astype(jnp.bfloat16)
    d_gate = (upstream * proj_out * gate_act * (1.0 - gate_act)).astype(jnp.bfloat16)
    d_normed = (
        jnp.einsum("ijc,hc->hij", d_proj, w_out, preferred_element_type=jnp.float32) * gain_out
    )
    d_tri = norm_backward(d_normed, normed_out, rstd_out, 0).astype(jnp.bfloat16)

    d_tri = d_tri.reshape(ch, dap, slice_h, own_rows, col_span)
    d_tri = jnp.transpose(d_tri, (1, 0, 2, 3, 4)).reshape(dap * ch, slice_h, own_rows, col_span)
    d_tri = lax.all_to_all(d_tri, ("dap", "ch"), split_axis=0, concat_axis=0, tiled=True)
    d_tri = d_tri.reshape(dap, ch, slice_h, own_rows, col_span)
    d_tri = jnp.transpose(d_tri, (2, 0, 3, 1, 4)).reshape(slice_h, dap * own_rows, all_cols)
    d_edge_a = jnp.einsum("hij,hjk->hik", d_tri, b_all, preferred_element_type=jnp.float32)
    d_edge_b = jnp.einsum("hij,hik->hjk", d_tri, a_all, preferred_element_type=jnp.float32)
    d_edges = jnp.stack((d_edge_a, d_edge_b)).astype(jnp.bfloat16)
    d_edges = d_edges.reshape(2, slice_h, dap, own_rows, all_cols)
    d_edges = jnp.transpose(d_edges, (2, 0, 1, 3, 4))
    d_edges = lax.all_to_all(d_edges, "dap", split_axis=0, concat_axis=0, tiled=True)
    d_edges = jnp.transpose(d_edges, (1, 0, 2, 3, 4)).reshape(2, hidden_local, own_rows, all_cols)

    def split_grad(d_edge, sig_val, proj_val):
        masked = d_edge * row_mask
        return (
            (masked * sig_val).astype(jnp.bfloat16),
            (masked * proj_val * sig_val * (1.0 - sig_val)).astype(jnp.bfloat16),
        )

    d_four = jnp.concatenate(
        split_grad(d_edges[0].astype(jnp.float32), a_sig, a_proj)
        + split_grad(d_edges[1].astype(jnp.float32), b_sig, b_proj),
        axis=0,
    )
    d_hidden = jnp.einsum("gik,cg->ikc", d_four, w_four, preferred_element_type=jnp.float32)
    if ch > 1:
        d_hidden = lax.psum_scatter(
            d_hidden.astype(jnp.bfloat16), "ch", scatter_dimension=1, tiled=True
        ).astype(jnp.float32)
    d_pair_norm = d_hidden + jnp.einsum(
        "ijd,cd->ijc", d_gate, w_gate, preferred_element_type=jnp.float32
    )
    normed_cols = lax.dynamic_slice_in_dim(normed_in, col_first, col_span, 1)
    rstd_cols = lax.dynamic_slice_in_dim(rstd_in, col_first, col_span, 1)
    grad_hat = d_pair_norm * ln_in_gain
    return norm_backward(grad_hat, normed_cols, rstd_cols, 2).astype(jnp.bfloat16)


F32 = jnp.float32
BF16 = jnp.bfloat16
SUBLANES = 8
LEVELS = 4
CORES = 2


def dot(lhs, rhs, lhs_dim, rhs_dim):
    return lax.dot_general(
        lhs, rhs, (((lhs_dim,), (rhs_dim,)), ((), ())), preferred_element_type=F32
    )


def across(row, count):
    return jnp.transpose(jnp.broadcast_to(row, (count, row.shape[1])))


def exchange_bit(first, second, weight):
    sublane = lax.broadcasted_iota(jnp.int32, first.shape, 1)
    low = sublane & weight == 0
    return (
        jnp.where(low, first, pltpu.roll(second, weight, 1)),
        jnp.where(low, pltpu.roll(first, SUBLANES - weight, 1), second),
    )


def falling(blocks):
    return jnp.concatenate([blocks[at : at + 1] for at in reversed(range(blocks.shape[0]))], axis=0)


def mesh_order(blocks):
    count, *rest = blocks.shape
    split = blocks.reshape(count // LEVELS // CORES, LEVELS, CORES, *rest)
    return jnp.swapaxes(falling(split), 0, 1).reshape(blocks.shape)


def list_order(blocks):
    count, *rest = blocks.shape
    split = blocks.reshape(LEVELS, count // LEVELS // CORES, CORES, *rest)
    return falling(jnp.swapaxes(split, 0, 1)).reshape(blocks.shape)


def split_channels(blocks, own):
    devices, block, cols = blocks.shape
    tiles = blocks.reshape(devices // 2, 2, block // SUBLANES, SUBLANES, cols)
    parts = []
    for tile in range(block // SUBLANES):
        parts.extend(exchange_bit(tiles[:, 0, tile], tiles[:, 1, tile], own))
    return [part.reshape(devices * own, cols) for part in parts]


def merge_channels(parts, own):
    rows, cols = parts[0].shape
    devices = rows // own
    tiles = [part.reshape(devices // 2, SUBLANES, cols) for part in parts]
    pairs = [exchange_bit(*pair, own) for pair in zip(tiles[::2], tiles[1::2])]
    both = [jnp.concatenate(side, axis=1) for side in zip(*pairs)]
    block = len(parts) * own
    return jnp.stack(both, axis=1).reshape(devices, block, cols)


def trade(parts):
    rows, cols = parts[0].shape
    a, b, c, d = (part.reshape(rows // SUBLANES, SUBLANES, cols) for part in parts)
    (a, b), (c, d) = exchange_bit(a, b, 1), exchange_bit(c, d, 1)
    (a, c), (b, d) = exchange_bit(a, c, 2), exchange_bit(b, d, 2)
    return [part.reshape(rows, cols) for part in (a, b, c, d)]


def edges_kernel(me_ref, *refs):
    sources, (out_ref, *local), (blocks, arrived, left) = refs[:9], refs[9:19], refs[19:]
    copies = [
        pltpu.make_async_copy(source, target, arrived.at[index])
        for index, (source, target) in enumerate(zip(sources, local))
    ]
    for copy in copies:
        copy.start()
    act_ref, gain_ref, bias_ref, rows_ref, valid_ref, *weights = local
    own, cols, chan = act_ref.shape
    half = out_ref.shape[1] // 2
    for copy in copies[:3]:
        copy.wait()
    act = jnp.concatenate([jnp.transpose(act_ref[r].astype(F32)) for r in range(own)], axis=1)
    gain = across(gain_ref[...], cols)
    bias = across(bias_ref[...], cols)
    centre = act - jnp.mean(act, axis=0, keepdims=True)
    inverse = lax.rsqrt(jnp.mean(centre * centre, axis=0, keepdims=True) + EPSILON)
    wide_gain, wide_bias = (jnp.concatenate([value] * own, axis=1) for value in (gain, bias))
    pair_norm = (centre * inverse * wide_gain + wide_bias).astype(BF16)
    for copy in copies[3:]:
        copy.wait()
    valid = valid_ref[...].astype(F32)
    mask = jnp.concatenate(
        [valid * rows_ref[me_ref[0] * own + r].astype(F32) for r in range(own)], axis=1
    )
    sent = []
    for side in range(2):
        proj = dot(weights[2 * side][...], pair_norm, 0, 0)
        edge = mask * jax.nn.sigmoid(dot(weights[2 * side + 1][...], pair_norm, 0, 0)) * proj
        parts = trade([edge[:, r * cols : (r + 1) * cols] for r in range(own)])
        blocks[side] = merge_channels(parts, own).astype(BF16)
        copy = pltpu.make_async_copy(
            blocks.at[side], out_ref.at[:, side * half : (side + 1) * half, :], left.at[side]
        )
        copy.start()
        sent.append(copy)
    for copy in sent:
        copy.wait()


def gates_kernel(
    me_ref, rows_ref, valid_ref, act_ref, grad_ref, gain_ref, bias_ref, gain_out_ref, bias_out_ref,
    wap, wag, wbp, wbg, w_gate, w_out,
    factors, normed_t, rstd_t, gain_t, d_normed, slope, gain_out_t, bias_out_t,
):
    own, cols, _ = act_ref.shape
    hidden = wap.shape[1]
    valid = valid_ref[...].astype(F32)
    gain = across(gain_ref[...], cols)
    bias = across(bias_ref[...], cols)
    gain_out = across(gain_out_ref[...], cols)
    gain_t[...] = gain
    gain_out_t[...] = gain_out
    bias_out_t[...] = across(bias_out_ref[...], cols)
    for r in range(own):
        act = jnp.transpose(act_ref[r].astype(F32))
        centre = act - jnp.mean(act, axis=0, keepdims=True)
        inverse = lax.rsqrt(jnp.mean(centre * centre, axis=0, keepdims=True) + EPSILON)
        normed = centre * inverse
        lanes = pl.ds(r * cols, cols)
        normed_t[:, lanes] = normed
        rstd_t[:, lanes] = inverse
        pair_norm = (normed * gain + bias).astype(BF16)
        mask = valid * rows_ref[me_ref[0] * own + r].astype(F32)
        for side, (w_proj, w_sig) in enumerate(((wap, wag), (wbp, wbg))):
            proj = dot(w_proj[...], pair_norm, 0, 0)
            sig = jax.nn.sigmoid(dot(w_sig[...], pair_norm, 0, 0))
            kept = mask * sig
            factors[2 * side, :, lanes] = kept
            factors[2 * side + 1, :, lanes] = kept * proj * (1.0 - sig)
        gate_act = jax.nn.sigmoid(dot(w_gate[...], pair_norm, 0, 0))
        d_proj = jnp.transpose(grad_ref[r].astype(F32)) * gate_act
        slope[:, lanes] = d_proj * (1.0 - gate_act)
        d_normed[pl.ds(r, hidden, stride=own), :] = (
            dot(w_out[...], d_proj.astype(BF16), 1, 0) * gain_out
        )


def triangle_kernel(own, in_ref, _, out_ref, a_ref, b_ref):
    half = out_ref.shape[1]
    sides = [
        split_channels(
            mesh_order(in_ref[:, side * half : (side + 1) * half, :].astype(F32)), own
        )
        for side in range(2)
    ]
    tri = []
    for c, (edge_a, edge_b) in enumerate(zip(*sides)):
        a_ref[c] = edge_a.astype(BF16)
        b_ref[c] = edge_b.astype(BF16)
        tri.append(dot(a_ref[c], b_ref[c], 1, 1))
    out_ref[...] = list_order(merge_channels(tri, own)).astype(BF16)


def fold(values, own):
    total = jnp.sum(values, axis=0)
    rows = total
    for shift in range(own, SUBLANES, own):
        rows = rows + pltpu.roll(total, shift, 0)
    return rows[None]


def tri_normed(tri_ref, hidden, own):
    cols = tri_ref.shape[-1]
    tri = tri_ref[...].astype(F32).reshape(hidden * own // SUBLANES, SUBLANES, cols)
    centre = tri - fold(tri, own) / hidden
    inverse = lax.rsqrt(fold(centre * centre, own) / hidden + EPSILON)
    return centre * inverse, inverse


def norm_kernel(own, tri_ref, grad_ref, slope, gain, bias, w_out, out_ref, gate_ref):
    devices, block, cols = tri_ref.shape
    hidden = w_out.shape[0]
    normed, inverse = tri_normed(tri_ref, hidden, own)
    grad = grad_ref[...].reshape(normed.shape)
    mean_grad = fold(grad, own) / hidden
    mean_proj = fold(grad * normed, own) / hidden
    d_tri = inverse * (grad - mean_grad - normed * mean_proj)
    out_ref[...] = d_tri.reshape(devices, block, cols).astype(BF16)
    parts = trade(split_channels(normed.reshape(devices, block, cols), own))
    tri_norm = jnp.concatenate([(part * gain[...] + bias[...]).astype(BF16) for part in parts], axis=1)
    gate_ref[...] = (slope[...] * dot(w_out[...], tri_norm, 0, 0)).astype(BF16)


def edge_grad_kernel(own, in_ref, a_ref, b_ref, out_ref):
    block = in_ref.shape[1]
    grads = ([], [])
    for c, part in enumerate(split_channels(mesh_order(in_ref[...].astype(F32)), own)):
        d_tri = part.astype(BF16)
        grads[0].append(dot(d_tri, b_ref[c], 1, 0))
        grads[1].append(dot(d_tri, a_ref[c], 0, 0))
    for side in range(2):
        out_ref[:, side * block : (side + 1) * block, :] = (
            list_order(merge_channels(grads[side], own)).astype(BF16)
        )


def input_grad_kernel(
    in_ref, factors, normed_t, rstd_t, gain_t, d_gate, wap, wag, wbp, wbg, w_gate, out_ref
):
    own, cols, _ = out_ref.shape
    half = in_ref.shape[1] // 2
    grads = []
    for side in range(2):
        blocks = in_ref[:, side * half : (side + 1) * half, :].astype(F32)
        d_edge = jnp.concatenate(trade(split_channels(blocks, own)), axis=1)
        for at in range(2):
            grads.append((d_edge * factors[2 * side + at]).astype(BF16))
    weights = [weight[...] for weight in (wap, wag, wbp, wbg, w_gate)]
    grads.append(d_gate[...])
    total = dot(jnp.concatenate(weights, axis=1), jnp.concatenate(grads, axis=0), 1, 0)
    grad_hat = total * jnp.concatenate([gain_t[...]] * own, axis=1)
    normed = normed_t[...]
    mean_grad = jnp.mean(grad_hat, axis=0, keepdims=True)
    mean_proj = jnp.mean(grad_hat * normed, axis=0, keepdims=True)
    grad = rstd_t[...] * (grad_hat - mean_grad - normed * mean_proj)
    for r in range(own):
        out_ref[r] = jnp.transpose(grad[:, r * cols : (r + 1) * cols]).astype(BF16)


VMEM = pl.BlockSpec(memory_space=pltpu.VMEM)
SMEM = pl.BlockSpec(memory_space=pltpu.SMEM)
HBM = pl.BlockSpec(memory_space=pltpu.HBM)


def call(kernel, name, outs, args, scratch=(), scalars=0, flops=0, spaces=None, to=VMEM, limit=32 * 2**20):
    shapes = [jax.ShapeDtypeStruct(shape, dtype) for shape, dtype in outs]
    moved = sum(value.size * value.dtype.itemsize for value in list(args) + shapes)
    result = pl.pallas_call(
        kernel,
        name=name,
        out_shape=shapes,
        in_specs=[SMEM] * scalars + (spaces or [VMEM] * (len(args) - scalars)),
        out_specs=[to] * len(outs),
        scratch_shapes=scratch,
        cost_estimate=pl.CostEstimate(flops=flops, bytes_accessed=moved, transcendentals=0),
        compiler_params=pltpu.CompilerParams(vmem_limit_bytes=limit),
    )(*args)
    return result[0] if len(outs) == 1 else result


def kernel_shards(
    dap,
    pair_act,
    out_grad,
    residue_mask,
    ln_in_gain,
    ln_in_bias,
    w_a_proj,
    w_a_gate,
    w_b_proj,
    w_b_gate,
    w_gate,
    ln_out_gain,
    ln_out_bias,
    w_out,
):
    own, cols, chan = pair_act.shape
    hidden = w_a_proj.shape[1]
    slice_h = hidden // dap
    rows = dap * own
    block = slice_h * own
    me = lax.axis_index("dap").reshape(1)
    valid = residue_mask.reshape(1, -1)
    gain_in, bias_in, gain_out, bias_out = (
        value.reshape(1, -1) for value in (ln_in_gain, ln_in_bias, ln_out_gain, ln_out_bias)
    )
    w_edges = (w_a_proj, w_a_gate, w_b_proj, w_b_gate)
    product = 2 * own * cols * chan * hidden

    span = dap // LEVELS
    listed = [
        quarter * span + pair * CORES + core
        for pair in reversed(range(span // CORES))
        for quarter in range(LEVELS)
        for core in range(CORES)
    ]

    def exchange(value):
        return lax.all_to_all(
            value, "dap", split_axis=0, concat_axis=0, axis_index_groups=[listed], tiled=True
        )

    first = (pair_act, gain_in, bias_in, residue_mask, valid, *w_edges)
    edges = call(
        edges_kernel,
        "edges",
        [((dap, 2 * block, cols), BF16)],
        (me, *first),
        scratch=[
            (pltpu.SMEM if value is residue_mask else pltpu.VMEM)(value.shape, value.dtype)
            for value in first
        ]
        + [pltpu.VMEM((2, dap, block, cols), BF16)]
        + [pltpu.SemaphoreType.DMA((len(first),)), pltpu.SemaphoreType.DMA((2,))],
        scalars=1,
        flops=4 * product,
        to=HBM,
        spaces=[HBM] * len(first),
        limit=None,
    )
    edges = exchange(edges)
    factors, normed_t, rstd_t, gain_t, d_normed, slope, gain_out_t, bias_out_t = call(
        gates_kernel,
        "gates",
        [
            ((4, hidden, own * cols), F32),
            ((chan, own * cols), F32),
            ((1, own * cols), F32),
            ((chan, cols), F32),
            ((hidden * own, cols), F32),
            ((chan, own * cols), F32),
            ((hidden, cols), F32),
            ((hidden, cols), F32),
        ],
        (me, residue_mask, valid, pair_act, out_grad, gain_in, bias_in, gain_out)
        + (bias_out, *w_edges, w_gate, w_out),
        scalars=2,
        flops=6 * product,
    )
    tri, edge_a, edge_b = call(
        functools.partial(triangle_kernel, own),
        "triangle",
        [
            ((dap, block, cols), BF16),
            ((slice_h, rows, cols), BF16),
            ((slice_h, rows, cols), BF16),
        ],
        (edges, d_normed),
        flops=product,
        spaces=[VMEM, pl.BlockSpec(memory_space=pl.ANY)],
    )
    tri = exchange(tri)
    d_tri, d_gate = call(
        functools.partial(norm_kernel, own),
        "norm",
        [((dap, block, cols), BF16), ((chan, own * cols), BF16)],
        (tri, d_normed, slope, gain_out_t, bias_out_t, w_out),
        flops=2 * product,
    )
    d_tri = exchange(d_tri)
    d_edges = call(
        functools.partial(edge_grad_kernel, own),
        "edge_grad",
        [((dap, 2 * block, cols), BF16)],
        (d_tri, edge_a, edge_b),
        flops=2 * product,
    )
    d_edges = exchange(d_edges)
    return call(
        input_grad_kernel,
        "input_grad",
        [((own, cols, chan), BF16)],
        (d_edges, factors, normed_t, rstd_t, gain_t, d_gate, *w_edges, w_gate),
        flops=4 * product,
    )


def fits_kernels(dap, ch, pair_act, w_proj):
    own, cols, chan = pair_act.shape
    hidden = w_proj.shape[1]
    block = hidden // dap * own
    return (
        ch == 1
        and hidden % dap == 0
        and own == SUBLANES // 2
        and block == own * own
        and dap % SUBLANES == 0
        and cols == dap * own
        and cols % 128 == chan % 128 == hidden % 128 == 0
    )


def solution(mesh):
    sizes = dict(mesh.shape)

    def program(*args):
        dap, ch = sizes["dap"], sizes["ch"]
        if fits_kernels(dap, ch, args[0], args[5]):
            return kernel_shards(dap, *args)
        return channel_shards(dap, ch, *args)

    in_specs = (
        P(("grp", "dap"), None, None),
        P(("grp", "dap"), "ch", None),
        P("grp"),
        P(),
        P(),
        P(None, "ch"),
        P(None, "ch"),
        P(None, "ch"),
        P(None, "ch"),
        P(),
        P(),
        P(),
        P(),
    )
    out_specs = P(("grp", "dap"), "ch", None)
    return jax.shard_map(
        program, mesh=mesh, in_specs=in_specs, out_specs=out_specs, check_vma=False
    )
```
